32 devices in a mesh: shot: 2 (over x), gx: 4 (over y, core), gy: 4 (over z).
Axes of the slice: x: 2, y: 2, z: 4, core: 2. Of those that a mesh axis runs over, the one named last changes fastest.
Arguments:
- velocity: bfloat16 [64, 32, 128], P('gx', 'gy'), may hold values from 0.024902344 to 0.079589844
- epsilon: bfloat16 [64, 32, 128], P('gx', 'gy'), may hold values from 0 to 0.29882812
- delta: bfloat16 [64, 32, 128], P('gx', 'gy'), may hold values from -0.099609375 to 0.14941406
- tilt: bfloat16 [64, 32, 128], P('gx', 'gy'), may hold values from -1.5 to 1.5
- azimuth: bfloat16 [64, 32, 128], P('gx', 'gy'), may hold values from -3.140625 to 3.140625
- aperture: int32 [8], P('shot'), parts along dimension 0, may hold values from 0 to 3
- source_cell: int32 [2], P('shot'), parts along dimension 0, may hold values from 0 to 2047
- wavelet: float32 [16], P('shot'), parts along dimension 0, may hold values from -24 to 24
- receiver_cell: int32 [1024], P('shot'), parts along dimension 0, may hold values from 0 to 2047
- traces: float32 [8, 1024], P(None, 'shot'), parts along dimension 1, may hold values from -12 to 12
- source_state: float32 [4, 128, 32, 128], P(None, ('shot', 'gx'), 'gy'), parts along dimension 1, may hold values from -6 to 6
- receiver_state: float32 [4, 128, 32, 128], P(None, ('shot', 'gx'), 'gy'), parts along dimension 1, may hold values from -6 to 6
Outputs:
- image: float32 [128, 32, 128], P(('shot', 'gx'), 'gy'), parts along dimension 0
- receiver_field: float32 [2, 128, 32, 128], P(None, ('shot', 'gx'), 'gy'), parts along dimension 1
The draws below stay inside these ranges and needn't reach their ends.
There are 2 independent parts, one for each index of `shot`. The reference program is written for one: setup_inputs(seed, part) draws one part's arguments, and reference() takes and returns one part's arrays. A program takes and returns all parts, laid end to end along the dimension named above; an argument that names none is the same for every part. Nothing has to cross between parts.
Inputs may be any that keep to these rules, and one draw needn't show every extreme that they name: `aperture`: several tile columns may read the same model block column, and some model block columns may be read by none. `source_cell`: the source sits at surface position x * 32 + y. `receiver_cell`: receiver positions are x * 32 + y; several receivers may share a cell.
All inputs are finite; a program needn't handle non-finite values.
Results may differ from the reference program's by a relative error of at most 0.0003.
Values may be sent and summed in bfloat16 or wider, within the bound.
No kernel may reach another device: no remote copies, remote signals or barrier semaphores. Data moves between devices by JAX's collectives and lax.ppermute only.
A program may use at most 64 MiB of HBM per device.

```python
import math
import jax
import jax.numpy as jnp
from jax import lax

CZ = 128
NREC = 512
NT = 8
SRC_DEPTH = 10
REC_DEPTH = 6
BLOCKS = 4
NX = 64
NY = 32
N_GX = 4


def set_ends(result, rng, smallest, top_value):
    extent = result.shape
    index_at = [jax.random.randint(jax.random.fold_in(rng, axis), (), 0, extent[axis]) for axis in range(len(extent))]
    result = result.at[tuple(index_at)].set(smallest)
    longest = extent.index(max(extent))
    index_at[longest] = (index_at[longest] + 1) % extent[longest]
    return result.at[tuple(index_at)].set(top_value)


def steps_of(stream_key, extent, shards, least, largest):
    loudness = 1.0
    for axis_at, blocks in shards:
        steps = jax.random.uniform(jax.random.fold_in(jax.random.fold_in(stream_key, 6), axis_at), (blocks,), jnp.float32, least / len(shards), largest / len(shards))
        loudness = loudness * jnp.repeat(jnp.exp(steps), extent[axis_at] // blocks).reshape((-1,) + (1,) * (len(extent) - 1 - axis_at))
    return loudness


def bell_draw(stream_key, extent, deviation, bound, pieces=(), dtype=jnp.bfloat16):
    factor_of = steps_of(stream_key, extent, pieces, -0.22, 0.18) if pieces else 1.0
    entries = jax.random.normal(stream_key, extent, jnp.float32) * deviation * factor_of
    return jnp.minimum(jnp.maximum(entries, -bound), bound).astype(dtype)


def setup_inputs(seed: int = 0, part: int = 0) -> dict:
    streams_of = jax.random.split(jax.random.key(seed), 13)
    own_keys = jax.random.split(jax.random.fold_in(streams_of[12], part), 13)
    return {
        "velocity": jnp.clip(jnp.exp(math.log(0.079589844) - 1.1619246 * jax.random.uniform(streams_of[0], (NX, NY, CZ), jnp.float32) ** steps_of(streams_of[0], (NX, NY, CZ), ((0, 4), (1, 4)), -0.2, 0.2)), 0.024902344, 0.079589844).astype(jnp.bfloat16),
        "epsilon": jnp.clip(0.29882812 * jax.random.uniform(streams_of[1], (NX, NY, CZ), jnp.float32) ** steps_of(streams_of[1], (NX, NY, CZ), ((0, 4), (1, 4)), -0.2, 0.2), 0.0, 0.29882812).astype(jnp.bfloat16),
        "delta": jnp.clip(-0.099609375 + 0.24902344 * jax.random.uniform(streams_of[2], (NX, NY, CZ), jnp.float32) ** steps_of(streams_of[2], (NX, NY, CZ), ((0, 4), (1, 4)), -0.2, 0.2), -0.099609375, 0.14941406).astype(jnp.bfloat16),
        "tilt": jnp.clip(jax.random.uniform(streams_of[3], (NX, NY, CZ), jnp.float32, -1.5, 1.5) * steps_of(streams_of[3], (NX, NY, CZ), ((0, 4), (1, 4)), -0.4, 0.0), -1.5, 1.5).astype(jnp.bfloat16),
        "azimuth": jnp.clip(jax.random.uniform(streams_of[4], (NX, NY, CZ), jnp.float32, -3.140625, 3.140625), -3.140625, 3.140625).astype(jnp.bfloat16),
        "aperture": set_ends(jax.random.randint(own_keys[5], (BLOCKS,), 0, BLOCKS), jax.random.fold_in(own_keys[5], 1), 0, BLOCKS - 1).astype(jnp.int32),
        "source_cell": jax.random.randint(own_keys[6], (1,), 0, NX * NY).astype(jnp.int32),
        "wavelet": bell_draw(own_keys[7], (NT,), 4.0, 24.0, (), jnp.float32),
        "receiver_cell": set_ends(jax.random.randint(own_keys[8], (NREC,), 0, NX * NY), jax.random.fold_in(own_keys[8], 1), 0, (NX * NY) - 1).astype(jnp.int32),
        "traces": bell_draw(own_keys[9], (NT, NREC), 2.0, 12.0, (), jnp.float32),
        "source_state": bell_draw(own_keys[10], (4, NX, NY, CZ), 1.0, 6.0, ((1, 4), (2, 4)), jnp.float32),
        "receiver_state": bell_draw(own_keys[11], (4, NX, NY, CZ), 1.0, 6.0, ((1, 4), (2, 4)), jnp.float32),
    }


second_taps = (-205.0 / 72.0, 8.0 / 5.0, -1.0 / 5.0, 8.0 / 315.0, -1.0 / 560.0)
first_taps = (4.0 / 5.0, -1.0 / 5.0, 4.0 / 105.0, -1.0 / 280.0)

def window(values, direction, start, number):
    return lax.slice_in_dim(values, start, start + number, axis=direction)

def second_along(values, direction):
    number = values.shape[direction] - 8
    summed = second_taps[0] * window(values, direction, 4, number)
    for offset in range(1, 5):
        summed = summed + second_taps[offset] * (window(values, direction, 4 + offset, number) + window(values, direction, 4 - offset, number))
    return summed

def first_along(values, direction):
    number = values.shape[direction] - 8
    summed = first_taps[0] * (window(values, direction, 5, number) - window(values, direction, 3, number))
    for offset in range(2, 5):
        summed = summed + first_taps[offset - 1] * (window(values, direction, 4 + offset, number) - window(values, direction, 4 - offset, number))
    return summed

def curvatures(wavefield):
    padded = jnp.pad(wavefield, ((0, 0), (0, 0), (4, 4)))
    curve_xx = second_along(padded[:, 4:-4, 4:-4], 0)
    curve_yy = second_along(padded[4:-4, :, 4:-4], 1)
    curve_zz = second_along(padded[4:-4, 4:-4, :], 2)
    slope_y = first_along(padded, 1)
    curve_xy = first_along(slope_y[:, :, 4:-4], 0)
    curve_yz = first_along(slope_y[4:-4], 2)
    slope_x = first_along(padded[:, 4:-4, :], 0)
    curve_xz = first_along(slope_x, 2)
    return (curve_xx, curve_yy, curve_zz, curve_xy, curve_yz, curve_xz)

def medium(velocity, epsilon, delta, tilt, azimuth):
    speed = velocity.astype(jnp.float32)
    stretch = epsilon.astype(jnp.float32)
    bending = delta.astype(jnp.float32)
    sin_tilt = jnp.sin(tilt.astype(jnp.float32))
    cos_tilt = jnp.cos(tilt.astype(jnp.float32))
    sin_azim = jnp.sin(azimuth.astype(jnp.float32))
    cos_azim = jnp.cos(azimuth.astype(jnp.float32))
    normal_x = sin_tilt * cos_azim
    normal_y = sin_tilt * sin_azim
    normal_z = cos_tilt
    return (speed, speed * (1.0 + 2.0 * stretch), speed * jnp.sqrt(1.0 + 2.0 * bending), normal_x * normal_x, normal_y * normal_y, normal_z * normal_z, 2.0 * normal_x * normal_y, 2.0 * normal_y * normal_z, 2.0 * normal_x * normal_z)

def leap(pressure, partner, pressure_old, partner_old, coefs):
    speed, speed_h, speed_v = (coefs[0], coefs[1], coefs[2])
    weights = coefs[3:]

    def tilted(curves):
        summed = weights[0] * curves[0]
        for member in range(1, 6):
            summed = summed + weights[member] * curves[member]
        return summed
    curve_p = curvatures(pressure)
    curve_q = curvatures(partner)
    tilted_p = tilted(curve_p)
    flat_p = curve_p[0] + curve_p[1] + curve_p[2] - tilted_p
    tilted_q = tilted(curve_q)
    middle_p = pressure[4:-4, 4:-4]
    middle_q = partner[4:-4, 4:-4]
    pressure_new = 2.0 * middle_p - pressure_old + (speed_h * flat_p + speed_v * tilted_q)
    partner_new = 2.0 * middle_q - partner_old + (speed_v * flat_p + speed * tilted_q)
    return (pressure_new, partner_new)

def spread(cells, amounts, start_x, start_y, extent_x, extent_y, span_y):
    across = cells // span_y - start_x
    along = cells % span_y - start_y
    row_hits = (across[:, None] == jnp.arange(extent_x)[None, :]).astype(jnp.float32)
    col_hits = (along[:, None] == jnp.arange(extent_y)[None, :]).astype(jnp.float32) * amounts[:, None]
    return jnp.dot(row_hits.T, col_hits, precision=lax.Precision.HIGHEST, preferred_element_type=jnp.float32)

def tile_model(model, aperture):
    width = model.shape[0] // N_GX
    blocks = [lax.dynamic_slice_in_dim(model, (aperture[member] * width).astype(jnp.int32), width, 0) for member in range(N_GX)]
    return jnp.concatenate(blocks, axis=0)

def reference(velocity, epsilon, delta, tilt, azimuth, aperture, source_cell, wavelet, receiver_cell, traces, source_state, receiver_state):
    coefs = medium(*[tile_model(model, aperture) for model in (velocity, epsilon, delta, tilt, azimuth)])
    margin = ((4, 4), (4, 4), (0, 0))

    def evolve(state, planner, level):
        current, earlier, partner, partner_old = (state[0], state[1], state[2], state[3])
        history = []
        for moment in range(1, NT + 1):
            following, partner_next = leap(jnp.pad(current, margin), jnp.pad(partner, margin), earlier, partner_old, coefs)
            plane = planner(moment)
            following = following.at[:, :, level].add(plane)
            partner_next = partner_next.at[:, :, level].add(plane)
            history.append(following)
            earlier, current, partner_old, partner = (current, following, partner, partner_next)
        return (history, current, partner)

    def source_plane(moment):
        amounts = jnp.broadcast_to(wavelet[moment - 1], source_cell.shape)
        return spread(source_cell, amounts, 0, 0, NX, NY, NY)

    def receiver_plane(moment):
        return spread(receiver_cell, traces[NT - moment], 0, 0, NX, NY, NY)
    source_history, source_last, source_aux = evolve(source_state, source_plane, SRC_DEPTH)
    receiver_history, receiver_last, receiver_aux = evolve(receiver_state, receiver_plane, REC_DEPTH)
    image = jnp.zeros(source_last.shape, jnp.float32)
    for moment in range(1, NT + 1):
        receiver_now = receiver_state[0] if moment == NT else receiver_history[NT - moment - 1]
        image = image + source_history[moment - 1] * receiver_now
    image = image / NT
    return (image, jnp.stack([receiver_last, receiver_aux]))
```

```python
import functools

import jax
import jax.numpy as jnp
from jax import lax
from jax.experimental import pallas as pl
from jax.experimental.pallas import tpu as pltpu
from jax.sharding import PartitionSpec as P

NT = 8
SRC_DEPTH = 10
REC_DEPTH = 6
HALO = 4
F32 = jnp.float32
BF16 = jnp.bfloat16

second_taps = (-205.0 / 72.0, 8.0 / 5.0, -1.0 / 5.0, 8.0 / 315.0, -1.0 / 560.0)
first_taps = (4.0 / 5.0, -1.0 / 5.0, 4.0 / 105.0, -1.0 / 280.0)
S1 = second_taps[1]
G1 = first_taps[0]
second_ratio = tuple(tap / S1 for tap in second_taps[2:])
first_ratio = tuple(tap / G1 for tap in first_taps[1:])
second_whole = (8064.0, -1008.0, 128.0, -9.0)
first_whole = (672.0, -168.0, 32.0, -3.0)
SECOND_UNIT = 1.0 / 5040.0
FIRST_UNIT = 1.0 / 840.0
VMEM = pl.BlockSpec(memory_space=pltpu.VMEM)
SMEM = pl.BlockSpec(memory_space=pltpu.SMEM)


def even_pairs(count):
    return [(i, i + 1) for i in range(0, count - 1, 2)]


def odd_pairs(count):
    return [(i, i + 1) for i in range(1, count - 1, 2)]


def both_ways(pairs):
    return [pair for a, b in pairs for pair in ((a, b), (b, a))]


def chip_swap(pairs):
    return [(2 * a + c, 2 * b + c) for a, b in pairs for c in range(2)]


def depth_matrices(size):
    rows = jnp.arange(size)[:, None]
    cols = jnp.arange(size)[None, :]
    first = jnp.zeros((size, size), F32)
    second = jnp.zeros((size, size), F32)
    for k in range(1, 5):
        up = (rows == cols + k).astype(F32)
        down = (rows == cols - k).astype(F32)
        first = first + first_whole[k - 1] * (up - down)
        second = second + second_whole[k - 1] * (up + down)
    return (
        jnp.concatenate([first, first]).astype(BF16),
        jnp.concatenate([second, second]).astype(BF16),
    )


def sums_and_slopes(shifted):
    up, down = shifted(1), shifted(-1)
    curve, slope = up + down, up - down
    for k in range(2, 5):
        up, down = shifted(k), shifted(-k)
        curve = curve + second_ratio[k - 2] * (up + down)
        slope = slope + first_ratio[k - 2] * (up - down)
    return curve, slope


def slope_only(shifted):
    slope = shifted(1) - shifted(-1)
    for k in range(2, 5):
        slope = slope + first_ratio[k - 2] * (shifted(k) - shifted(-k))
    return slope


def split(values):
    high = values.astype(BF16)
    low = (values - high.astype(F32)).astype(BF16)
    return high, low


def leap_in_kernel(src, x0, row0, rows, count, scratch, mats, old_at, coef_at, inject_at, store):
    slope_y, curve_y, parts, parts_z, slope_x = scratch
    mat_first, mat_second = mats
    group = 4

    def along_y(p, carry):
        for f in range(2):
            curve, slope = sums_and_slopes(
                lambda k: src[f, x0 + p, pl.ds(row0 + k, rows), :]
            )
            slope_y[f, p, :rows] = slope
            curve_y[f, p, :rows] = curve
        return carry

    lax.fori_loop(0, count + 8, along_y, 0, unroll=2)

    def along_x(q, carry):
        base = q * group
        for f in range(2):
            for r in range(0, rows, 8):
                line = [src[f, x0 + base + k, pl.ds(row0 + r, 8), :] for k in range(group + 8)]
                slant = [slope_y[f, base + k, pl.ds(r, 8), :] for k in range(group + 8)]
                for g in range(group):
                    curve, slope = sums_and_slopes(lambda k: line[g + 4 + k])
                    parts[0, f, base + g, pl.ds(r, 8), :] = curve
                    slope_x[f, base + g, pl.ds(r, 8), :] = slope
                    parts[1, f, base + g, pl.ds(r, 8), :] = slope_only(lambda k: slant[g + 4 + k])
        return carry

    lax.fori_loop(0, count // group, along_x, 0)

    lines = count * rows
    for f in range(2):
        field = src[f, pl.ds(x0 + 4, count), pl.ds(row0, rows), :].reshape(lines, 128)
        tilt_y = slope_y[f, pl.ds(4, count), :rows, :].reshape(lines, 128)
        tilt_x = slope_x[f, pl.ds(0, count), :rows, :].reshape(lines, 128)
        for slot, (values, mat) in enumerate(
            ((field, mat_second), (tilt_y, mat_first), (tilt_x, mat_first))
        ):
            both = jnp.concatenate(split(values), axis=1)
            product = jnp.dot(both, mat[...], preferred_element_type=F32)
            parts_z[slot, f, pl.ds(0, count), :rows, :] = product.reshape(count, rows, 128)

    def combine(i, carry):
        speed, speed_h, speed_v, wx, wy, wz, wxy, wyz, wxz = coef_at(i)
        add = inject_at(i)
        fields = []
        for f in range(2):
            xx = parts[0, f, i, :rows]
            xy = parts[1, f, i, :rows]
            yy = curve_y[f, i + 4, :rows]
            zz = parts_z[0, f, i, :rows]
            yz = parts_z[1, f, i, :rows]
            xz = parts_z[2, f, i, :rows]
            here = src[f, x0 + i + 4, pl.ds(row0, rows), :]
            mixed = wxy * xy + wyz * yz + wxz * xz
            if f == 0:
                fields.append(
                    (2.0 * second_taps[0]) * here
                    + (S1 - wx) * xx
                    + (S1 - wy) * yy
                    + (SECOND_UNIT - wz) * zz
                    - mixed
                )
            else:
                fields.append(second_taps[0] * here + wx * xx + wy * yy + wz * zz + mixed)
        flat, tilted = fields
        now_p = src[0, x0 + i + 4, pl.ds(row0, rows), :]
        now_q = src[1, x0 + i + 4, pl.ds(row0, rows), :]
        new_p = 2.0 * now_p - old_at(0, i) + (speed_h * flat + speed_v * tilted) + add
        new_q = 2.0 * now_q - old_at(1, i) + (speed_v * flat + speed * tilted) + add
        store(i, new_p, new_q)
        return carry

    lax.fori_loop(0, count, combine, 0, unroll=2)


def stride_kernel(
    moment, wide, count, size_x, size_y,
    place, own, got_even, got_odd, old, coefs, inject, mat_first, mat_second,
    tile_out, edge_out, old_out, hist_out,
    window, middle, slope_y, curve_y, parts, parts_z, slope_x,
):
    first_at, tile_at, parity, level, edge_at = (place[0], place[1], place[2], place[3], place[4])
    scratch = (slope_y, curve_y, parts, parts_z, slope_x)
    mats = (mat_first, mat_second)
    lane = lax.broadcasted_iota(jnp.int32, (8, 128), 1)
    mask = (lane == level).astype(F32)

    for f in range(2):
        window[f, pl.ds(0, 4)] = jnp.zeros((4, 32, 128), F32)
        window[f, pl.ds(wide + 4, 4)] = jnp.zeros((4, 32, 128), F32)
        middle[f, pl.ds(0, 4)] = jnp.zeros((4, 24, 128), F32)
        middle[f, pl.ds(count + 4, 4)] = jnp.zeros((4, 24, 128), F32)
        window[f, pl.ds(4, wide), pl.ds(12, 8), :] = own[f]

    @pl.when(parity == 0)
    def _():
        for f in range(2):
            window[f, pl.ds(4, wide), pl.ds(4, 8), :] = got_odd[f]
            window[f, pl.ds(4, wide), pl.ds(20, 8), :] = got_even[f]

    @pl.when(parity == 1)
    def _():
        for f in range(2):
            window[f, pl.ds(4, wide), pl.ds(4, 8), :] = got_even[f]
            window[f, pl.ds(4, wide), pl.ds(20, 8), :] = got_odd[f]

    def store_first(i, new_p, new_q):
        for f, new in enumerate((new_p, new_q)):
            old_out[f, i] = new
            middle[f, i + 4, pl.ds(4, size_y + 8), :] = new

    leap_in_kernel(
        window, first_at, 8, size_y + 8, count, scratch, mats,
        lambda f, i: old[f, i],
        lambda i: [coefs[m, i] for m in range(9)],
        lambda i: jnp.concatenate(
            [inject[i, pl.ds(r, 8), moment : moment + 1] * mask for r in range(0, size_y + 8, 8)]
        ),
        store_first,
    )

    def store_second(i, new_p, new_q):
        tile_out[0, i] = new_p
        tile_out[1, i] = new_q
        hist_out[i] = middle[0, tile_at + i + 4, pl.ds(8, size_y), :]

    leap_in_kernel(
        middle, tile_at, 8, size_y, size_x, scratch, mats,
        lambda f, i: own[f, first_at + tile_at + i],
        lambda i: [coefs[m, tile_at + i, pl.ds(4, size_y), :] for m in range(9)],
        lambda i: inject[tile_at + i, pl.ds(4, size_y), moment + 1 : moment + 2] * mask,
        store_second,
    )
    for f in range(2):
        edge_out[f] = tile_out[f, pl.ds(edge_at, 8)]


def stride(moment, place, own, got_even, got_odd, old, coefs, inject, mats):
    wide, size_y = own.shape[1], own.shape[2]
    count = old.shape[1]
    size_x = 32
    rows = size_y + 8
    return pl.pallas_call(
        functools.partial(stride_kernel, moment, wide, count, size_x, size_y),
        out_shape=(
            jax.ShapeDtypeStruct((2, size_x, size_y, 128), F32),
            jax.ShapeDtypeStruct((2, 8, size_y, 128), F32),
            jax.ShapeDtypeStruct((2, count, rows, 128), F32),
            jax.ShapeDtypeStruct((size_x, size_y, 128), F32),
        ),
        in_specs=[SMEM] + [VMEM] * 8,
        out_specs=(VMEM,) * 4,
        scratch_shapes=[
            pltpu.VMEM((2, wide + 8, 32, 128), F32),
            pltpu.VMEM((2, count + 8, 24, 128), F32),
            pltpu.VMEM((2, count + 8, rows, 128), F32),
            pltpu.VMEM((2, count + 8, rows, 128), F32),
            pltpu.VMEM((2, 2, count, rows, 128), F32),
            pltpu.VMEM((3, 2, count, rows, 128), F32),
            pltpu.VMEM((2, count, rows, 128), F32),
        ],
        compiler_params=pltpu.CompilerParams(vmem_limit_bytes=40 * 2**20),
        name="stride",
    )(place, own, got_even, got_odd, old, coefs, inject, *mats)


def sine_cosine(angle):
    square = angle * angle
    sine = 1.0 / 6227020800.0
    for factor in (-1.0 / 39916800.0, 1.0 / 362880.0, -1.0 / 5040.0, 1.0 / 120.0, -1.0 / 6.0):
        sine = sine * square + factor
    sine = angle + angle * square * sine
    cosine = 1.0 / 479001600.0
    for factor in (-1.0 / 3628800.0, 1.0 / 40320.0, -1.0 / 720.0, 1.0 / 24.0, -0.5):
        cosine = cosine * square + factor
    return sine, 1.0 + square * cosine


def setup_kernel(
    count, size_x, size_y, total_x, total_y,
    place, aperture, model, cells, amounts, coefs, inject, hits,
):
    start_x, start_y = place[0], place[1]
    rows = size_y + 8

    def medium(i, carry):
        x = start_x + i
        block = jnp.clip(x // size_x, 0, total_x // size_x - 1)
        inside = jnp.logical_and(x >= 0, x < total_x)
        at = aperture[block] * size_x + lax.rem(x + size_x, size_x)
        speed, stretch, bending, tilt, azimuth = [model[m, at].astype(F32) for m in range(5)]
        speed = jnp.where(inside, speed, 0.0)
        sin_t, cos_t = sine_cosine(tilt)
        sin_half, cos_half = sine_cosine(0.5 * azimuth)
        normal_x = sin_t * (1.0 - 2.0 * sin_half * sin_half)
        normal_y = sin_t * (2.0 * sin_half * cos_half)
        coefs[0, i] = speed
        coefs[1, i] = speed * (1.0 + 2.0 * stretch)
        coefs[2, i] = speed * jnp.sqrt(1.0 + 2.0 * bending)
        coefs[3, i] = S1 * (normal_x * normal_x)
        coefs[4, i] = S1 * (normal_y * normal_y)
        coefs[5, i] = SECOND_UNIT * (cos_t * cos_t)
        coefs[6, i] = (2.0 * G1 * G1) * (normal_x * normal_y)
        coefs[7, i] = (2.0 * G1 * FIRST_UNIT) * (normal_y * cos_t)
        coefs[8, i] = (2.0 * G1 * FIRST_UNIT) * (normal_x * cos_t)
        return carry

    lax.fori_loop(0, count, medium, 0, unroll=2)

    number = cells.shape[1]
    row = lax.broadcasted_iota(jnp.int32, (rows, number), 0)

    def mark(i, carry):
        y = start_y + row
        code = (start_x + i) * total_y + y
        code = jnp.where(jnp.logical_and(y >= 0, y < total_y), code, -2)
        hits[i] = jnp.where(code == cells[...], 1.0, 0.0).astype(BF16)
        return carry

    lax.fori_loop(0, count, mark, 0)
    rest = amounts[...]
    total = None
    for _ in range(3):
        piece = rest.astype(BF16)
        rest = rest - piece.astype(F32)
        term = lax.dot_general(
            hits[...].reshape(count * rows, number), piece, (((1,), (1,)), ((), ())),
            preferred_element_type=F32,
        )
        total = term if total is None else total + term
    inject[...] = total.reshape(count, rows, NT)


def setup(place, aperture, model, cells, amounts, count, total_x, total_y, size_x):
    rows = model.shape[2]
    return pl.pallas_call(
        functools.partial(setup_kernel, count, size_x, rows - 8, total_x, total_y),
        out_shape=(
            jax.ShapeDtypeStruct((9, count, rows, 128), F32),
            jax.ShapeDtypeStruct((count, rows, NT), F32),
        ),
        in_specs=[SMEM, SMEM, VMEM, VMEM, VMEM],
        out_specs=(VMEM, VMEM),
        scratch_shapes=[pltpu.VMEM((count, rows, cells.shape[1]), BF16)],
        compiler_params=pltpu.CompilerParams(vmem_limit_bytes=40 * 2**20),
        name="setup",
    )(place, aperture, model, cells, amounts)


def pack_kernel(size, place, last_q, *refs):
    levels, out = refs[: NT + 1], refs[NT + 1]
    core = place[0]

    @pl.when(core == 0)
    def _():
        for t in range(NT):
            out[t] = levels[t + 1][pl.ds(size, size)]
        out[NT] = jnp.zeros(out.shape[1:], F32)
        out[NT + 1] = jnp.zeros(out.shape[1:], F32)

    @pl.when(core == 1)
    def _():
        for t in range(NT):
            out[t] = levels[NT - 1 - t][pl.ds(0, size)]
        out[NT] = levels[NT][pl.ds(0, size)]
        out[NT + 1] = last_q[pl.ds(0, size)]


def close_kernel(size, place, last_q, got, *refs):
    levels, image, field = refs[: NT + 1], refs[NT + 1], refs[NT + 2]
    core = place[0]

    @pl.when(core == 0)
    def _():
        total = levels[1][pl.ds(0, size)] * got[0]
        for t in range(1, NT):
            total = total + levels[t + 1][pl.ds(0, size)] * got[t]
        image[...] = total * (1.0 / NT)
        field[0] = got[NT]
        field[1] = got[NT + 1]

    @pl.when(core == 1)
    def _():
        total = levels[NT - 1][pl.ds(size, size)] * got[0]
        for t in range(1, NT):
            total = total + levels[NT - 1 - t][pl.ds(size, size)] * got[t]
        image[...] = total * (1.0 / NT)
        field[0] = levels[NT][pl.ds(size, size)]
        field[1] = last_q[pl.ds(size, size)]


def per_device(
    velocity,
    epsilon,
    delta,
    tilt,
    azimuth,
    aperture,
    source_cell,
    wavelet,
    receiver_cell,
    traces,
    source_state,
    receiver_state,
):
    block_x, size_y, _ = velocity.shape
    devices_x, devices_y = lax.axis_size("gx"), lax.axis_size("gy")
    columns = devices_x // 2
    total_x, total_y = block_x * devices_x, size_y * devices_y
    size_x = 2 * block_x
    at_x, at_y = lax.axis_index("gx"), lax.axis_index("gy")
    core, column = at_x % 2, at_x // 2
    parity = at_y % 2
    is_source = core == 0

    one_sided = columns == 2
    if one_sided:
        wide, count = size_x + 8, size_x + 4
        first_at = 4 * column
        tile_at = 4 * column
        edge_at = jnp.where(column == 0, size_x - 8, 0)
        start_x = column * size_x - 4 * column
    else:
        wide, count = size_x + 16, size_x + 8
        first_at = jnp.int32(4)
        tile_at = jnp.int32(4)
        edge_at = jnp.where(column % 2 == 0, size_x - 8, 0)
        start_x = column * size_x - 4
    level = jnp.where(is_source, SRC_DEPTH, REC_DEPTH)

    def int32s(*values):
        return jnp.stack([jnp.asarray(value, jnp.int32) for value in values])

    place = int32s(first_at, tile_at, parity, level, edge_at)
    mats = depth_matrices(128)

    def swap_y(values):
        return (
            lax.ppermute(values, "gy", both_ways(even_pairs(devices_y))),
            lax.ppermute(values, "gy", both_ways(odd_pairs(devices_y))),
        )

    def widen(tile, edge):
        even = lax.ppermute(edge, "gx", both_ways(chip_swap(even_pairs(columns))))
        if one_sided:
            return jnp.where(
                column == 0,
                jnp.concatenate([tile, even], axis=1),
                jnp.concatenate([even, tile], axis=1),
            )
        other = jnp.where(column % 2 == 0, tile[:, :8], tile[:, size_x - 8 :])
        odd = lax.ppermute(other, "gx", both_ways(chip_swap(odd_pairs(columns))))
        low = jnp.where(column % 2 == 0, odd, even)
        high = jnp.where(column % 2 == 0, even, odd)
        return jnp.concatenate([low, tile, high], axis=1)

    trade = both_ways([(2 * c, 2 * c + 1) for c in range(columns)])
    kept = jnp.where(is_source, source_state, receiver_state)
    got = lax.ppermute(jnp.where(is_source, receiver_state, source_state), "gx", trade)
    state = jnp.where(
        is_source, jnp.concatenate([kept, got], axis=1), jnp.concatenate([got, kept], axis=1)
    )
    state = jnp.stack([state[0], state[2], state[1], state[3]])
    edge = lax.dynamic_slice_in_dim(state, edge_at, 8, axis=1)
    extended = widen(state, edge)
    even, odd = swap_y(extended)
    below = jnp.where(parity == 0, odd, even)[2:, :, size_y - 4 :]
    above = jnp.where(parity == 0, even, odd)[2:, :, :4]
    old = jnp.concatenate([below, extended[2:], above], axis=2)
    old = lax.dynamic_slice_in_dim(old, first_at, count, axis=1)

    model = jnp.stack([velocity, epsilon, delta, tilt, azimuth])
    upper, lower = model[:, :, size_y - 4 :], model[:, :, :4]
    model_even = lax.ppermute(
        jnp.where(parity == 0, upper, lower), "gy", both_ways(even_pairs(devices_y))
    )
    model_odd = lax.ppermute(
        jnp.where(parity == 0, lower, upper), "gy", both_ways(odd_pairs(devices_y))
    )
    model = jnp.concatenate(
        [
            jnp.where(parity == 0, model_odd, model_even),
            model,
            jnp.where(parity == 0, model_even, model_odd),
        ],
        axis=2,
    )
    model = lax.all_gather(model, "gx", axis=1, tiled=True)

    number = receiver_cell.shape[0]
    lonely = jnp.full((number - source_cell.shape[0],), -1, jnp.int32)
    cells = jnp.where(is_source, jnp.concatenate([source_cell, lonely]), receiver_cell)[None, :]
    first = jnp.concatenate([wavelet[:, None], jnp.zeros((NT, number - 1), F32)], axis=1)
    amounts = jnp.where(is_source, first, traces[::-1])
    coefs, inject = setup(
        int32s(start_x, at_y * size_y - 4),
        aperture, model, cells, amounts, count, total_x, total_y, block_x,
    )

    tile = state[:2]
    extended, even, odd = extended[:2], even[:2], odd[:2]
    levels = [tile[0]]
    for moment in range(0, NT, 2):
        if moment:
            extended = widen(tile, edge)
            even, odd = swap_y(extended)
        tile, edge, old, halfway = stride(
            moment, place, extended, even, odd, old, coefs, inject, mats
        )
        levels += [halfway, tile[0]]

    which = int32s(core)
    shape = (block_x, size_y, 128)
    sent = pl.pallas_call(
        functools.partial(pack_kernel, block_x),
        out_shape=jax.ShapeDtypeStruct((NT + 2,) + shape, F32),
        in_specs=[SMEM] + [VMEM] * (NT + 2),
        out_specs=VMEM,
        name="pack",
    )(which, tile[1], *levels)
    got = lax.ppermute(sent, "gx", trade)
    return pl.pallas_call(
        functools.partial(close_kernel, block_x),
        out_shape=(jax.ShapeDtypeStruct(shape, F32), jax.ShapeDtypeStruct((2,) + shape, F32)),
        in_specs=[SMEM] + [VMEM] * (NT + 3),
        out_specs=(VMEM, VMEM),
        name="close",
    )(which, tile[1], got, *levels)


def solution(mesh):
    in_specs = (
        P("gx", "gy", None),
        P("gx", "gy", None),
        P("gx", "gy", None),
        P("gx", "gy", None),
        P("gx", "gy", None),
        P("shot"),
        P("shot"),
        P("shot"),
        P("shot"),
        P(None, "shot"),
        P(None, ("shot", "gx"), "gy", None),
        P(None, ("shot", "gx"), "gy", None),
    )
    out_specs = (P(("shot", "gx"), "gy", None), P(None, ("shot", "gx"), "gy", None))
    return jax.shard_map(
        per_device, mesh=mesh, in_specs=in_specs, out_specs=out_specs, check_vma=False
    )
```

```python
import functools

import jax
import jax.numpy as jnp
from jax import lax
from jax.experimental import pallas as pl
from jax.experimental.pallas import tpu as pltpu
from jax.sharding import PartitionSpec as P

NT = 8
SRC_DEPTH = 10
REC_DEPTH = 6
HALO = 4
F32 = jnp.float32
BF16 = jnp.bfloat16

second_taps = (-205.0 / 72.0, 8.0 / 5.0, -1.0 / 5.0, 8.0 / 315.0, -1.0 / 560.0)
first_taps = (4.0 / 5.0, -1.0 / 5.0, 4.0 / 105.0, -1.0 / 280.0)
S1 = second_taps[1]
G1 = first_taps[0]
second_ratio = tuple(tap / S1 for tap in second_taps[2:])
first_ratio = tuple(tap / G1 for tap in first_taps[1:])
second_whole = (8064.0, -1008.0, 128.0, -9.0)
first_whole = (672.0, -168.0, 32.0, -3.0)
SECOND_UNIT = 1.0 / 5040.0
FIRST_UNIT = 1.0 / 840.0
VMEM = pl.BlockSpec(memory_space=pltpu.VMEM)
SMEM = pl.BlockSpec(memory_space=pltpu.SMEM)


def even_pairs(count):
    return [(i, i + 1) for i in range(0, count - 1, 2)]


def odd_pairs(count):
    return [(i, i + 1) for i in range(1, count - 1, 2)]


def both_ways(pairs):
    return [pair for a, b in pairs for pair in ((a, b), (b, a))]


def chip_swap(pairs):
    return [(2 * a + c, 2 * b + c) for a, b in pairs for c in range(2)]


def depth_matrices(size):
    rows = jnp.arange(size)[:, None]
    cols = jnp.arange(size)[None, :]
    first = jnp.zeros((size, size), F32)
    second = jnp.zeros((size, size), F32)
    for k in range(1, 5):
        up = (rows == cols + k).astype(F32)
        down = (rows == cols - k).astype(F32)
        first = first + first_whole[k - 1] * (up - down)
        second = second + second_whole[k - 1] * (up + down)
    return (
        jnp.concatenate([first, first]).astype(BF16),
        jnp.concatenate([second, second]).astype(BF16),
    )


def sums_and_slopes(shifted):
    up, down = shifted(1), shifted(-1)
    curve, slope = up + down, up - down
    for k in range(2, 5):
        up, down = shifted(k), shifted(-k)
        curve = curve + second_ratio[k - 2] * (up + down)
        slope = slope + first_ratio[k - 2] * (up - down)
    return curve, slope


def slope_only(shifted):
    slope = shifted(1) - shifted(-1)
    for k in range(2, 5):
        slope = slope + first_ratio[k - 2] * (shifted(k) - shifted(-k))
    return slope


def split(values):
    high = values.astype(BF16)
    low = (values - high.astype(F32)).astype(BF16)
    return high, low


def leap_in_kernel(src, x0, row0, rows, count, scratch, mats, old_at, coef_at, inject_at, store):
    slope_y, curve_y, parts, parts_z, slope_x = scratch
    mat_first, mat_second = mats
    group = 4

    def along_y(p, carry):
        for f in range(2):
            curve, slope = sums_and_slopes(
                lambda k: src[f, x0 + p, pl.ds(row0 + k, rows), :]
            )
            slope_y[f, p, :rows] = slope
            curve_y[f, p, :rows] = curve
        return carry

    lax.fori_loop(0, count + 8, along_y, 0, unroll=4)

    def along_x(q, carry):
        base = q * group
        for f in range(2):
            for r in range(0, rows, 8):
                line = [src[f, x0 + base + k, pl.ds(row0 + r, 8), :] for k in range(group + 8)]
                slant = [slope_y[f, base + k, pl.ds(r, 8), :] for k in range(group + 8)]
                for g in range(group):
                    curve, slope = sums_and_slopes(lambda k: line[g + 4 + k])
                    parts[0, f, base + g, pl.ds(r, 8), :] = curve
                    slope_x[f, base + g, pl.ds(r, 8), :] = slope
                    parts[1, f, base + g, pl.ds(r, 8), :] = slope_only(lambda k: slant[g + 4 + k])
        return carry

    lax.fori_loop(0, count // group, along_x, 0, unroll=2)

    lines = count * rows
    for f in range(2):
        field = src[f, pl.ds(x0 + 4, count), pl.ds(row0, rows), :].reshape(lines, 128)
        tilt_y = slope_y[f, pl.ds(4, count), :rows, :].reshape(lines, 128)
        tilt_x = slope_x[f, pl.ds(0, count), :rows, :].reshape(lines, 128)
        for slot, (values, mat) in enumerate(
            ((field, mat_second), (tilt_y, mat_first), (tilt_x, mat_first))
        ):
            both = jnp.concatenate(split(values), axis=1)
            product = jnp.dot(both, mat[...], preferred_element_type=F32)
            parts_z[slot, f, pl.ds(0, count), :rows, :] = product.reshape(count, rows, 128)

    def combine(i, carry):
        speed, speed_h, speed_v, wx, wy, wz, wxy, wyz, wxz = coef_at(i)
        add = inject_at(i)
        fields, here = [], []
        for f in range(2):
            xx = parts[0, f, i, :rows]
            xy = parts[1, f, i, :rows]
            yy = curve_y[f, i + 4, :rows]
            zz = parts_z[0, f, i, :rows]
            yz = parts_z[1, f, i, :rows]
            xz = parts_z[2, f, i, :rows]
            here.append(src[f, x0 + i + 4, pl.ds(row0, rows), :])
            mixed = wxy * xy + wyz * yz + wxz * xz
            if f == 0:
                fields.append(
                    (2.0 * second_taps[0]) * here[0]
                    + (S1 - wx) * xx
                    + (S1 - wy) * yy
                    + (SECOND_UNIT - wz) * zz
                    - mixed
                )
            else:
                fields.append(second_taps[0] * here[1] + wx * xx + wy * yy + wz * zz + mixed)
        flat, tilted = fields
        new_p = 2.0 * here[0] - old_at(0, i) + (speed_h * flat + speed_v * tilted) + add
        new_q = 2.0 * here[1] - old_at(1, i) + (speed_v * flat + speed * tilted) + add
        store(i, new_p, new_q)
        return carry

    lax.fori_loop(0, count, combine, 0, unroll=4)


def limits(mebibytes):
    return pltpu.CompilerParams(vmem_limit_bytes=mebibytes * 2**20)


TOP = 32000.0
GROUP = 8


def tiles_of(fields):
    return fields * 4 + fields // 2


def encode(value_at, out, group, fields):
    lane = lax.broadcasted_iota(jnp.int32, (8, 128), 1)
    for pair in range(fields // 2):
        codes = []
        for f in (2 * pair, 2 * pair + 1):
            values = [value_at(f, p) for p in range(GROUP)]
            sizes = jnp.full((8, 128), 1e-30, F32)
            for p in range(GROUP):
                largest = jnp.max(jnp.abs(values[p]), axis=1, keepdims=True)
                sizes = jnp.where(lane == p, jnp.maximum(largest, 1e-30), sizes)
            code = jnp.ceil(jnp.log2(sizes) * 256.0)
            factor = TOP * jnp.exp2(code * (-1.0 / 256.0))
            codes.append(code)
            for q in range(GROUP // 2):
                both = [
                    jnp.floor(values[p] * factor[:, p : p + 1] + 0.5) for p in (2 * q, 2 * q + 1)
                ]
                whole = jnp.concatenate(both).astype(jnp.int32).astype(jnp.int16)
                out[group, f * 4 + q] = whole
        out[group, fields * 4 + pair] = jnp.concatenate(codes).astype(jnp.int32).astype(jnp.int16)


def decode(payload, group, fields, put):
    for pair in range(fields // 2):
        code = payload[group, fields * 4 + pair].astype(jnp.int32).astype(F32)
        factor = jnp.exp2(code * (1.0 / 256.0)) * (1.0 / TOP)
        for slot in range(2):
            f = 2 * pair + slot
            own = factor[slot * 8 : slot * 8 + 8]
            for q in range(GROUP // 2):
                both = payload[group, f * 4 + q].astype(jnp.int32).astype(F32)
                put(f, 2 * q, both[:8] * own[:, 2 * q : 2 * q + 1])
                put(f, 2 * q + 1, both[8:] * own[:, 2 * q + 1 : 2 * q + 2])


def first_kernel(size, place, kept, got, tile, old, payload, *edges):
    core = place[0]
    for source, at in ((kept, core * size), (got, (1 - core) * size)):
        for f in range(2):
            tile[f, pl.ds(at, size)] = source[2 * f]
            old[f, pl.ds(at, size)] = source[2 * f + 1]

    def group(g, carry):
        def value_at(f, p):
            where = tile if f < 2 else old
            return where[f % 2, g * GROUP + p]

        encode(value_at, payload, g, 4)
        return carry

    lax.fori_loop(0, 2 * size // GROUP, group, 0)
    for k, edge in enumerate(edges):
        edge[0] = payload[place[1 + k]]


def first(place, kept, got, sides):
    size, size_y = kept.shape[1], kept.shape[2]
    groups, tiles = 2 * size // GROUP, tiles_of(4)
    field = jax.ShapeDtypeStruct((2, 2 * size, size_y, 128), F32)
    edge = jax.ShapeDtypeStruct((1, tiles, 16, 128), jnp.int16)
    outs = (field, field, jax.ShapeDtypeStruct((groups, tiles, 16, 128), jnp.int16))
    outs = outs + (edge,) * sides
    return pl.pallas_call(
        functools.partial(first_kernel, size),
        out_shape=outs,
        in_specs=[SMEM, VMEM, VMEM],
        out_specs=(VMEM,) * len(outs),
        compiler_params=limits(16),
        name="first",
    )(place, kept, got)


def stride_kernel(moment, sides, wide, count, size_x, size_y, place, tile, old, coefs, inject,
                  mat_first, mat_second, *refs):
    opening, closing = moment == 0, moment == NT - 2
    refs = list(refs)

    def take(number):
        taken = refs[:number]
        del refs[:number]
        return taken

    beside = take(sides)
    even, odd = take(1)[0], take(1)[0]
    even_beside, odd_beside = take(sides), take(sides)
    levels = take(2 * (NT // 2 - 1) + 1) if closing else []
    if closing:
        kept_out, sent_out = take(2)
    else:
        tile_out, old_out, half_out, payload_out = take(4)
        edges_out = take(sides)
    window, middle, slope_y, curve_y, parts, parts_z, slope_x, old_wide = take(8)
    if closing:
        tile_out, half_out = take(2)

    first_at, tile_at, parity, level = place[0], place[1], place[2], place[3]
    own_at = first_at + tile_at
    fields = 4 if opening else 2
    groups = size_x // GROUP
    scratch = (slope_y, curve_y, parts, parts_z, slope_x)
    mats = (mat_first, mat_second)
    lane = lax.broadcasted_iota(jnp.int32, (8, 128), 1)
    mask = (lane == level).astype(F32)

    for f in range(2):
        window[f, pl.ds(0, 4)] = jnp.zeros((4, 32, 128), F32)
        window[f, pl.ds(wide + 4, 4)] = jnp.zeros((4, 32, 128), F32)
        middle[f, pl.ds(0, 4)] = jnp.zeros((4, 24, 128), F32)
        middle[f, pl.ds(count + 4, 4)] = jnp.zeros((4, 24, 128), F32)
        window[f, pl.ds(own_at + 4, size_x), pl.ds(12, 8), :] = tile[f]
        if opening:
            old_wide[f, pl.ds(own_at, size_x), pl.ds(4, 8), :] = old[f]

    def lay(payload, group, plane, row):
        def put(f, p, rows):
            if f < 2:
                window[f, plane + p + 4, pl.ds(row + 12, 8), :] = rows
            elif row == 0:
                old_wide[f - 2, plane + p, pl.ds(4, 8), :] = rows
            elif row < 0:
                old_wide[f - 2, plane + p, pl.ds(0, 4), :] = rows[4:]
            else:
                old_wide[f - 2, plane + p, pl.ds(12, 4), :] = rows[:4]

        decode(payload, group, fields, put)

    for k in range(sides):
        lay(beside[k], 0, place[4 + k], 0)

    def lay_y(below, above, below_beside, above_beside):
        for payload, parts_beside, row in (
            (below, below_beside, -8), (above, above_beside, 8)
        ):
            def group(g, carry):
                lay(payload, g, own_at + g * GROUP, row)
                return carry

            lax.fori_loop(0, groups, group, 0)
            for k in range(sides):
                lay(parts_beside[k], 0, place[4 + k], row)

    @pl.when(parity == 0)
    def _():
        lay_y(odd, even, odd_beside, even_beside)

    @pl.when(parity == 1)
    def _():
        lay_y(even, odd, even_beside, odd_beside)

    def store_first(i, new_p, new_q):
        for f, new in enumerate((new_p, new_q)):
            if not closing:
                old_out[f, i] = new
            middle[f, i + 4, pl.ds(4, size_y + 8), :] = new

    leap_in_kernel(
        window, first_at, 8, size_y + 8, count, scratch, mats,
        (lambda f, i: old_wide[f, first_at + i]) if opening else (lambda f, i: old[f, i]),
        lambda i: [coefs[m, i] for m in range(9)],
        lambda i: jnp.concatenate(
            [inject[i, pl.ds(r, 8), moment : moment + 1] * mask for r in range(0, size_y + 8, 8)]
        ),
        store_first,
    )

    def store_second(i, new_p, new_q):
        tile_out[0, i] = new_p
        tile_out[1, i] = new_q
        half_out[i] = middle[0, tile_at + i + 4, pl.ds(8, size_y), :]

    leap_in_kernel(
        middle, tile_at, 8, size_y, size_x, scratch, mats,
        lambda f, i: tile[f, i],
        lambda i: [coefs[m, tile_at + i, pl.ds(4, size_y), :] for m in range(9)],
        lambda i: inject[tile_at + i, pl.ds(4, size_y), moment + 1 : moment + 2] * mask,
        store_second,
    )
    if not closing:
        def group(g, carry):
            encode(lambda f, p: tile_out[f, g * GROUP + p], payload_out, g, 2)
            return carry

        lax.fori_loop(0, groups, group, 0)
        for k in range(sides):
            edges_out[k][0] = payload_out[place[6 + k]]
        return

    half = size_x // 2

    def level_at(step, planes):
        if step == NT - 1:
            return half_out[planes]
        if step == NT:
            return tile_out[0, planes]
        where = levels[step]
        return where[0, planes] if len(where.shape) == 4 else where[planes]

    core = place[8]
    for mine in range(2):
        @pl.when(core == mine)
        def _():
            stay, leave = pl.ds(mine * half, half), pl.ds((1 - mine) * half, half)
            for t in range(1, NT + 1):
                step = t if mine == 0 else NT - t
                kept_out[t - 1] = level_at(step, stay)
                sent_out[t - 1] = level_at(step, leave)
            for f in range(2):
                kept_out[NT + f] = tile_out[f, stay]
                sent_out[NT + f] = tile_out[f, leave]


def stride(moment, place, tile, old, coefs, inject, mats, near, levels):
    beside, even, odd, even_beside, odd_beside = near
    sides = len(beside)
    size_x, size_y = tile.shape[1], tile.shape[2]
    count, rows = coefs.shape[1], size_y + 8
    wide = size_x + GROUP * sides
    closing = moment == NT - 2
    field = jax.ShapeDtypeStruct((2, size_x, size_y, 128), F32)
    if closing:
        share = jax.ShapeDtypeStruct((NT + 2, size_x // 2, size_y, 128), F32)
        outs = (share, share)
    else:
        tiles = tiles_of(2)
        outs = (
            field,
            jax.ShapeDtypeStruct((2, count, rows, 128), F32),
            jax.ShapeDtypeStruct((size_x, size_y, 128), F32),
            jax.ShapeDtypeStruct((size_x // GROUP, tiles, 16, 128), jnp.int16),
        ) + (jax.ShapeDtypeStruct((1, tiles, 16, 128), jnp.int16),) * sides
    args = [tile, old, coefs, inject, *mats, *beside, even, odd, *even_beside, *odd_beside]
    args += levels if closing else []
    scratch = [
        pltpu.VMEM((2, wide + 8, 32, 128), F32),
        pltpu.VMEM((2, count + 8, 24, 128), F32),
        pltpu.VMEM((2, count + 8, rows, 128), F32),
        pltpu.VMEM((2, count + 8, rows, 128), F32),
        pltpu.VMEM((2, 2, count, rows, 128), F32),
        pltpu.VMEM((3, 2, count, rows, 128), F32),
        pltpu.VMEM((2, count, rows, 128), F32),
        pltpu.VMEM((2, wide, rows, 128) if moment == 0 else (8, 128), F32),
    ]
    if closing:
        scratch += [pltpu.VMEM(field.shape, F32), pltpu.VMEM(field.shape[1:], F32)]
    return pl.pallas_call(
        functools.partial(stride_kernel, moment, sides, wide, count, size_x, size_y),
        out_shape=outs,
        in_specs=[SMEM] + [VMEM] * len(args),
        out_specs=(VMEM,) * len(outs),
        scratch_shapes=scratch,
        compiler_params=limits(24),
        name="stride",
    )(place, *args)


def sine_cosine(angle):
    square = angle * angle
    sine = 1.0 / 6227020800.0
    for factor in (-1.0 / 39916800.0, 1.0 / 362880.0, -1.0 / 5040.0, 1.0 / 120.0, -1.0 / 6.0):
        sine = sine * square + factor
    sine = angle + angle * square * sine
    cosine = 1.0 / 479001600.0
    for factor in (-1.0 / 3628800.0, 1.0 / 40320.0, -1.0 / 720.0, 1.0 / 24.0, -0.5):
        cosine = cosine * square + factor
    return sine, 1.0 + square * cosine


def rim_kernel(size_x, size_y, place, *refs):
    models, (even, odd) = refs[:5], refs[5:]

    def pack(out, row):
        for m in range(5):
            for x in range(0, size_x, 4):
                values = [models[m][x + k].astype(F32)[row : row + 4] for k in range(4)]
                out[m, x // 4] = jnp.concatenate(values).astype(BF16)

    @pl.when(place[2] == 0)
    def _():
        pack(even, size_y - 4)
        pack(odd, 0)

    @pl.when(place[2] == 1)
    def _():
        pack(odd, size_y - 4)
        pack(even, 0)


def join_kernel(size_x, size_y, place, *refs):
    models, even, odd, out = refs[:5], refs[5], refs[6], refs[7]

    def fill(below, above):
        for m in range(5):
            for x in range(0, size_x, 4):
                low, high = below[m, x // 4].astype(F32), above[m, x // 4].astype(F32)
                for k in range(4):
                    own = models[m][x + k].astype(F32)
                    rows = [low[4 * k : 4 * k + 4], own, high[4 * k : 4 * k + 4]]
                    out[m, x + k] = jnp.concatenate(rows).astype(BF16)

    @pl.when(place[2] == 0)
    def _():
        fill(odd, even)

    @pl.when(place[2] == 1)
    def _():
        fill(even, odd)


def setup_kernel(count, size_x, total_x, place, aperture, *refs):
    models, coefs, blocks = refs[:-2], refs[-2], refs[-1]
    start_x = place[0]
    if len(models) > 1:
        for k, model in enumerate(models):
            blocks[:, pl.ds(place[2 + k] * size_x, size_x)] = model[...]
        source = blocks
    else:
        source = models[0]

    def medium(i, carry):
        x = start_x + i
        block = jnp.clip(x // size_x, 0, total_x // size_x - 1)
        inside = jnp.logical_and(x >= 0, x < total_x)
        at = aperture[block] * size_x + lax.rem(x + size_x, size_x)
        speed, stretch, bending, tilt, azimuth = [source[m, at].astype(F32) for m in range(5)]
        speed = jnp.where(inside, speed, 0.0)
        sin_t, cos_t = sine_cosine(tilt)
        sin_half, cos_half = sine_cosine(0.5 * azimuth)
        normal_x = sin_t * (1.0 - 2.0 * sin_half * sin_half)
        normal_y = sin_t * (2.0 * sin_half * cos_half)
        coefs[0, i] = speed
        coefs[1, i] = speed * (1.0 + 2.0 * stretch)
        coefs[2, i] = speed * jnp.sqrt(1.0 + 2.0 * bending)
        coefs[3, i] = S1 * (normal_x * normal_x)
        coefs[4, i] = S1 * (normal_y * normal_y)
        coefs[5, i] = SECOND_UNIT * (cos_t * cos_t)
        coefs[6, i] = (2.0 * G1 * G1) * (normal_x * normal_y)
        coefs[7, i] = (2.0 * G1 * FIRST_UNIT) * (normal_y * cos_t)
        coefs[8, i] = (2.0 * G1 * FIRST_UNIT) * (normal_x * cos_t)
        return carry

    lax.fori_loop(0, count, medium, 0, unroll=2)


def setup(place, aperture, models, count, total_x, size_x):
    rows = models[0].shape[2]
    held = (5, total_x, rows, 128) if len(models) > 1 else (16, 128)
    return pl.pallas_call(
        functools.partial(setup_kernel, count, size_x, total_x),
        out_shape=jax.ShapeDtypeStruct((9, count, rows, 128), F32),
        in_specs=[SMEM, SMEM] + [VMEM] * len(models),
        out_specs=VMEM,
        scratch_shapes=[pltpu.VMEM(held, BF16)],
        compiler_params=limits(24),
        name="setup",
    )(place, aperture, *models)


def inject_kernel(count, rows, total_y, place, source_cell, wavelet, cells, traces, out, hits):
    start_x, start_y, core = place[0], place[1], place[6]
    number = cells.shape[1]
    row = lax.broadcasted_iota(jnp.int32, (rows, number), 0)
    lane = lax.broadcasted_iota(jnp.int32, (1, number), 1)
    is_source = core == 0
    lonely = jnp.where(lane == 0, source_cell[0], -1)
    aims = jnp.where(is_source, lonely, cells[...])

    def mark(i, carry):
        y = start_y + row
        code = (start_x + i) * total_y + y
        code = jnp.where(jnp.logical_and(y >= 0, y < total_y), code, -2)
        hits[i] = jnp.where(code == aims, 1.0, 0.0).astype(BF16)
        return carry

    lax.fori_loop(0, count, mark, 0, unroll=2)
    leap = lax.broadcasted_iota(jnp.int32, (NT, number), 0)
    amounts = jnp.zeros((NT, number), F32)
    for k in range(NT):
        amounts = jnp.where(leap == k, wavelet[k], amounts)
    backward = jnp.concatenate([traces[k : k + 1] for k in reversed(range(NT))])
    rest = jnp.where(is_source, amounts, backward)
    total = None
    for _ in range(3):
        piece = rest.astype(BF16)
        rest = rest - piece.astype(F32)
        term = lax.dot_general(
            hits[...].reshape(count * rows, number), piece, (((1,), (1,)), ((), ())),
            preferred_element_type=F32,
        )
        total = term if total is None else total + term
    out[...] = total.reshape(count, rows, NT)


def injection(place, source_cell, wavelet, cells, traces, count, rows, total_y):
    number = cells.shape[0]
    return pl.pallas_call(
        functools.partial(inject_kernel, count, rows, total_y),
        out_shape=jax.ShapeDtypeStruct((count, rows, NT), F32),
        in_specs=[SMEM, SMEM, SMEM, VMEM, VMEM],
        out_specs=VMEM,
        scratch_shapes=[pltpu.VMEM((count, rows, number), BF16)],
        compiler_params=limits(16),
        name="injection",
    )(place, source_cell, wavelet, cells[None, :], traces)


def close_kernel(place, kept, got, image, field):
    total = kept[0] * got[0]
    for t in range(1, NT):
        total = total + kept[t] * got[t]
    image[...] = total * (1.0 / NT)
    core = place[0]

    @pl.when(core == 0)
    def _():
        field[...] = got[pl.ds(NT, 2)]

    @pl.when(core == 1)
    def _():
        field[...] = kept[pl.ds(NT, 2)]


def per_device(
    velocity,
    epsilon,
    delta,
    tilt,
    azimuth,
    aperture,
    source_cell,
    wavelet,
    receiver_cell,
    traces,
    source_state,
    receiver_state,
):
    block_x, size_y, _ = velocity.shape
    devices_x, devices_y = lax.axis_size("gx"), lax.axis_size("gy")
    columns = devices_x // 2
    total_x, total_y = block_x * devices_x, size_y * devices_y
    size_x = 2 * block_x
    at_x, at_y = lax.axis_index("gx"), lax.axis_index("gy")
    core, column = at_x % 2, at_x // 2
    parity = at_y % 2
    is_source = core == 0
    last_group = size_x // GROUP - 1

    one_sided = columns == 2
    if one_sided:
        sides = 1
        count = size_x + 4
        first_at = tile_at = 4 * column
        start_x = column * size_x - 4 * column
        beside_at = [size_x * (1 - column), 0]
        edge_group = [last_group * (1 - column), 0]
    else:
        sides = 2
        count = size_x + 8
        first_at = tile_at = 4
        start_x = column * size_x - 4
        first_side = column % 2 == 0
        beside_at = [
            jnp.where(first_side, size_x + GROUP, 0), jnp.where(first_side, 0, size_x + GROUP)
        ]
        edge_group = [jnp.where(first_side, last_group, 0), jnp.where(first_side, 0, last_group)]
    level = jnp.where(is_source, SRC_DEPTH, REC_DEPTH)

    def int32s(*values):
        return jnp.stack([jnp.asarray(value, jnp.int32) for value in values])

    place = int32s(first_at, tile_at, parity, level, *beside_at, *edge_group, core)
    mats = depth_matrices(128)
    chip_pairs = [even_pairs(columns), odd_pairs(columns)][:sides]
    row_pairs = [even_pairs(devices_y), odd_pairs(devices_y)]

    def over_gy(values, pairs):
        return lax.ppermute(values, "gy", both_ways(pairs))

    def over_gx(values, pairs):
        return lax.ppermute(values, "gx", both_ways(chip_swap(pairs)))

    def over_both(values, pairs_x, pairs_y):
        pairs = [
            (a * devices_y + c, b * devices_y + d)
            for a, b in both_ways(chip_swap(pairs_x))
            for c, d in both_ways(pairs_y)
        ]
        return lax.ppermute(values, ("gx", "gy"), pairs)

    def exchange(payload, edges):
        even, odd = [over_gy(payload, pairs) for pairs in row_pairs]
        beside = [over_gx(edge, pairs) for edge, pairs in zip(edges, chip_pairs)]
        corners = [
            [over_both(edge, pairs, rows) for edge, pairs in zip(edges, chip_pairs)]
            for rows in row_pairs
        ]
        return beside, even, odd, corners[0], corners[1]

    trade = both_ways([(2 * c, 2 * c + 1) for c in range(columns)])
    kept = jnp.where(is_source, source_state, receiver_state)
    got = lax.ppermute(jnp.where(is_source, receiver_state, source_state), "gx", trade)
    tile, old, payload, *edges = first(int32s(core, *edge_group), kept, got, sides)
    near = exchange(payload, edges)

    other = 1 - column
    spot = int32s(
        start_x, at_y * size_y - 4,
        2 * column + core, 2 * column + 1 - core, 2 * other + core, 2 * other + 1 - core, core,
    )
    models = (velocity, epsilon, delta, tilt, azimuth)
    rim = jax.ShapeDtypeStruct((5, block_x // 4, 16, 128), BF16)
    rims = pl.pallas_call(
        functools.partial(rim_kernel, block_x, size_y),
        out_shape=(rim, rim),
        in_specs=[SMEM] + [VMEM] * 5,
        out_specs=(VMEM, VMEM),
        name="rim",
    )(place, *models)
    rims = [over_gy(values, pairs) for values, pairs in zip(rims, row_pairs)]
    model = pl.pallas_call(
        functools.partial(join_kernel, block_x, size_y),
        out_shape=jax.ShapeDtypeStruct((5, block_x, size_y + 8, 128), BF16),
        in_specs=[SMEM] + [VMEM] * 7,
        out_specs=VMEM,
        name="join",
    )(place, *models, *rims)
    if one_sided:
        across = over_gx(model, chip_pairs[0])
        gathered = [model, lax.ppermute(model, "gx", trade)]
        gathered += [across, lax.ppermute(across, "gx", trade)]
    else:
        gathered = [lax.all_gather(model, "gx", axis=1, tiled=True)]
    coefs = setup(spot, aperture, gathered, count, total_x, block_x)
    inject = injection(
        spot, source_cell, wavelet, receiver_cell, traces, count, size_y + 8, total_y
    )

    levels = [tile]
    for moment in range(0, NT - 2, 2):
        tile, old, halfway, payload, *edges = stride(
            moment, place, tile, old, coefs, inject, mats, near, levels
        )
        near = exchange(payload, edges)
        levels += [halfway, tile]
    kept, sent = stride(NT - 2, place, tile, old, coefs, inject, mats, near, levels)
    got = lax.ppermute(sent, "gx", trade)
    shape = (block_x, size_y, 128)
    return pl.pallas_call(
        close_kernel,
        out_shape=(jax.ShapeDtypeStruct(shape, F32), jax.ShapeDtypeStruct((2,) + shape, F32)),
        in_specs=[SMEM, VMEM, VMEM],
        out_specs=(VMEM, VMEM),
        name="close",
    )(int32s(core), kept, got)


def solution(mesh):
    in_specs = (
        P("gx", "gy", None),
        P("gx", "gy", None),
        P("gx", "gy", None),
        P("gx", "gy", None),
        P("gx", "gy", None),
        P("shot"),
        P("shot"),
        P("shot"),
        P("shot"),
        P(None, "shot"),
        P(None, ("shot", "gx"), "gy", None),
        P(None, ("shot", "gx"), "gy", None),
    )
    out_specs = (P(("shot", "gx"), "gy", None), P(None, ("shot", "gx"), "gy", None))
    return jax.shard_map(
        per_device, mesh=mesh, in_specs=in_specs, out_specs=out_specs, check_vma=False
    )
```

```python
import functools

import jax
import jax.numpy as jnp
from jax import lax
from jax.experimental import pallas as pl
from jax.experimental.pallas import tpu as pltpu
from jax.sharding import PartitionSpec as P

NT = 8
SRC_DEPTH = 10
REC_DEPTH = 6
F32 = jnp.float32
BF16 = jnp.bfloat16

second_taps = (-205.0 / 72.0, 8.0 / 5.0, -1.0 / 5.0, 8.0 / 315.0, -1.0 / 560.0)
first_taps = (4.0 / 5.0, -1.0 / 5.0, 4.0 / 105.0, -1.0 / 280.0)
CENTRE = second_taps[0]
S1 = second_taps[1]
G1 = first_taps[0]
second_ratio = tuple(tap / S1 for tap in second_taps[2:])
first_ratio = tuple(tap / G1 for tap in first_taps[1:])
second_whole = (8064.0, -1008.0, 128.0, -9.0)
first_whole = (672.0, -168.0, 32.0, -3.0)
SECOND_UNIT = 1.0 / 5040.0
FIRST_UNIT = 1.0 / 840.0
VMEM = pl.BlockSpec(memory_space=pltpu.VMEM)
SMEM = pl.BlockSpec(memory_space=pltpu.SMEM)


def even_pairs(count):
    return [(i, i + 1) for i in range(0, count - 1, 2)]


def odd_pairs(count):
    return [(i, i + 1) for i in range(1, count - 1, 2)]


def both_ways(pairs):
    return [pair for a, b in pairs for pair in ((a, b), (b, a))]


def chip_swap(pairs):
    return [(2 * a + c, 2 * b + c) for a, b in pairs for c in range(2)]


class Place:
    def __init__(self, size_x, columns):
        at_x = lax.axis_index("gx")
        self.core, self.column = lax.rem(at_x, 2), lax.div(at_x, 2)
        self.at_y = lax.axis_index("gy")
        self.parity = lax.rem(self.at_y, 2)
        if columns == 2:
            side = self.column
            self.count = size_x + 4
            self.first_at = self.tile_at = 4 * side
            self.start_x = side * (size_x - 4)
            self.beside_at = [size_x * (1 - side)]
            self.edge_at = [(size_x - GROUP) * (1 - side)]
            self.rest_at, self.rest = GROUP * side, size_x - GROUP
        else:
            side = lax.rem(self.column, 2)
            self.count = size_x + 8
            self.first_at = self.tile_at = 4
            self.start_x = self.column * size_x - 4
            self.beside_at = [(size_x + GROUP) * (1 - side), (size_x + GROUP) * side]
            self.edge_at = [(size_x - GROUP) * (1 - side), (size_x - GROUP) * side]
            self.rest_at, self.rest = GROUP, size_x - 2 * GROUP
        self.sides = len(self.beside_at)
        self.own_at = self.first_at + self.tile_at
        self.wide = size_x + GROUP * self.sides


def call(kernel, outs, scratch, mebibytes, name, args, scalars=0, work=10**6):
    outs = tuple(jax.ShapeDtypeStruct(shape, dtype) for shape, dtype in outs)
    return pl.pallas_call(
        kernel,
        out_shape=outs,
        in_specs=[SMEM] * scalars + [VMEM] * (len(args) - scalars),
        out_specs=(VMEM,) * len(outs),
        scratch_shapes=[pltpu.VMEM(shape, dtype) for shape, dtype in scratch],
        compiler_params=pltpu.CompilerParams(vmem_limit_bytes=mebibytes * 2**20),
        cost_estimate=pl.CostEstimate(flops=work, bytes_accessed=work, transcendentals=0),
        name=name,
    )(*args)


def loop(trips, body, wanted):
    unroll = max(u for u in range(1, wanted + 1) if trips % u == 0)

    def step(i, carry):
        body(i)
        return carry

    lax.fori_loop(0, trips, step, 0, unroll=unroll)


def depth_matrices(size):
    rows = jnp.arange(size)[:, None]
    cols = jnp.arange(size)[None, :]
    first = jnp.zeros((size, size), F32)
    second = jnp.zeros((size, size), F32)
    for k in range(1, 5):
        up = (rows == cols + k).astype(F32)
        down = (rows == cols - k).astype(F32)
        first = first + first_whole[k - 1] * (up - down)
        second = second + second_whole[k - 1] * (up + down)
    return (
        jnp.concatenate([first, first]).astype(BF16),
        jnp.concatenate([second, second]).astype(BF16),
    )


def sums_and_slopes(shifted):
    up, down = shifted(1), shifted(-1)
    curve, slope = up + down, up - down
    for k in range(2, 5):
        up, down = shifted(k), shifted(-k)
        curve = curve + second_ratio[k - 2] * (up + down)
        slope = slope + first_ratio[k - 2] * (up - down)
    return curve, slope


def slope_only(shifted):
    slope = shifted(1) - shifted(-1)
    for k in range(2, 5):
        slope = slope + first_ratio[k - 2] * (shifted(k) - shifted(-k))
    return slope


def split(values):
    high = values.astype(BF16)
    low = (values - high.astype(F32)).astype(BF16)
    return high, low


TOP = 32000.0
GROUP = 8


def tiles_of(fields):
    return fields * 4 + fields // 2


def encode(value_at, out, group, fields):
    lane = lax.broadcasted_iota(jnp.int32, (8, 128), 1)
    for pair in range(fields // 2):
        codes = []
        for f in (2 * pair, 2 * pair + 1):
            values = [value_at(f, p) for p in range(GROUP)]
            sizes = jnp.full((8, 128), 1e-30, F32)
            for p in range(GROUP):
                largest = jnp.max(jnp.abs(values[p]), axis=1, keepdims=True)
                sizes = jnp.where(lane == p, jnp.maximum(largest, 1e-30), sizes)
            code = jnp.ceil(jnp.log2(sizes) * 256.0)
            factor = TOP * jnp.exp2(code * (-1.0 / 256.0))
            codes.append(code)
            for q in range(GROUP // 2):
                both = [
                    jnp.floor(values[p] * factor[:, p : p + 1] + 0.5) for p in (2 * q, 2 * q + 1)
                ]
                whole = jnp.concatenate(both).astype(jnp.int32).astype(jnp.int16)
                out[group, f * 4 + q] = whole
        out[group, fields * 4 + pair] = jnp.concatenate(codes).astype(jnp.int32).astype(jnp.int16)


def decode(payload, group, fields, put):
    for pair in range(fields // 2):
        code = payload[group, fields * 4 + pair].astype(jnp.int32).astype(F32)
        factor = jnp.exp2(code * (1.0 / 256.0)) * (1.0 / TOP)
        for slot in range(2):
            f = 2 * pair + slot
            own = factor[slot * 8 : slot * 8 + 8]
            for q in range(GROUP // 2):
                both = payload[group, f * 4 + q].astype(jnp.int32).astype(F32)
                put(f, 2 * q, both[:8] * own[:, 2 * q : 2 * q + 1])
                put(f, 2 * q + 1, both[8:] * own[:, 2 * q + 1 : 2 * q + 2])


def leap(src, x0, row0, rows, count, scratch, mats, coef, old_at, inject_at, store):
    slope_y, curve_y, part, halves, product = scratch
    mat_first, mat_second = mats
    planes = 16 // rows
    group = 4

    def field(f, p, r=0, number=rows):
        return src[f, x0 + p, pl.ds(row0 + r, number), :]

    def joined(values):
        return jnp.concatenate(values) if len(values) > 1 else values[0]

    def put_halves(kind, f, unit, values):
        high, low = split(values)
        halves[kind, f, unit, :, :128] = high
        halves[kind, f, unit, :, 128:] = low

    def along_y(u):
        for f in range(2):
            here, slopes = [], []
            for v in range(planes):
                p = u * planes + v
                curve, slope = sums_and_slopes(lambda k: field(f, p, k))
                slope_y[f, p, :rows] = slope
                curve_y[f, p, :rows] = curve
                slopes.append(slope)
                here.append(field(f, p))
            put_halves(0, f, u, joined(here))
            put_halves(1, f, u, joined(slopes))

    loop((count + 8) // planes, along_y, 4)

    def along_x(q):
        base = q * group
        for f in range(2):
            slopes = [[] for g in range(group)]
            for r in range(0, rows, 8):
                line = [field(f, base + k, r, 8) for k in range(group + 8)]
                slant = [slope_y[f, base + k, pl.ds(r, 8), :] for k in range(group + 8)]
                for g in range(group):
                    i = base + g
                    xx, slope = sums_and_slopes(lambda k: line[g + 4 + k])
                    xy = slope_only(lambda k: slant[g + 4 + k])
                    yy = curve_y[f, i + 4, pl.ds(r, 8), :]
                    wx, wy, wxy = [coef(m, i, r, 8) for m in (3, 4, 6)]
                    if f == 0:
                        total = (2.0 * CENTRE) * line[g + 4] + (S1 - wx) * xx
                        total = total + (S1 - wy) * yy - wxy * xy
                    else:
                        total = CENTRE * line[g + 4] + wx * xx
                        total = total + wy * yy + wxy * xy
                    part[f, i, pl.ds(r, 8), :] = total
                    slopes[g].append(slope)
            pieces = [piece for rest in slopes for piece in rest]
            for k in range(0, len(pieces), 2):
                put_halves(2, f, q * (len(pieces) // 2) + k // 2, joined(pieces[k : k + 2]))

    loop(count // group, along_x, 1)

    units = count // planes
    for kind, mat, at in ((0, mat_second, 4 // planes), (1, mat_first, 4 // planes), (2, mat_first, 0)):
        for f in range(2):
            both = halves[kind, f, pl.ds(at, units)].reshape(units * 16, 256)
            out = jnp.dot(both, mat[...], preferred_element_type=F32)
            product[kind, f, pl.ds(0, units)] = out.reshape(units, 16, 128)

    def combine(u):
        where = [u * planes + v for v in range(planes)]
        speed, speed_h, speed_v, wz, wyz, wxz = [
            joined([coef(m, i, 0, rows) for i in where]) for m in (0, 1, 2, 5, 7, 8)
        ]
        zz, yz, xz = [[product[kind, f, u] for f in range(2)] for kind in range(3)]
        parts = [joined([part[f, i, :rows] for i in where]) for f in range(2)]
        here = [joined([field(f, i + 4) for i in where]) for f in range(2)]
        old = [joined([old_at(f, i) for i in where]) for f in range(2)]
        add = joined([inject_at(i) for i in where])
        flat = parts[0] + (SECOND_UNIT - wz) * zz[0] - (wyz * yz[0] + wxz * xz[0])
        tilted = parts[1] + wz * zz[1] + (wyz * yz[1] + wxz * xz[1])
        new_p = (2.0 * here[0] - old[0] + add) + (speed_h * flat + speed_v * tilted)
        new_q = (2.0 * here[1] - old[1] + add) + (speed_v * flat + speed * tilted)
        for v, i in enumerate(where):
            cut = slice(v * rows, v * rows + rows)
            store(i, new_p[cut], new_q[cut])

    loop(units, combine, 4)


def leap_scratch(count):
    lines = (2, count + 8, 16, 128)
    return [
        (lines, F32),
        (lines, F32),
        ((2, count, 16, 128), F32),
        ((3, 2, count + 8, 16, 256), BF16),
        ((3, 2, count, 16, 128), F32),
    ]


def first_kernel(columns, kept, got, tile, old, payload, *edges):
    size = kept.shape[1]
    place = Place(2 * size, columns)
    for source, at in ((kept, place.core * size), (got, (1 - place.core) * size)):
        for f in range(2):
            tile[f, pl.ds(at, size)] = source[2 * f]
            old[f, pl.ds(at, size)] = source[2 * f + 1]

    def group(g):
        encode(lambda f, p: (tile if f < 2 else old)[f % 2, g * GROUP + p], payload, g, 4)

    loop(2 * size // GROUP, group, 1)
    for k, edge in enumerate(edges):
        edge[0] = payload[lax.div(place.edge_at[k], GROUP)]


def second_leap(moment, place, size_y, start, count, middle, tile, coefs, inject, scratch, mats, store):
    leap(
        middle, place.tile_at + start, 8, size_y, count, scratch, mats,
        lambda m, i, r, number: coefs[m, place.tile_at + start + i, pl.ds(4 + r, number), :],
        lambda f, i: tile[f, start + i],
        lambda i: inject[moment + 1, place.tile_at + start + i, pl.ds(4, size_y), :],
        store,
    )


def lead_kernel(moment, columns, tile, old, coefs, inject, mat_first, mat_second, *refs):
    opening, closing = moment == 0, moment == NT - 2
    size_x, size_y = tile.shape[1], tile.shape[2]
    place = Place(size_x, columns)
    sides, count, wide = place.sides, place.count, place.wide
    refs = list(refs)

    def take(number):
        taken = refs[:number]
        del refs[:number]
        return taken

    beside = take(sides)
    even, odd = take(2)
    if closing:
        levels = take(NT - 1)
        kept_out, sent_out = take(2)
        middle, tile_out = take(2)
    else:
        middle, old_out = take(2)
        edges_out, codes_out = take(sides), take(sides)
    window, old_wide = take(2)
    scratch, mats = refs, (mat_first, mat_second)
    fields = 4 if opening else 2

    for f in range(2):
        window[f, pl.ds(0, 4)] = jnp.zeros((4, 32, 128), F32)
        window[f, pl.ds(wide + 4, 4)] = jnp.zeros((4, 32, 128), F32)
        middle[f, pl.ds(0, 4)] = jnp.zeros((4, 24, 128), F32)
        middle[f, pl.ds(count + 4, 4)] = jnp.zeros((4, 24, 128), F32)
        window[f, pl.ds(place.own_at + 4, size_x), pl.ds(12, 8), :] = tile[f]
        if opening:
            old_wide[f, pl.ds(place.own_at, size_x), pl.ds(4, 8), :] = old[f]

    def lay(payload, group, plane, row):
        def put(f, p, rows):
            if f < 2:
                window[f, plane + p + 4, pl.ds(row + 12, 8), :] = rows
            elif row == 0:
                old_wide[f - 2, plane + p, pl.ds(4, 8), :] = rows
            elif row < 0:
                old_wide[f - 2, plane + p, pl.ds(0, 4), :] = rows[4:]
            else:
                old_wide[f - 2, plane + p, pl.ds(12, 4), :] = rows[:4]

        decode(payload, group, fields, put)

    groups = size_x // GROUP
    for k in range(sides):
        lay(beside[k], 0, place.beside_at[k], 0)

    def lay_y(below, above):
        for payload, row in ((below, -8), (above, 8)):
            loop(groups, lambda g: lay(payload, g, place.own_at + g * GROUP, row), 2)
            for k in range(sides):
                lay(payload, groups + k, place.beside_at[k], row)

    pl.when(place.parity == 0)(lambda: lay_y(odd, even))
    pl.when(place.parity == 1)(lambda: lay_y(even, odd))

    def store(i, new_p, new_q):
        for f, new in enumerate((new_p, new_q)):
            if not closing:
                old_out[f, i] = new
            middle[f, i + 4, pl.ds(4, size_y + 8), :] = new

    leap(
        window, place.first_at, 8, size_y + 8, count, scratch, mats,
        lambda m, i, r, number: coefs[m, i, pl.ds(r, number), :],
        (lambda f, i: old_wide[f, place.first_at + i]) if opening else (lambda f, i: old[f, i]),
        lambda i: inject[moment, i],
        store,
    )

    if not closing:
        for k in range(sides):
            def store_edge(i, new_p, new_q):
                edges_out[k][0, i] = new_p
                edges_out[k][1, i] = new_q

            second_leap(
                moment, place, size_y, place.edge_at[k], GROUP, middle, tile, coefs, inject,
                scratch, mats, store_edge,
            )
            encode(lambda f, p: edges_out[k][f, p], codes_out[k], 0, 2)
        return

    def store_tile(i, new_p, new_q):
        tile_out[0, i] = new_p
        tile_out[1, i] = new_q

    second_leap(
        moment, place, size_y, 0, size_x, middle, tile, coefs, inject, scratch, mats, store_tile
    )

    half = size_x // 2

    def level_at(step, start):
        planes = pl.ds(start, half)
        if step == NT:
            return tile_out[0, planes]
        if step == NT - 1:
            return middle[0, pl.ds(place.tile_at + 4 + start, half), pl.ds(8, size_y), :]
        where = levels[step]
        if step % 2 == 0:
            return where[0, planes]
        return where[0, pl.ds(place.tile_at + start, half), pl.ds(4, size_y), :]

    for mine in range(2):
        @pl.when(place.core == mine)
        def _():
            stay, leave = mine * half, (1 - mine) * half
            for t in range(1, NT + 1):
                step = t if mine == 0 else NT - t
                kept_out[t - 1] = level_at(step, stay)
                sent_out[t - 1] = level_at(step, leave)
            for f in range(2):
                kept_out[NT + f] = tile_out[f, pl.ds(stay, half)]
                sent_out[NT + f] = tile_out[f, pl.ds(leave, half)]


def rest_kernel(moment, columns, tile, middle, coefs, inject, mat_first, mat_second, *refs):
    size_x, size_y = tile.shape[1], tile.shape[2]
    place = Place(size_x, columns)
    edges, (tile_out, payload), scratch = (
        refs[: place.sides], refs[place.sides : place.sides + 2], refs[place.sides + 2 :]
    )
    for k, edge in enumerate(edges):
        tile_out[:, pl.ds(place.edge_at[k], GROUP)] = edge[...]

    def store(i, new_p, new_q):
        tile_out[0, place.rest_at + i] = new_p
        tile_out[1, place.rest_at + i] = new_q

    second_leap(
        moment, place, size_y, place.rest_at, place.rest, middle, tile, coefs, inject, scratch,
        (mat_first, mat_second), store,
    )
    loop(
        size_x // GROUP,
        lambda g: encode(lambda f, p: tile_out[f, g * GROUP + p], payload, g, 2),
        1,
    )


def sine_cosine(angle):
    square = angle * angle
    sine = 1.0 / 6227020800.0
    for factor in (-1.0 / 39916800.0, 1.0 / 362880.0, -1.0 / 5040.0, 1.0 / 120.0, -1.0 / 6.0):
        sine = sine * square + factor
    sine = angle + angle * square * sine
    cosine = 1.0 / 479001600.0
    for factor in (-1.0 / 3628800.0, 1.0 / 40320.0, -1.0 / 720.0, 1.0 / 24.0, -0.5):
        cosine = cosine * square + factor
    return sine, 1.0 + square * cosine


def rim_kernel(velocity, epsilon, delta, tilt, azimuth, even, odd, own):
    models = (velocity, epsilon, delta, tilt, azimuth)
    parity = lax.rem(lax.axis_index("gy"), 2)
    for m in range(5):
        own[m] = models[m][...]

    def pack(out, row):
        for m in range(5):
            for u in range(0, models[m].shape[0], 2):
                pairs = [models[m][u + k].astype(F32) for k in range(2)]
                values = [pair[v + row : v + row + 4] for pair in pairs for v in (0, 8)]
                out[m, u // 2] = jnp.concatenate(values).astype(BF16)

    @pl.when(parity == 0)
    def _():
        pack(even, 4)
        pack(odd, 0)

    @pl.when(parity == 1)
    def _():
        pack(odd, 4)
        pack(even, 0)


def join_kernel(own, even, odd, out):
    parity = lax.rem(lax.axis_index("gy"), 2)

    def fill(below, above):
        for m in range(5):
            for u in range(own.shape[1]):
                low, high = below[m, u // 2].astype(F32), above[m, u // 2].astype(F32)
                pair = own[m, u].astype(F32)
                for v in range(2):
                    k = 2 * (u % 2) + v
                    rows = [low[4 * k : 4 * k + 4], pair[8 * v : 8 * v + 8], high[4 * k : 4 * k + 4]]
                    out[m, 2 * u + v] = jnp.concatenate(rows).astype(BF16)

    pl.when(parity == 0)(lambda: fill(odd, even))
    pl.when(parity == 1)(lambda: fill(even, odd))


def setup_kernel(columns, size_x, total_x, aperture, *refs):
    models, coefs, blocks = refs[:-2], refs[-2], refs[-1]
    place = Place(2 * size_x, columns)
    if len(models) > 1:
        mine, given = models
        for k, column in enumerate((place.column, 1 - place.column)):
            for ref, core in ((mine, place.core), (given, 1 - place.core)):
                blocks[:, pl.ds((2 * column + core) * size_x, size_x)] = ref[k]
        source = blocks
    else:
        source = models[0]

    def medium(i):
        x = place.start_x + i
        block = jnp.clip(x // size_x, 0, total_x // size_x - 1)
        inside = jnp.logical_and(x >= 0, x < total_x)
        at = aperture[block] * size_x + lax.rem(x + size_x, size_x)
        speed, stretch, bending, tilt, azimuth = [source[m, at].astype(F32) for m in range(5)]
        speed = jnp.where(inside, speed, 0.0)
        sin_t, cos_t = sine_cosine(tilt)
        sin_half, cos_half = sine_cosine(0.5 * azimuth)
        normal_x = sin_t * (1.0 - 2.0 * sin_half * sin_half)
        normal_y = sin_t * (2.0 * sin_half * cos_half)
        coefs[0, i] = speed
        coefs[1, i] = speed * (1.0 + 2.0 * stretch)
        coefs[2, i] = speed * jnp.sqrt(1.0 + 2.0 * bending)
        coefs[3, i] = S1 * (normal_x * normal_x)
        coefs[4, i] = S1 * (normal_y * normal_y)
        coefs[5, i] = SECOND_UNIT * (cos_t * cos_t)
        coefs[6, i] = (2.0 * G1 * G1) * (normal_x * normal_y)
        coefs[7, i] = (2.0 * G1 * FIRST_UNIT) * (normal_y * cos_t)
        coefs[8, i] = (2.0 * G1 * FIRST_UNIT) * (normal_x * cos_t)

    loop(place.count, medium, 4)


def injection_kernel(
    columns, size_x, size_y, total_y, source_cell, wavelet, cells, traces, out, hits, lanes
):
    place = Place(size_x, columns)
    count, rows = hits.shape[:2]
    number = cells.shape[1]
    row = lax.broadcasted_iota(jnp.int32, (rows, number), 0)
    lane = lax.broadcasted_iota(jnp.int32, (1, number), 1)
    is_source = place.core == 0
    lonely = jnp.where(lane == 0, source_cell[0], -1)
    aims = jnp.where(is_source, lonely, cells[...])
    y = place.at_y * size_y - 4 + row
    valid = jnp.logical_and(y >= 0, y < total_y)

    def mark(i):
        code = jnp.where(valid, (place.start_x + i) * total_y + y, -2)
        hits[i] = jnp.where(code == aims, 1.0, 0.0).astype(BF16)

    loop(count, mark, 2)
    step = lax.broadcasted_iota(jnp.int32, (NT, number), 0)
    amounts = jnp.zeros((NT, number), F32)
    for k in range(NT):
        amounts = jnp.where(step == k, wavelet[k], amounts)
    backward = jnp.concatenate([traces[k : k + 1] for k in reversed(range(NT))])
    rest = jnp.where(is_source, amounts, backward)
    total = None
    for _ in range(3):
        piece = rest.astype(BF16)
        rest = rest - piece.astype(F32)
        term = lax.dot_general(
            hits[...].reshape(count * rows, number), piece, (((1,), (1,)), ((), ())),
            preferred_element_type=F32,
        )
        total = term if total is None else total + term
    lanes[...] = total.reshape(count, rows, NT)
    level = jnp.where(is_source, SRC_DEPTH, REC_DEPTH)
    mask = (lax.broadcasted_iota(jnp.int32, (rows, 128), 1) == level).astype(F32)

    def expand(i):
        values = lanes[i]
        for k in range(NT):
            out[k, i] = values[:, k : k + 1] * mask

    loop(count, expand, 2)


def close_kernel(kept, got, image, field):
    total = kept[0] * got[0]
    for t in range(1, NT):
        total = total + kept[t] * got[t]
    image[...] = total * (1.0 / NT)
    core = lax.rem(lax.axis_index("gx"), 2)

    @pl.when(core == 0)
    def _():
        field[...] = got[pl.ds(NT, 2)]

    @pl.when(core == 1)
    def _():
        field[...] = kept[pl.ds(NT, 2)]


def per_device(
    velocity,
    epsilon,
    delta,
    tilt,
    azimuth,
    aperture,
    source_cell,
    wavelet,
    receiver_cell,
    traces,
    source_state,
    receiver_state,
):
    block_x, size_y, _ = velocity.shape
    devices_x, devices_y = lax.axis_size("gx"), lax.axis_size("gy")
    columns = devices_x // 2
    total_x, total_y = block_x * devices_x, size_y * devices_y
    size_x, rows = 2 * block_x, size_y + 8
    is_source = lax.axis_index("gx") % 2 == 0
    place = Place(size_x, columns)
    sides, count = place.sides, place.count
    groups = size_x // GROUP
    mats = depth_matrices(128)
    chip_pairs = [even_pairs(columns), odd_pairs(columns)][:sides]
    row_pairs = [even_pairs(devices_y), odd_pairs(devices_y)]
    trade = both_ways([(2 * c, 2 * c + 1) for c in range(columns)])

    def over_gy(values, pairs):
        return lax.ppermute(values, "gy", both_ways(pairs))

    def over_gx(values, pairs):
        return lax.ppermute(values, "gx", both_ways(chip_swap(pairs)))

    def beside_of(edges):
        return [over_gx(edge, pairs) for edge, pairs in zip(edges, chip_pairs)]

    def near_of(payload, beside):
        wide = jnp.concatenate([payload, *beside])
        return wide, [over_gy(wide, pairs) for pairs in row_pairs]

    def codes(number, fields):
        return ((number, tiles_of(fields), 16, 128), jnp.int16)

    models = [
        values.reshape(block_x // 2, 16, 128) for values in (velocity, epsilon, delta, tilt, azimuth)
    ]
    rim = ((5, block_x // 4, 16, 128), BF16)
    *rims, own = call(
        rim_kernel, (rim, rim, ((5, block_x // 2, 16, 128), BF16)), (), 8, "rim", models
    )
    rims = [over_gy(values, pairs) for values, pairs in zip(rims, row_pairs)]

    kept = jnp.where(is_source, source_state, receiver_state)
    got = lax.ppermute(jnp.where(is_source, receiver_state, source_state), "gx", trade)
    field = ((2, size_x, size_y, 128), F32)
    tile, old, payload, *edges = call(
        functools.partial(first_kernel, columns),
        (field, field, codes(groups, 4)) + (codes(1, 4),) * sides,
        (), 16, "first", (kept, got),
    )
    beside = beside_of(edges)
    wide, near = near_of(payload, beside)

    (model,) = call(
        join_kernel, (((5, block_x, rows, 128), BF16),), (), 8, "join", (own, *rims)
    )
    if columns == 2:
        across = over_gx(model, chip_pairs[0])
        across, _ = lax.optimization_barrier((across, wide))
        both = jnp.stack([model, across])
        gathered, held = [both, lax.ppermute(both, "gx", trade)], (5, total_x, rows, 128)
    else:
        gathered, held = [lax.all_gather(model, "gx", axis=1, tiled=True)], (16, 128)
    (coefs,) = call(
        functools.partial(setup_kernel, columns, block_x, total_x),
        (((9, count, rows, 128), F32),), ((held, BF16),), 24, "setup", (aperture, *gathered),
        scalars=1,
    )
    number = receiver_cell.shape[0]
    (inject,) = call(
        functools.partial(injection_kernel, columns, size_x, size_y, total_y),
        (((NT, count, rows, 128), F32),),
        (((count, rows, number), BF16), ((count, rows, NT), F32)),
        16, "injection", (source_cell, wavelet, receiver_cell[None, :], traces), scalars=2,
    )

    window = ((2, place.wide + 8, 32, 128), F32)
    middle = ((2, count + 8, 24, 128), F32)
    lines = ((2, count, rows, 128), F32)
    levels = [tile]
    for moment in range(0, NT - 2, 2):
        old_wide = ((2, place.wide, rows, 128) if moment == 0 else (8, 128), F32)
        between, old, *edges = call(
            functools.partial(lead_kernel, moment, columns),
            (middle, lines) + (((2, GROUP, size_y, 128), F32),) * sides + (codes(1, 2),) * sides,
            [window, old_wide] + leap_scratch(count), 24, "lead",
            (tile, old, coefs, inject, *mats, *beside, *near), work=4 * 10**6,
        )
        edges, edge_codes = edges[:sides], edges[sides:]
        beside = beside_of(edge_codes)
        tile, payload = call(
            functools.partial(rest_kernel, moment, columns),
            (field, codes(groups, 2)), leap_scratch(size_x), 24, "rest",
            (tile, between, coefs, inject, *mats, *edges), work=4 * 10**6,
        )
        wide, near = near_of(payload, beside)
        levels += [old, tile]
    share = ((NT + 2, block_x, size_y, 128), F32)
    kept, sent = call(
        functools.partial(lead_kernel, NT - 2, columns),
        (share, share),
        [middle, field, window, ((8, 128), F32)] + leap_scratch(count), 24, "last",
        (tile, old, coefs, inject, *mats, *beside, *near, *levels),
    )
    got = lax.ppermute(sent, "gx", trade)
    shape = (block_x, size_y, 128)
    return call(close_kernel, ((shape, F32), ((2,) + shape, F32)), (), 8, "close", (kept, got))


def solution(mesh):
    in_specs = (
        P("gx", "gy", None),
        P("gx", "gy", None),
        P("gx", "gy", None),
        P("gx", "gy", None),
        P("gx", "gy", None),
        P("shot"),
        P("shot"),
        P("shot"),
        P("shot"),
        P(None, "shot"),
        P(None, ("shot", "gx"), "gy", None),
        P(None, ("shot", "gx"), "gy", None),
    )
    out_specs = (P(("shot", "gx"), "gy", None), P(None, ("shot", "gx"), "gy", None))
    return jax.shard_map(
        per_device, mesh=mesh, in_specs=in_specs, out_specs=out_specs, check_vma=False
    )
```

```python
import functools

import jax
import jax.numpy as jnp
from jax import lax
from jax.experimental import pallas as pl
from jax.experimental.pallas import tpu as pltpu
from jax.sharding import PartitionSpec as P

NT = 8
SRC_DEPTH = 10
REC_DEPTH = 6
F32 = jnp.float32
BF16 = jnp.bfloat16

second_taps = (-205.0 / 72.0, 8.0 / 5.0, -1.0 / 5.0, 8.0 / 315.0, -1.0 / 560.0)
first_taps = (4.0 / 5.0, -1.0 / 5.0, 4.0 / 105.0, -1.0 / 280.0)
CENTRE = second_taps[0]
S1 = second_taps[1]
G1 = first_taps[0]
second_ratio = tuple(tap / S1 for tap in second_taps[2:])
first_ratio = tuple(tap / G1 for tap in first_taps[1:])
second_whole = (8064.0, -1008.0, 128.0, -9.0)
first_whole = (672.0, -168.0, 32.0, -3.0)
SECOND_UNIT = 1.0 / 5040.0
FIRST_UNIT = 1.0 / 840.0
VMEM = pl.BlockSpec(memory_space=pltpu.VMEM)
SMEM = pl.BlockSpec(memory_space=pltpu.SMEM)
HBM = pl.BlockSpec(memory_space=pltpu.HBM)


def even_pairs(count):
    return [(i, i + 1) for i in range(0, count - 1, 2)]


def odd_pairs(count):
    return [(i, i + 1) for i in range(1, count - 1, 2)]


def both_ways(pairs):
    return [pair for a, b in pairs for pair in ((a, b), (b, a))]


def chip_swap(pairs):
    return [(2 * a + c, 2 * b + c) for a, b in pairs for c in range(2)]


class Place:
    def __init__(self, size_x, columns):
        at_x = lax.axis_index("gx")
        self.core, self.column = lax.rem(at_x, 2), lax.div(at_x, 2)
        self.at_y = lax.axis_index("gy")
        self.parity = lax.rem(self.at_y, 2)
        if columns == 2:
            side = self.column
            self.count = size_x + 4
            self.first_at = self.tile_at = 4 * side
            self.start_x = side * (size_x - 4)
            self.beside_at = [size_x * (1 - side)]
            self.edge_at = [(size_x - GROUP) * (1 - side)]
            self.rest_at, self.rest = GROUP * side, size_x - GROUP
        else:
            side = lax.rem(self.column, 2)
            self.count = size_x + 8
            self.first_at = self.tile_at = 4
            self.start_x = self.column * size_x - 4
            self.beside_at = [(size_x + GROUP) * (1 - side), (size_x + GROUP) * side]
            self.edge_at = [(size_x - GROUP) * (1 - side), (size_x - GROUP) * side]
            self.rest_at, self.rest = GROUP, size_x - 2 * GROUP
        self.sides = len(self.beside_at)
        self.own_at = self.first_at + self.tile_at
        self.wide = size_x + GROUP * self.sides


def call(kernel, outs, scratch, mebibytes, name, args, scalars=0, work=10**6):
    outs = tuple(jax.ShapeDtypeStruct(shape, dtype) for shape, dtype in outs)
    return pl.pallas_call(
        kernel,
        out_shape=outs,
        in_specs=[SMEM] * scalars + [VMEM] * (len(args) - scalars),
        out_specs=(VMEM,) * len(outs),
        scratch_shapes=[pltpu.VMEM(shape, dtype) for shape, dtype in scratch],
        compiler_params=pltpu.CompilerParams(vmem_limit_bytes=mebibytes * 2**20),
        cost_estimate=pl.CostEstimate(flops=work, bytes_accessed=work, transcendentals=0),
        name=name,
    )(*args)


def loop(trips, body, wanted):
    unroll = max(u for u in range(1, wanted + 1) if trips % u == 0)

    def step(i, carry):
        body(i)
        return carry

    lax.fori_loop(0, trips, step, 0, unroll=unroll)


def depth_matrices(size):
    rows = jnp.arange(size)[:, None]
    cols = jnp.arange(size)[None, :]
    first = jnp.zeros((size, size), F32)
    second = jnp.zeros((size, size), F32)
    for k in range(1, 5):
        up = (rows == cols + k).astype(F32)
        down = (rows == cols - k).astype(F32)
        first = first + first_whole[k - 1] * (up - down)
        second = second + second_whole[k - 1] * (up + down)
    return (
        jnp.concatenate([first, first]).astype(BF16),
        jnp.concatenate([second, second]).astype(BF16),
    )


def sums_and_slopes(shifted):
    up, down = shifted(1), shifted(-1)
    curve, slope = up + down, up - down
    for k in range(2, 5):
        up, down = shifted(k), shifted(-k)
        curve = curve + second_ratio[k - 2] * (up + down)
        slope = slope + first_ratio[k - 2] * (up - down)
    return curve, slope


def slope_only(shifted):
    slope = shifted(1) - shifted(-1)
    for k in range(2, 5):
        slope = slope + first_ratio[k - 2] * (shifted(k) - shifted(-k))
    return slope


def split(values):
    high = values.astype(BF16)
    low = (values - high.astype(F32)).astype(BF16)
    return high, low


TOP = 32000.0
GROUP = 8


def tiles_of(fields):
    return fields * 4 + fields // 2


def encode(value_at, out, group, fields):
    lane = lax.broadcasted_iota(jnp.int32, (8, 128), 1)
    for pair in range(fields // 2):
        codes = []
        for f in (2 * pair, 2 * pair + 1):
            values = [value_at(f, p) for p in range(GROUP)]
            sizes = jnp.full((8, 128), 1e-30, F32)
            for p in range(GROUP):
                largest = jnp.max(jnp.abs(values[p]), axis=1, keepdims=True)
                sizes = jnp.where(lane == p, jnp.maximum(largest, 1e-30), sizes)
            code = jnp.ceil(jnp.log2(sizes) * 256.0)
            factor = TOP * jnp.exp2(code * (-1.0 / 256.0))
            codes.append(code)
            for q in range(GROUP // 2):
                both = [
                    jnp.floor(values[p] * factor[:, p : p + 1] + 0.5) for p in (2 * q, 2 * q + 1)
                ]
                whole = jnp.concatenate(both).astype(jnp.int32).astype(jnp.int16)
                out[group, f * 4 + q] = whole
        out[group, fields * 4 + pair] = jnp.concatenate(codes).astype(jnp.int32).astype(jnp.int16)


def decode(payload, group, fields, put):
    for pair in range(fields // 2):
        code = payload[group, fields * 4 + pair].astype(jnp.int32).astype(F32)
        factor = jnp.exp2(code * (1.0 / 256.0)) * (1.0 / TOP)
        for slot in range(2):
            f = 2 * pair + slot
            own = factor[slot * 8 : slot * 8 + 8]
            for q in range(GROUP // 2):
                both = payload[group, f * 4 + q].astype(jnp.int32).astype(F32)
                put(f, 2 * q, both[:8] * own[:, 2 * q : 2 * q + 1])
                put(f, 2 * q + 1, both[8:] * own[:, 2 * q + 1 : 2 * q + 2])


def leap(src, x0, row0, rows, count, scratch, mats, coef, old_at, inject_at, store):
    slope_y, curve_y, part, halves, product = scratch
    mat_first, mat_second = mats
    planes = 16 // rows
    group = 4

    def field(f, p, r=0, number=rows):
        return src[f, x0 + p, pl.ds(row0 + r, number), :]

    def joined(values):
        return jnp.concatenate(values) if len(values) > 1 else values[0]

    def put_halves(kind, f, unit, values):
        high, low = split(values)
        halves[kind, f, unit, :, :128] = high
        halves[kind, f, unit, :, 128:] = low

    def along_y(u):
        for f in range(2):
            here, slopes = [], []
            for v in range(planes):
                p = u * planes + v
                curve, slope = sums_and_slopes(lambda k: field(f, p, k))
                slope_y[f, p, :rows] = slope
                curve_y[f, p, :rows] = curve
                slopes.append(slope)
                here.append(field(f, p))
            put_halves(0, f, u, joined(here))
            put_halves(1, f, u, joined(slopes))

    loop((count + 8) // planes, along_y, 4)

    def along_x(q):
        base = q * group
        for f in range(2):
            slopes = [[] for g in range(group)]
            for r in range(0, rows, 8):
                line = [field(f, base + k, r, 8) for k in range(group + 8)]
                slant = [slope_y[f, base + k, pl.ds(r, 8), :] for k in range(group + 8)]
                for g in range(group):
                    i = base + g
                    xx, slope = sums_and_slopes(lambda k: line[g + 4 + k])
                    xy = slope_only(lambda k: slant[g + 4 + k])
                    yy = curve_y[f, i + 4, pl.ds(r, 8), :]
                    wx, wy, wxy = [coef(m, i, r, 8) for m in (3, 4, 6)]
                    if f == 0:
                        total = (2.0 * CENTRE) * line[g + 4] + (S1 - wx) * xx
                        total = total + (S1 - wy) * yy - wxy * xy
                    else:
                        total = CENTRE * line[g + 4] + wx * xx
                        total = total + wy * yy + wxy * xy
                    part[f, i, pl.ds(r, 8), :] = total
                    slopes[g].append(slope)
            pieces = [piece for rest in slopes for piece in rest]
            for k in range(0, len(pieces), 2):
                put_halves(2, f, q * (len(pieces) // 2) + k // 2, joined(pieces[k : k + 2]))

    loop(count // group, along_x, 1)

    units = count // planes
    for kind, mat, at in ((0, mat_second, 4 // planes), (1, mat_first, 4 // planes), (2, mat_first, 0)):
        for f in range(2):
            both = halves[kind, f, pl.ds(at, units)].reshape(units * 16, 256)
            out = jnp.dot(both, mat[...], preferred_element_type=F32)
            product[kind, f, pl.ds(0, units)] = out.reshape(units, 16, 128)

    def combine(u):
        where = [u * planes + v for v in range(planes)]
        speed, speed_h, speed_v, wz, wyz, wxz = [
            joined([coef(m, i, 0, rows) for i in where]) for m in (0, 1, 2, 5, 7, 8)
        ]
        zz, yz, xz = [[product[kind, f, u] for f in range(2)] for kind in range(3)]
        parts = [joined([part[f, i, :rows] for i in where]) for f in range(2)]
        here = [joined([field(f, i + 4) for i in where]) for f in range(2)]
        old = [joined([old_at(f, i) for i in where]) for f in range(2)]
        add = joined([inject_at(i) for i in where])
        flat = parts[0] + (SECOND_UNIT - wz) * zz[0] - (wyz * yz[0] + wxz * xz[0])
        tilted = parts[1] + wz * zz[1] + (wyz * yz[1] + wxz * xz[1])
        new_p = (2.0 * here[0] - old[0] + add) + (speed_h * flat + speed_v * tilted)
        new_q = (2.0 * here[1] - old[1] + add) + (speed_v * flat + speed * tilted)
        for v, i in enumerate(where):
            cut = slice(v * rows, v * rows + rows)
            store(i, new_p[cut], new_q[cut])

    loop(units, combine, 4)


def leap_scratch(count):
    lines = (2, count + 8, 16, 128)
    return [
        (lines, F32),
        (lines, F32),
        ((2, count, 16, 128), F32),
        ((3, 2, count + 8, 16, 256), BF16),
        ((3, 2, count, 16, 128), F32),
    ]


def first_kernel(columns, kept, got, near_side, far_side, tile, old, payload):
    size = kept.shape[1]
    place = Place(2 * size, columns)
    for source, at in ((kept, place.core * size), (got, (1 - place.core) * size)):
        for f in range(2):
            tile[f, pl.ds(at, size)] = source[2 * f]
            old[f, pl.ds(at, size)] = source[2 * f + 1]

    def group(g):
        encode(lambda f, p: (tile if f < 2 else old)[f % 2, g * GROUP + p], payload, g, 4)

    groups = 2 * size // GROUP
    loop(groups, group, 1)

    def beside(k, source):
        encode(lambda f, p: source[2 * (f % 2) + f // 2, p], payload, groups + k, 4)

    if place.sides == 1:
        pl.when(place.core == place.column)(lambda: beside(0, near_side))
        pl.when(place.core != place.column)(lambda: beside(0, far_side))
    else:
        above_first = lax.rem(place.column, 2)
        for core, (above, below) in enumerate(((near_side, far_side), (far_side, near_side))):
            for swapped in range(2):
                @pl.when(jnp.logical_and(place.core == core, above_first == swapped))
                def _():
                    beside(swapped, above)
                    beside(1 - swapped, below)


def second_leap(moment, place, size_y, start, count, middle, tile, coefs, inject, scratch, mats, store):
    leap(
        middle, place.tile_at + start, 8, size_y, count, scratch, mats,
        lambda m, i, r, number: coefs[m, place.tile_at + start + i, pl.ds(4 + r, number), :],
        lambda f, i: tile[f, start + i],
        lambda i: inject[moment + 1, place.tile_at + start + i, pl.ds(4, size_y), :],
        store,
    )


def lead_kernel(moment, columns, tile, old, coefs, inject, mat_first, mat_second, *refs):
    opening, closing = moment == 0, moment == NT - 2
    size_x, size_y = tile.shape[1], tile.shape[2]
    place = Place(size_x, columns)
    sides, count, wide = place.sides, place.count, place.wide
    refs = list(refs)

    def take(number):
        taken = refs[:number]
        del refs[:number]
        return taken

    beside = take(1 if opening else sides)
    even, odd = take(2)
    if closing:
        levels = take(NT - 1)
        kept_out, sent_out = take(2)
        middle, tile_out = take(2)
    else:
        middle, old_out = take(2)
        edges_out, codes_out = take(sides), take(sides)
    window, old_wide = take(2)
    scratch, mats = refs, (mat_first, mat_second)
    fields = 4 if opening else 2

    for f in range(2):
        window[f, pl.ds(0, 4)] = jnp.zeros((4, 32, 128), F32)
        window[f, pl.ds(wide + 4, 4)] = jnp.zeros((4, 32, 128), F32)
        middle[f, pl.ds(0, 4)] = jnp.zeros((4, 24, 128), F32)
        middle[f, pl.ds(count + 4, 4)] = jnp.zeros((4, 24, 128), F32)
        window[f, pl.ds(place.own_at + 4, size_x), pl.ds(12, 8), :] = tile[f]
        if opening:
            old_wide[f, pl.ds(place.own_at, size_x), pl.ds(4, 8), :] = old[f]

    def lay(payload, group, plane, row):
        def put(f, p, rows):
            if f < 2:
                window[f, plane + p + 4, pl.ds(row + 12, 8), :] = rows
            elif row == 0:
                old_wide[f - 2, plane + p, pl.ds(4, 8), :] = rows
            elif row < 0:
                old_wide[f - 2, plane + p, pl.ds(0, 4), :] = rows[4:]
            else:
                old_wide[f - 2, plane + p, pl.ds(12, 4), :] = rows[:4]

        decode(payload, group, fields, put)

    groups = size_x // GROUP
    for k in range(sides):
        if opening:
            lay(beside[0], groups + k, place.beside_at[k], 0)
        else:
            lay(beside[k], 0, place.beside_at[k], 0)

    def lay_y(below, above):
        for payload, row in ((below, -8), (above, 8)):
            loop(groups, lambda g: lay(payload, g, place.own_at + g * GROUP, row), 2)
            for k in range(sides):
                lay(payload, groups + k, place.beside_at[k], row)

    pl.when(place.parity == 0)(lambda: lay_y(odd, even))
    pl.when(place.parity == 1)(lambda: lay_y(even, odd))

    def store(i, new_p, new_q):
        for f, new in enumerate((new_p, new_q)):
            if not closing:
                old_out[f, i] = new
            middle[f, i + 4, pl.ds(4, size_y + 8), :] = new

    leap(
        window, place.first_at, 8, size_y + 8, count, scratch, mats,
        lambda m, i, r, number: coefs[m, i, pl.ds(r, number), :],
        (lambda f, i: old_wide[f, place.first_at + i]) if opening else (lambda f, i: old[f, i]),
        lambda i: inject[moment, i],
        store,
    )

    if not closing:
        for k in range(sides):
            def store_edge(i, new_p, new_q):
                edges_out[k][0, i] = new_p
                edges_out[k][1, i] = new_q

            second_leap(
                moment, place, size_y, place.edge_at[k], GROUP, middle, tile, coefs, inject,
                scratch, mats, store_edge,
            )
            encode(lambda f, p: edges_out[k][f, p], codes_out[k], 0, 2)
        return

    def store_tile(i, new_p, new_q):
        tile_out[0, i] = new_p
        tile_out[1, i] = new_q

    second_leap(
        moment, place, size_y, 0, size_x, middle, tile, coefs, inject, scratch, mats, store_tile
    )

    half = size_x // 2

    def level_at(step, start):
        planes = pl.ds(start, half)
        if step == NT:
            return tile_out[0, planes]
        if step == NT - 1:
            return middle[0, pl.ds(place.tile_at + 4 + start, half), pl.ds(8, size_y), :]
        where = levels[step]
        if step % 2 == 0:
            return where[0, planes]
        return where[0, pl.ds(place.tile_at + start, half), pl.ds(4, size_y), :]

    for mine in range(2):
        @pl.when(place.core == mine)
        def _():
            stay, leave = mine * half, (1 - mine) * half
            for t in range(1, NT + 1):
                step = t if mine == 0 else NT - t
                kept_out[t - 1] = level_at(step, stay)
                sent_out[t - 1] = level_at(step, leave)
            for f in range(2):
                kept_out[NT + f] = tile_out[f, pl.ds(stay, half)]
                sent_out[NT + f] = tile_out[f, pl.ds(leave, half)]


def rest_kernel(moment, columns, tile, middle, coefs, inject, mat_first, mat_second, *refs):
    size_x, size_y = tile.shape[1], tile.shape[2]
    place = Place(size_x, columns)
    edges, (tile_out, payload), scratch = (
        refs[: place.sides], refs[place.sides : place.sides + 2], refs[place.sides + 2 :]
    )
    for k, edge in enumerate(edges):
        tile_out[:, pl.ds(place.edge_at[k], GROUP)] = edge[...]

    def store(i, new_p, new_q):
        tile_out[0, place.rest_at + i] = new_p
        tile_out[1, place.rest_at + i] = new_q

    second_leap(
        moment, place, size_y, place.rest_at, place.rest, middle, tile, coefs, inject, scratch,
        (mat_first, mat_second), store,
    )
    loop(
        size_x // GROUP,
        lambda g: encode(lambda f, p: tile_out[f, g * GROUP + p], payload, g, 2),
        1,
    )


def sine_cosine(angle):
    square = angle * angle
    sine = 1.0 / 6227020800.0
    for factor in (-1.0 / 39916800.0, 1.0 / 362880.0, -1.0 / 5040.0, 1.0 / 120.0, -1.0 / 6.0):
        sine = sine * square + factor
    sine = angle + angle * square * sine
    cosine = 1.0 / 479001600.0
    for factor in (-1.0 / 3628800.0, 1.0 / 40320.0, -1.0 / 720.0, 1.0 / 24.0, -0.5):
        cosine = cosine * square + factor
    return sine, 1.0 + square * cosine


def open_kernel(
    velocity, epsilon, delta, tilt, azimuth, source, receiver, even, odd, own, kept, given,
    near_side, far_side, arrived,
):
    models = (velocity, epsilon, delta, tilt, azimuth)
    parity = lax.rem(lax.axis_index("gy"), 2)
    core = lax.rem(lax.axis_index("gx"), 2)
    copies = [pltpu.make_async_copy(models[m], own.at[m], arrived.at[m]) for m in range(5)]

    def states(mine):
        stay, leave = (source, receiver) if mine == 0 else (receiver, source)
        return (
            pltpu.make_async_copy(stay, kept, arrived.at[5]),
            pltpu.make_async_copy(leave, given, arrived.at[6]),
        )

    for copy in copies:
        copy.start()
    for mine in range(2):
        @pl.when(core == mine)
        def _():
            for copy in states(mine):
                copy.start()

    for copy in copies:
        copy.wait()

    def pack(out, row):
        for m in range(5):
            for u in range(0, own.shape[1], 2):
                pairs = [own[m, u + k].astype(F32) for k in range(2)]
                values = [pair[v + row : v + row + 4] for pair in pairs for v in (0, 8)]
                out[m, u // 2] = jnp.concatenate(values).astype(BF16)

    @pl.when(parity == 0)
    def _():
        pack(even, 4)
        pack(odd, 0)

    @pl.when(parity == 1)
    def _():
        pack(odd, 4)
        pack(even, 0)

    for mine in range(2):
        @pl.when(core == mine)
        def _():
            for copy in states(mine):
                copy.wait()
            edge = pl.ds(mine * (kept.shape[1] - GROUP), GROUP)
            near_side[...] = kept[:, edge]
            far_side[...] = given[:, edge]


def join_kernel(own, even, odd, out):
    parity = lax.rem(lax.axis_index("gy"), 2)

    def fill(below, above):
        for m in range(5):
            for u in range(own.shape[1]):
                low, high = below[m, u // 2].astype(F32), above[m, u // 2].astype(F32)
                pair = own[m, u].astype(F32)
                for v in range(2):
                    k = 2 * (u % 2) + v
                    rows = [low[4 * k : 4 * k + 4], pair[8 * v : 8 * v + 8], high[4 * k : 4 * k + 4]]
                    out[m, 2 * u + v] = jnp.concatenate(rows).astype(BF16)

    pl.when(parity == 0)(lambda: fill(odd, even))
    pl.when(parity == 1)(lambda: fill(even, odd))


def setup_kernel(columns, size_x, total_x, aperture, *refs):
    models, coefs, blocks = refs[:-2], refs[-2], refs[-1]
    place = Place(2 * size_x, columns)
    if len(models) > 1:
        for k, column in enumerate((place.column, 1 - place.column)):
            for j, core in enumerate((place.core, 1 - place.core)):
                blocks[:, pl.ds((2 * column + core) * size_x, size_x)] = models[2 * k + j][...]
        source = blocks
    else:
        source = models[0]

    def medium(i):
        x = place.start_x + i
        block = jnp.clip(x // size_x, 0, total_x // size_x - 1)
        inside = jnp.logical_and(x >= 0, x < total_x)
        at = aperture[block] * size_x + lax.rem(x + size_x, size_x)
        speed, stretch, bending, tilt, azimuth = [source[m, at].astype(F32) for m in range(5)]
        speed = jnp.where(inside, speed, 0.0)
        sin_t, cos_t = sine_cosine(tilt)
        sin_half, cos_half = sine_cosine(0.5 * azimuth)
        normal_x = sin_t * (1.0 - 2.0 * sin_half * sin_half)
        normal_y = sin_t * (2.0 * sin_half * cos_half)
        coefs[0, i] = speed
        coefs[1, i] = speed * (1.0 + 2.0 * stretch)
        coefs[2, i] = speed * jnp.sqrt(1.0 + 2.0 * bending)
        coefs[3, i] = S1 * (normal_x * normal_x)
        coefs[4, i] = S1 * (normal_y * normal_y)
        coefs[5, i] = SECOND_UNIT * (cos_t * cos_t)
        coefs[6, i] = (2.0 * G1 * G1) * (normal_x * normal_y)
        coefs[7, i] = (2.0 * G1 * FIRST_UNIT) * (normal_y * cos_t)
        coefs[8, i] = (2.0 * G1 * FIRST_UNIT) * (normal_x * cos_t)

    loop(place.count, medium, 4)


def injection_kernel(
    columns, size_x, size_y, total_y, source_cell, wavelet, cells, traces, out, hits, lanes
):
    place = Place(size_x, columns)
    count, rows = hits.shape[:2]
    number = cells.shape[1]
    row = lax.broadcasted_iota(jnp.int32, (rows, number), 0)
    lane = lax.broadcasted_iota(jnp.int32, (1, number), 1)
    is_source = place.core == 0
    lonely = jnp.where(lane == 0, source_cell[0], -1)
    aims = jnp.where(is_source, lonely, cells[...])
    y = place.at_y * size_y - 4 + row
    valid = jnp.logical_and(y >= 0, y < total_y)

    def mark(i):
        code = jnp.where(valid, (place.start_x + i) * total_y + y, -2)
        hits[i] = jnp.where(code == aims, 1.0, 0.0).astype(BF16)

    loop(count, mark, 2)
    step = lax.broadcasted_iota(jnp.int32, (NT, number), 0)
    amounts = jnp.zeros((NT, number), F32)
    for k in range(NT):
        amounts = jnp.where(step == k, wavelet[k], amounts)
    backward = jnp.concatenate([traces[k : k + 1] for k in reversed(range(NT))])
    rest = jnp.where(is_source, amounts, backward)
    total = None
    for _ in range(3):
        piece = rest.astype(BF16)
        rest = rest - piece.astype(F32)
        term = lax.dot_general(
            hits[...].reshape(count * rows, number), piece, (((1,), (1,)), ((), ())),
            preferred_element_type=F32,
        )
        total = term if total is None else total + term
    lanes[...] = total.reshape(count, rows, NT)
    level = jnp.where(is_source, SRC_DEPTH, REC_DEPTH)
    mask = (lax.broadcasted_iota(jnp.int32, (rows, 128), 1) == level).astype(F32)

    def expand(i):
        values = lanes[i]
        for k in range(NT):
            out[k, i] = values[:, k : k + 1] * mask

    loop(count, expand, 2)


def close_kernel(kept, got, image, field):
    total = kept[0] * got[0]
    for t in range(1, NT):
        total = total + kept[t] * got[t]
    image[...] = total * (1.0 / NT)
    core = lax.rem(lax.axis_index("gx"), 2)

    @pl.when(core == 0)
    def _():
        field[...] = got[pl.ds(NT, 2)]

    @pl.when(core == 1)
    def _():
        field[...] = kept[pl.ds(NT, 2)]


def per_device(
    velocity,
    epsilon,
    delta,
    tilt,
    azimuth,
    aperture,
    source_cell,
    wavelet,
    receiver_cell,
    traces,
    source_state,
    receiver_state,
):
    block_x, size_y, _ = velocity.shape
    devices_x, devices_y = lax.axis_size("gx"), lax.axis_size("gy")
    columns = devices_x // 2
    total_x, total_y = block_x * devices_x, size_y * devices_y
    size_x, rows = 2 * block_x, size_y + 8
    is_source = lax.axis_index("gx") % 2 == 0
    place = Place(size_x, columns)
    sides, count = place.sides, place.count
    groups = size_x // GROUP
    mats = depth_matrices(128)
    chip_pairs = [even_pairs(columns), odd_pairs(columns)][:sides]
    row_pairs = [even_pairs(devices_y), odd_pairs(devices_y)]
    trade = both_ways([(2 * c, 2 * c + 1) for c in range(columns)])

    def over_gy(values, pairs):
        return lax.ppermute(values, "gy", both_ways(pairs))

    def over_gx(values, pairs):
        return lax.ppermute(values, "gx", both_ways(chip_swap(pairs)))

    def beside_of(edges):
        return [over_gx(edge, pairs) for edge, pairs in zip(edges, chip_pairs)]

    def near_of(payload, beside):
        wide = jnp.concatenate([payload, *beside])
        return wide, [over_gy(wide, pairs) for pairs in row_pairs]

    def codes(number, fields):
        return ((number, tiles_of(fields), 16, 128), jnp.int16)

    models = [
        values.reshape(block_x // 2, 16, 128) for values in (velocity, epsilon, delta, tilt, azimuth)
    ]
    rim = ((5, block_x // 4, 16, 128), BF16)
    states = (source_state, receiver_state)
    state = (source_state.shape, F32)
    side = ((4, GROUP, size_y, 128), F32)
    *rims, own, kept, given, near_side, far_side = pl.pallas_call(
        open_kernel,
        out_shape=tuple(
            jax.ShapeDtypeStruct(*out)
            for out in (rim, rim, ((5, block_x // 2, 16, 128), BF16), state, state, side, side)
        ),
        in_specs=[HBM] * 7,
        out_specs=(VMEM,) * 7,
        scratch_shapes=[pltpu.SemaphoreType.DMA((7,))],
        compiler_params=pltpu.CompilerParams(vmem_limit_bytes=8 * 2**20),
        name="open",
    )(*[pltpu.with_memory_space_constraint(x, pltpu.HBM) for x in (*models, *states)])
    rims = [over_gy(values, pairs) for values, pairs in zip(rims, row_pairs)]

    got = lax.ppermute(given, "gx", trade)
    pairs = [(c, c + 1) for c in range(columns - 1)]
    near_side = lax.ppermute(
        near_side, "gx", [(2 * a + 1, 2 * b + 1) for a, b in pairs] + [(2 * b, 2 * a) for a, b in pairs]
    )
    far_side = lax.ppermute(
        far_side, "gx", [(2 * a + 1, 2 * b) for a, b in pairs] + [(2 * b, 2 * a + 1) for a, b in pairs]
    )
    field = ((2, size_x, size_y, 128), F32)
    tile, old, wide = call(
        functools.partial(first_kernel, columns),
        (field, field, codes(groups + sides, 4)),
        (), 16, "first", (kept, got, near_side, far_side),
    )
    beside, near = [wide], [over_gy(wide, pairs) for pairs in row_pairs]

    (model,) = call(
        join_kernel, (((5, block_x, rows, 128), BF16),), (), 8, "join", (own, *rims), work=1000
    )
    number = receiver_cell.shape[0]
    cells, _ = lax.optimization_barrier((receiver_cell[None, :], wide))
    (inject,) = call(
        functools.partial(injection_kernel, columns, size_x, size_y, total_y),
        (((NT, count, rows, 128), F32),),
        (((count, rows, number), BF16), ((count, rows, NT), F32)),
        16, "injection", (source_cell, wavelet, cells, traces), scalars=2,
    )
    if columns == 2:
        across = over_gx(model, chip_pairs[0])
        other = lax.ppermute(model, "gx", trade)
        across, _ = lax.optimization_barrier((across, inject))
        gathered = [model, other, across, lax.ppermute(across, "gx", trade)]
        held = (5, total_x, rows, 128)
    else:
        gathered, held = [lax.all_gather(model, "gx", axis=1, tiled=True)], (16, 128)
    (coefs,) = call(
        functools.partial(setup_kernel, columns, block_x, total_x),
        (((9, count, rows, 128), F32),), ((held, BF16),), 24, "setup", (aperture, *gathered),
        scalars=1, work=0,
    )

    window = ((2, place.wide + 8, 32, 128), F32)
    middle = ((2, count + 8, 24, 128), F32)
    lines = ((2, count, rows, 128), F32)
    levels = [tile]
    for moment in range(0, NT - 2, 2):
        old_wide = ((2, place.wide, rows, 128) if moment == 0 else (8, 128), F32)
        between, old, *edges = call(
            functools.partial(lead_kernel, moment, columns),
            (middle, lines) + (((2, GROUP, size_y, 128), F32),) * sides + (codes(1, 2),) * sides,
            [window, old_wide] + leap_scratch(count), 24, "lead",
            (tile, old, coefs, inject, *mats, *beside, *near), work=4 * 10**6,
        )
        edges, edge_codes = edges[:sides], edges[sides:]
        beside = beside_of(edge_codes)
        tile, payload = call(
            functools.partial(rest_kernel, moment, columns),
            (field, codes(groups, 2)), leap_scratch(size_x), 24, "rest",
            (tile, between, coefs, inject, *mats, *edges), work=4 * 10**6,
        )
        wide, near = near_of(payload, beside)
        levels += [old, tile]
    share = ((NT + 2, block_x, size_y, 128), F32)
    kept, sent = call(
        functools.partial(lead_kernel, NT - 2, columns),
        (share, share),
        [middle, field, window, ((8, 128), F32)] + leap_scratch(count), 24, "last",
        (tile, old, coefs, inject, *mats, *beside, *near, *levels),
    )
    got = lax.ppermute(sent, "gx", trade)
    shape = (block_x, size_y, 128)
    return call(close_kernel, ((shape, F32), ((2,) + shape, F32)), (), 8, "close", (kept, got))


def solution(mesh):
    in_specs = (
        P("gx", "gy", None),
        P("gx", "gy", None),
        P("gx", "gy", None),
        P("gx", "gy", None),
        P("gx", "gy", None),
        P("shot"),
        P("shot"),
        P("shot"),
        P("shot"),
        P(None, "shot"),
        P(None, ("shot", "gx"), "gy", None),
        P(None, ("shot", "gx"), "gy", None),
    )
    out_specs = (P(("shot", "gx"), "gy", None), P(None, ("shot", "gx"), "gy", None))
    return jax.shard_map(
        per_device, mesh=mesh, in_specs=in_specs, out_specs=out_specs, check_vma=False
    )
```

```python
import functools

import jax
import jax.numpy as jnp
from jax import lax
from jax.experimental import pallas as pl
from jax.experimental.pallas import tpu as pltpu
from jax.sharding import PartitionSpec as P

NT = 8
SRC_DEPTH = 10
REC_DEPTH = 6
F32 = jnp.float32
BF16 = jnp.bfloat16

second_taps = (-205.0 / 72.0, 8.0 / 5.0, -1.0 / 5.0, 8.0 / 315.0, -1.0 / 560.0)
first_taps = (4.0 / 5.0, -1.0 / 5.0, 4.0 / 105.0, -1.0 / 280.0)
CENTRE = second_taps[0]
S1 = second_taps[1]
G1 = first_taps[0]
second_ratio = tuple(tap / S1 for tap in second_taps[2:])
first_ratio = tuple(tap / G1 for tap in first_taps[1:])
second_whole = (8064.0, -1008.0, 128.0, -9.0)
first_whole = (672.0, -168.0, 32.0, -3.0)
SECOND_UNIT = 1.0 / 5040.0
FIRST_UNIT = 1.0 / 840.0
VMEM = pl.BlockSpec(memory_space=pltpu.VMEM)
SMEM = pl.BlockSpec(memory_space=pltpu.SMEM)
HBM = pl.BlockSpec(memory_space=pltpu.HBM)


def even_pairs(count):
    return [(i, i + 1) for i in range(0, count - 1, 2)]


def odd_pairs(count):
    return [(i, i + 1) for i in range(1, count - 1, 2)]


def both_ways(pairs):
    return [pair for a, b in pairs for pair in ((a, b), (b, a))]


def chip_swap(pairs):
    return [(2 * a + c, 2 * b + c) for a, b in pairs for c in range(2)]


class Place:
    def __init__(self, size_x, columns):
        at_x = lax.axis_index("gx")
        self.core, self.column = lax.rem(at_x, 2), lax.div(at_x, 2)
        self.at_y = lax.axis_index("gy")
        self.parity = lax.rem(self.at_y, 2)
        if columns == 2:
            side = self.column
            self.count = size_x + 4
            self.first_at = self.tile_at = 4 * side
            self.start_x = side * (size_x - 4)
            self.beside_at = [size_x * (1 - side)]
            self.edge_at = [(size_x - GROUP) * (1 - side)]
            self.rest_at, self.rest = GROUP * side, size_x - GROUP
        else:
            side = lax.rem(self.column, 2)
            self.count = size_x + 8
            self.first_at = self.tile_at = 4
            self.start_x = self.column * size_x - 4
            self.beside_at = [(size_x + GROUP) * (1 - side), (size_x + GROUP) * side]
            self.edge_at = [(size_x - GROUP) * (1 - side), (size_x - GROUP) * side]
            self.rest_at, self.rest = GROUP, size_x - 2 * GROUP
        self.sides = len(self.beside_at)
        self.own_at = self.first_at + self.tile_at
        self.wide = size_x + GROUP * self.sides


def call(kernel, outs, scratch, mebibytes, name, args, scalars=0, work=10**6):
    outs = tuple(jax.ShapeDtypeStruct(shape, dtype) for shape, dtype in outs)
    return pl.pallas_call(
        kernel,
        out_shape=outs,
        in_specs=[SMEM] * scalars + [VMEM] * (len(args) - scalars),
        out_specs=(VMEM,) * len(outs),
        scratch_shapes=[pltpu.VMEM(shape, dtype) for shape, dtype in scratch],
        compiler_params=pltpu.CompilerParams(vmem_limit_bytes=mebibytes * 2**20),
        cost_estimate=pl.CostEstimate(flops=work, bytes_accessed=work, transcendentals=0),
        name=name,
    )(*args)


def loop(trips, body, wanted):
    unroll = max(u for u in range(1, wanted + 1) if trips % u == 0)

    def step(i, carry):
        body(i)
        return carry

    lax.fori_loop(0, trips, step, 0, unroll=unroll)


def depth_matrices(size):
    rows = jnp.arange(size)[:, None]
    cols = jnp.arange(size)[None, :]
    first = jnp.zeros((size, size), F32)
    second = jnp.zeros((size, size), F32)
    for k in range(1, 5):
        up = (rows == cols + k).astype(F32)
        down = (rows == cols - k).astype(F32)
        first = first + first_whole[k - 1] * (up - down)
        second = second + second_whole[k - 1] * (up + down)
    return (
        jnp.concatenate([first, first]).astype(BF16),
        jnp.concatenate([second, second]).astype(BF16),
    )


def sums_and_slopes(shifted):
    up, down = shifted(1), shifted(-1)
    curve, slope = up + down, up - down
    for k in range(2, 5):
        up, down = shifted(k), shifted(-k)
        curve = curve + second_ratio[k - 2] * (up + down)
        slope = slope + first_ratio[k - 2] * (up - down)
    return curve, slope


def slope_only(shifted):
    slope = shifted(1) - shifted(-1)
    for k in range(2, 5):
        slope = slope + first_ratio[k - 2] * (shifted(k) - shifted(-k))
    return slope


def split(values):
    high = values.astype(BF16)
    low = (values - high.astype(F32)).astype(BF16)
    return high, low


TOP = 32000.0
GROUP = 8


def tiles_of(fields):
    return fields * 4 + fields // 2


def encode(value_at, out, group, fields):
    lane = lax.broadcasted_iota(jnp.int32, (8, 128), 1)
    for pair in range(fields // 2):
        codes = []
        for f in (2 * pair, 2 * pair + 1):
            values = [value_at(f, p) for p in range(GROUP)]
            sizes = jnp.full((8, 128), 1e-30, F32)
            for p in range(GROUP):
                largest = jnp.max(jnp.abs(values[p]), axis=1, keepdims=True)
                sizes = jnp.where(lane == p, jnp.maximum(largest, 1e-30), sizes)
            code = jnp.ceil(jnp.log2(sizes) * 256.0)
            factor = TOP * jnp.exp2(code * (-1.0 / 256.0))
            codes.append(code)
            for q in range(GROUP // 2):
                both = [
                    jnp.floor(values[p] * factor[:, p : p + 1] + 0.5) for p in (2 * q, 2 * q + 1)
                ]
                whole = jnp.concatenate(both).astype(jnp.int32).astype(jnp.int16)
                out[group, f * 4 + q] = whole
        out[group, fields * 4 + pair] = jnp.concatenate(codes).astype(jnp.int32).astype(jnp.int16)


def decode(payload, group, fields, put):
    for pair in range(fields // 2):
        code = payload[group, fields * 4 + pair].astype(jnp.int32).astype(F32)
        factor = jnp.exp2(code * (1.0 / 256.0)) * (1.0 / TOP)
        for slot in range(2):
            f = 2 * pair + slot
            own = factor[slot * 8 : slot * 8 + 8]
            for q in range(GROUP // 2):
                both = payload[group, f * 4 + q].astype(jnp.int32).astype(F32)
                put(f, 2 * q, both[:8] * own[:, 2 * q : 2 * q + 1])
                put(f, 2 * q + 1, both[8:] * own[:, 2 * q + 1 : 2 * q + 2])


def leap(src, x0, row0, rows, count, scratch, mats, coef, old_at, inject_at, store):
    slope_y, curve_y, part, halves, product = scratch
    mat_first, mat_second = mats
    planes = 16 // rows
    group = 4

    def field(f, p, r=0, number=rows):
        return src[f, x0 + p, pl.ds(row0 + r, number), :]

    def joined(values):
        return jnp.concatenate(values) if len(values) > 1 else values[0]

    def put_halves(kind, f, unit, values):
        high, low = split(values)
        halves[kind, f, unit, :, :128] = high
        halves[kind, f, unit, :, 128:] = low

    def along_y(u):
        for f in range(2):
            here, slopes = [], []
            for v in range(planes):
                p = u * planes + v
                curve, slope = sums_and_slopes(lambda k: field(f, p, k))
                slope_y[f, p, :rows] = slope
                curve_y[f, p, :rows] = curve
                slopes.append(slope)
                here.append(field(f, p))
            put_halves(0, f, u, joined(here))
            put_halves(1, f, u, joined(slopes))

    loop((count + 8) // planes, along_y, 4)

    def along_x(q):
        base = q * group
        for f in range(2):
            slopes = [[] for g in range(group)]
            for r in range(0, rows, 8):
                line = [field(f, base + k, r, 8) for k in range(group + 8)]
                slant = [slope_y[f, base + k, pl.ds(r, 8), :] for k in range(group + 8)]
                for g in range(group):
                    i = base + g
                    xx, slope = sums_and_slopes(lambda k: line[g + 4 + k])
                    xy = slope_only(lambda k: slant[g + 4 + k])
                    yy = curve_y[f, i + 4, pl.ds(r, 8), :]
                    wx, wy, wxy = [coef(m, i, r, 8) for m in (3, 4, 6)]
                    if f == 0:
                        total = (2.0 * CENTRE) * line[g + 4] + (S1 - wx) * xx
                        total = total + (S1 - wy) * yy - wxy * xy
                    else:
                        total = CENTRE * line[g + 4] + wx * xx
                        total = total + wy * yy + wxy * xy
                    part[f, i, pl.ds(r, 8), :] = total
                    slopes[g].append(slope)
            pieces = [piece for rest in slopes for piece in rest]
            for k in range(0, len(pieces), 2):
                put_halves(2, f, q * (len(pieces) // 2) + k // 2, joined(pieces[k : k + 2]))

    loop(count // group, along_x, 1)

    units = count // planes
    for kind, mat, at in ((0, mat_second, 4 // planes), (1, mat_first, 4 // planes), (2, mat_first, 0)):
        for f in range(2):
            both = halves[kind, f, pl.ds(at, units)].reshape(units * 16, 256)
            out = jnp.dot(both, mat[...], preferred_element_type=F32)
            product[kind, f, pl.ds(0, units)] = out.reshape(units, 16, 128)

    def combine(u):
        where = [u * planes + v for v in range(planes)]
        speed, speed_h, speed_v, wz, wyz, wxz = [
            joined([coef(m, i, 0, rows) for i in where]) for m in (0, 1, 2, 5, 7, 8)
        ]
        zz, yz, xz = [[product[kind, f, u] for f in range(2)] for kind in range(3)]
        parts = [joined([part[f, i, :rows] for i in where]) for f in range(2)]
        here = [joined([field(f, i + 4) for i in where]) for f in range(2)]
        old = [joined([old_at(f, i) for i in where]) for f in range(2)]
        add = joined([inject_at(i) for i in where])
        flat = parts[0] + (SECOND_UNIT - wz) * zz[0] - (wyz * yz[0] + wxz * xz[0])
        tilted = parts[1] + wz * zz[1] + (wyz * yz[1] + wxz * xz[1])
        new_p = (2.0 * here[0] - old[0] + add) + (speed_h * flat + speed_v * tilted)
        new_q = (2.0 * here[1] - old[1] + add) + (speed_v * flat + speed * tilted)
        for v, i in enumerate(where):
            cut = slice(v * rows, v * rows + rows)
            store(i, new_p[cut], new_q[cut])

    loop(units, combine, 4)


def leap_scratch(count):
    lines = (2, count + 8, 16, 128)
    return [
        (lines, F32),
        (lines, F32),
        ((2, count, 16, 128), F32),
        ((3, 2, count + 8, 16, 256), BF16),
        ((3, 2, count, 16, 128), F32),
    ]


def first_kernel(columns, kept, got, tile, old, payload, *edges):
    size = kept.shape[1]
    place = Place(2 * size, columns)
    for source, at in ((kept, place.core * size), (got, (1 - place.core) * size)):
        for f in range(2):
            tile[f, pl.ds(at, size)] = source[2 * f]
            old[f, pl.ds(at, size)] = source[2 * f + 1]

    def group(g):
        encode(lambda f, p: (tile if f < 2 else old)[f % 2, g * GROUP + p], payload, g, 4)

    loop(2 * size // GROUP, group, 1)
    for k, edge in enumerate(edges):
        edge[0] = payload[lax.div(place.edge_at[k], GROUP)]


def second_leap(moment, place, size_y, start, count, middle, tile, coefs, inject, scratch, mats, store):
    leap(
        middle, place.tile_at + start, 8, size_y, count, scratch, mats,
        lambda m, i, r, number: coefs[m, place.tile_at + start + i, pl.ds(4 + r, number), :],
        lambda f, i: tile[f, start + i],
        lambda i: inject[1, place.tile_at + start + i, pl.ds(4, size_y), :],
        store,
    )


def lead_kernel(moment, columns, tile, old, coefs, inject, mat_first, mat_second, *refs):
    opening, closing = moment == 0, moment == NT - 2
    size_x, size_y = tile.shape[1], tile.shape[2]
    place = Place(size_x, columns)
    sides, count, wide = place.sides, place.count, place.wide
    refs = list(refs)

    def take(number):
        taken = refs[:number]
        del refs[:number]
        return taken

    beside = take(sides)
    even, odd = take(2)
    if closing:
        kept_out, sent_out = take(2)
        middle, tile_out = take(2)
    else:
        middle, old_out = take(2)
        edges_out, codes_out = take(sides), take(sides)
    window, old_wide = take(2)
    scratch, mats = refs, (mat_first, mat_second)
    fields = 4 if opening else 2

    for f in range(2):
        window[f, pl.ds(0, 4)] = jnp.zeros((4, 32, 128), F32)
        window[f, pl.ds(wide + 4, 4)] = jnp.zeros((4, 32, 128), F32)
        middle[f, pl.ds(0, 4)] = jnp.zeros((4, 24, 128), F32)
        middle[f, pl.ds(count + 4, 4)] = jnp.zeros((4, 24, 128), F32)
        window[f, pl.ds(place.own_at + 4, size_x), pl.ds(12, 8), :] = tile[f]
        if opening:
            old_wide[f, pl.ds(place.own_at, size_x), pl.ds(4, 8), :] = old[f]

    def lay(payload, group, plane, row):
        def put(f, p, rows):
            if f < 2:
                window[f, plane + p + 4, pl.ds(row + 12, 8), :] = rows
            elif row == 0:
                old_wide[f - 2, plane + p, pl.ds(4, 8), :] = rows
            elif row < 0:
                old_wide[f - 2, plane + p, pl.ds(0, 4), :] = rows[4:]
            else:
                old_wide[f - 2, plane + p, pl.ds(12, 4), :] = rows[:4]

        decode(payload, group, fields, put)

    groups = size_x // GROUP
    for k in range(sides):
        lay(beside[k], 0, place.beside_at[k], 0)

    def lay_y(below, above):
        for payload, row in ((below, -8), (above, 8)):
            loop(groups, lambda g: lay(payload, g, place.own_at + g * GROUP, row), 2)
            for k in range(sides):
                lay(payload, groups + k, place.beside_at[k], row)

    pl.when(place.parity == 0)(lambda: lay_y(odd, even))
    pl.when(place.parity == 1)(lambda: lay_y(even, odd))

    def store(i, new_p, new_q):
        for f, new in enumerate((new_p, new_q)):
            if not closing:
                old_out[f, i] = new
            middle[f, i + 4, pl.ds(4, size_y + 8), :] = new

    leap(
        window, place.first_at, 8, size_y + 8, count, scratch, mats,
        lambda m, i, r, number: coefs[m, i, pl.ds(r, number), :],
        (lambda f, i: old_wide[f, place.first_at + i]) if opening else (lambda f, i: old[f, i]),
        lambda i: inject[0, i],
        store,
    )

    if not closing:
        for k in range(sides):
            def store_edge(i, new_p, new_q):
                edges_out[k][0, i] = new_p
                edges_out[k][1, i] = new_q

            second_leap(
                moment, place, size_y, place.edge_at[k], GROUP, middle, tile, coefs, inject,
                scratch, mats, store_edge,
            )
            encode(lambda f, p: edges_out[k][f, p], codes_out[k], 0, 2)
        return

    def store_tile(i, new_p, new_q):
        tile_out[0, i] = new_p
        tile_out[1, i] = new_q

    second_leap(
        moment, place, size_y, 0, size_x, middle, tile, coefs, inject, scratch, mats, store_tile
    )

    half = size_x // 2
    for mine in range(2):
        @pl.when(place.core == mine)
        def _():
            for out, start in ((kept_out, mine * half), (sent_out, (1 - mine) * half)):
                planes = pl.ds(start, half)
                inner = pl.ds(place.tile_at + 4 + start, half)
                out[0] = middle[0, inner, pl.ds(8, size_y), :]
                out[1] = tile_out[0, planes]
                out[2] = tile_out[1, planes]


def rest_kernel(moment, columns, tile, middle, coefs, inject, mat_first, mat_second, *refs):
    size_x, size_y = tile.shape[1], tile.shape[2]
    place = Place(size_x, columns)
    edges, (tile_out, payload), scratch = (
        refs[: place.sides], refs[place.sides : place.sides + 2], refs[place.sides + 2 :]
    )
    for k, edge in enumerate(edges):
        tile_out[:, pl.ds(place.edge_at[k], GROUP)] = edge[...]

    def store(i, new_p, new_q):
        tile_out[0, place.rest_at + i] = new_p
        tile_out[1, place.rest_at + i] = new_q

    second_leap(
        moment, place, size_y, place.rest_at, place.rest, middle, tile, coefs, inject, scratch,
        (mat_first, mat_second), store,
    )
    loop(
        size_x // GROUP,
        lambda g: encode(lambda f, p: tile_out[f, g * GROUP + p], payload, g, 2),
        1,
    )


def sine_cosine(angle):
    square = angle * angle
    sine = 1.0 / 6227020800.0
    for factor in (-1.0 / 39916800.0, 1.0 / 362880.0, -1.0 / 5040.0, 1.0 / 120.0, -1.0 / 6.0):
        sine = sine * square + factor
    sine = angle + angle * square * sine
    cosine = 1.0 / 479001600.0
    for factor in (-1.0 / 3628800.0, 1.0 / 40320.0, -1.0 / 720.0, 1.0 / 24.0, -0.5):
        cosine = cosine * square + factor
    return sine, 1.0 + square * cosine


def open_kernel(
    velocity, epsilon, delta, tilt, azimuth, source, receiver, even, odd, own, kept, given, arrived
):
    models = (velocity, epsilon, delta, tilt, azimuth)
    parity = lax.rem(lax.axis_index("gy"), 2)
    core = lax.rem(lax.axis_index("gx"), 2)
    copies = [pltpu.make_async_copy(models[m], own.at[m], arrived.at[m]) for m in range(5)]

    def states(mine):
        stay, leave = (source, receiver) if mine == 0 else (receiver, source)
        return (
            pltpu.make_async_copy(stay, kept, arrived.at[5]),
            pltpu.make_async_copy(leave, given, arrived.at[6]),
        )

    for copy in copies:
        copy.start()
    for mine in range(2):
        @pl.when(core == mine)
        def _():
            for copy in states(mine):
                copy.start()

    for copy in copies:
        copy.wait()

    def pack(out, row):
        for m in range(5):
            for u in range(0, own.shape[1], 2):
                pairs = [own[m, u + k].astype(F32) for k in range(2)]
                values = [pair[v + row : v + row + 4] for pair in pairs for v in (0, 8)]
                out[m, u // 2] = jnp.concatenate(values).astype(BF16)

    @pl.when(parity == 0)
    def _():
        pack(even, 4)
        pack(odd, 0)

    @pl.when(parity == 1)
    def _():
        pack(odd, 4)
        pack(even, 0)

    for mine in range(2):
        @pl.when(core == mine)
        def _():
            for copy in states(mine):
                copy.wait()


def join_kernel(own, even, odd, out):
    parity = lax.rem(lax.axis_index("gy"), 2)

    def fill(below, above):
        for m in range(5):
            for u in range(own.shape[1]):
                low, high = below[m, u // 2].astype(F32), above[m, u // 2].astype(F32)
                pair = own[m, u].astype(F32)
                for v in range(2):
                    k = 2 * (u % 2) + v
                    rows = [low[4 * k : 4 * k + 4], pair[8 * v : 8 * v + 8], high[4 * k : 4 * k + 4]]
                    out[m, 2 * u + v] = jnp.concatenate(rows).astype(BF16)

    pl.when(parity == 0)(lambda: fill(odd, even))
    pl.when(parity == 1)(lambda: fill(even, odd))


def setup_kernel(columns, size_x, total_x, aperture, *refs):
    models, coefs, blocks = refs[:-2], refs[-2], refs[-1]
    place = Place(2 * size_x, columns)
    if len(models) > 1:
        for k, column in enumerate((place.column, 1 - place.column)):
            for j, core in enumerate((place.core, 1 - place.core)):
                blocks[:, pl.ds((2 * column + core) * size_x, size_x)] = models[2 * k + j][...]
        source = blocks
    else:
        source = models[0]

    def medium(i):
        x = place.start_x + i
        block = jnp.clip(x // size_x, 0, total_x // size_x - 1)
        inside = jnp.logical_and(x >= 0, x < total_x)
        at = aperture[block] * size_x + lax.rem(x + size_x, size_x)
        speed, stretch, bending, tilt, azimuth = [source[m, at].astype(F32) for m in range(5)]
        speed = jnp.where(inside, speed, 0.0)
        sin_t, cos_t = sine_cosine(tilt)
        sin_half, cos_half = sine_cosine(0.5 * azimuth)
        normal_x = sin_t * (1.0 - 2.0 * sin_half * sin_half)
        normal_y = sin_t * (2.0 * sin_half * cos_half)
        coefs[0, i] = speed
        coefs[1, i] = speed * (1.0 + 2.0 * stretch)
        coefs[2, i] = speed * jnp.sqrt(1.0 + 2.0 * bending)
        coefs[3, i] = S1 * (normal_x * normal_x)
        coefs[4, i] = S1 * (normal_y * normal_y)
        coefs[5, i] = SECOND_UNIT * (cos_t * cos_t)
        coefs[6, i] = (2.0 * G1 * G1) * (normal_x * normal_y)
        coefs[7, i] = (2.0 * G1 * FIRST_UNIT) * (normal_y * cos_t)
        coefs[8, i] = (2.0 * G1 * FIRST_UNIT) * (normal_x * cos_t)

    loop(place.count, medium, 4)


def injection_kernel(
    columns, size_x, size_y, total_y, source_cell, wavelet, cells, traces, out, hits
):
    place = Place(size_x, columns)
    count, rows = hits.shape[:2]
    number = cells.shape[1]
    row = lax.broadcasted_iota(jnp.int32, (rows, number), 0)
    lane = lax.broadcasted_iota(jnp.int32, (1, number), 1)
    is_source = place.core == 0
    lonely = jnp.where(lane == 0, source_cell[0], -1)
    aims = jnp.where(is_source, lonely, cells[...])
    y = place.at_y * size_y - 4 + row
    valid = jnp.logical_and(y >= 0, y < total_y)

    def mark(i):
        code = jnp.where(valid, (place.start_x + i) * total_y + y, -2)
        hits[i] = jnp.where(code == aims, 1.0, 0.0).astype(BF16)

    loop(count, mark, 2)
    step = lax.broadcasted_iota(jnp.int32, (NT, number), 0)
    amounts = jnp.zeros((NT, number), F32)
    for k in range(NT):
        amounts = jnp.where(step == k, wavelet[k], amounts)
    backward = jnp.concatenate([traces[k : k + 1] for k in reversed(range(NT))])
    rest = jnp.where(is_source, amounts, backward)
    total = None
    for _ in range(3):
        piece = rest.astype(BF16)
        rest = rest - piece.astype(F32)
        term = lax.dot_general(
            hits[...].reshape(count * rows, number), piece, (((1,), (1,)), ((), ())),
            preferred_element_type=F32,
        )
        total = term if total is None else total + term
    out[...] = total.reshape(count, rows, NT)


def spread_kernel(moment, lanes, out):
    core = lax.rem(lax.axis_index("gx"), 2)
    level = jnp.where(core == 0, SRC_DEPTH, REC_DEPTH)
    mask = (lax.broadcasted_iota(jnp.int32, (lanes.shape[1], 128), 1) == level).astype(F32)

    def expand(i):
        values = lanes[i]
        for k in range(2):
            out[k, i] = values[:, moment + k : moment + k + 1] * mask

    loop(lanes.shape[0], expand, 6)


def sort_kernel(columns, *refs):
    levels, (kept, sent) = refs[: NT - 1], refs[NT - 1 :]
    half, size_y = kept.shape[1:3]
    place = Place(2 * half, columns)

    def level_at(step, start):
        where = levels[step]
        if step % 2 == 0:
            return where[0, pl.ds(start, half)]
        return where[0, pl.ds(place.tile_at + start, half), pl.ds(4, size_y), :]

    for mine in range(2):
        @pl.when(place.core == mine)
        def _():
            for step in range(NT - 1):
                t = step if mine == 0 else NT - step
                if t > 0:
                    kept[t - 1] = level_at(step, mine * half)
                    sent[t - 1] = level_at(step, (1 - mine) * half)


def close_kernel(kept, got, last_kept, last_got, image, field):
    core = lax.rem(lax.axis_index("gx"), 2)
    total = kept[1] * got[1]
    for t in range(2, NT - 2):
        total = total + kept[t] * got[t]

    @pl.when(core == 0)
    def _():
        image[...] = (
            total + kept[0] * last_got[0] + last_kept[0] * got[NT - 2] + last_kept[1] * got[NT - 1]
        ) * (1.0 / NT)
        field[...] = last_got[pl.ds(1, 2)]

    @pl.when(core == 1)
    def _():
        image[...] = (
            total + last_kept[0] * got[0] + kept[NT - 2] * last_got[0] + kept[NT - 1] * last_got[1]
        ) * (1.0 / NT)
        field[...] = last_kept[pl.ds(1, 2)]


def per_device(
    velocity,
    epsilon,
    delta,
    tilt,
    azimuth,
    aperture,
    source_cell,
    wavelet,
    receiver_cell,
    traces,
    source_state,
    receiver_state,
):
    block_x, size_y, _ = velocity.shape
    devices_x, devices_y = lax.axis_size("gx"), lax.axis_size("gy")
    columns = devices_x // 2
    total_x, total_y = block_x * devices_x, size_y * devices_y
    size_x, rows = 2 * block_x, size_y + 8
    is_source = lax.axis_index("gx") % 2 == 0
    place = Place(size_x, columns)
    sides, count = place.sides, place.count
    groups = size_x // GROUP
    mats = depth_matrices(128)
    chip_pairs = [even_pairs(columns), odd_pairs(columns)][:sides]
    row_pairs = [even_pairs(devices_y), odd_pairs(devices_y)]
    trade = both_ways([(2 * c, 2 * c + 1) for c in range(columns)])

    def over_gy(values, pairs):
        return lax.ppermute(values, "gy", both_ways(pairs))

    def over_gx(values, pairs):
        return lax.ppermute(values, "gx", both_ways(chip_swap(pairs)))

    def beside_of(edges):
        return [over_gx(edge, pairs) for edge, pairs in zip(edges, chip_pairs)]

    def near_of(payload, beside):
        wide = jnp.concatenate([payload, *beside])
        return wide, [over_gy(wide, pairs) for pairs in row_pairs]

    def codes(number, fields):
        return ((number, tiles_of(fields), 16, 128), jnp.int16)

    models = [
        values.reshape(block_x // 2, 16, 128) for values in (velocity, epsilon, delta, tilt, azimuth)
    ]
    rim = ((5, block_x // 4, 16, 128), BF16)
    states = (source_state, receiver_state)
    state = (source_state.shape, F32)
    *rims, own, kept, given = pl.pallas_call(
        open_kernel,
        out_shape=tuple(
            jax.ShapeDtypeStruct(*out)
            for out in (rim, rim, ((5, block_x // 2, 16, 128), BF16), state, state)
        ),
        in_specs=[HBM] * 7,
        out_specs=(VMEM,) * 5,
        scratch_shapes=[pltpu.SemaphoreType.DMA((7,))],
        compiler_params=pltpu.CompilerParams(vmem_limit_bytes=8 * 2**20),
        name="open",
    )(*[pltpu.with_memory_space_constraint(x, pltpu.HBM) for x in (*models, *states)])
    rims = [over_gy(values, pairs) for values, pairs in zip(rims, row_pairs)]

    got = lax.ppermute(given, "gx", trade)
    field = ((2, size_x, size_y, 128), F32)
    tile, old, payload, *edges = call(
        functools.partial(first_kernel, columns),
        (field, field, codes(groups, 4)) + (codes(1, 4),) * sides,
        (), 16, "first", (kept, got),
    )
    beside = beside_of(edges)
    wide, near = near_of(payload, beside)

    (model,) = call(
        join_kernel, (((5, block_x, rows, 128), BF16),), (), 8, "join", (own, *rims), work=1000
    )
    number = receiver_cell.shape[0]
    (amounts,) = call(
        functools.partial(injection_kernel, columns, size_x, size_y, total_y),
        (((count, rows, NT), F32),), (((count, rows, number), BF16),),
        16, "injection", (source_cell, wavelet, receiver_cell[None, :], traces), scalars=2,
    )
    if columns == 2:
        later, _ = lax.optimization_barrier((model, wide))
        across = over_gx(later, chip_pairs[0])
        other = lax.ppermute(model, "gx", trade)
        gathered = [model, other, across, lax.ppermute(across, "gx", trade)]
        held = (5, total_x, rows, 128)
    else:
        gathered, held = [lax.all_gather(model, "gx", axis=1, tiled=True)], (16, 128)
    (coefs,) = call(
        functools.partial(setup_kernel, columns, block_x, total_x),
        (((9, count, rows, 128), F32),), ((held, BF16),), 24, "setup", (aperture, *gathered),
        scalars=1, work=0,
    )

    window = ((2, place.wide + 8, 32, 128), F32)
    middle = ((2, count + 8, 24, 128), F32)
    lines = ((2, count, rows, 128), F32)
    def spread(moment, after):
        lanes, _ = lax.optimization_barrier((amounts, after))
        (out,) = call(
            functools.partial(spread_kernel, moment), (((2, count, rows, 128), F32),), (), 8,
            "spread", (lanes,),
        )
        return out

    levels = [tile]
    for moment in range(0, NT - 2, 2):
        inject = spread(moment, wide)
        old_wide = ((2, place.wide, rows, 128) if moment == 0 else (8, 128), F32)
        between, old, *edges = call(
            functools.partial(lead_kernel, moment, columns),
            (middle, lines) + (((2, GROUP, size_y, 128), F32),) * sides + (codes(1, 2),) * sides,
            [window, old_wide] + leap_scratch(count), 24, "lead",
            (tile, old, coefs, inject, *mats, *beside, *near), work=4 * 10**6,
        )
        edges, edge_codes = edges[:sides], edges[sides:]
        beside = beside_of(edge_codes)
        tile, payload = call(
            functools.partial(rest_kernel, moment, columns),
            (field, codes(groups, 2)), leap_scratch(size_x), 24, "rest",
            (tile, between, coefs, inject, *mats, *edges), work=4 * 10**6,
        )
        wide, near = near_of(payload, beside)
        levels += [old, tile]
    shape = (block_x, size_y, 128)
    inject = spread(NT - 2, wide)
    share = ((NT,) + shape, F32)
    kept, sent = call(
        functools.partial(sort_kernel, columns), (share, share), (), 8, "sort",
        lax.optimization_barrier((*levels, inject))[: NT - 1],
    )
    got = lax.ppermute(sent, "gx", trade)
    share = ((3,) + shape, F32)
    last_kept, last_sent = call(
        functools.partial(lead_kernel, NT - 2, columns),
        (share, share),
        [middle, field, window, ((8, 128), F32)] + leap_scratch(count), 24, "last",
        (tile, old, coefs, inject, *mats, *beside, *near),
    )
    last_got = lax.ppermute(last_sent, "gx", trade)
    return call(
        close_kernel, ((shape, F32), ((2,) + shape, F32)), (), 8, "close",
        (kept, got, last_kept, last_got),
    )


def solution(mesh):
    in_specs = (
        P("gx", "gy", None),
        P("gx", "gy", None),
        P("gx", "gy", None),
        P("gx", "gy", None),
        P("gx", "gy", None),
        P("shot"),
        P("shot"),
        P("shot"),
        P("shot"),
        P(None, "shot"),
        P(None, ("shot", "gx"), "gy", None),
        P(None, ("shot", "gx"), "gy", None),
    )
    out_specs = (P(("shot", "gx"), "gy", None), P(None, ("shot", "gx"), "gy", None))
    return jax.shard_map(
        per_device, mesh=mesh, in_specs=in_specs, out_specs=out_specs, check_vma=False
    )
```

```python
import functools

import jax
import jax.numpy as jnp
from jax import lax
from jax.experimental import pallas as pl
from jax.experimental.pallas import tpu as pltpu
from jax.sharding import PartitionSpec as P

NT = 8
SRC_DEPTH = 10
REC_DEPTH = 6
F32 = jnp.float32
BF16 = jnp.bfloat16

second_taps = (-205.0 / 72.0, 8.0 / 5.0, -1.0 / 5.0, 8.0 / 315.0, -1.0 / 560.0)
first_taps = (4.0 / 5.0, -1.0 / 5.0, 4.0 / 105.0, -1.0 / 280.0)
CENTRE = second_taps[0]
S1 = second_taps[1]
G1 = first_taps[0]
second_ratio = tuple(tap / S1 for tap in second_taps[2:])
first_ratio = tuple(tap / G1 for tap in first_taps[1:])
second_whole = (8064.0, -1008.0, 128.0, -9.0)
first_whole = (672.0, -168.0, 32.0, -3.0)
SECOND_UNIT = 1.0 / 5040.0
FIRST_UNIT = 1.0 / 840.0
VMEM = pl.BlockSpec(memory_space=pltpu.VMEM)
SMEM = pl.BlockSpec(memory_space=pltpu.SMEM)
HBM = pl.BlockSpec(memory_space=pltpu.HBM)


def even_pairs(count):
    return [(i, i + 1) for i in range(0, count - 1, 2)]


def odd_pairs(count):
    return [(i, i + 1) for i in range(1, count - 1, 2)]


def both_ways(pairs):
    return [pair for a, b in pairs for pair in ((a, b), (b, a))]


def chip_swap(pairs):
    return [(2 * a + c, 2 * b + c) for a, b in pairs for c in range(2)]


class Place:
    def __init__(self, size_x, columns):
        at_x = lax.axis_index("gx")
        self.core, self.column = lax.rem(at_x, 2), lax.div(at_x, 2)
        self.at_y = lax.axis_index("gy")
        self.parity = lax.rem(self.at_y, 2)
        if columns == 2:
            side = self.column
            self.count = size_x + 4
            self.first_at = self.tile_at = 4 * side
            self.start_x = side * (size_x - 4)
            self.beside_at = [size_x * (1 - side)]
            self.edge_at = [(size_x - GROUP) * (1 - side)]
            self.rest_at, self.rest = GROUP * side, size_x - GROUP
        else:
            side = lax.rem(self.column, 2)
            self.count = size_x + 8
            self.first_at = self.tile_at = 4
            self.start_x = self.column * size_x - 4
            self.beside_at = [(size_x + GROUP) * (1 - side), (size_x + GROUP) * side]
            self.edge_at = [(size_x - GROUP) * (1 - side), (size_x - GROUP) * side]
            self.rest_at, self.rest = GROUP, size_x - 2 * GROUP
        self.sides = len(self.beside_at)
        self.own_at = self.first_at + self.tile_at
        self.wide = size_x + GROUP * self.sides


def call(kernel, outs, scratch, mebibytes, name, args, scalars=0, work=10**6):
    outs = tuple(jax.ShapeDtypeStruct(shape, dtype) for shape, dtype in outs)
    return pl.pallas_call(
        kernel,
        out_shape=outs,
        in_specs=[SMEM] * scalars + [VMEM] * (len(args) - scalars),
        out_specs=(VMEM,) * len(outs),
        scratch_shapes=[pltpu.VMEM(shape, dtype) for shape, dtype in scratch],
        compiler_params=pltpu.CompilerParams(vmem_limit_bytes=mebibytes * 2**20),
        cost_estimate=pl.CostEstimate(flops=work, bytes_accessed=work, transcendentals=0),
        name=name,
    )(*args)


def loop(trips, body, wanted):
    unroll = max(u for u in range(1, wanted + 1) if trips % u == 0)

    def step(i, carry):
        body(i)
        return carry

    lax.fori_loop(0, trips, step, 0, unroll=unroll)


def depth_matrices(size):
    rows = jnp.arange(size)[:, None]
    cols = jnp.arange(size)[None, :]
    first = jnp.zeros((size, size), F32)
    second = jnp.zeros((size, size), F32)
    for k in range(1, 5):
        up = (rows == cols + k).astype(F32)
        down = (rows == cols - k).astype(F32)
        first = first + first_whole[k - 1] * (up - down)
        second = second + second_whole[k - 1] * (up + down)
    return (
        jnp.concatenate([first, first]).astype(BF16),
        jnp.concatenate([second, second]).astype(BF16),
    )


def sums_and_slopes(shifted):
    up, down = shifted(1), shifted(-1)
    curve, slope = up + down, up - down
    for k in range(2, 5):
        up, down = shifted(k), shifted(-k)
        curve = curve + second_ratio[k - 2] * (up + down)
        slope = slope + first_ratio[k - 2] * (up - down)
    return curve, slope


def slope_only(shifted):
    slope = shifted(1) - shifted(-1)
    for k in range(2, 5):
        slope = slope + first_ratio[k - 2] * (shifted(k) - shifted(-k))
    return slope


def split(values):
    high = values.astype(BF16)
    low = (values - high.astype(F32)).astype(BF16)
    return high, low


TOP = 32000.0
GROUP = 8


def tiles_of(fields):
    return fields * 4 + fields // 2


def encode(value_at, out, group, fields):
    for pair in range(fields // 2):
        codes = []
        for f in (2 * pair, 2 * pair + 1):
            values = [value_at(f, p) for p in range(GROUP)]
            size = jnp.full((8, 128), 1e-30, F32)
            for value in values:
                size = jnp.maximum(size, jnp.abs(value))
            code = jnp.ceil(jnp.log2(size) * 256.0)
            factor = TOP * jnp.exp2(code * (-1.0 / 256.0))
            codes.append(code)
            for q in range(GROUP // 2):
                both = [jnp.floor(value * factor + 0.5) for value in values[2 * q : 2 * q + 2]]
                out[group, f * 4 + q] = jnp.concatenate(both).astype(jnp.int32).astype(jnp.int16)
        out[group, fields * 4 + pair] = jnp.concatenate(codes).astype(jnp.int32).astype(jnp.int16)


def decode(payload, group, fields, put):
    for pair in range(fields // 2):
        code = payload[group, fields * 4 + pair].astype(jnp.int32).astype(F32)
        factor = jnp.exp2(code * (1.0 / 256.0)) * (1.0 / TOP)
        for slot in range(2):
            f = 2 * pair + slot
            own = factor[slot * 8 : slot * 8 + 8]
            for q in range(GROUP // 2):
                both = payload[group, f * 4 + q].astype(jnp.int32).astype(F32)
                put(f, 2 * q, both[:8] * own)
                put(f, 2 * q + 1, both[8:] * own)


def leap(src, x0, row0, rows, count, scratch, mats, coef, old_at, inject_at, store):
    slope_y, curve_y, part, halves, product = scratch
    mat_first, mat_second = mats
    planes = 16 // rows
    group = 4

    def field(f, p, r=0, number=rows):
        return src[f, x0 + p, pl.ds(row0 + r, number), :]

    def joined(values):
        return jnp.concatenate(values) if len(values) > 1 else values[0]

    def put_halves(kind, f, unit, values):
        high, low = split(values)
        halves[kind, f, unit, :, :128] = high
        halves[kind, f, unit, :, 128:] = low

    def along_y(u):
        for f in range(2):
            here, slopes = [], []
            for v in range(planes):
                p = u * planes + v
                curve, slope = sums_and_slopes(lambda k: field(f, p, k))
                slope_y[f, p, :rows] = slope
                curve_y[f, p, :rows] = curve
                slopes.append(slope)
                here.append(field(f, p))
            put_halves(0, f, u, joined(here))
            put_halves(1, f, u, joined(slopes))

    loop((count + 8) // planes, along_y, 6)

    def along_x(q):
        base = q * group
        for f in range(2):
            slopes = [[] for g in range(group)]
            for r in range(0, rows, 8):
                line = [field(f, base + k, r, 8) for k in range(group + 8)]
                slant = [slope_y[f, base + k, pl.ds(r, 8), :] for k in range(group + 8)]
                for g in range(group):
                    i = base + g
                    xx, slope = sums_and_slopes(lambda k: line[g + 4 + k])
                    xy = slope_only(lambda k: slant[g + 4 + k])
                    yy = curve_y[f, i + 4, pl.ds(r, 8), :]
                    wx, wy, wxy = [coef(m, i, r, 8) for m in (3, 4, 6)]
                    if f == 0:
                        total = (2.0 * CENTRE) * line[g + 4] + (S1 - wx) * xx
                        total = total + (S1 - wy) * yy - wxy * xy
                    else:
                        total = CENTRE * line[g + 4] + wx * xx
                        total = total + wy * yy + wxy * xy
                    part[f, i, pl.ds(r, 8), :] = total
                    slopes[g].append(slope)
            pieces = [piece for rest in slopes for piece in rest]
            for k in range(0, len(pieces), 2):
                put_halves(2, f, q * (len(pieces) // 2) + k // 2, joined(pieces[k : k + 2]))

    loop(count // group, along_x, 3)

    units = count // planes
    for kind, mat, at in ((0, mat_second, 4 // planes), (1, mat_first, 4 // planes), (2, mat_first, 0)):
        for f in range(2):
            both = halves[kind, f, pl.ds(at, units)].reshape(units * 16, 256)
            out = jnp.dot(both, mat[...], preferred_element_type=F32)
            product[kind, f, pl.ds(0, units)] = out.reshape(units, 16, 128)

    def combine(u):
        where = [u * planes + v for v in range(planes)]
        speed, speed_h, speed_v, wz, wyz, wxz = [
            joined([coef(m, i, 0, rows) for i in where]) for m in (0, 1, 2, 5, 7, 8)
        ]
        zz, yz, xz = [[product[kind, f, u] for f in range(2)] for kind in range(3)]
        parts = [joined([part[f, i, :rows] for i in where]) for f in range(2)]
        here = [joined([field(f, i + 4) for i in where]) for f in range(2)]
        old = [joined([old_at(f, i) for i in where]) for f in range(2)]
        add = joined([inject_at(i) for i in where])
        flat = parts[0] + (SECOND_UNIT - wz) * zz[0] - (wyz * yz[0] + wxz * xz[0])
        tilted = parts[1] + wz * zz[1] + (wyz * yz[1] + wxz * xz[1])
        new_p = (2.0 * here[0] - old[0] + add) + (speed_h * flat + speed_v * tilted)
        new_q = (2.0 * here[1] - old[1] + add) + (speed_v * flat + speed * tilted)
        for v, i in enumerate(where):
            cut = slice(v * rows, v * rows + rows)
            store(i, new_p[cut], new_q[cut])

    loop(units, combine, 12)


def leap_scratch(count):
    lines = (2, count + 8, 16, 128)
    return [
        (lines, F32),
        (lines, F32),
        ((2, count, 16, 128), F32),
        ((3, 2, count + 8, 16, 256), BF16),
        ((3, 2, count, 16, 128), F32),
    ]


def first_kernel(columns, kept, got, tile, old, payload, *edges):
    size = kept.shape[1]
    place = Place(2 * size, columns)
    for source, at in ((kept, place.core * size), (got, (1 - place.core) * size)):
        for f in range(2):
            tile[f, pl.ds(at, size)] = source[2 * f]
            old[f, pl.ds(at, size)] = source[2 * f + 1]

    def group(g):
        encode(lambda f, p: (tile if f < 2 else old)[f % 2, g * GROUP + p], payload, g, 4)

    loop(2 * size // GROUP, group, 1)
    for k, edge in enumerate(edges):
        edge[0] = payload[lax.div(place.edge_at[k], GROUP)]


def second_leap(moment, place, size_y, start, count, middle, tile, coefs, inject, scratch, mats, store):
    leap(
        middle, place.tile_at + start, 8, size_y, count, scratch, mats,
        lambda m, i, r, number: coefs[m, place.tile_at + start + i, pl.ds(4 + r, number), :],
        lambda f, i: tile[f, start + i],
        lambda i: inject[1, place.tile_at + start + i, pl.ds(4, size_y), :],
        store,
    )


def lead_kernel(moment, columns, tile, old, coefs, inject, mat_first, mat_second, *refs):
    opening, closing = moment == 0, moment == NT - 2
    size_x, size_y = tile.shape[1], tile.shape[2]
    place = Place(size_x, columns)
    sides, count, wide = place.sides, place.count, place.wide
    refs = list(refs)

    def take(number):
        taken = refs[:number]
        del refs[:number]
        return taken

    beside = take(sides)
    even, odd = take(2)
    if closing:
        kept_out, sent_out = take(2)
        middle, tile_out = take(2)
    else:
        middle, old_out = take(2)
        edges_out, codes_out = take(sides), take(sides)
    window, old_wide = take(2)
    scratch, mats = refs, (mat_first, mat_second)
    fields = 4 if opening else 2

    for f in range(2):
        window[f, pl.ds(0, 4)] = jnp.zeros((4, 32, 128), F32)
        window[f, pl.ds(wide + 4, 4)] = jnp.zeros((4, 32, 128), F32)
        middle[f, pl.ds(0, 4)] = jnp.zeros((4, 24, 128), F32)
        middle[f, pl.ds(count + 4, 4)] = jnp.zeros((4, 24, 128), F32)
        window[f, pl.ds(place.own_at + 4, size_x), pl.ds(12, 8), :] = tile[f]
        if opening:
            old_wide[f, pl.ds(place.own_at, size_x), pl.ds(4, 8), :] = old[f]

    def lay(payload, group, plane, row):
        def put(f, p, rows):
            if f < 2:
                window[f, plane + p + 4, pl.ds(row + 12, 8), :] = rows
            elif row == 0:
                old_wide[f - 2, plane + p, pl.ds(4, 8), :] = rows
            elif row < 0:
                old_wide[f - 2, plane + p, pl.ds(0, 4), :] = rows[4:]
            else:
                old_wide[f - 2, plane + p, pl.ds(12, 4), :] = rows[:4]

        decode(payload, group, fields, put)

    groups = size_x // GROUP
    for k in range(sides):
        lay(beside[k], 0, place.beside_at[k], 0)

    def lay_y(below, above):
        for payload, row in ((below, -8), (above, 8)):
            loop(groups, lambda g: lay(payload, g, place.own_at + g * GROUP, row), 2)
            for k in range(sides):
                lay(payload, groups + k, place.beside_at[k], row)

    pl.when(place.parity == 0)(lambda: lay_y(odd, even))
    pl.when(place.parity == 1)(lambda: lay_y(even, odd))

    def store(i, new_p, new_q):
        for f, new in enumerate((new_p, new_q)):
            if not closing:
                old_out[f, i] = new
            middle[f, i + 4, pl.ds(4, size_y + 8), :] = new

    leap(
        window, place.first_at, 8, size_y + 8, count, scratch, mats,
        lambda m, i, r, number: coefs[m, i, pl.ds(r, number), :],
        (lambda f, i: old_wide[f, place.first_at + i]) if opening else (lambda f, i: old[f, i]),
        lambda i: inject[0, i],
        store,
    )

    if not closing:
        for k in range(sides):
            def store_edge(i, new_p, new_q):
                edges_out[k][0, i] = new_p
                edges_out[k][1, i] = new_q

            second_leap(
                moment, place, size_y, place.edge_at[k], GROUP, middle, tile, coefs, inject,
                scratch, mats, store_edge,
            )
            encode(lambda f, p: edges_out[k][f, p], codes_out[k], 0, 2)
        return

    def store_tile(i, new_p, new_q):
        tile_out[0, i] = new_p
        tile_out[1, i] = new_q

    second_leap(
        moment, place, size_y, 0, size_x, middle, tile, coefs, inject, scratch, mats, store_tile
    )

    half = size_x // 2
    for mine in range(2):
        @pl.when(place.core == mine)
        def _():
            for out, start in ((kept_out, mine * half), (sent_out, (1 - mine) * half)):
                planes = pl.ds(start, half)
                inner = pl.ds(place.tile_at + 4 + start, half)
                out[0] = middle[0, inner, pl.ds(8, size_y), :]
                out[1] = tile_out[0, planes]
                out[2] = tile_out[1, planes]


def rest_kernel(moment, columns, tile, middle, coefs, inject, mat_first, mat_second, *refs):
    size_x, size_y = tile.shape[1], tile.shape[2]
    place = Place(size_x, columns)
    edges, (tile_out, payload), scratch = (
        refs[: place.sides], refs[place.sides : place.sides + 2], refs[place.sides + 2 :]
    )
    for k, edge in enumerate(edges):
        tile_out[:, pl.ds(place.edge_at[k], GROUP)] = edge[...]

    def store(i, new_p, new_q):
        tile_out[0, place.rest_at + i] = new_p
        tile_out[1, place.rest_at + i] = new_q

    second_leap(
        moment, place, size_y, place.rest_at, place.rest, middle, tile, coefs, inject, scratch,
        (mat_first, mat_second), store,
    )
    loop(
        size_x // GROUP,
        lambda g: encode(lambda f, p: tile_out[f, g * GROUP + p], payload, g, 2),
        1,
    )


def sine_cosine(angle):
    square = angle * angle
    sine = 1.0 / 6227020800.0
    for factor in (-1.0 / 39916800.0, 1.0 / 362880.0, -1.0 / 5040.0, 1.0 / 120.0, -1.0 / 6.0):
        sine = sine * square + factor
    sine = angle + angle * square * sine
    cosine = 1.0 / 479001600.0
    for factor in (-1.0 / 3628800.0, 1.0 / 40320.0, -1.0 / 720.0, 1.0 / 24.0, -0.5):
        cosine = cosine * square + factor
    return sine, 1.0 + square * cosine


def open_kernel(
    velocity, epsilon, delta, tilt, azimuth, source, receiver, *refs
):
    models = (velocity, epsilon, delta, tilt, azimuth)
    parity = lax.rem(lax.axis_index("gy"), 2)
    core = lax.rem(lax.axis_index("gx"), 2)
    small, (even, odd, own, kept, given), brought, arrived = (
        refs[:3], refs[3:8], refs[8:11], refs[11]
    )
    copies = [pltpu.make_async_copy(models[m], own.at[m], arrived.at[m]) for m in range(5)]
    others = [
        pltpu.make_async_copy(small[m], brought[m], arrived.at[7 + m]) for m in range(3)
    ]

    def states(mine):
        stay, leave = (source, receiver) if mine == 0 else (receiver, source)
        return (
            pltpu.make_async_copy(stay, kept, arrived.at[5]),
            pltpu.make_async_copy(leave, given, arrived.at[6]),
        )

    for copy in copies + others:
        copy.start()
    for mine in range(2):
        @pl.when(core == mine)
        def _():
            for copy in states(mine):
                copy.start()

    for copy in copies:
        copy.wait()

    def pack(out, row):
        for m in range(5):
            for u in range(0, own.shape[1], 2):
                pairs = [own[m, u + k].astype(F32) for k in range(2)]
                values = [pair[v + row : v + row + 4] for pair in pairs for v in (0, 8)]
                out[m, u // 2] = jnp.concatenate(values).astype(BF16)

    @pl.when(parity == 0)
    def _():
        pack(even, 4)
        pack(odd, 0)

    @pl.when(parity == 1)
    def _():
        pack(odd, 4)
        pack(even, 0)

    for mine in range(2):
        @pl.when(core == mine)
        def _():
            for copy in states(mine):
                copy.wait()
    for copy in others:
        copy.wait()


def join_kernel(own, even, odd, out):
    parity = lax.rem(lax.axis_index("gy"), 2)

    def fill(below, above):
        for m in range(5):
            for u in range(own.shape[1]):
                low, high = below[m, u // 2].astype(F32), above[m, u // 2].astype(F32)
                pair = own[m, u].astype(F32)
                for v in range(2):
                    k = 2 * (u % 2) + v
                    rows = [low[4 * k : 4 * k + 4], pair[8 * v : 8 * v + 8], high[4 * k : 4 * k + 4]]
                    out[m, 2 * u + v] = jnp.concatenate(rows).astype(BF16)

    pl.when(parity == 0)(lambda: fill(odd, even))
    pl.when(parity == 1)(lambda: fill(even, odd))


def setup_kernel(columns, size_x, total_x, aperture, *refs):
    models, coefs, blocks = refs[:-2], refs[-2], refs[-1]
    place = Place(2 * size_x, columns)
    if len(models) > 1:
        for k, column in enumerate((place.column, 1 - place.column)):
            for j, core in enumerate((place.core, 1 - place.core)):
                blocks[:, pl.ds((2 * column + core) * size_x, size_x)] = models[2 * k + j][...]
        source = blocks
    else:
        source = models[0]

    def medium(i):
        x = place.start_x + i
        block = jnp.clip(x // size_x, 0, total_x // size_x - 1)
        inside = jnp.logical_and(x >= 0, x < total_x)
        at = aperture[block] * size_x + lax.rem(x + size_x, size_x)
        speed, stretch, bending, tilt, azimuth = [source[m, at].astype(F32) for m in range(5)]
        speed = jnp.where(inside, speed, 0.0)
        sin_t, cos_t = sine_cosine(tilt)
        sin_half, cos_half = sine_cosine(0.5 * azimuth)
        normal_x = sin_t * (1.0 - 2.0 * sin_half * sin_half)
        normal_y = sin_t * (2.0 * sin_half * cos_half)
        coefs[0, i] = speed
        coefs[1, i] = speed * (1.0 + 2.0 * stretch)
        coefs[2, i] = speed * jnp.sqrt(1.0 + 2.0 * bending)
        coefs[3, i] = S1 * (normal_x * normal_x)
        coefs[4, i] = S1 * (normal_y * normal_y)
        coefs[5, i] = SECOND_UNIT * (cos_t * cos_t)
        coefs[6, i] = (2.0 * G1 * G1) * (normal_x * normal_y)
        coefs[7, i] = (2.0 * G1 * FIRST_UNIT) * (normal_y * cos_t)
        coefs[8, i] = (2.0 * G1 * FIRST_UNIT) * (normal_x * cos_t)

    loop(place.count, medium, 4)


def injection_kernel(
    columns, size_x, size_y, total_y, source_cell, wavelet, cells, traces, out, hits
):
    place = Place(size_x, columns)
    count, rows = hits.shape[:2]
    number = cells.shape[1]
    row = lax.broadcasted_iota(jnp.int32, (rows, number), 0)
    lane = lax.broadcasted_iota(jnp.int32, (1, number), 1)
    is_source = place.core == 0
    lonely = jnp.where(lane == 0, source_cell[0], -1)
    aims = jnp.where(is_source, lonely, cells[...])
    y = place.at_y * size_y - 4 + row
    valid = jnp.logical_and(y >= 0, y < total_y)

    def mark(i):
        code = jnp.where(valid, (place.start_x + i) * total_y + y, -2)
        hits[i] = jnp.where(code == aims, 1.0, 0.0).astype(BF16)

    loop(count, mark, 2)
    step = lax.broadcasted_iota(jnp.int32, (NT, number), 0)
    amounts = jnp.zeros((NT, number), F32)
    for k in range(NT):
        amounts = jnp.where(step == k, wavelet[:, k : k + 1], amounts)
    backward = jnp.concatenate([traces[k : k + 1] for k in reversed(range(NT))])
    rest = jnp.where(is_source, amounts, backward)
    total = None
    for _ in range(3):
        piece = rest.astype(BF16)
        rest = rest - piece.astype(F32)
        term = lax.dot_general(
            hits[...].reshape(count * rows, number), piece, (((1,), (1,)), ((), ())),
            preferred_element_type=F32,
        )
        total = term if total is None else total + term
    out[...] = total.reshape(count, rows, NT)


def spread_kernel(moment, lanes, out):
    core = lax.rem(lax.axis_index("gx"), 2)
    level = jnp.where(core == 0, SRC_DEPTH, REC_DEPTH)
    mask = (lax.broadcasted_iota(jnp.int32, (lanes.shape[1], 128), 1) == level).astype(F32)

    def expand(i):
        values = lanes[i]
        for k in range(2):
            out[k, i] = values[:, moment + k : moment + k + 1] * mask

    loop(lanes.shape[0], expand, 6)


def sort_kernel(columns, *refs):
    levels, (kept, sent) = refs[: NT - 1], refs[NT - 1 :]
    half, size_y = kept.shape[1:3]
    place = Place(2 * half, columns)

    def level_at(step, start):
        where = levels[step]
        if step % 2 == 0:
            return where[0, pl.ds(start, half)]
        return where[0, pl.ds(place.tile_at + start, half), pl.ds(4, size_y), :]

    for mine in range(2):
        @pl.when(place.core == mine)
        def _():
            for step in range(NT - 1):
                t = step if mine == 0 else NT - step
                if t > 0:
                    kept[t - 1] = level_at(step, mine * half)
                    sent[t - 1] = level_at(step, (1 - mine) * half)


def close_kernel(kept, got, last_kept, last_got, image, field):
    core = lax.rem(lax.axis_index("gx"), 2)
    total = kept[1] * got[1]
    for t in range(2, NT - 2):
        total = total + kept[t] * got[t]

    @pl.when(core == 0)
    def _():
        image[...] = (
            total + kept[0] * last_got[0] + last_kept[0] * got[NT - 2] + last_kept[1] * got[NT - 1]
        ) * (1.0 / NT)
        field[...] = last_got[pl.ds(1, 2)]

    @pl.when(core == 1)
    def _():
        image[...] = (
            total + last_kept[0] * got[0] + kept[NT - 2] * last_got[0] + kept[NT - 1] * last_got[1]
        ) * (1.0 / NT)
        field[...] = last_kept[pl.ds(1, 2)]


def per_device(
    velocity,
    epsilon,
    delta,
    tilt,
    azimuth,
    aperture,
    source_cell,
    wavelet,
    receiver_cell,
    traces,
    source_state,
    receiver_state,
):
    block_x, size_y, _ = velocity.shape
    devices_x, devices_y = lax.axis_size("gx"), lax.axis_size("gy")
    columns = devices_x // 2
    total_x, total_y = block_x * devices_x, size_y * devices_y
    size_x, rows = 2 * block_x, size_y + 8
    is_source = lax.axis_index("gx") % 2 == 0
    place = Place(size_x, columns)
    sides, count = place.sides, place.count
    groups = size_x // GROUP
    mats = depth_matrices(128)
    chip_pairs = [even_pairs(columns), odd_pairs(columns)][:sides]
    row_pairs = [even_pairs(devices_y), odd_pairs(devices_y)]
    trade = both_ways([(2 * c, 2 * c + 1) for c in range(columns)])

    def over_gy(values, pairs):
        return lax.ppermute(values, "gy", both_ways(pairs))

    def over_gx(values, pairs):
        return lax.ppermute(values, "gx", both_ways(chip_swap(pairs)))

    def beside_of(edges):
        return [over_gx(edge, pairs) for edge, pairs in zip(edges, chip_pairs)]

    def near_of(payload, beside):
        wide = jnp.concatenate([payload, *beside])
        return wide, [over_gy(wide, pairs) for pairs in row_pairs]

    def codes(number, fields):
        return ((number, tiles_of(fields), 16, 128), jnp.int16)

    models = [
        values.reshape(block_x // 2, 16, 128) for values in (velocity, epsilon, delta, tilt, azimuth)
    ]
    small = (wavelet[None, :], receiver_cell[None, :], traces)
    rim = ((5, block_x // 4, 16, 128), BF16)
    states = (source_state, receiver_state)
    state = (source_state.shape, F32)
    *rims, own, kept, given, series, cells, data = pl.pallas_call(
        open_kernel,
        out_shape=tuple(
            jax.ShapeDtypeStruct(*out)
            for out in (rim, rim, ((5, block_x // 2, 16, 128), BF16), state, state)
            + tuple((x.shape, x.dtype) for x in small)
        ),
        in_specs=[HBM] * 10,
        out_specs=(VMEM,) * 8,
        scratch_shapes=[pltpu.SemaphoreType.DMA((10,))],
        compiler_params=pltpu.CompilerParams(vmem_limit_bytes=8 * 2**20),
        name="open",
    )(*[pltpu.with_memory_space_constraint(x, pltpu.HBM) for x in (*models, *states, *small)])
    rims = [over_gy(values, pairs) for values, pairs in zip(rims, row_pairs)]

    got = lax.ppermute(given, "gx", trade)
    field = ((2, size_x, size_y, 128), F32)
    tile, old, payload, *edges = call(
        functools.partial(first_kernel, columns),
        (field, field, codes(groups, 4)) + (codes(1, 4),) * sides,
        (), 16, "first", (kept, got),
    )
    number = receiver_cell.shape[0]
    cells, _ = lax.optimization_barrier((cells, edges[0]))
    (amounts,) = call(
        functools.partial(injection_kernel, columns, size_x, size_y, total_y),
        (((count, rows, NT), F32),), (((count, rows, number), BF16),),
        16, "injection", (source_cell, series, cells, data), scalars=1,
    )
    beside = beside_of(edges)
    payload, _ = lax.optimization_barrier((payload, amounts))
    wide, near = near_of(payload, beside)

    (model,) = call(
        join_kernel, (((5, block_x, rows, 128), BF16),), (), 8, "join", (own, *rims), work=1000
    )
    if columns == 2:
        later, _ = lax.optimization_barrier((model, wide))
        across = over_gx(later, chip_pairs[0])
        other = lax.ppermute(model, "gx", trade)
        gathered = [model, other, across, lax.ppermute(across, "gx", trade)]
        held = (5, total_x, rows, 128)
    else:
        gathered, held = [lax.all_gather(model, "gx", axis=1, tiled=True)], (16, 128)
    (coefs,) = call(
        functools.partial(setup_kernel, columns, block_x, total_x),
        (((9, count, rows, 128), F32),), ((held, BF16),), 24, "setup", (aperture, *gathered),
        scalars=1, work=0,
    )

    window = ((2, place.wide + 8, 32, 128), F32)
    middle = ((2, count + 8, 24, 128), F32)
    lines = ((2, count, rows, 128), F32)
    def spread(moment, after):
        lanes, _ = lax.optimization_barrier((amounts, after))
        (out,) = call(
            functools.partial(spread_kernel, moment), (((2, count, rows, 128), F32),), (), 8,
            "spread", (lanes,),
        )
        return out

    levels = [tile]
    for moment in range(0, NT - 2, 2):
        inject = spread(moment, wide)
        old_wide = ((2, place.wide, rows, 128) if moment == 0 else (8, 128), F32)
        between, old, *edges = call(
            functools.partial(lead_kernel, moment, columns),
            (middle, lines) + (((2, GROUP, size_y, 128), F32),) * sides + (codes(1, 2),) * sides,
            [window, old_wide] + leap_scratch(count), 24, "lead",
            (tile, old, coefs, inject, *mats, *beside, *near), work=4 * 10**6,
        )
        edges, edge_codes = edges[:sides], edges[sides:]
        beside = beside_of(edge_codes)
        tile, payload = call(
            functools.partial(rest_kernel, moment, columns),
            (field, codes(groups, 2)), leap_scratch(size_x), 24, "rest",
            (tile, between, coefs, inject, *mats, *edges), work=4 * 10**6,
        )
        wide, near = near_of(payload, beside)
        levels += [old, tile]
    shape = (block_x, size_y, 128)
    inject = spread(NT - 2, wide)
    share = ((NT,) + shape, F32)
    kept, sent = call(
        functools.partial(sort_kernel, columns), (share, share), (), 8, "sort",
        lax.optimization_barrier((*levels, *near))[: NT - 1],
    )
    got = lax.ppermute(sent, "gx", trade)
    share = ((3,) + shape, F32)
    last_kept, last_sent = call(
        functools.partial(lead_kernel, NT - 2, columns),
        (share, share),
        [middle, field, window, ((8, 128), F32)] + leap_scratch(count), 24, "last",
        (tile, old, coefs, inject, *mats, *beside, *near),
    )
    last_got = lax.ppermute(last_sent, "gx", trade)
    return call(
        close_kernel, ((shape, F32), ((2,) + shape, F32)), (), 8, "close",
        (kept, got, last_kept, last_got),
    )


def solution(mesh):
    in_specs = (
        P("gx", "gy", None),
        P("gx", "gy", None),
        P("gx", "gy", None),
        P("gx", "gy", None),
        P("gx", "gy", None),
        P("shot"),
        P("shot"),
        P("shot"),
        P("shot"),
        P(None, "shot"),
        P(None, ("shot", "gx"), "gy", None),
        P(None, ("shot", "gx"), "gy", None),
    )
    out_specs = (P(("shot", "gx"), "gy", None), P(None, ("shot", "gx"), "gy", None))
    return jax.shard_map(
        per_device, mesh=mesh, in_specs=in_specs, out_specs=out_specs, check_vma=False
    )
```

```python
import functools

import jax
import jax.numpy as jnp
from jax import lax
from jax.experimental import pallas as pl
from jax.experimental.pallas import tpu as pltpu
from jax.sharding import PartitionSpec as P

NT = 8
SRC_DEPTH = 10
REC_DEPTH = 6
F32 = jnp.float32
BF16 = jnp.bfloat16

second_taps = (-205.0 / 72.0, 8.0 / 5.0, -1.0 / 5.0, 8.0 / 315.0, -1.0 / 560.0)
first_taps = (4.0 / 5.0, -1.0 / 5.0, 4.0 / 105.0, -1.0 / 280.0)
CENTRE = second_taps[0]
S1 = second_taps[1]
G1 = first_taps[0]
second_ratio = tuple(tap / S1 for tap in second_taps[2:])
first_ratio = tuple(tap / G1 for tap in first_taps[1:])
second_whole = (8064.0, -1008.0, 128.0, -9.0)
first_whole = (672.0, -168.0, 32.0, -3.0)
SECOND_UNIT = 1.0 / 5040.0
FIRST_UNIT = 1.0 / 840.0
VMEM = pl.BlockSpec(memory_space=pltpu.VMEM)
SMEM = pl.BlockSpec(memory_space=pltpu.SMEM)
HBM = pl.BlockSpec(memory_space=pltpu.HBM)


def even_pairs(count):
    return [(i, i + 1) for i in range(0, count - 1, 2)]


def odd_pairs(count):
    return [(i, i + 1) for i in range(1, count - 1, 2)]


def both_ways(pairs):
    return [pair for a, b in pairs for pair in ((a, b), (b, a))]


def chip_swap(pairs):
    return [(2 * a + c, 2 * b + c) for a, b in pairs for c in range(2)]


class Place:
    def __init__(self, size_x, columns):
        at_x = lax.axis_index("gx")
        self.core, self.column = lax.rem(at_x, 2), lax.div(at_x, 2)
        self.at_y = lax.axis_index("gy")
        self.parity = lax.rem(self.at_y, 2)
        if columns == 2:
            side = self.column
            self.count = size_x + 4
            self.first_at = self.tile_at = 4 * side
            self.start_x = side * (size_x - 4)
            self.beside_at = [size_x * (1 - side)]
            self.edge_at = [(size_x - GROUP) * (1 - side)]
            self.rest_at, self.rest = GROUP * side, size_x - GROUP
            self.first_rest_at = AROUND * side
        else:
            side = lax.rem(self.column, 2)
            self.count = size_x + 8
            self.first_at = self.tile_at = 4
            self.start_x = self.column * size_x - 4
            self.beside_at = [(size_x + GROUP) * (1 - side), (size_x + GROUP) * side]
            self.edge_at = [(size_x - GROUP) * (1 - side), (size_x - GROUP) * side]
            self.rest_at, self.rest = GROUP, size_x - 2 * GROUP
            self.first_rest_at = AROUND
        self.sides = len(self.beside_at)
        self.around_at = [self.tile_at + at - 4 for at in self.edge_at]
        self.own_at = self.first_at + self.tile_at
        self.wide = size_x + GROUP * self.sides


def call(kernel, outs, scratch, mebibytes, name, args, scalars=0, work=10**6):
    outs = tuple(jax.ShapeDtypeStruct(shape, dtype) for shape, dtype in outs)
    return pl.pallas_call(
        kernel,
        out_shape=outs,
        in_specs=[SMEM] * scalars + [VMEM] * (len(args) - scalars),
        out_specs=(VMEM,) * len(outs),
        scratch_shapes=[pltpu.VMEM(shape, dtype) for shape, dtype in scratch],
        compiler_params=pltpu.CompilerParams(vmem_limit_bytes=mebibytes * 2**20),
        cost_estimate=pl.CostEstimate(flops=work, bytes_accessed=work, transcendentals=0),
        name=name,
    )(*args)


def loop(trips, body, wanted):
    unroll = max(u for u in range(1, wanted + 1) if trips % u == 0)

    def step(i, carry):
        body(i)
        return carry

    lax.fori_loop(0, trips, step, 0, unroll=unroll)


def depth_matrices(size):
    rows = jnp.arange(size)[:, None]
    cols = jnp.arange(size)[None, :]
    first = jnp.zeros((size, size), F32)
    second = jnp.zeros((size, size), F32)
    for k in range(1, 5):
        up = (rows == cols + k).astype(F32)
        down = (rows == cols - k).astype(F32)
        first = first + first_whole[k - 1] * (up - down)
        second = second + second_whole[k - 1] * (up + down)
    return (
        jnp.concatenate([first, first]).astype(BF16),
        jnp.concatenate([second, second]).astype(BF16),
    )


def sums_and_slopes(shifted):
    up, down = shifted(1), shifted(-1)
    curve, slope = up + down, up - down
    for k in range(2, 5):
        up, down = shifted(k), shifted(-k)
        curve = curve + second_ratio[k - 2] * (up + down)
        slope = slope + first_ratio[k - 2] * (up - down)
    return curve, slope


def slope_only(shifted):
    slope = shifted(1) - shifted(-1)
    for k in range(2, 5):
        slope = slope + first_ratio[k - 2] * (shifted(k) - shifted(-k))
    return slope


def split(values):
    high = values.astype(BF16)
    low = (values - high.astype(F32)).astype(BF16)
    return high, low


TOP = 32000.0
GROUP = 8
AROUND = GROUP + 8


def tiles_of(fields):
    return fields * 4 + fields // 2


def encode(value_at, out, group, fields):
    for pair in range(fields // 2):
        codes = []
        for f in (2 * pair, 2 * pair + 1):
            values = [value_at(f, p) for p in range(GROUP)]
            size = jnp.full((8, 128), 1e-30, F32)
            for value in values:
                size = jnp.maximum(size, jnp.abs(value))
            code = jnp.ceil(jnp.log2(size) * 256.0)
            factor = TOP * jnp.exp2(code * (-1.0 / 256.0))
            codes.append(code)
            for q in range(GROUP // 2):
                both = [jnp.floor(value * factor + 0.5) for value in values[2 * q : 2 * q + 2]]
                out[group, f * 4 + q] = jnp.concatenate(both).astype(jnp.int32).astype(jnp.int16)
        out[group, fields * 4 + pair] = jnp.concatenate(codes).astype(jnp.int32).astype(jnp.int16)


def decode(payload, group, fields, put):
    for pair in range(fields // 2):
        code = payload[group, fields * 4 + pair].astype(jnp.int32).astype(F32)
        factor = jnp.exp2(code * (1.0 / 256.0)) * (1.0 / TOP)
        for slot in range(2):
            f = 2 * pair + slot
            own = factor[slot * 8 : slot * 8 + 8]
            for q in range(GROUP // 2):
                both = payload[group, f * 4 + q].astype(jnp.int32).astype(F32)
                put(f, 2 * q, both[:8] * own)
                put(f, 2 * q + 1, both[8:] * own)


def leap(src, x0, row0, rows, count, scratch, mats, coef, old_at, inject_at, store):
    slope_y, curve_y, part, halves, product = scratch
    mat_first, mat_second = mats
    planes = 16 // rows
    group = 4

    def field(f, p, r=0, number=rows):
        return src[f, x0 + p, pl.ds(row0 + r, number), :]

    def joined(values):
        return jnp.concatenate(values) if len(values) > 1 else values[0]

    def put_halves(kind, f, unit, values):
        high, low = split(values)
        halves[kind, f, unit, :, :128] = high
        halves[kind, f, unit, :, 128:] = low

    def along_y(u):
        for f in range(2):
            here, slopes = [], []
            for v in range(planes):
                p = u * planes + v
                curve, slope = sums_and_slopes(lambda k: field(f, p, k))
                slope_y[f, p, :rows] = slope
                curve_y[f, p, :rows] = curve
                slopes.append(slope)
                here.append(field(f, p))
            put_halves(0, f, u, joined(here))
            put_halves(1, f, u, joined(slopes))

    loop((count + 8) // planes, along_y, 6)

    def along_x(q):
        base = q * group
        for f in range(2):
            slopes = [[] for g in range(group)]
            for r in range(0, rows, 8):
                line = [field(f, base + k, r, 8) for k in range(group + 8)]
                slant = [slope_y[f, base + k, pl.ds(r, 8), :] for k in range(group + 8)]
                for g in range(group):
                    i = base + g
                    xx, slope = sums_and_slopes(lambda k: line[g + 4 + k])
                    xy = slope_only(lambda k: slant[g + 4 + k])
                    yy = curve_y[f, i + 4, pl.ds(r, 8), :]
                    wx, wy, wxy = [coef(m, i, r, 8) for m in (3, 4, 6)]
                    if f == 0:
                        total = (2.0 * CENTRE) * line[g + 4] + (S1 - wx) * xx
                        total = total + (S1 - wy) * yy - wxy * xy
                    else:
                        total = CENTRE * line[g + 4] + wx * xx
                        total = total + wy * yy + wxy * xy
                    part[f, i, pl.ds(r, 8), :] = total
                    slopes[g].append(slope)
            pieces = [piece for rest in slopes for piece in rest]
            for k in range(0, len(pieces), 2):
                put_halves(2, f, q * (len(pieces) // 2) + k // 2, joined(pieces[k : k + 2]))

    loop(count // group, along_x, 5)

    units = count // planes
    for kind, mat, at in ((0, mat_second, 4 // planes), (1, mat_first, 4 // planes), (2, mat_first, 0)):
        for f in range(2):
            both = halves[kind, f, pl.ds(at, units)].reshape(units * 16, 256)
            out = jnp.dot(both, mat[...], preferred_element_type=F32)
            product[kind, f, pl.ds(0, units)] = out.reshape(units, 16, 128)

    def combine(u):
        where = [u * planes + v for v in range(planes)]
        speed, speed_h, speed_v, wz, wyz, wxz = [
            joined([coef(m, i, 0, rows) for i in where]) for m in (0, 1, 2, 5, 7, 8)
        ]
        zz, yz, xz = [[product[kind, f, u] for f in range(2)] for kind in range(3)]
        parts = [joined([part[f, i, :rows] for i in where]) for f in range(2)]
        here = [joined([field(f, i + 4) for i in where]) for f in range(2)]
        old = [joined([old_at(f, i) for i in where]) for f in range(2)]
        add = joined([inject_at(i) for i in where])
        flat = parts[0] + (SECOND_UNIT - wz) * zz[0] - (wyz * yz[0] + wxz * xz[0])
        tilted = parts[1] + wz * zz[1] + (wyz * yz[1] + wxz * xz[1])
        new_p = (2.0 * here[0] - old[0] + add) + (speed_h * flat + speed_v * tilted)
        new_q = (2.0 * here[1] - old[1] + add) + (speed_v * flat + speed * tilted)
        for v, i in enumerate(where):
            cut = slice(v * rows, v * rows + rows)
            store(i, new_p[cut], new_q[cut])

    loop(units, combine, 10)


def leap_scratch(count):
    lines = (2, count + 8, 16, 128)
    return [
        (lines, F32),
        (lines, F32),
        ((2, count, 16, 128), F32),
        ((3, 2, count + 8, 16, 256), BF16),
        ((3, 2, count, 16, 128), F32),
    ]


def first_kernel(columns, kept, got, tile, old, payload, *edges):
    size = kept.shape[1]
    place = Place(2 * size, columns)
    for source, at in ((kept, place.core * size), (got, (1 - place.core) * size)):
        for f in range(2):
            tile[f, pl.ds(at, size)] = source[2 * f]
            old[f, pl.ds(at, size)] = source[2 * f + 1]

    def group(g):
        encode(lambda f, p: (tile if f < 2 else old)[f % 2, g * GROUP + p], payload, g, 4)

    loop(2 * size // GROUP, group, 1)
    for k, edge in enumerate(edges):
        edge[0] = payload[lax.div(place.edge_at[k], GROUP)]


def first_leap(place, start, count, window, old, old_start, coefs, inject, scratch, mats, store):
    leap(
        window, place.first_at + start, 8, coefs.shape[2], count, scratch, mats,
        lambda m, i, r, number: coefs[m, start + i, pl.ds(r, number), :],
        lambda f, i: old[f, old_start + start + i],
        lambda i: inject[0, start + i],
        store,
    )


def second_leap(
    place, start, count, source, source_start, tile, coefs, inject, scratch, mats, store
):
    rows = tile.shape[2]
    at = place.tile_at + start
    leap(
        source, source_start, 8, rows, count, scratch, mats,
        lambda m, i, r, number: coefs[m, at + i, pl.ds(4 + r, number), :],
        lambda f, i: tile[f, start + i],
        lambda i: inject[1, at + i, pl.ds(4, rows), :],
        store,
    )


def fill(place, tile, old, beside, even, odd, window, old_wide):
    size_x = tile.shape[1]
    groups = size_x // GROUP
    fields = 2 if old_wide is None else 4
    for f in range(2):
        window[f, pl.ds(0, 4)] = jnp.zeros((4, 32, 128), F32)
        window[f, pl.ds(place.wide + 4, 4)] = jnp.zeros((4, 32, 128), F32)
        window[f, pl.ds(place.own_at + 4, size_x), pl.ds(12, 8), :] = tile[f]
        if fields == 4:
            old_wide[f, pl.ds(place.own_at, size_x), pl.ds(4, 8), :] = old[f]

    def lay(payload, group, plane, row):
        def put(f, p, rows):
            if f < 2:
                window[f, plane + p + 4, pl.ds(row + 12, 8), :] = rows
            elif row == 0:
                old_wide[f - 2, plane + p, pl.ds(4, 8), :] = rows
            elif row < 0:
                old_wide[f - 2, plane + p, pl.ds(0, 4), :] = rows[4:]
            else:
                old_wide[f - 2, plane + p, pl.ds(12, 4), :] = rows[:4]

        decode(payload, group, fields, put)

    for k in range(place.sides):
        lay(beside[k], 0, place.beside_at[k], 0)

    def lay_y(below, above):
        for payload, row in ((below, -8), (above, 8)):
            loop(groups, lambda g: lay(payload, g, place.own_at + g * GROUP, row), 2)
            for k in range(place.sides):
                lay(payload, groups + k, place.beside_at[k], row)

    pl.when(place.parity == 0)(lambda: lay_y(odd, even))
    pl.when(place.parity == 1)(lambda: lay_y(even, odd))


def lead_kernel(opening, columns, tile, old, coefs, inject, mat_first, mat_second, *refs):
    place = Place(tile.shape[1], columns)
    refs = list(refs)

    def take(number):
        taken = refs[:number]
        del refs[:number]
        return taken

    sides = place.sides
    beside = take(sides)
    even, odd, window = take(3)
    old_wide = take(1)[0] if opening else None
    around_out, edges_out, codes_out = take(sides), take(sides), take(sides)
    middle = take(1)[0]
    scratch, mats = refs, (mat_first, mat_second)
    fill(place, tile, old, beside, even, odd, window, old_wide)
    for k in range(sides):
        def store_around(i, new_p, new_q):
            for f, new in enumerate((new_p, new_q)):
                around_out[k][f, i] = new
                middle[f, i, pl.ds(4, new.shape[0]), :] = new

        def store_edge(i, new_p, new_q):
            edges_out[k][0, i] = new_p
            edges_out[k][1, i] = new_q

        first_leap(
            place, place.around_at[k], AROUND, window, old_wide if opening else old,
            place.first_at if opening else 0, coefs, inject, scratch, mats, store_around,
        )
        second_leap(
            place, place.edge_at[k], GROUP, middle, 0, tile, coefs, inject, scratch, mats,
            store_edge,
        )
        encode(lambda f, p: edges_out[k][f, p], codes_out[k], 0, 2)


def rest_kernel(opening, columns, tile, old, window, coefs, inject, mat_first, mat_second, *refs):
    size_x, size_y = tile.shape[1], tile.shape[2]
    place = Place(size_x, columns)
    sides, count = place.sides, place.count
    around, edges = refs[:sides], refs[sides : 2 * sides]
    tile_out, payload, old_out, middle, *scratch = refs[2 * sides :]
    mats = (mat_first, mat_second)
    for f in range(2):
        middle[f, pl.ds(0, 4)] = jnp.zeros((4, 24, 128), F32)
        middle[f, pl.ds(count + 4, 4)] = jnp.zeros((4, 24, 128), F32)
        for k in range(sides):
            at = place.around_at[k]
            middle[f, pl.ds(at + 4, AROUND), pl.ds(4, size_y + 8), :] = around[k][f]
            old_out[f, pl.ds(at, AROUND)] = around[k][f]
            tile_out[f, pl.ds(place.edge_at[k], GROUP)] = edges[k][f]

    def store_first(i, new_p, new_q):
        for f, new in enumerate((new_p, new_q)):
            old_out[f, place.first_rest_at + i] = new
            middle[f, place.first_rest_at + i + 4, pl.ds(4, size_y + 8), :] = new

    def store_second(i, new_p, new_q):
        tile_out[0, place.rest_at + i] = new_p
        tile_out[1, place.rest_at + i] = new_q

    first_leap(
        place, place.first_rest_at, count - AROUND * sides, window, old,
        place.first_at if opening else 0, coefs, inject, scratch, mats, store_first,
    )
    second_leap(
        place, place.rest_at, place.rest, middle, place.tile_at + place.rest_at, tile, coefs,
        inject, scratch, mats, store_second,
    )
    loop(
        size_x // GROUP,
        lambda g: encode(lambda f, p: tile_out[f, g * GROUP + p], payload, g, 2),
        1,
    )


def last_kernel(columns, tile, old, coefs, inject, mat_first, mat_second, *refs):
    size_x, size_y = tile.shape[1], tile.shape[2]
    place = Place(size_x, columns)
    sides, count = place.sides, place.count
    even, odd, kept, sent, middle, tile_out, window, *scratch = refs[sides:]
    mats = (mat_first, mat_second)
    fill(place, tile, old, refs[:sides], even, odd, window, None)
    for f in range(2):
        middle[f, pl.ds(0, 4)] = jnp.zeros((4, 24, 128), F32)
        middle[f, pl.ds(count + 4, 4)] = jnp.zeros((4, 24, 128), F32)

    def store_first(i, new_p, new_q):
        for f, new in enumerate((new_p, new_q)):
            middle[f, i + 4, pl.ds(4, size_y + 8), :] = new

    def store_second(i, new_p, new_q):
        tile_out[0, i] = new_p
        tile_out[1, i] = new_q

    first_leap(place, 0, count, window, old, 0, coefs, inject, scratch, mats, store_first)
    second_leap(
        place, 0, size_x, middle, place.tile_at, tile, coefs, inject, scratch, mats, store_second
    )
    half = size_x // 2
    for mine in range(2):
        @pl.when(place.core == mine)
        def _():
            for out, start in ((kept, mine * half), (sent, (1 - mine) * half)):
                planes = pl.ds(start, half)
                inner = pl.ds(place.tile_at + 4 + start, half)
                out[0] = middle[0, inner, pl.ds(8, size_y), :]
                out[1] = tile_out[0, planes]
                out[2] = tile_out[1, planes]


def sine_cosine(angle):
    square = angle * angle
    sine = 1.0 / 6227020800.0
    for factor in (-1.0 / 39916800.0, 1.0 / 362880.0, -1.0 / 5040.0, 1.0 / 120.0, -1.0 / 6.0):
        sine = sine * square + factor
    sine = angle + angle * square * sine
    cosine = 1.0 / 479001600.0
    for factor in (-1.0 / 3628800.0, 1.0 / 40320.0, -1.0 / 720.0, 1.0 / 24.0, -0.5):
        cosine = cosine * square + factor
    return sine, 1.0 + square * cosine


def open_kernel(
    velocity, epsilon, delta, tilt, azimuth, source, receiver, *refs
):
    models = (velocity, epsilon, delta, tilt, azimuth)
    parity = lax.rem(lax.axis_index("gy"), 2)
    core = lax.rem(lax.axis_index("gx"), 2)
    small, (even, odd, own, kept, given), brought, arrived = (
        refs[:3], refs[3:8], refs[8:11], refs[11]
    )
    copies = [pltpu.make_async_copy(models[m], own.at[m], arrived.at[m]) for m in range(5)]
    others = [
        pltpu.make_async_copy(small[m], brought[m], arrived.at[7 + m]) for m in range(3)
    ]

    def states(mine):
        stay, leave = (source, receiver) if mine == 0 else (receiver, source)
        return (
            pltpu.make_async_copy(stay, kept, arrived.at[5]),
            pltpu.make_async_copy(leave, given, arrived.at[6]),
        )

    for copy in copies + others:
        copy.start()
    for mine in range(2):
        @pl.when(core == mine)
        def _():
            for copy in states(mine):
                copy.start()

    for copy in copies:
        copy.wait()

    def pack(out, row):
        for m in range(5):
            for u in range(0, own.shape[1], 2):
                pairs = [own[m, u + k].astype(F32) for k in range(2)]
                values = [pair[v + row : v + row + 4] for pair in pairs for v in (0, 8)]
                out[m, u // 2] = jnp.concatenate(values).astype(BF16)

    @pl.when(parity == 0)
    def _():
        pack(even, 4)
        pack(odd, 0)

    @pl.when(parity == 1)
    def _():
        pack(odd, 4)
        pack(even, 0)

    for mine in range(2):
        @pl.when(core == mine)
        def _():
            for copy in states(mine):
                copy.wait()
    for copy in others:
        copy.wait()


def join_kernel(own, even, odd, out):
    parity = lax.rem(lax.axis_index("gy"), 2)

    def fill(below, above):
        for m in range(5):
            for u in range(own.shape[1]):
                low, high = below[m, u // 2].astype(F32), above[m, u // 2].astype(F32)
                pair = own[m, u].astype(F32)
                for v in range(2):
                    k = 2 * (u % 2) + v
                    rows = [low[4 * k : 4 * k + 4], pair[8 * v : 8 * v + 8], high[4 * k : 4 * k + 4]]
                    out[m, 2 * u + v] = jnp.concatenate(rows).astype(BF16)

    pl.when(parity == 0)(lambda: fill(odd, even))
    pl.when(parity == 1)(lambda: fill(even, odd))


def setup_kernel(columns, size_x, total_x, aperture, *refs):
    models, coefs, blocks = refs[:-2], refs[-2], refs[-1]
    place = Place(2 * size_x, columns)
    if len(models) > 1:
        for k, column in enumerate((place.column, 1 - place.column)):
            for j, core in enumerate((place.core, 1 - place.core)):
                blocks[:, pl.ds((2 * column + core) * size_x, size_x)] = models[2 * k + j][...]
        source = blocks
    else:
        source = models[0]

    def medium(i):
        x = place.start_x + i
        block = jnp.clip(x // size_x, 0, total_x // size_x - 1)
        inside = jnp.logical_and(x >= 0, x < total_x)
        at = aperture[block] * size_x + lax.rem(x + size_x, size_x)
        speed, stretch, bending, tilt, azimuth = [source[m, at].astype(F32) for m in range(5)]
        speed = jnp.where(inside, speed, 0.0)
        sin_t, cos_t = sine_cosine(tilt)
        sin_half, cos_half = sine_cosine(0.5 * azimuth)
        normal_x = sin_t * (1.0 - 2.0 * sin_half * sin_half)
        normal_y = sin_t * (2.0 * sin_half * cos_half)
        coefs[0, i] = speed
        coefs[1, i] = speed * (1.0 + 2.0 * stretch)
        coefs[2, i] = speed * jnp.sqrt(1.0 + 2.0 * bending)
        coefs[3, i] = S1 * (normal_x * normal_x)
        coefs[4, i] = S1 * (normal_y * normal_y)
        coefs[5, i] = SECOND_UNIT * (cos_t * cos_t)
        coefs[6, i] = (2.0 * G1 * G1) * (normal_x * normal_y)
        coefs[7, i] = (2.0 * G1 * FIRST_UNIT) * (normal_y * cos_t)
        coefs[8, i] = (2.0 * G1 * FIRST_UNIT) * (normal_x * cos_t)

    loop(place.count, medium, 6)


def injection_kernel(
    columns, size_x, size_y, total_y, source_cell, wavelet, cells, traces, out, hits
):
    place = Place(size_x, columns)
    count, rows = hits.shape[:2]
    number = cells.shape[1]
    row = lax.broadcasted_iota(jnp.int32, (rows, number), 0)
    lane = lax.broadcasted_iota(jnp.int32, (1, number), 1)
    is_source = place.core == 0
    lonely = jnp.where(lane == 0, source_cell[0], -1)
    aims = jnp.where(is_source, lonely, cells[...])
    y = place.at_y * size_y - 4 + row
    valid = jnp.logical_and(y >= 0, y < total_y)

    def mark(i):
        code = jnp.where(valid, (place.start_x + i) * total_y + y, -2)
        hits[i] = jnp.where(code == aims, 1.0, 0.0).astype(BF16)

    loop(count, mark, 2)
    step = lax.broadcasted_iota(jnp.int32, (NT, number), 0)
    amounts = jnp.zeros((NT, number), F32)
    for k in range(NT):
        amounts = jnp.where(step == k, wavelet[:, k : k + 1], amounts)
    backward = jnp.concatenate([traces[k : k + 1] for k in reversed(range(NT))])
    rest = jnp.where(is_source, amounts, backward)
    total = None
    for _ in range(3):
        piece = rest.astype(BF16)
        rest = rest - piece.astype(F32)
        term = lax.dot_general(
            hits[...].reshape(count * rows, number), piece, (((1,), (1,)), ((), ())),
            preferred_element_type=F32,
        )
        total = term if total is None else total + term
    out[...] = total.reshape(count, rows, NT)


def spread_kernel(moment, lanes, out):
    core = lax.rem(lax.axis_index("gx"), 2)
    level = jnp.where(core == 0, SRC_DEPTH, REC_DEPTH)
    mask = (lax.broadcasted_iota(jnp.int32, (lanes.shape[1], 128), 1) == level).astype(F32)

    def expand(i):
        values = lanes[i]
        for k in range(2):
            out[k, i] = values[:, moment + k : moment + k + 1] * mask

    loop(lanes.shape[0], expand, 6)


def sort_kernel(columns, *refs):
    levels, (kept, sent) = refs[: NT - 1], refs[NT - 1 :]
    half, size_y = kept.shape[1:3]
    place = Place(2 * half, columns)

    def level_at(step, start):
        where = levels[step]
        if step % 2 == 0:
            return where[0, pl.ds(start, half)]
        return where[0, pl.ds(place.tile_at + start, half), pl.ds(4, size_y), :]

    for mine in range(2):
        @pl.when(place.core == mine)
        def _():
            for step in range(NT - 1):
                t = step if mine == 0 else NT - step
                if t > 0:
                    kept[t - 1] = level_at(step, mine * half)
                    sent[t - 1] = level_at(step, (1 - mine) * half)


def close_kernel(kept, got, last_kept, last_got, image, field):
    core = lax.rem(lax.axis_index("gx"), 2)
    total = kept[1] * got[1]
    for t in range(2, NT - 2):
        total = total + kept[t] * got[t]

    @pl.when(core == 0)
    def _():
        image[...] = (
            total + kept[0] * last_got[0] + last_kept[0] * got[NT - 2] + last_kept[1] * got[NT - 1]
        ) * (1.0 / NT)
        field[...] = last_got[pl.ds(1, 2)]

    @pl.when(core == 1)
    def _():
        image[...] = (
            total + last_kept[0] * got[0] + kept[NT - 2] * last_got[0] + kept[NT - 1] * last_got[1]
        ) * (1.0 / NT)
        field[...] = last_kept[pl.ds(1, 2)]


def per_device(
    velocity,
    epsilon,
    delta,
    tilt,
    azimuth,
    aperture,
    source_cell,
    wavelet,
    receiver_cell,
    traces,
    source_state,
    receiver_state,
):
    block_x, size_y, _ = velocity.shape
    devices_x, devices_y = lax.axis_size("gx"), lax.axis_size("gy")
    columns = devices_x // 2
    total_x, total_y = block_x * devices_x, size_y * devices_y
    size_x, rows = 2 * block_x, size_y + 8
    is_source = lax.axis_index("gx") % 2 == 0
    place = Place(size_x, columns)
    sides, count = place.sides, place.count
    groups = size_x // GROUP
    mats = depth_matrices(128)
    chip_pairs = [even_pairs(columns), odd_pairs(columns)][:sides]
    row_pairs = [even_pairs(devices_y), odd_pairs(devices_y)]
    trade = both_ways([(2 * c, 2 * c + 1) for c in range(columns)])

    def over_gy(values, pairs):
        return lax.ppermute(values, "gy", both_ways(pairs))

    def over_gx(values, pairs):
        return lax.ppermute(values, "gx", both_ways(chip_swap(pairs)))

    def beside_of(edges):
        return [over_gx(edge, pairs) for edge, pairs in zip(edges, chip_pairs)]

    def near_of(payload, beside):
        wide = jnp.concatenate([payload, *beside])
        return wide, [over_gy(wide, pairs) for pairs in row_pairs]

    def codes(number, fields):
        return ((number, tiles_of(fields), 16, 128), jnp.int16)

    models = [
        values.reshape(block_x // 2, 16, 128) for values in (velocity, epsilon, delta, tilt, azimuth)
    ]
    small = (wavelet[None, :], receiver_cell[None, :], traces)
    rim = ((5, block_x // 4, 16, 128), BF16)
    states = (source_state, receiver_state)
    state = (source_state.shape, F32)
    *rims, own, kept, given, series, cells, data = pl.pallas_call(
        open_kernel,
        out_shape=tuple(
            jax.ShapeDtypeStruct(*out)
            for out in (rim, rim, ((5, block_x // 2, 16, 128), BF16), state, state)
            + tuple((x.shape, x.dtype) for x in small)
        ),
        in_specs=[HBM] * 10,
        out_specs=(VMEM,) * 8,
        scratch_shapes=[pltpu.SemaphoreType.DMA((10,))],
        compiler_params=pltpu.CompilerParams(vmem_limit_bytes=8 * 2**20),
        name="open",
    )(*[pltpu.with_memory_space_constraint(x, pltpu.HBM) for x in (*models, *states, *small)])
    rims = [over_gy(values, pairs) for values, pairs in zip(rims, row_pairs)]

    got = lax.ppermute(given, "gx", trade)
    field = ((2, size_x, size_y, 128), F32)
    tile, old, payload, *edges = call(
        functools.partial(first_kernel, columns),
        (field, field, codes(groups, 4)) + (codes(1, 4),) * sides,
        (), 16, "first", (kept, got),
    )
    number = receiver_cell.shape[0]
    cells, _ = lax.optimization_barrier((cells, edges[0]))
    (amounts,) = call(
        functools.partial(injection_kernel, columns, size_x, size_y, total_y),
        (((count, rows, NT), F32),), (((count, rows, number), BF16),),
        16, "injection", (source_cell, series, cells, data), scalars=1,
    )
    beside = beside_of(edges)
    payload, _ = lax.optimization_barrier((payload, amounts))
    wide, near = near_of(payload, beside)

    rims = lax.optimization_barrier((*rims, edges[0]))[:2]
    (model,) = call(
        join_kernel, (((5, block_x, rows, 128), BF16),), (), 8, "join", (own, *rims), work=1000
    )
    if columns == 2:
        later, _ = lax.optimization_barrier((model, wide))
        across = over_gx(later, chip_pairs[0])
        other = lax.ppermute(model, "gx", trade)
        gathered = [model, other, across, lax.ppermute(across, "gx", trade)]
        held = (5, total_x, rows, 128)
    else:
        gathered, held = [lax.all_gather(model, "gx", axis=1, tiled=True)], (16, 128)
    (coefs,) = call(
        functools.partial(setup_kernel, columns, block_x, total_x),
        (((9, count, rows, 128), F32),), ((held, BF16),), 24, "setup", (aperture, *gathered),
        scalars=1, work=0,
    )

    window = ((2, place.wide + 8, 32, 128), F32)
    middle = ((2, count + 8, 24, 128), F32)
    lines = ((2, count, rows, 128), F32)
    def spread(moment, after):
        lanes, _ = lax.optimization_barrier((amounts, after))
        (out,) = call(
            functools.partial(spread_kernel, moment), (((2, count, rows, 128), F32),), (), 8,
            "spread", (lanes,),
        )
        return out

    levels = [tile]
    for moment in range(0, NT - 2, 2):
        inject = spread(moment, wide)
        opening = moment == 0
        old_wide = (((2, place.wide, rows, 128), F32),) * opening
        around = (((2, AROUND, rows, 128), F32),) * sides
        edge = (((2, GROUP, size_y, 128), F32),) * sides
        fields, *outs = call(
            functools.partial(lead_kernel, opening, columns),
            (window,) + old_wide + around + edge + (codes(1, 2),) * sides,
            [((2, AROUND, 24, 128), F32)] + leap_scratch(AROUND), 24, "lead",
            (tile, old, coefs, inject, *mats, *beside, *near), work=2 * 10**6,
        )
        if opening:
            old, *outs = outs
        beside = beside_of(outs[2 * sides :])
        tile, payload, old = call(
            functools.partial(rest_kernel, opening, columns),
            (field, codes(groups, 2), lines), [middle] + leap_scratch(place.rest), 24, "rest",
            (tile, old, fields, coefs, inject, *mats, *outs[: 2 * sides]), work=4 * 10**6,
        )
        wide, near = near_of(payload, beside)
        levels += [old, tile]
    shape = (block_x, size_y, 128)
    inject = spread(NT - 2, wide)
    share = ((NT,) + shape, F32)
    kept, sent = call(
        functools.partial(sort_kernel, columns), (share, share), (), 8, "sort",
        lax.optimization_barrier((*levels, *near, inject))[: NT - 1],
    )
    got = lax.ppermute(sent, "gx", trade)
    share = ((3,) + shape, F32)
    last_kept, last_sent = call(
        functools.partial(last_kernel, columns),
        (share, share), [middle, field, window] + leap_scratch(count), 24, "last",
        (tile, old, coefs, inject, *mats, *beside, *near),
    )
    last_got = lax.ppermute(last_sent, "gx", trade)
    return call(
        close_kernel, ((shape, F32), ((2,) + shape, F32)), (), 8, "close",
        (kept, got, last_kept, last_got),
    )


def solution(mesh):
    in_specs = (
        P("gx", "gy", None),
        P("gx", "gy", None),
        P("gx", "gy", None),
        P("gx", "gy", None),
        P("gx", "gy", None),
        P("shot"),
        P("shot"),
        P("shot"),
        P("shot"),
        P(None, "shot"),
        P(None, ("shot", "gx"), "gy", None),
        P(None, ("shot", "gx"), "gy", None),
    )
    out_specs = (P(("shot", "gx"), "gy", None), P(None, ("shot", "gx"), "gy", None))
    return jax.shard_map(
        per_device, mesh=mesh, in_specs=in_specs, out_specs=out_specs, check_vma=False
    )
```

```python
import functools

import jax
import jax.numpy as jnp
from jax import lax
from jax.experimental import pallas as pl
from jax.experimental.pallas import tpu as pltpu
from jax.sharding import PartitionSpec as P

NT = 8
SRC_DEPTH = 10
REC_DEPTH = 6
F32 = jnp.float32
BF16 = jnp.bfloat16

second_taps = (-205.0 / 72.0, 8.0 / 5.0, -1.0 / 5.0, 8.0 / 315.0, -1.0 / 560.0)
first_taps = (4.0 / 5.0, -1.0 / 5.0, 4.0 / 105.0, -1.0 / 280.0)
CENTRE = second_taps[0]
S1 = second_taps[1]
G1 = first_taps[0]
second_ratio = tuple(tap / S1 for tap in second_taps[2:])
first_ratio = tuple(tap / G1 for tap in first_taps[1:])
second_whole = (8064.0, -1008.0, 128.0, -9.0)
first_whole = (672.0, -168.0, 32.0, -3.0)
SECOND_UNIT = 1.0 / 5040.0
FIRST_UNIT = 1.0 / 840.0
VMEM = pl.BlockSpec(memory_space=pltpu.VMEM)
SMEM = pl.BlockSpec(memory_space=pltpu.SMEM)
HBM = pl.BlockSpec(memory_space=pltpu.HBM)


def even_pairs(count):
    return [(i, i + 1) for i in range(0, count - 1, 2)]


def odd_pairs(count):
    return [(i, i + 1) for i in range(1, count - 1, 2)]


def both_ways(pairs):
    return [pair for a, b in pairs for pair in ((a, b), (b, a))]


def chip_swap(pairs):
    return [(2 * a + c, 2 * b + c) for a, b in pairs for c in range(2)]


class Place:
    def __init__(self, size_x, columns):
        at_x = lax.axis_index("gx")
        self.core, self.column = lax.rem(at_x, 2), lax.div(at_x, 2)
        self.at_y = lax.axis_index("gy")
        self.parity = lax.rem(self.at_y, 2)
        if columns == 2:
            side = self.column
            self.count = size_x + 4
            self.first_at = self.tile_at = 4 * side
            self.start_x = side * (size_x - 4)
            self.beside_at = [size_x * (1 - side)]
            self.edge_at = [(size_x - GROUP) * (1 - side)]
            self.rest_at, self.rest = GROUP * side, size_x - GROUP
            self.first_rest_at = AROUND * side
        else:
            side = lax.rem(self.column, 2)
            self.count = size_x + 8
            self.first_at = self.tile_at = 4
            self.start_x = self.column * size_x - 4
            self.beside_at = [(size_x + GROUP) * (1 - side), (size_x + GROUP) * side]
            self.edge_at = [(size_x - GROUP) * (1 - side), (size_x - GROUP) * side]
            self.rest_at, self.rest = GROUP, size_x - 2 * GROUP
            self.first_rest_at = AROUND
        self.sides = len(self.beside_at)
        self.around_at = [self.tile_at + at - 4 for at in self.edge_at]
        self.own_at = self.first_at + self.tile_at
        self.wide = size_x + GROUP * self.sides


def call(kernel, outs, scratch, mebibytes, name, args, scalars=0, work=10**6):
    outs = tuple(jax.ShapeDtypeStruct(shape, dtype) for shape, dtype in outs)
    return pl.pallas_call(
        kernel,
        out_shape=outs,
        in_specs=[SMEM] * scalars + [VMEM] * (len(args) - scalars),
        out_specs=(VMEM,) * len(outs),
        scratch_shapes=[pltpu.VMEM(shape, dtype) for shape, dtype in scratch],
        compiler_params=pltpu.CompilerParams(vmem_limit_bytes=mebibytes * 2**20),
        cost_estimate=pl.CostEstimate(flops=work, bytes_accessed=work, transcendentals=0),
        name=name,
    )(*args)


def loop(trips, body, wanted):
    unroll = max(u for u in range(1, wanted + 1) if trips % u == 0)

    def step(i, carry):
        body(i)
        return carry

    lax.fori_loop(0, trips, step, 0, unroll=unroll)


def depth_matrices(size):
    rows = jnp.arange(size)[:, None]
    cols = jnp.arange(size)[None, :]
    first = jnp.zeros((size, size), F32)
    second = jnp.zeros((size, size), F32)
    for k in range(1, 5):
        up = (rows == cols + k).astype(F32)
        down = (rows == cols - k).astype(F32)
        first = first + first_whole[k - 1] * (up - down)
        second = second + second_whole[k - 1] * (up + down)
    return (
        jnp.concatenate([first, first]).astype(BF16),
        jnp.concatenate([second, second]).astype(BF16),
    )


def sums_and_slopes(shifted):
    up, down = shifted(1), shifted(-1)
    curve, slope = up + down, up - down
    for k in range(2, 5):
        up, down = shifted(k), shifted(-k)
        curve = curve + second_ratio[k - 2] * (up + down)
        slope = slope + first_ratio[k - 2] * (up - down)
    return curve, slope


def slope_only(shifted):
    slope = shifted(1) - shifted(-1)
    for k in range(2, 5):
        slope = slope + first_ratio[k - 2] * (shifted(k) - shifted(-k))
    return slope


def split(values):
    high = values.astype(BF16)
    low = (values - high.astype(F32)).astype(BF16)
    return high, low


TOP = 32000.0
GROUP = 8
AROUND = GROUP + 8
TILES = GROUP


def block_size(planes, old_rows=0):
    return planes + 1 + planes * old_rows // 8


def scale_of(value_at, planes):
    def grow(i, size):
        for f in range(2):
            size = jnp.maximum(size, jnp.abs(value_at(f, i)))
        return size

    size = lax.fori_loop(0, planes, grow, jnp.full((8, 128), 1e-30, F32), unroll=8)
    code = jnp.ceil(jnp.log2(size) * 256.0)
    return code, TOP * jnp.exp2(code * (-1.0 / 256.0))


def as_code(pieces):
    return jnp.concatenate(pieces).astype(jnp.int32).astype(jnp.int16)


def encode(value_at, planes, out, old_at=None):
    code, factor = scale_of(value_at, planes)
    old_code, old_factor = scale_of(old_at, planes) if old_at else (code, None)

    def put(source, base, by):
        def group(g):
            for f in range(2):
                for q in range(4):
                    pair = [source(f, g * GROUP + 2 * q + v) for v in range(2)]
                    whole = [jnp.floor(value * by + 0.5) for value in pair]
                    out[base + g * TILES + 4 * f + q] = as_code(whole)

        loop(planes // GROUP, group, 1)

    put(value_at, 0, factor)
    out[planes] = as_code([code, old_code])
    if old_at:
        put(old_at, planes + 1, old_factor)


def factor_of(scales, half):
    code = scales.astype(jnp.int32).astype(F32)[8 * half : 8 * half + 8]
    return jnp.exp2(code * (1.0 / 256.0)) * (1.0 / TOP)


def decode(block, base, factor, put):
    for f in range(2):
        for q in range(4):
            both = block[base + 4 * f + q].astype(jnp.int32).astype(F32)
            put(f, 2 * q, both[:8] * factor)
            put(f, 2 * q + 1, both[8:] * factor)


def decode_nearest(block, base, factor, put):
    by = jnp.concatenate([factor] * 4)
    for f in range(2):
        for q in range(2):
            rows = block[base + 2 * f + q].astype(jnp.int32).astype(F32) * by
            for v in range(4):
                put(f, 4 * q + v, rows[4 * v : 4 * v + 4])


def leap(src, x0, row0, rows, count, scratch, mats, coef, old_at, inject_at, store):
    slope_y, curve_y, part, halves, product = scratch
    mat_first, mat_second = mats
    planes = 16 // rows
    group = 4

    def field(f, p, r=0, number=rows):
        return src[f, x0 + p, pl.ds(row0 + r, number), :]

    def joined(values):
        return jnp.concatenate(values) if len(values) > 1 else values[0]

    def put_halves(kind, f, unit, values):
        high, low = split(values)
        halves[kind, f, unit, :, :128] = high
        halves[kind, f, unit, :, 128:] = low

    def along_y(u):
        for f in range(2):
            here, slopes = [], []
            for v in range(planes):
                p = u * planes + v
                curve, slope = sums_and_slopes(lambda k: field(f, p, k))
                slope_y[f, p, :rows] = slope
                curve_y[f, p, :rows] = curve
                slopes.append(slope)
                here.append(field(f, p))
            put_halves(0, f, u, joined(here))
            put_halves(1, f, u, joined(slopes))

    loop((count + 8) // planes, along_y, 6)

    def along_x(q):
        base = q * group
        for f in range(2):
            slopes = [[] for g in range(group)]
            for r in range(0, rows, 8):
                line = [field(f, base + k, r, 8) for k in range(group + 8)]
                slant = [slope_y[f, base + k, pl.ds(r, 8), :] for k in range(group + 8)]
                for g in range(group):
                    i = base + g
                    xx, slope = sums_and_slopes(lambda k: line[g + 4 + k])
                    xy = slope_only(lambda k: slant[g + 4 + k])
                    yy = curve_y[f, i + 4, pl.ds(r, 8), :]
                    wx, wy, wxy = [coef(m, i, r, 8) for m in (3, 4, 6)]
                    if f == 0:
                        total = (2.0 * CENTRE) * line[g + 4] + (S1 - wx) * xx
                        total = total + (S1 - wy) * yy - wxy * xy
                    else:
                        total = CENTRE * line[g + 4] + wx * xx
                        total = total + wy * yy + wxy * xy
                    part[f, i, pl.ds(r, 8), :] = total
                    slopes[g].append(slope)
            pieces = [piece for rest in slopes for piece in rest]
            for k in range(0, len(pieces), 2):
                put_halves(2, f, q * (len(pieces) // 2) + k // 2, joined(pieces[k : k + 2]))

    loop(count // group, along_x, 5)

    units = count // planes
    for kind, mat, at in ((0, mat_second, 4 // planes), (1, mat_first, 4 // planes), (2, mat_first, 0)):
        for f in range(2):
            both = halves[kind, f, pl.ds(at, units)].reshape(units * 16, 256)
            out = jnp.dot(both, mat[...], preferred_element_type=F32)
            product[kind, f, pl.ds(0, units)] = out.reshape(units, 16, 128)

    def combine(u):
        where = [u * planes + v for v in range(planes)]
        speed, speed_h, speed_v, wz, wyz, wxz = [
            joined([coef(m, i, 0, rows) for i in where]) for m in (0, 1, 2, 5, 7, 8)
        ]
        zz, yz, xz = [[product[kind, f, u] for f in range(2)] for kind in range(3)]
        parts = [joined([part[f, i, :rows] for i in where]) for f in range(2)]
        here = [joined([field(f, i + 4) for i in where]) for f in range(2)]
        old = [joined([old_at(f, i) for i in where]) for f in range(2)]
        add = joined([inject_at(i) for i in where])
        flat = parts[0] + (SECOND_UNIT - wz) * zz[0] - (wyz * yz[0] + wxz * xz[0])
        tilted = parts[1] + wz * zz[1] + (wyz * yz[1] + wxz * xz[1])
        new_p = (2.0 * here[0] - old[0] + add) + (speed_h * flat + speed_v * tilted)
        new_q = (2.0 * here[1] - old[1] + add) + (speed_v * flat + speed * tilted)
        for v, i in enumerate(where):
            cut = slice(v * rows, v * rows + rows)
            store(i, new_p[cut], new_q[cut])

    loop(units, combine, 10)


def leap_scratch(count):
    lines = (2, count + 8, 16, 128)
    return [
        (lines, F32),
        (lines, F32),
        ((2, count, 16, 128), F32),
        ((3, 2, count + 8, 16, 256), BF16),
        ((3, 2, count, 16, 128), F32),
    ]


def first_kernel(columns, kept, got, tile, old, payload, *edges):
    size = kept.shape[1]
    place = Place(2 * size, columns)
    for source, at in ((kept, place.core * size), (got, (1 - place.core) * size)):
        for f in range(2):
            tile[f, pl.ds(at, size)] = source[2 * f]
            old[f, pl.ds(at, size)] = source[2 * f + 1]

    encode(lambda f, p: tile[f, p], 2 * size, payload, lambda f, p: old[f, p])
    for k, edge in enumerate(edges):
        group = lax.div(place.edge_at[k], GROUP) * TILES
        for base in (0, 2 * size + 1):
            edge[pl.ds(base and GROUP + 1, TILES)] = payload[pl.ds(base + group, TILES)]
        edge[GROUP] = payload[2 * size]


def cut_kernel(payload, *refs):
    beside, (odd, even) = refs[:-2], refs[-2:]
    parity = lax.rem(lax.axis_index("gy"), 2)

    def cut(out, row):
        base = 0
        for block in (payload, *beside):
            planes = block.shape[0] // 2
            out[pl.ds(base, planes + 1)] = block[: planes + 1]
            for u in range(0, planes, 2):
                pairs = [block[planes + 1 + u + v].astype(jnp.int32) for v in range(2)]
                rows = [pair[r + row : r + row + 4] for pair in pairs for r in (0, 8)]
                out[base + planes + 1 + u // 2] = jnp.concatenate(rows).astype(jnp.int16)
            base += block_size(planes, 4)

    @pl.when(parity == 0)
    def _():
        cut(even, 4)
        cut(odd, 0)

    @pl.when(parity == 1)
    def _():
        cut(odd, 4)
        cut(even, 0)


def first_leap(place, start, count, window, old, old_start, coefs, inject, scratch, mats, store):
    leap(
        window, place.first_at + start, 8, coefs.shape[2], count, scratch, mats,
        lambda m, i, r, number: coefs[m, start + i, pl.ds(r, number), :],
        lambda f, i: old[f, old_start + start + i],
        lambda i: inject[0, start + i],
        store,
    )


def second_leap(
    place, start, count, source, source_start, tile, coefs, inject, scratch, mats, store
):
    rows = tile.shape[2]
    at = place.tile_at + start
    leap(
        source, source_start, 8, rows, count, scratch, mats,
        lambda m, i, r, number: coefs[m, at + i, pl.ds(4 + r, number), :],
        lambda f, i: tile[f, start + i],
        lambda i: inject[1, at + i, pl.ds(4, rows), :],
        store,
    )


def fill(place, tile, old, beside, even, odd, window, old_wide):
    size_x = tile.shape[1]
    opening = old_wide is not None
    for f in range(2):
        window[f, pl.ds(0, 4)] = jnp.zeros((4, 32, 128), F32)
        window[f, pl.ds(place.wide + 4, 4)] = jnp.zeros((4, 32, 128), F32)
        window[f, pl.ds(place.own_at + 4, size_x), pl.ds(12, 8), :] = tile[f]
        if opening:
            old_wide[f, pl.ds(place.own_at, size_x), pl.ds(4, 8), :] = old[f]

    def lay(block, base, planes, at, row):
        factor = factor_of(block[base + planes], 0)

        def group(g):
            def put(f, p, rows):
                window[f, at + g * GROUP + p + 4, pl.ds(row + 12, 8), :] = rows

            decode(block, base + g * TILES, factor, put)

        loop(planes // GROUP, group, 2)
        if not opening:
            return
        factor = factor_of(block[base + planes], 1)

        def old_group(g):
            def put(f, p, rows):
                first = 0 if row < 0 else row + 4
                old_wide[f, at + g * GROUP + p, pl.ds(first, rows.shape[0]), :] = rows

            start = base + planes + 1
            if row == 0:
                decode(block, start + g * TILES, factor, put)
            else:
                near = factor[4:] if row < 0 else factor[:4]
                decode_nearest(block, start + g * (TILES // 2), near, put)

        loop(planes // GROUP, old_group, 2)

    for k in range(place.sides):
        lay(beside[k], 0, GROUP, place.beside_at[k], 0)

    def lay_y(below, above):
        kept = 4 if opening else 0
        for block, row in ((below, -8), (above, 8)):
            lay(block, 0, size_x, place.own_at, row)
            for k in range(place.sides):
                base = block_size(size_x, kept) + k * block_size(GROUP, kept)
                lay(block, base, GROUP, place.beside_at[k], row)

    pl.when(place.parity == 0)(lambda: lay_y(odd, even))
    pl.when(place.parity == 1)(lambda: lay_y(even, odd))


def lead_kernel(opening, columns, tile, old, coefs, inject, mat_first, mat_second, *refs):
    place = Place(tile.shape[1], columns)
    refs = list(refs)

    def take(number):
        taken = refs[:number]
        del refs[:number]
        return taken

    sides = place.sides
    beside = take(sides)
    even, odd, window = take(3)
    old_wide = take(1)[0] if opening else None
    around_out, edges_out, codes_out = take(sides), take(sides), take(sides)
    middle = take(1)[0]
    scratch, mats = refs, (mat_first, mat_second)
    fill(place, tile, old, beside, even, odd, window, old_wide)
    for k in range(sides):
        def store_around(i, new_p, new_q):
            for f, new in enumerate((new_p, new_q)):
                around_out[k][f, i] = new
                middle[f, i, pl.ds(4, new.shape[0]), :] = new

        def store_edge(i, new_p, new_q):
            edges_out[k][0, i] = new_p
            edges_out[k][1, i] = new_q

        first_leap(
            place, place.around_at[k], AROUND, window, old_wide if opening else old,
            place.first_at if opening else 0, coefs, inject, scratch, mats, store_around,
        )
        second_leap(
            place, place.edge_at[k], GROUP, middle, 0, tile, coefs, inject, scratch, mats,
            store_edge,
        )
        encode(lambda f, p: edges_out[k][f, p], GROUP, codes_out[k])


def rest_kernel(opening, columns, tile, old, window, coefs, inject, mat_first, mat_second, *refs):
    size_x, size_y = tile.shape[1], tile.shape[2]
    place = Place(size_x, columns)
    sides, count = place.sides, place.count
    around, edges = refs[:sides], refs[sides : 2 * sides]
    tile_out, payload, old_out, middle, *scratch = refs[2 * sides :]
    mats = (mat_first, mat_second)
    for f in range(2):
        middle[f, pl.ds(0, 4)] = jnp.zeros((4, 24, 128), F32)
        middle[f, pl.ds(count + 4, 4)] = jnp.zeros((4, 24, 128), F32)
        for k in range(sides):
            at = place.around_at[k]
            middle[f, pl.ds(at + 4, AROUND), pl.ds(4, size_y + 8), :] = around[k][f]
            old_out[f, pl.ds(at, AROUND)] = around[k][f]
            tile_out[f, pl.ds(place.edge_at[k], GROUP)] = edges[k][f]

    def store_first(i, new_p, new_q):
        for f, new in enumerate((new_p, new_q)):
            old_out[f, place.first_rest_at + i] = new
            middle[f, place.first_rest_at + i + 4, pl.ds(4, size_y + 8), :] = new

    def store_second(i, new_p, new_q):
        tile_out[0, place.rest_at + i] = new_p
        tile_out[1, place.rest_at + i] = new_q

    first_leap(
        place, place.first_rest_at, count - AROUND * sides, window, old,
        place.first_at if opening else 0, coefs, inject, scratch, mats, store_first,
    )
    second_leap(
        place, place.rest_at, place.rest, middle, place.tile_at + place.rest_at, tile, coefs,
        inject, scratch, mats, store_second,
    )
    encode(lambda f, p: tile_out[f, p], size_x, payload)


def last_kernel(columns, tile, old, coefs, inject, mat_first, mat_second, *refs):
    size_x, size_y = tile.shape[1], tile.shape[2]
    place = Place(size_x, columns)
    sides, count = place.sides, place.count
    even, odd, kept, sent, middle, tile_out, window, *scratch = refs[sides:]
    mats = (mat_first, mat_second)
    fill(place, tile, old, refs[:sides], even, odd, window, None)
    for f in range(2):
        middle[f, pl.ds(0, 4)] = jnp.zeros((4, 24, 128), F32)
        middle[f, pl.ds(count + 4, 4)] = jnp.zeros((4, 24, 128), F32)

    def store_first(i, new_p, new_q):
        for f, new in enumerate((new_p, new_q)):
            middle[f, i + 4, pl.ds(4, size_y + 8), :] = new

    def store_second(i, new_p, new_q):
        tile_out[0, i] = new_p
        tile_out[1, i] = new_q

    first_leap(place, 0, count, window, old, 0, coefs, inject, scratch, mats, store_first)
    second_leap(
        place, 0, size_x, middle, place.tile_at, tile, coefs, inject, scratch, mats, store_second
    )
    half = size_x // 2
    for mine in range(2):
        @pl.when(place.core == mine)
        def _():
            for out, start in ((kept, mine * half), (sent, (1 - mine) * half)):
                planes = pl.ds(start, half)
                inner = pl.ds(place.tile_at + 4 + start, half)
                out[0] = middle[0, inner, pl.ds(8, size_y), :]
                out[1] = tile_out[0, planes]
                out[2] = tile_out[1, planes]


def sine_cosine(angle):
    square = angle * angle
    sine = 1.0 / 6227020800.0
    for factor in (-1.0 / 39916800.0, 1.0 / 362880.0, -1.0 / 5040.0, 1.0 / 120.0, -1.0 / 6.0):
        sine = sine * square + factor
    sine = angle + angle * square * sine
    cosine = 1.0 / 479001600.0
    for factor in (-1.0 / 3628800.0, 1.0 / 40320.0, -1.0 / 720.0, 1.0 / 24.0, -0.5):
        cosine = cosine * square + factor
    return sine, 1.0 + square * cosine


def open_kernel(
    velocity, epsilon, delta, tilt, azimuth, source, receiver, *refs
):
    models = (velocity, epsilon, delta, tilt, azimuth)
    parity = lax.rem(lax.axis_index("gy"), 2)
    core = lax.rem(lax.axis_index("gx"), 2)
    small, (even, odd, own, kept, given), brought, arrived = (
        refs[:3], refs[3:8], refs[8:11], refs[11]
    )
    copies = [pltpu.make_async_copy(models[m], own.at[m], arrived.at[m]) for m in range(5)]
    others = [
        pltpu.make_async_copy(small[m], brought[m], arrived.at[7 + m]) for m in range(3)
    ]

    def states(mine):
        stay, leave = (source, receiver) if mine == 0 else (receiver, source)
        return (
            pltpu.make_async_copy(stay, kept, arrived.at[5]),
            pltpu.make_async_copy(leave, given, arrived.at[6]),
        )

    for copy in copies + others:
        copy.start()
    for mine in range(2):
        @pl.when(core == mine)
        def _():
            for copy in states(mine):
                copy.start()

    for copy in copies:
        copy.wait()

    def pack(out, row):
        for m in range(5):
            for u in range(0, own.shape[1], 2):
                pairs = [own[m, u + k].astype(F32) for k in range(2)]
                values = [pair[v + row : v + row + 4] for pair in pairs for v in (0, 8)]
                out[m, u // 2] = jnp.concatenate(values).astype(BF16)

    @pl.when(parity == 0)
    def _():
        pack(even, 4)
        pack(odd, 0)

    @pl.when(parity == 1)
    def _():
        pack(odd, 4)
        pack(even, 0)

    for mine in range(2):
        @pl.when(core == mine)
        def _():
            for copy in states(mine):
                copy.wait()
    for copy in others:
        copy.wait()


def join_kernel(own, even, odd, out):
    parity = lax.rem(lax.axis_index("gy"), 2)

    def fill(below, above):
        for m in range(5):
            for u in range(own.shape[1]):
                low, high = below[m, u // 2].astype(F32), above[m, u // 2].astype(F32)
                pair = own[m, u].astype(F32)
                for v in range(2):
                    k = 2 * (u % 2) + v
                    rows = [low[4 * k : 4 * k + 4], pair[8 * v : 8 * v + 8], high[4 * k : 4 * k + 4]]
                    out[m, 2 * u + v] = jnp.concatenate(rows).astype(BF16)

    pl.when(parity == 0)(lambda: fill(odd, even))
    pl.when(parity == 1)(lambda: fill(even, odd))


def setup_kernel(columns, size_x, total_x, aperture, *refs):
    models, coefs, blocks = refs[:-2], refs[-2], refs[-1]
    place = Place(2 * size_x, columns)
    if len(models) > 1:
        for k, column in enumerate((place.column, 1 - place.column)):
            for j, core in enumerate((place.core, 1 - place.core)):
                blocks[:, pl.ds((2 * column + core) * size_x, size_x)] = models[2 * k + j][...]
        source = blocks
    else:
        source = models[0]

    def medium(i):
        x = place.start_x + i
        block = jnp.clip(x // size_x, 0, total_x // size_x - 1)
        inside = jnp.logical_and(x >= 0, x < total_x)
        at = aperture[block] * size_x + lax.rem(x + size_x, size_x)
        speed, stretch, bending, tilt, azimuth = [source[m, at].astype(F32) for m in range(5)]
        speed = jnp.where(inside, speed, 0.0)
        sin_t, cos_t = sine_cosine(tilt)
        sin_half, cos_half = sine_cosine(0.5 * azimuth)
        normal_x = sin_t * (1.0 - 2.0 * sin_half * sin_half)
        normal_y = sin_t * (2.0 * sin_half * cos_half)
        coefs[0, i] = speed
        coefs[1, i] = speed * (1.0 + 2.0 * stretch)
        coefs[2, i] = speed * jnp.sqrt(1.0 + 2.0 * bending)
        coefs[3, i] = S1 * (normal_x * normal_x)
        coefs[4, i] = S1 * (normal_y * normal_y)
        coefs[5, i] = SECOND_UNIT * (cos_t * cos_t)
        coefs[6, i] = (2.0 * G1 * G1) * (normal_x * normal_y)
        coefs[7, i] = (2.0 * G1 * FIRST_UNIT) * (normal_y * cos_t)
        coefs[8, i] = (2.0 * G1 * FIRST_UNIT) * (normal_x * cos_t)

    loop(place.count, medium, 6)


def injection_kernel(
    columns, size_x, size_y, total_y, source_cell, wavelet, cells, traces, out, hits
):
    place = Place(size_x, columns)
    count, rows = hits.shape[:2]
    number = cells.shape[1]
    row = lax.broadcasted_iota(jnp.int32, (rows, number), 0)
    lane = lax.broadcasted_iota(jnp.int32, (1, number), 1)
    is_source = place.core == 0
    lonely = jnp.where(lane == 0, source_cell[0], -1)
    aims = jnp.where(is_source, lonely, cells[...])
    y = place.at_y * size_y - 4 + row
    valid = jnp.logical_and(y >= 0, y < total_y)

    def mark(i):
        code = jnp.where(valid, (place.start_x + i) * total_y + y, -2)
        hits[i] = jnp.where(code == aims, 1.0, 0.0).astype(BF16)

    loop(count, mark, 2)
    step = lax.broadcasted_iota(jnp.int32, (NT, number), 0)
    amounts = jnp.zeros((NT, number), F32)
    for k in range(NT):
        amounts = jnp.where(step == k, wavelet[:, k : k + 1], amounts)
    backward = jnp.concatenate([traces[k : k + 1] for k in reversed(range(NT))])
    rest = jnp.where(is_source, amounts, backward)
    total = None
    for _ in range(3):
        piece = rest.astype(BF16)
        rest = rest - piece.astype(F32)
        term = lax.dot_general(
            hits[...].reshape(count * rows, number), piece, (((1,), (1,)), ((), ())),
            preferred_element_type=F32,
        )
        total = term if total is None else total + term
    out[...] = total.reshape(count, rows, NT)


def spread_kernel(moment, lanes, out):
    core = lax.rem(lax.axis_index("gx"), 2)
    level = jnp.where(core == 0, SRC_DEPTH, REC_DEPTH)
    mask = (lax.broadcasted_iota(jnp.int32, (lanes.shape[1], 128), 1) == level).astype(F32)

    def expand(i):
        values = lanes[i]
        for k in range(2):
            out[k, i] = values[:, moment + k : moment + k + 1] * mask

    loop(lanes.shape[0], expand, 6)


def sort_kernel(columns, *refs):
    levels, (kept, sent) = refs[: NT - 1], refs[NT - 1 :]
    half, size_y = kept.shape[1:3]
    place = Place(2 * half, columns)

    def level_at(step, start):
        where = levels[step]
        if step % 2 == 0:
            return where[0, pl.ds(start, half)]
        return where[0, pl.ds(place.tile_at + start, half), pl.ds(4, size_y), :]

    for mine in range(2):
        @pl.when(place.core == mine)
        def _():
            for step in range(NT - 1):
                t = step if mine == 0 else NT - step
                if t > 0:
                    kept[t - 1] = level_at(step, mine * half)
                    sent[t - 1] = level_at(step, (1 - mine) * half)


def close_kernel(kept, got, last_kept, last_got, image, field):
    core = lax.rem(lax.axis_index("gx"), 2)
    total = kept[1] * got[1]
    for t in range(2, NT - 2):
        total = total + kept[t] * got[t]

    @pl.when(core == 0)
    def _():
        image[...] = (
            total + kept[0] * last_got[0] + last_kept[0] * got[NT - 2] + last_kept[1] * got[NT - 1]
        ) * (1.0 / NT)
        field[...] = last_got[pl.ds(1, 2)]

    @pl.when(core == 1)
    def _():
        image[...] = (
            total + last_kept[0] * got[0] + kept[NT - 2] * last_got[0] + kept[NT - 1] * last_got[1]
        ) * (1.0 / NT)
        field[...] = last_kept[pl.ds(1, 2)]


def per_device(
    velocity,
    epsilon,
    delta,
    tilt,
    azimuth,
    aperture,
    source_cell,
    wavelet,
    receiver_cell,
    traces,
    source_state,
    receiver_state,
):
    block_x, size_y, _ = velocity.shape
    devices_x, devices_y = lax.axis_size("gx"), lax.axis_size("gy")
    columns = devices_x // 2
    total_x, total_y = block_x * devices_x, size_y * devices_y
    size_x, rows = 2 * block_x, size_y + 8
    is_source = lax.axis_index("gx") % 2 == 0
    place = Place(size_x, columns)
    sides, count = place.sides, place.count
    mats = depth_matrices(128)
    chip_pairs = [even_pairs(columns), odd_pairs(columns)][:sides]
    row_pairs = [even_pairs(devices_y), odd_pairs(devices_y)]
    trade = both_ways([(2 * c, 2 * c + 1) for c in range(columns)])

    def over_gy(values, pairs):
        return lax.ppermute(values, "gy", both_ways(pairs))

    def over_gx(values, pairs):
        return lax.ppermute(values, "gx", both_ways(chip_swap(pairs)))

    def beside_of(edges):
        return [over_gx(edge, pairs) for edge, pairs in zip(edges, chip_pairs)]

    def near_of(even, odd):
        odd = over_gy(odd, row_pairs[1])
        return over_gy(even, row_pairs[0]), odd

    def codes(planes, old_rows=0):
        return ((block_size(planes, old_rows), 16, 128), jnp.int16)

    models = [
        values.reshape(block_x // 2, 16, 128) for values in (velocity, epsilon, delta, tilt, azimuth)
    ]
    small = (wavelet[None, :], receiver_cell[None, :], traces)
    rim = ((5, block_x // 4, 16, 128), BF16)
    states = (source_state, receiver_state)
    state = (source_state.shape, F32)
    *rims, own, kept, given, series, cells, data = pl.pallas_call(
        open_kernel,
        out_shape=tuple(
            jax.ShapeDtypeStruct(*out)
            for out in (rim, rim, ((5, block_x // 2, 16, 128), BF16), state, state)
            + tuple((x.shape, x.dtype) for x in small)
        ),
        in_specs=[HBM] * 10,
        out_specs=(VMEM,) * 8,
        scratch_shapes=[pltpu.SemaphoreType.DMA((10,))],
        compiler_params=pltpu.CompilerParams(vmem_limit_bytes=8 * 2**20),
        name="open",
    )(*[pltpu.with_memory_space_constraint(x, pltpu.HBM) for x in (*models, *states, *small)])
    rims = [over_gy(values, pairs) for values, pairs in zip(rims, row_pairs)]

    got = lax.ppermute(given, "gx", trade)
    field = ((2, size_x, size_y, 128), F32)
    tile, old, payload, *edges = call(
        functools.partial(first_kernel, columns),
        (field, field, codes(size_x, 8)) + (codes(GROUP, 8),) * sides,
        (), 16, "first", (kept, got),
    )
    number = receiver_cell.shape[0]
    cells, _ = lax.optimization_barrier((cells, edges[0]))
    (amounts,) = call(
        functools.partial(injection_kernel, columns, size_x, size_y, total_y),
        (((count, rows, NT), F32),), (((count, rows, number), BF16),),
        16, "injection", (source_cell, series, cells, data), scalars=1,
    )
    beside = beside_of(edges)
    payload, _ = lax.optimization_barrier((payload, amounts))
    total = block_size(size_x, 4) + sides * block_size(GROUP, 4)
    wide = call(
        cut_kernel, (((total, 16, 128), jnp.int16),) * 2, (), 8, "cut", (payload, *beside)
    )
    near = near_of(*wide[::-1])

    rims = lax.optimization_barrier((*rims, edges[0]))[:2]
    (model,) = call(
        join_kernel, (((5, block_x, rows, 128), BF16),), (), 8, "join", (own, *rims), work=1000
    )
    if columns == 2:
        later, _ = lax.optimization_barrier((model, wide[0]))
        across = over_gx(later, chip_pairs[0])
        early, _ = lax.optimization_barrier((model, across))
        other = lax.ppermute(early, "gx", trade)
        gathered = [model, other, across, lax.ppermute(across, "gx", trade)]
        held = (5, total_x, rows, 128)
    else:
        gathered, held = [lax.all_gather(model, "gx", axis=1, tiled=True)], (16, 128)
    (coefs,) = call(
        functools.partial(setup_kernel, columns, block_x, total_x),
        (((9, count, rows, 128), F32),), ((held, BF16),), 24, "setup", (aperture, *gathered),
        scalars=1, work=0,
    )

    window = ((2, place.wide + 8, 32, 128), F32)
    middle = ((2, count + 8, 24, 128), F32)
    lines = ((2, count, rows, 128), F32)
    def spread(moment, after):
        lanes, _ = lax.optimization_barrier((amounts, after[0]))
        (out,) = call(
            functools.partial(spread_kernel, moment), (((2, count, rows, 128), F32),), (), 8,
            "spread", (lanes,),
        )
        return out

    levels = [tile]
    for moment in range(0, NT - 2, 2):
        inject = spread(moment, wide)
        opening = moment == 0
        old_wide = (((2, place.wide, rows, 128), F32),) * opening
        around = (((2, AROUND, rows, 128), F32),) * sides
        edge = (((2, GROUP, size_y, 128), F32),) * sides
        fields, *outs = call(
            functools.partial(lead_kernel, opening, columns),
            (window,) + old_wide + around + edge + (codes(GROUP),) * sides,
            [((2, AROUND, 24, 128), F32)] + leap_scratch(AROUND), 24, "lead",
            (tile, old, coefs, inject, *mats, *beside, *near), work=2 * 10**6,
        )
        if opening:
            old, *outs = outs
        beside = beside_of(outs[2 * sides :])
        tile, payload, old = call(
            functools.partial(rest_kernel, opening, columns),
            (field, codes(size_x), lines), [middle] + leap_scratch(place.rest), 24, "rest",
            (tile, old, fields, coefs, inject, *mats, *outs[: 2 * sides]), work=4 * 10**6,
        )
        wide = (jnp.concatenate([payload, *beside]),) * 2
        near = near_of(*wide)
        levels += [old, tile]
    shape = (block_x, size_y, 128)
    inject = spread(NT - 2, wide)
    share = ((NT,) + shape, F32)
    kept, sent = call(
        functools.partial(sort_kernel, columns), (share, share), (), 8, "sort",
        lax.optimization_barrier((*levels, *near, inject))[: NT - 1],
    )
    got = lax.ppermute(sent, "gx", trade)
    share = ((3,) + shape, F32)
    last_kept, last_sent = call(
        functools.partial(last_kernel, columns),
        (share, share), [middle, field, window] + leap_scratch(count), 24, "last",
        (tile, old, coefs, inject, *mats, *beside, *near),
    )
    last_got = lax.ppermute(last_sent, "gx", trade)
    return call(
        close_kernel, ((shape, F32), ((2,) + shape, F32)), (), 8, "close",
        (kept, got, last_kept, last_got),
    )


def solution(mesh):
    in_specs = (
        P("gx", "gy", None),
        P("gx", "gy", None),
        P("gx", "gy", None),
        P("gx", "gy", None),
        P("gx", "gy", None),
        P("shot"),
        P("shot"),
        P("shot"),
        P("shot"),
        P(None, "shot"),
        P(None, ("shot", "gx"), "gy", None),
        P(None, ("shot", "gx"), "gy", None),
    )
    out_specs = (P(("shot", "gx"), "gy", None), P(None, ("shot", "gx"), "gy", None))
    return jax.shard_map(
        per_device, mesh=mesh, in_specs=in_specs, out_specs=out_specs, check_vma=False
    )
```

```python
import functools

import jax
import jax.numpy as jnp
from jax import lax
from jax.experimental import pallas as pl
from jax.experimental.pallas import tpu as pltpu
from jax.sharding import PartitionSpec as P

NT = 8
SRC_DEPTH = 10
REC_DEPTH = 6
F32 = jnp.float32
BF16 = jnp.bfloat16

second_taps = (-205.0 / 72.0, 8.0 / 5.0, -1.0 / 5.0, 8.0 / 315.0, -1.0 / 560.0)
first_taps = (4.0 / 5.0, -1.0 / 5.0, 4.0 / 105.0, -1.0 / 280.0)
CENTRE = second_taps[0]
S1 = second_taps[1]
G1 = first_taps[0]
second_ratio = tuple(tap / S1 for tap in second_taps[2:])
first_ratio = tuple(tap / G1 for tap in first_taps[1:])
second_whole = (8064.0, -1008.0, 128.0, -9.0)
first_whole = (672.0, -168.0, 32.0, -3.0)
SECOND_UNIT = 1.0 / 5040.0
FIRST_UNIT = 1.0 / 840.0
VMEM = pl.BlockSpec(memory_space=pltpu.VMEM)
SMEM = pl.BlockSpec(memory_space=pltpu.SMEM)
HBM = pl.BlockSpec(memory_space=pltpu.HBM)


def even_pairs(count):
    return [(i, i + 1) for i in range(0, count - 1, 2)]


def odd_pairs(count):
    return [(i, i + 1) for i in range(1, count - 1, 2)]


def both_ways(pairs):
    return [pair for a, b in pairs for pair in ((a, b), (b, a))]


def everyone(pairs, count):
    paired = {i for pair in pairs for i in pair}
    return both_ways(pairs) + [(i, i) for i in range(count) if i not in paired]


def chip_swap(pairs):
    return [(2 * a + c, 2 * b + c) for a, b in pairs for c in range(2)]


class Place:
    def __init__(self, size_x, columns):
        at_x = lax.axis_index("gx")
        self.core, self.column = lax.rem(at_x, 2), lax.div(at_x, 2)
        self.at_y = lax.axis_index("gy")
        self.parity = lax.rem(self.at_y, 2)
        self.has_below = jnp.where(self.at_y > 0, 1.0, 0.0)
        self.has_above = jnp.where(self.at_y < lax.axis_size("gy") - 1, 1.0, 0.0)
        if columns == 2:
            side = self.column
            self.count = size_x + 4
            self.first_at = self.tile_at = 4 * side
            self.start_x = side * (size_x - 4)
            self.beside_at = [size_x * (1 - side)]
            self.edge_at = [(size_x - GROUP) * (1 - side)]
            self.rest_at, self.rest = GROUP * side, size_x - GROUP
            self.first_rest_at = AROUND * side
        else:
            side = lax.rem(self.column, 2)
            self.count = size_x + 8
            self.first_at = self.tile_at = 4
            self.start_x = self.column * size_x - 4
            self.beside_at = [(size_x + GROUP) * (1 - side), (size_x + GROUP) * side]
            self.edge_at = [(size_x - GROUP) * (1 - side), (size_x - GROUP) * side]
            self.rest_at, self.rest = GROUP, size_x - 2 * GROUP
            self.first_rest_at = AROUND
        self.sides = len(self.beside_at)
        self.around_at = [self.tile_at + at - 4 for at in self.edge_at]
        self.own_at = self.first_at + self.tile_at
        self.wide = size_x + GROUP * self.sides


def call(kernel, outs, scratch, mebibytes, name, args, scalars=0, work=10**6):
    outs = tuple(jax.ShapeDtypeStruct(shape, dtype) for shape, dtype in outs)
    return pl.pallas_call(
        kernel,
        out_shape=outs,
        in_specs=[SMEM] * scalars + [VMEM] * (len(args) - scalars),
        out_specs=(VMEM,) * len(outs),
        scratch_shapes=[pltpu.VMEM(shape, dtype) for shape, dtype in scratch],
        compiler_params=pltpu.CompilerParams(vmem_limit_bytes=mebibytes * 2**20),
        cost_estimate=pl.CostEstimate(flops=work, bytes_accessed=work, transcendentals=0),
        name=name,
    )(*args)


def loop(trips, body, wanted):
    unroll = max(u for u in range(1, wanted + 1) if trips % u == 0)

    def step(i, carry):
        body(i)
        return carry

    lax.fori_loop(0, trips, step, 0, unroll=unroll)


def depth_matrices(size):
    rows = jnp.arange(size)[:, None]
    cols = jnp.arange(size)[None, :]
    first = jnp.zeros((size, size), F32)
    second = jnp.zeros((size, size), F32)
    for k in range(1, 5):
        up = (rows == cols + k).astype(F32)
        down = (rows == cols - k).astype(F32)
        first = first + first_whole[k - 1] * (up - down)
        second = second + second_whole[k - 1] * (up + down)
    return (
        jnp.concatenate([first, first]).astype(BF16),
        jnp.concatenate([second, second]).astype(BF16),
    )


def sums_and_slopes(shifted):
    up, down = shifted(1), shifted(-1)
    curve, slope = up + down, up - down
    for k in range(2, 5):
        up, down = shifted(k), shifted(-k)
        curve = curve + second_ratio[k - 2] * (up + down)
        slope = slope + first_ratio[k - 2] * (up - down)
    return curve, slope


def slope_only(shifted):
    slope = shifted(1) - shifted(-1)
    for k in range(2, 5):
        slope = slope + first_ratio[k - 2] * (shifted(k) - shifted(-k))
    return slope


def split(values):
    high = values.astype(BF16)
    low = (values - high.astype(F32)).astype(BF16)
    return high, low


TOP = 32000.0
GROUP = 8
AROUND = GROUP + 8
TILES = GROUP


def block_size(planes, old_rows=0):
    return planes + 1 + planes * old_rows // 8


def scale_of(value_at, planes):
    def grow(i, size):
        for f in range(2):
            size = jnp.maximum(size, jnp.abs(value_at(f, i)))
        return size

    size = lax.fori_loop(0, planes, grow, jnp.full((8, 128), 1e-30, F32), unroll=8)
    code = jnp.ceil(jnp.log2(size) * 256.0)
    return code, TOP * jnp.exp2(code * (-1.0 / 256.0))


def as_code(pieces):
    return jnp.concatenate(pieces).astype(jnp.int32).astype(jnp.int16)


def encode(value_at, planes, out, old_at=None):
    code, factor = scale_of(value_at, planes)
    old_code, old_factor = scale_of(old_at, planes) if old_at else (code, None)

    def put(source, base, by):
        def group(g):
            for f in range(2):
                for q in range(4):
                    pair = [source(f, g * GROUP + 2 * q + v) for v in range(2)]
                    whole = [jnp.floor(value * by + 0.5) for value in pair]
                    out[base + g * TILES + 4 * f + q] = as_code(whole)

        loop(planes // GROUP, group, 1)

    put(value_at, 0, factor)
    out[planes] = as_code([code, old_code])
    if old_at:
        put(old_at, planes + 1, old_factor)


def factor_of(scales, half):
    code = scales.astype(jnp.int32).astype(F32)[8 * half : 8 * half + 8]
    return jnp.exp2(code * (1.0 / 256.0)) * (1.0 / TOP)


def decode(block, base, factor, put):
    for f in range(2):
        for q in range(4):
            both = block[base + 4 * f + q].astype(jnp.int32).astype(F32)
            put(f, 2 * q, both[:8] * factor)
            put(f, 2 * q + 1, both[8:] * factor)


def decode_nearest(block, base, factor, put):
    by = jnp.concatenate([factor] * 4)
    for f in range(2):
        for q in range(2):
            rows = block[base + 2 * f + q].astype(jnp.int32).astype(F32) * by
            for v in range(4):
                put(f, 4 * q + v, rows[4 * v : 4 * v + 4])


def leap(src, x0, row0, rows, count, scratch, mats, coef, old_at, inject_at, store):
    slope_y, curve_y, part, halves, product = scratch
    mat_first, mat_second = mats
    planes = 16 // rows
    group = 4

    def field(f, p, r=0, number=rows):
        return src[f, x0 + p, pl.ds(row0 + r, number), :]

    def joined(values):
        return jnp.concatenate(values) if len(values) > 1 else values[0]

    def put_halves(kind, f, unit, values):
        high, low = split(values)
        halves[kind, f, unit, :, :128] = high
        halves[kind, f, unit, :, 128:] = low

    def along_y(u):
        for f in range(2):
            here, slopes = [], []
            for v in range(planes):
                p = u * planes + v
                curve, slope = sums_and_slopes(lambda k: field(f, p, k))
                slope_y[f, p, :rows] = slope
                curve_y[f, p, :rows] = curve
                slopes.append(slope)
                here.append(field(f, p))
            put_halves(0, f, u, joined(here))
            put_halves(1, f, u, joined(slopes))

    loop((count + 8) // planes, along_y, 6)

    def along_x(q):
        base = q * group
        for f in range(2):
            slopes = [[] for g in range(group)]
            for r in range(0, rows, 8):
                line = [field(f, base + k, r, 8) for k in range(group + 8)]
                slant = [slope_y[f, base + k, pl.ds(r, 8), :] for k in range(group + 8)]
                for g in range(group):
                    i = base + g
                    xx, slope = sums_and_slopes(lambda k: line[g + 4 + k])
                    xy = slope_only(lambda k: slant[g + 4 + k])
                    yy = curve_y[f, i + 4, pl.ds(r, 8), :]
                    wx, wy, wxy = [coef(m, i, r, 8) for m in (3, 4, 6)]
                    if f == 0:
                        total = (2.0 * CENTRE) * line[g + 4] + (S1 - wx) * xx
                        total = total + (S1 - wy) * yy - wxy * xy
                    else:
                        total = CENTRE * line[g + 4] + wx * xx
                        total = total + wy * yy + wxy * xy
                    part[f, i, pl.ds(r, 8), :] = total
                    slopes[g].append(slope)
            pieces = [piece for rest in slopes for piece in rest]
            for k in range(0, len(pieces), 2):
                put_halves(2, f, q * (len(pieces) // 2) + k // 2, joined(pieces[k : k + 2]))

    loop(count // group, along_x, 5)

    units = count // planes
    for kind, mat, at in ((0, mat_second, 4 // planes), (1, mat_first, 4 // planes), (2, mat_first, 0)):
        for f in range(2):
            both = halves[kind, f, pl.ds(at, units)].reshape(units * 16, 256)
            out = jnp.dot(both, mat[...], preferred_element_type=F32)
            product[kind, f, pl.ds(0, units)] = out.reshape(units, 16, 128)

    def combine(u):
        where = [u * planes + v for v in range(planes)]
        speed, speed_h, speed_v, wz, wyz, wxz = [
            joined([coef(m, i, 0, rows) for i in where]) for m in (0, 1, 2, 5, 7, 8)
        ]
        zz, yz, xz = [[product[kind, f, u] for f in range(2)] for kind in range(3)]
        parts = [joined([part[f, i, :rows] for i in where]) for f in range(2)]
        here = [joined([field(f, i + 4) for i in where]) for f in range(2)]
        old = [joined([old_at(f, i) for i in where]) for f in range(2)]
        add = joined([inject_at(i) for i in where])
        flat = parts[0] + (SECOND_UNIT - wz) * zz[0] - (wyz * yz[0] + wxz * xz[0])
        tilted = parts[1] + wz * zz[1] + (wyz * yz[1] + wxz * xz[1])
        new_p = (2.0 * here[0] - old[0] + add) + (speed_h * flat + speed_v * tilted)
        new_q = (2.0 * here[1] - old[1] + add) + (speed_v * flat + speed * tilted)
        for v, i in enumerate(where):
            cut = slice(v * rows, v * rows + rows)
            store(i, new_p[cut], new_q[cut])

    loop(units, combine, 10)


def leap_scratch(count):
    lines = (2, count + 8, 16, 128)
    return [
        (lines, F32),
        (lines, F32),
        ((2, count, 16, 128), F32),
        ((3, 2, count + 8, 16, 256), BF16),
        ((3, 2, count, 16, 128), F32),
    ]


def first_kernel(columns, kept, got, tile, old, payload, *edges):
    size = kept.shape[1]
    place = Place(2 * size, columns)
    for source, at in ((kept, place.core * size), (got, (1 - place.core) * size)):
        for f in range(2):
            tile[f, pl.ds(at, size)] = source[2 * f]
            old[f, pl.ds(at, size)] = source[2 * f + 1]

    encode(lambda f, p: tile[f, p], 2 * size, payload, lambda f, p: old[f, p])
    for k, edge in enumerate(edges):
        group = lax.div(place.edge_at[k], GROUP) * TILES
        for base in (0, 2 * size + 1):
            edge[pl.ds(base and GROUP + 1, TILES)] = payload[pl.ds(base + group, TILES)]
        edge[GROUP] = payload[2 * size]


def cut_kernel(payload, *refs):
    beside, (odd, even) = refs[:-2], refs[-2:]
    parity = lax.rem(lax.axis_index("gy"), 2)

    def cut(out, row):
        base = 0
        for block in (payload, *beside):
            planes = block.shape[0] // 2
            out[pl.ds(base, planes + 1)] = block[: planes + 1]
            for u in range(0, planes, 2):
                pairs = [block[planes + 1 + u + v].astype(jnp.int32) for v in range(2)]
                rows = [pair[r + row : r + row + 4] for pair in pairs for r in (0, 8)]
                out[base + planes + 1 + u // 2] = jnp.concatenate(rows).astype(jnp.int16)
            base += block_size(planes, 4)

    @pl.when(parity == 0)
    def _():
        cut(even, 4)
        cut(odd, 0)

    @pl.when(parity == 1)
    def _():
        cut(odd, 4)
        cut(even, 0)


def first_leap(place, start, count, window, old, old_start, coefs, inject, scratch, mats, store):
    leap(
        window, place.first_at + start, 8, coefs.shape[2], count, scratch, mats,
        lambda m, i, r, number: coefs[m, start + i, pl.ds(r, number), :],
        lambda f, i: old[f, old_start + start + i],
        lambda i: inject[0, start + i],
        store,
    )


def second_leap(
    place, start, count, source, source_start, tile, coefs, inject, scratch, mats, store
):
    rows = tile.shape[2]
    at = place.tile_at + start
    leap(
        source, source_start, 8, rows, count, scratch, mats,
        lambda m, i, r, number: coefs[m, at + i, pl.ds(4 + r, number), :],
        lambda f, i: tile[f, start + i],
        lambda i: inject[1, at + i, pl.ds(4, rows), :],
        store,
    )


def fill(place, tile, old, beside, even, odd, window, old_wide):
    size_x = tile.shape[1]
    opening = old_wide is not None
    for f in range(2):
        window[f, pl.ds(0, 4)] = jnp.zeros((4, 32, 128), F32)
        window[f, pl.ds(place.wide + 4, 4)] = jnp.zeros((4, 32, 128), F32)
        window[f, pl.ds(place.own_at + 4, size_x), pl.ds(12, 8), :] = tile[f]
        if opening:
            old_wide[f, pl.ds(place.own_at, size_x), pl.ds(4, 8), :] = old[f]

    def lay(block, base, planes, at, row):
        there = {-8: place.has_below, 0: 1.0, 8: place.has_above}[row]
        factor = factor_of(block[base + planes], 0) * there

        def group(g):
            def put(f, p, rows):
                window[f, at + g * GROUP + p + 4, pl.ds(row + 12, 8), :] = rows

            decode(block, base + g * TILES, factor, put)

        loop(planes // GROUP, group, 2)
        if not opening:
            return
        factor = factor_of(block[base + planes], 1) * there

        def old_group(g):
            def put(f, p, rows):
                first = 0 if row < 0 else row + 4
                old_wide[f, at + g * GROUP + p, pl.ds(first, rows.shape[0]), :] = rows

            start = base + planes + 1
            if row == 0:
                decode(block, start + g * TILES, factor, put)
            else:
                near = factor[4:] if row < 0 else factor[:4]
                decode_nearest(block, start + g * (TILES // 2), near, put)

        loop(planes // GROUP, old_group, 2)

    for k in range(place.sides):
        lay(beside[k], 0, GROUP, place.beside_at[k], 0)

    def lay_y(below, above):
        kept = 4 if opening else 0
        for block, row in ((below, -8), (above, 8)):
            lay(block, 0, size_x, place.own_at, row)
            for k in range(place.sides):
                base = block_size(size_x, kept) + k * block_size(GROUP, kept)
                lay(block, base, GROUP, place.beside_at[k], row)

    pl.when(place.parity == 0)(lambda: lay_y(odd, even))
    pl.when(place.parity == 1)(lambda: lay_y(even, odd))


def lead_kernel(opening, columns, tile, old, coefs, inject, mat_first, mat_second, *refs):
    place = Place(tile.shape[1], columns)
    refs = list(refs)

    def take(number):
        taken = refs[:number]
        del refs[:number]
        return taken

    sides = place.sides
    beside = take(sides)
    even, odd, window = take(3)
    old_wide = take(1)[0] if opening else None
    around_out, edges_out, codes_out = take(sides), take(sides), take(sides)
    middle = take(1)[0]
    scratch, mats = refs, (mat_first, mat_second)
    fill(place, tile, old, beside, even, odd, window, old_wide)
    for k in range(sides):
        def store_around(i, new_p, new_q):
            for f, new in enumerate((new_p, new_q)):
                around_out[k][f, i] = new
                middle[f, i, pl.ds(4, new.shape[0]), :] = new

        def store_edge(i, new_p, new_q):
            edges_out[k][0, i] = new_p
            edges_out[k][1, i] = new_q

        first_leap(
            place, place.around_at[k], AROUND, window, old_wide if opening else old,
            place.first_at if opening else 0, coefs, inject, scratch, mats, store_around,
        )
        second_leap(
            place, place.edge_at[k], GROUP, middle, 0, tile, coefs, inject, scratch, mats,
            store_edge,
        )
        encode(lambda f, p: edges_out[k][f, p], GROUP, codes_out[k])


def rest_kernel(opening, columns, tile, old, window, coefs, inject, mat_first, mat_second, *refs):
    size_x, size_y = tile.shape[1], tile.shape[2]
    place = Place(size_x, columns)
    sides, count = place.sides, place.count
    around, edges = refs[:sides], refs[sides : 2 * sides]
    tile_out, payload, old_out, middle, *scratch = refs[2 * sides :]
    mats = (mat_first, mat_second)
    for f in range(2):
        middle[f, pl.ds(0, 4)] = jnp.zeros((4, 24, 128), F32)
        middle[f, pl.ds(count + 4, 4)] = jnp.zeros((4, 24, 128), F32)
        for k in range(sides):
            at = place.around_at[k]
            middle[f, pl.ds(at + 4, AROUND), pl.ds(4, size_y + 8), :] = around[k][f]
            old_out[f, pl.ds(at, AROUND)] = around[k][f]
            tile_out[f, pl.ds(place.edge_at[k], GROUP)] = edges[k][f]

    def store_first(i, new_p, new_q):
        for f, new in enumerate((new_p, new_q)):
            old_out[f, place.first_rest_at + i] = new
            middle[f, place.first_rest_at + i + 4, pl.ds(4, size_y + 8), :] = new

    def store_second(i, new_p, new_q):
        tile_out[0, place.rest_at + i] = new_p
        tile_out[1, place.rest_at + i] = new_q

    first_leap(
        place, place.first_rest_at, count - AROUND * sides, window, old,
        place.first_at if opening else 0, coefs, inject, scratch, mats, store_first,
    )
    second_leap(
        place, place.rest_at, place.rest, middle, place.tile_at + place.rest_at, tile, coefs,
        inject, scratch, mats, store_second,
    )
    encode(lambda f, p: tile_out[f, p], size_x, payload)


def last_kernel(columns, tile, old, coefs, inject, mat_first, mat_second, *refs):
    size_x, size_y = tile.shape[1], tile.shape[2]
    place = Place(size_x, columns)
    sides, count = place.sides, place.count
    even, odd, kept, sent, middle, tile_out, window, *scratch = refs[sides:]
    mats = (mat_first, mat_second)
    fill(place, tile, old, refs[:sides], even, odd, window, None)
    for f in range(2):
        middle[f, pl.ds(0, 4)] = jnp.zeros((4, 24, 128), F32)
        middle[f, pl.ds(count + 4, 4)] = jnp.zeros((4, 24, 128), F32)

    def store_first(i, new_p, new_q):
        for f, new in enumerate((new_p, new_q)):
            middle[f, i + 4, pl.ds(4, size_y + 8), :] = new

    def store_second(i, new_p, new_q):
        tile_out[0, i] = new_p
        tile_out[1, i] = new_q

    first_leap(place, 0, count, window, old, 0, coefs, inject, scratch, mats, store_first)
    second_leap(
        place, 0, size_x, middle, place.tile_at, tile, coefs, inject, scratch, mats, store_second
    )
    half = size_x // 2
    for mine in range(2):
        @pl.when(place.core == mine)
        def _():
            for out, start in ((kept, mine * half), (sent, (1 - mine) * half)):
                planes = pl.ds(start, half)
                inner = pl.ds(place.tile_at + 4 + start, half)
                out[0] = middle[0, inner, pl.ds(8, size_y), :]
                out[1] = tile_out[0, planes]
                out[2] = tile_out[1, planes]


def sine_cosine(angle):
    square = angle * angle
    sine = 1.0 / 6227020800.0
    for factor in (-1.0 / 39916800.0, 1.0 / 362880.0, -1.0 / 5040.0, 1.0 / 120.0, -1.0 / 6.0):
        sine = sine * square + factor
    sine = angle + angle * square * sine
    cosine = 1.0 / 479001600.0
    for factor in (-1.0 / 3628800.0, 1.0 / 40320.0, -1.0 / 720.0, 1.0 / 24.0, -0.5):
        cosine = cosine * square + factor
    return sine, 1.0 + square * cosine


def open_kernel(
    velocity, epsilon, delta, tilt, azimuth, source, receiver, *refs
):
    models = (velocity, epsilon, delta, tilt, azimuth)
    parity = lax.rem(lax.axis_index("gy"), 2)
    core = lax.rem(lax.axis_index("gx"), 2)
    small, (even, odd, own, kept, given), brought, arrived = (
        refs[:3], refs[3:8], refs[8:11], refs[11]
    )
    copies = [pltpu.make_async_copy(models[m], own.at[m], arrived.at[m]) for m in range(5)]
    others = [
        pltpu.make_async_copy(small[m], brought[m], arrived.at[7 + m]) for m in range(3)
    ]

    def states(mine):
        stay, leave = (source, receiver) if mine == 0 else (receiver, source)
        return (
            pltpu.make_async_copy(stay, kept, arrived.at[5]),
            pltpu.make_async_copy(leave, given, arrived.at[6]),
        )

    for copy in copies + others:
        copy.start()
    for mine in range(2):
        @pl.when(core == mine)
        def _():
            for copy in states(mine):
                copy.start()

    for copy in copies:
        copy.wait()

    def pack(out, row):
        for m in range(5):
            for u in range(0, own.shape[1], 2):
                pairs = [own[m, u + k].astype(F32) for k in range(2)]
                values = [pair[v + row : v + row + 4] for pair in pairs for v in (0, 8)]
                out[m, u // 2] = jnp.concatenate(values).astype(BF16)

    @pl.when(parity == 0)
    def _():
        pack(even, 4)
        pack(odd, 0)

    @pl.when(parity == 1)
    def _():
        pack(odd, 4)
        pack(even, 0)

    for mine in range(2):
        @pl.when(core == mine)
        def _():
            for copy in states(mine):
                copy.wait()
    for copy in others:
        copy.wait()


def join_kernel(own, even, odd, out):
    at_y = lax.axis_index("gy")
    parity = lax.rem(at_y, 2)
    has_below = jnp.where(at_y > 0, 1.0, 0.0)
    has_above = jnp.where(at_y < lax.axis_size("gy") - 1, 1.0, 0.0)

    def fill(below, above):
        for m in range(5):
            for u in range(own.shape[1]):
                low = below[m, u // 2].astype(F32) * has_below
                high = above[m, u // 2].astype(F32) * has_above
                pair = own[m, u].astype(F32)
                for v in range(2):
                    k = 2 * (u % 2) + v
                    rows = [low[4 * k : 4 * k + 4], pair[8 * v : 8 * v + 8], high[4 * k : 4 * k + 4]]
                    out[m, 2 * u + v] = jnp.concatenate(rows).astype(BF16)

    pl.when(parity == 0)(lambda: fill(odd, even))
    pl.when(parity == 1)(lambda: fill(even, odd))


def setup_kernel(columns, size_x, total_x, aperture, *refs):
    models, coefs, blocks = refs[:-2], refs[-2], refs[-1]
    place = Place(2 * size_x, columns)
    if len(models) > 1:
        for k, column in enumerate((place.column, 1 - place.column)):
            for j, core in enumerate((place.core, 1 - place.core)):
                blocks[:, pl.ds((2 * column + core) * size_x, size_x)] = models[2 * k + j][...]
        source = blocks
    else:
        source = models[0]

    def medium(i):
        x = place.start_x + i
        block = jnp.clip(x // size_x, 0, total_x // size_x - 1)
        inside = jnp.logical_and(x >= 0, x < total_x)
        at = aperture[block] * size_x + lax.rem(x + size_x, size_x)
        speed, stretch, bending, tilt, azimuth = [source[m, at].astype(F32) for m in range(5)]
        speed = jnp.where(inside, speed, 0.0)
        sin_t, cos_t = sine_cosine(tilt)
        sin_half, cos_half = sine_cosine(0.5 * azimuth)
        normal_x = sin_t * (1.0 - 2.0 * sin_half * sin_half)
        normal_y = sin_t * (2.0 * sin_half * cos_half)
        coefs[0, i] = speed
        coefs[1, i] = speed * (1.0 + 2.0 * stretch)
        coefs[2, i] = speed * jnp.sqrt(1.0 + 2.0 * bending)
        coefs[3, i] = S1 * (normal_x * normal_x)
        coefs[4, i] = S1 * (normal_y * normal_y)
        coefs[5, i] = SECOND_UNIT * (cos_t * cos_t)
        coefs[6, i] = (2.0 * G1 * G1) * (normal_x * normal_y)
        coefs[7, i] = (2.0 * G1 * FIRST_UNIT) * (normal_y * cos_t)
        coefs[8, i] = (2.0 * G1 * FIRST_UNIT) * (normal_x * cos_t)

    loop(place.count, medium, 6)


def injection_kernel(
    columns, size_x, size_y, total_y, source_cell, wavelet, cells, traces, out, hits
):
    place = Place(size_x, columns)
    count, rows = hits.shape[:2]
    number = cells.shape[1]
    row = lax.broadcasted_iota(jnp.int32, (rows, number), 0)
    lane = lax.broadcasted_iota(jnp.int32, (1, number), 1)
    is_source = place.core == 0
    lonely = jnp.where(lane == 0, source_cell[0], -1)
    aims = jnp.where(is_source, lonely, cells[...])
    y = place.at_y * size_y - 4 + row
    valid = jnp.logical_and(y >= 0, y < total_y)

    def mark(i):
        code = jnp.where(valid, (place.start_x + i) * total_y + y, -2)
        hits[i] = jnp.where(code == aims, 1.0, 0.0).astype(BF16)

    loop(count, mark, 2)
    step = lax.broadcasted_iota(jnp.int32, (NT, number), 0)
    amounts = jnp.zeros((NT, number), F32)
    for k in range(NT):
        amounts = jnp.where(step == k, wavelet[:, k : k + 1], amounts)
    backward = jnp.concatenate([traces[k : k + 1] for k in reversed(range(NT))])
    rest = jnp.where(is_source, amounts, backward)
    total = None
    for _ in range(3):
        piece = rest.astype(BF16)
        rest = rest - piece.astype(F32)
        term = lax.dot_general(
            hits[...].reshape(count * rows, number), piece, (((1,), (1,)), ((), ())),
            preferred_element_type=F32,
        )
        total = term if total is None else total + term
    out[...] = total.reshape(count, rows, NT)


def spread_kernel(moment, lanes, out):
    core = lax.rem(lax.axis_index("gx"), 2)
    level = jnp.where(core == 0, SRC_DEPTH, REC_DEPTH)
    mask = (lax.broadcasted_iota(jnp.int32, (lanes.shape[1], 128), 1) == level).astype(F32)

    def expand(i):
        values = lanes[i]
        for k in range(2):
            out[k, i] = values[:, moment + k : moment + k + 1] * mask

    loop(lanes.shape[0], expand, 6)


def sort_kernel(columns, *refs):
    levels, (kept, sent) = refs[: NT - 1], refs[NT - 1 :]
    half, size_y = kept.shape[1:3]
    place = Place(2 * half, columns)

    def level_at(step, start):
        where = levels[step]
        if step % 2 == 0:
            return where[0, pl.ds(start, half)]
        return where[0, pl.ds(place.tile_at + start, half), pl.ds(4, size_y), :]

    for mine in range(2):
        @pl.when(place.core == mine)
        def _():
            for step in range(NT - 1):
                t = step if mine == 0 else NT - step
                if t > 0:
                    kept[t - 1] = level_at(step, mine * half)
                    sent[t - 1] = level_at(step, (1 - mine) * half)


def close_kernel(kept, got, last_kept, last_got, image, field):
    core = lax.rem(lax.axis_index("gx"), 2)
    total = kept[1] * got[1]
    for t in range(2, NT - 2):
        total = total + kept[t] * got[t]

    @pl.when(core == 0)
    def _():
        image[...] = (
            total + kept[0] * last_got[0] + last_kept[0] * got[NT - 2] + last_kept[1] * got[NT - 1]
        ) * (1.0 / NT)
        field[...] = last_got[pl.ds(1, 2)]

    @pl.when(core == 1)
    def _():
        image[...] = (
            total + last_kept[0] * got[0] + kept[NT - 2] * last_got[0] + kept[NT - 1] * last_got[1]
        ) * (1.0 / NT)
        field[...] = last_kept[pl.ds(1, 2)]


def per_device(
    velocity,
    epsilon,
    delta,
    tilt,
    azimuth,
    aperture,
    source_cell,
    wavelet,
    receiver_cell,
    traces,
    source_state,
    receiver_state,
):
    block_x, size_y, _ = velocity.shape
    devices_x, devices_y = lax.axis_size("gx"), lax.axis_size("gy")
    columns = devices_x // 2
    total_x, total_y = block_x * devices_x, size_y * devices_y
    size_x, rows = 2 * block_x, size_y + 8
    is_source = lax.axis_index("gx") % 2 == 0
    place = Place(size_x, columns)
    sides, count = place.sides, place.count
    mats = depth_matrices(128)
    chip_pairs = [even_pairs(columns), odd_pairs(columns)][:sides]
    row_pairs = [even_pairs(devices_y), odd_pairs(devices_y)]
    trade = both_ways([(2 * c, 2 * c + 1) for c in range(columns)])

    def over_gy(values, pairs):
        return lax.ppermute(values, "gy", everyone(pairs, devices_y))

    def over_gx(values, pairs):
        return lax.ppermute(values, "gx", both_ways(chip_swap(pairs)))

    def beside_of(edges):
        return [over_gx(edge, pairs) for edge, pairs in zip(edges, chip_pairs)]

    def near_of(even, odd):
        odd = over_gy(odd, row_pairs[1])
        return over_gy(even, row_pairs[0]), odd

    def codes(planes, old_rows=0):
        return ((block_size(planes, old_rows), 16, 128), jnp.int16)

    models = [
        values.reshape(block_x // 2, 16, 128) for values in (velocity, epsilon, delta, tilt, azimuth)
    ]
    small = (wavelet[None, :], receiver_cell[None, :], traces)
    rim = ((5, block_x // 4, 16, 128), BF16)
    states = (source_state, receiver_state)
    state = (source_state.shape, F32)
    *rims, own, kept, given, series, cells, data = pl.pallas_call(
        open_kernel,
        out_shape=tuple(
            jax.ShapeDtypeStruct(*out)
            for out in (rim, rim, ((5, block_x // 2, 16, 128), BF16), state, state)
            + tuple((x.shape, x.dtype) for x in small)
        ),
        in_specs=[HBM] * 10,
        out_specs=(VMEM,) * 8,
        scratch_shapes=[pltpu.SemaphoreType.DMA((10,))],
        compiler_params=pltpu.CompilerParams(vmem_limit_bytes=8 * 2**20),
        name="open",
    )(*[pltpu.with_memory_space_constraint(x, pltpu.HBM) for x in (*models, *states, *small)])
    rims = [over_gy(values, pairs) for values, pairs in zip(rims, row_pairs)]

    got = lax.ppermute(given, "gx", trade)
    field = ((2, size_x, size_y, 128), F32)
    tile, old, payload, *edges = call(
        functools.partial(first_kernel, columns),
        (field, field, codes(size_x, 8)) + (codes(GROUP, 8),) * sides,
        (), 16, "first", (kept, got),
    )
    number = receiver_cell.shape[0]
    cells, _ = lax.optimization_barrier((cells, edges[0]))
    (amounts,) = call(
        functools.partial(injection_kernel, columns, size_x, size_y, total_y),
        (((count, rows, NT), F32),), (((count, rows, number), BF16),),
        16, "injection", (source_cell, series, cells, data), scalars=1,
    )
    beside = beside_of(edges)
    payload, _ = lax.optimization_barrier((payload, amounts))
    total = block_size(size_x, 4) + sides * block_size(GROUP, 4)
    wide = call(
        cut_kernel, (((total, 16, 128), jnp.int16),) * 2, (), 8, "cut", (payload, *beside)
    )
    near = near_of(*wide[::-1])

    def spread(moment, after):
        lanes, _ = lax.optimization_barrier((amounts, after[0]))
        (out,) = call(
            functools.partial(spread_kernel, moment), (((2, count, rows, 128), F32),), (), 8,
            "spread", (lanes,),
        )
        return out

    inject = spread(0, wide)

    rims = lax.optimization_barrier((*rims, edges[0]))[:2]
    (model,) = call(
        join_kernel, (((5, block_x, rows, 128), BF16),), (), 8, "join", (own, *rims), work=1000
    )
    if columns == 2:
        later, _ = lax.optimization_barrier((model, wide[0]))
        across = over_gx(later, chip_pairs[0])
        early, _ = lax.optimization_barrier((model, inject))
        other = lax.ppermute(early, "gx", trade)
        gathered = [model, other, across, lax.ppermute(across, "gx", trade)]
        held = (5, total_x, rows, 128)
    else:
        gathered, held = [lax.all_gather(model, "gx", axis=1, tiled=True)], (16, 128)
    (coefs,) = call(
        functools.partial(setup_kernel, columns, block_x, total_x),
        (((9, count, rows, 128), F32),), ((held, BF16),), 24, "setup", (aperture, *gathered),
        scalars=1, work=0,
    )

    window = ((2, place.wide + 8, 32, 128), F32)
    middle = ((2, count + 8, 24, 128), F32)
    lines = ((2, count, rows, 128), F32)
    levels = [tile]
    for moment in range(0, NT - 2, 2):
        opening = moment == 0
        inject = inject if opening else spread(moment, wide)
        old_wide = (((2, place.wide, rows, 128), F32),) * opening
        around = (((2, AROUND, rows, 128), F32),) * sides
        edge = (((2, GROUP, size_y, 128), F32),) * sides
        fields, *outs = call(
            functools.partial(lead_kernel, opening, columns),
            (window,) + old_wide + around + edge + (codes(GROUP),) * sides,
            [((2, AROUND, 24, 128), F32)] + leap_scratch(AROUND), 24, "lead",
            (tile, old, coefs, inject, *mats, *beside, *near), work=2 * 10**6,
        )
        if opening:
            old, *outs = outs
        beside = beside_of(outs[2 * sides :])
        tile, payload, old = call(
            functools.partial(rest_kernel, opening, columns),
            (field, codes(size_x), lines), [middle] + leap_scratch(place.rest), 24, "rest",
            (tile, old, fields, coefs, inject, *mats, *outs[: 2 * sides]), work=4 * 10**6,
        )
        wide = (jnp.concatenate([payload, *beside]),) * 2
        near = near_of(*wide)
        levels += [old, tile]
    shape = (block_x, size_y, 128)
    inject = spread(NT - 2, wide)
    share = ((NT,) + shape, F32)
    kept, sent = call(
        functools.partial(sort_kernel, columns), (share, share), (), 8, "sort",
        lax.optimization_barrier((*levels, *near, inject))[: NT - 1],
    )
    got = lax.ppermute(sent, "gx", trade)
    share = ((3,) + shape, F32)
    last_kept, last_sent = call(
        functools.partial(last_kernel, columns),
        (share, share), [middle, field, window] + leap_scratch(count), 24, "last",
        (tile, old, coefs, inject, *mats, *beside, *near),
    )
    last_got = lax.ppermute(last_sent, "gx", trade)
    return call(
        close_kernel, ((shape, F32), ((2,) + shape, F32)), (), 8, "close",
        (kept, got, last_kept, last_got),
    )


def solution(mesh):
    in_specs = (
        P("gx", "gy", None),
        P("gx", "gy", None),
        P("gx", "gy", None),
        P("gx", "gy", None),
        P("gx", "gy", None),
        P("shot"),
        P("shot"),
        P("shot"),
        P("shot"),
        P(None, "shot"),
        P(None, ("shot", "gx"), "gy", None),
        P(None, ("shot", "gx"), "gy", None),
    )
    out_specs = (P(("shot", "gx"), "gy", None), P(None, ("shot", "gx"), "gy", None))
    return jax.shard_map(
        per_device, mesh=mesh, in_specs=in_specs, out_specs=out_specs, check_vma=False
    )
```

```python
import functools

import jax
import jax.numpy as jnp
from jax import lax
from jax.experimental import pallas as pl
from jax.experimental.pallas import tpu as pltpu
from jax.sharding import PartitionSpec as P

NT = 8
SRC_DEPTH = 10
REC_DEPTH = 6
F32 = jnp.float32
BF16 = jnp.bfloat16

second_taps = (-205.0 / 72.0, 8.0 / 5.0, -1.0 / 5.0, 8.0 / 315.0, -1.0 / 560.0)
first_taps = (4.0 / 5.0, -1.0 / 5.0, 4.0 / 105.0, -1.0 / 280.0)
CENTRE = second_taps[0]
S1 = second_taps[1]
G1 = first_taps[0]
second_ratio = tuple(tap / S1 for tap in second_taps[2:])
first_ratio = tuple(tap / G1 for tap in first_taps[1:])
second_whole = (8064.0, -1008.0, 128.0, -9.0)
first_whole = (672.0, -168.0, 32.0, -3.0)
SECOND_UNIT = 1.0 / 5040.0
FIRST_UNIT = 1.0 / 840.0
VMEM = pl.BlockSpec(memory_space=pltpu.VMEM)
SMEM = pl.BlockSpec(memory_space=pltpu.SMEM)
HBM = pl.BlockSpec(memory_space=pltpu.HBM)


def even_pairs(count):
    return [(i, i + 1) for i in range(0, count - 1, 2)]


def odd_pairs(count):
    return [(i, i + 1) for i in range(1, count - 1, 2)]


def both_ways(pairs):
    return [pair for a, b in pairs for pair in ((a, b), (b, a))]


def chip_swap(pairs):
    return [(2 * a + c, 2 * b + c) for a, b in pairs for c in range(2)]


class Place:
    def __init__(self, size_x, columns):
        at_x = lax.axis_index("gx")
        self.core, self.column = lax.rem(at_x, 2), lax.div(at_x, 2)
        self.at_y = lax.axis_index("gy")
        self.parity = lax.rem(self.at_y, 2)
        self.has_below = jnp.where(self.at_y > 0, 1.0, 0.0)
        self.has_above = jnp.where(self.at_y < lax.axis_size("gy") - 1, 1.0, 0.0)
        if columns == 2:
            side = self.column
            self.count = size_x + 4
            self.first_at = self.tile_at = 4 * side
            self.start_x = side * (size_x - 4)
            self.beside_at = [size_x * (1 - side)]
            self.edge_at = [(size_x - GROUP) * (1 - side)]
            self.rest_at, self.rest = GROUP * side, size_x - GROUP
            self.first_rest_at = AROUND * side
        else:
            side = lax.rem(self.column, 2)
            self.count = size_x + 8
            self.first_at = self.tile_at = 4
            self.start_x = self.column * size_x - 4
            self.beside_at = [(size_x + GROUP) * (1 - side), (size_x + GROUP) * side]
            self.edge_at = [(size_x - GROUP) * (1 - side), (size_x - GROUP) * side]
            self.rest_at, self.rest = GROUP, size_x - 2 * GROUP
            self.first_rest_at = AROUND
        self.sides = len(self.beside_at)
        self.around_at = [self.tile_at + at - 4 for at in self.edge_at]
        self.own_at = self.first_at + self.tile_at
        self.wide = size_x + GROUP * self.sides


def call(kernel, outs, scratch, mebibytes, name, args, scalars=0, work=10**6):
    outs = tuple(jax.ShapeDtypeStruct(shape, dtype) for shape, dtype in outs)
    return pl.pallas_call(
        kernel,
        out_shape=outs,
        in_specs=[SMEM] * scalars + [VMEM] * (len(args) - scalars),
        out_specs=(VMEM,) * len(outs),
        scratch_shapes=[pltpu.VMEM(shape, dtype) for shape, dtype in scratch],
        compiler_params=pltpu.CompilerParams(vmem_limit_bytes=mebibytes * 2**20),
        cost_estimate=pl.CostEstimate(flops=work, bytes_accessed=work, transcendentals=0),
        name=name,
    )(*args)


def loop(trips, body, wanted):
    unroll = max(u for u in range(1, wanted + 1) if trips % u == 0)

    def step(i, carry):
        body(i)
        return carry

    lax.fori_loop(0, trips, step, 0, unroll=unroll)


def depth_matrices(size):
    rows = jnp.arange(size)[:, None]
    cols = jnp.arange(size)[None, :]
    first = jnp.zeros((size, size), F32)
    second = jnp.zeros((size, size), F32)
    for k in range(1, 5):
        up = (rows == cols + k).astype(F32)
        down = (rows == cols - k).astype(F32)
        first = first + first_whole[k - 1] * (up - down)
        second = second + second_whole[k - 1] * (up + down)
    return (
        jnp.concatenate([first, first]).astype(BF16),
        jnp.concatenate([second, second]).astype(BF16),
    )


def sums_and_slopes(shifted):
    up, down = shifted(1), shifted(-1)
    curve, slope = up + down, up - down
    for k in range(2, 5):
        up, down = shifted(k), shifted(-k)
        curve = curve + second_ratio[k - 2] * (up + down)
        slope = slope + first_ratio[k - 2] * (up - down)
    return curve, slope


def slope_only(shifted):
    slope = shifted(1) - shifted(-1)
    for k in range(2, 5):
        slope = slope + first_ratio[k - 2] * (shifted(k) - shifted(-k))
    return slope


def split(values):
    high = values.astype(BF16)
    low = (values - high.astype(F32)).astype(BF16)
    return high, low


TOP = 32000.0
GROUP = 8
AROUND = GROUP + 8
TILES = GROUP


def block_size(planes, old_rows=0):
    return planes + 1 + planes * old_rows // 8


def scale_of(value_at, planes):
    def grow(i, size):
        for f in range(2):
            size = jnp.maximum(size, jnp.abs(value_at(f, i)))
        return size

    size = lax.fori_loop(0, planes, grow, jnp.full((8, 128), 1e-30, F32), unroll=8)
    code = jnp.ceil(jnp.log2(size) * 256.0)
    return code, TOP * jnp.exp2(code * (-1.0 / 256.0))


def as_code(pieces):
    return jnp.concatenate(pieces).astype(jnp.int32).astype(jnp.int16)


def encode(value_at, planes, out, old_at=None):
    code, factor = scale_of(value_at, planes)
    old_code, old_factor = scale_of(old_at, planes) if old_at else (code, None)

    def put(source, base, by):
        def group(g):
            for f in range(2):
                for q in range(4):
                    pair = [source(f, g * GROUP + 2 * q + v) for v in range(2)]
                    whole = [jnp.floor(value * by + 0.5) for value in pair]
                    out[base + g * TILES + 4 * f + q] = as_code(whole)

        loop(planes // GROUP, group, 1)

    put(value_at, 0, factor)
    out[planes] = as_code([code, old_code])
    if old_at:
        put(old_at, planes + 1, old_factor)


def factor_of(scales, half):
    code = scales.astype(jnp.int32).astype(F32)[8 * half : 8 * half + 8]
    return jnp.exp2(code * (1.0 / 256.0)) * (1.0 / TOP)


def decode(block, base, factor, put):
    for f in range(2):
        for q in range(4):
            both = block[base + 4 * f + q].astype(jnp.int32).astype(F32)
            put(f, 2 * q, both[:8] * factor)
            put(f, 2 * q + 1, both[8:] * factor)


def decode_nearest(block, base, factor, put):
    by = jnp.concatenate([factor] * 4)
    for f in range(2):
        for q in range(2):
            rows = block[base + 2 * f + q].astype(jnp.int32).astype(F32) * by
            for v in range(4):
                put(f, 4 * q + v, rows[4 * v : 4 * v + 4])


def leap(src, x0, row0, rows, count, scratch, mats, coef, old_at, inject_at, store):
    slope_y, curve_y, part, halves, product = scratch
    mat_first, mat_second = mats
    planes = 16 // rows
    group = 4

    def field(f, p, r=0, number=rows):
        return src[f, x0 + p, pl.ds(row0 + r, number), :]

    def joined(values):
        return jnp.concatenate(values) if len(values) > 1 else values[0]

    def put_halves(kind, f, unit, values):
        high, low = split(values)
        halves[kind, f, unit, :, :128] = high
        halves[kind, f, unit, :, 128:] = low

    def along_y(u):
        for f in range(2):
            here, slopes = [], []
            for v in range(planes):
                p = u * planes + v
                curve, slope = sums_and_slopes(lambda k: field(f, p, k))
                slope_y[f, p, :rows] = slope
                curve_y[f, p, :rows] = curve
                slopes.append(slope)
                here.append(field(f, p))
            put_halves(0, f, u, joined(here))
            put_halves(1, f, u, joined(slopes))

    loop((count + 8) // planes, along_y, 12)

    def along_x(q):
        base = q * group
        for f in range(2):
            slopes = [[] for g in range(group)]
            for r in range(0, rows, 8):
                line = [field(f, base + k, r, 8) for k in range(group + 8)]
                slant = [slope_y[f, base + k, pl.ds(r, 8), :] for k in range(group + 8)]
                for g in range(group):
                    i = base + g
                    xx, slope = sums_and_slopes(lambda k: line[g + 4 + k])
                    xy = slope_only(lambda k: slant[g + 4 + k])
                    yy = curve_y[f, i + 4, pl.ds(r, 8), :]
                    wx, wy, wxy = [coef(m, i, r, 8) for m in (3, 4, 6)]
                    if f == 0:
                        total = (2.0 * CENTRE) * line[g + 4] + (S1 - wx) * xx
                        total = total + (S1 - wy) * yy - wxy * xy
                    else:
                        total = CENTRE * line[g + 4] + wx * xx
                        total = total + wy * yy + wxy * xy
                    part[f, i, pl.ds(r, 8), :] = total
                    slopes[g].append(slope)
            pieces = [piece for rest in slopes for piece in rest]
            for k in range(0, len(pieces), 2):
                put_halves(2, f, q * (len(pieces) // 2) + k // 2, joined(pieces[k : k + 2]))

    loop(count // group, along_x, 5)

    units = count // planes
    for kind, mat, at in ((0, mat_second, 4 // planes), (1, mat_first, 4 // planes), (2, mat_first, 0)):
        for f in range(2):
            both = halves[kind, f, pl.ds(at, units)].reshape(units * 16, 256)
            out = jnp.dot(both, mat[...], preferred_element_type=F32)
            product[kind, f, pl.ds(0, units)] = out.reshape(units, 16, 128)

    def combine(u):
        where = [u * planes + v for v in range(planes)]
        speed, speed_h, speed_v, wz, wyz, wxz = [
            joined([coef(m, i, 0, rows) for i in where]) for m in (0, 1, 2, 5, 7, 8)
        ]
        zz, yz, xz = [[product[kind, f, u] for f in range(2)] for kind in range(3)]
        parts = [joined([part[f, i, :rows] for i in where]) for f in range(2)]
        here = [joined([field(f, i + 4) for i in where]) for f in range(2)]
        old = [joined([old_at(f, i) for i in where]) for f in range(2)]
        add = joined([inject_at(i) for i in where])
        flat = parts[0] + (SECOND_UNIT - wz) * zz[0] - (wyz * yz[0] + wxz * xz[0])
        tilted = parts[1] + wz * zz[1] + (wyz * yz[1] + wxz * xz[1])
        new_p = (2.0 * here[0] - old[0] + add) + (speed_h * flat + speed_v * tilted)
        new_q = (2.0 * here[1] - old[1] + add) + (speed_v * flat + speed * tilted)
        for v, i in enumerate(where):
            cut = slice(v * rows, v * rows + rows)
            store(i, new_p[cut], new_q[cut])

    loop(units, combine, 18)


def leap_scratch(count):
    lines = (2, count + 8, 16, 128)
    return [
        (lines, F32),
        (lines, F32),
        ((2, count, 16, 128), F32),
        ((3, 2, count + 8, 16, 256), BF16),
        ((3, 2, count, 16, 128), F32),
    ]


def first_kernel(columns, kept, got, tile, old, payload, *edges):
    size = kept.shape[1]
    place = Place(2 * size, columns)
    for source, at in ((kept, place.core * size), (got, (1 - place.core) * size)):
        for f in range(2):
            tile[f, pl.ds(at, size)] = source[2 * f]
            old[f, pl.ds(at, size)] = source[2 * f + 1]

    encode(lambda f, p: tile[f, p], 2 * size, payload, lambda f, p: old[f, p])
    for k, edge in enumerate(edges):
        group = lax.div(place.edge_at[k], GROUP) * TILES
        for base in (0, 2 * size + 1):
            edge[pl.ds(base and GROUP + 1, TILES)] = payload[pl.ds(base + group, TILES)]
        edge[GROUP] = payload[2 * size]


def cut_kernel(payload, *refs):
    beside, (odd, even) = refs[:-2], refs[-2:]
    parity = lax.rem(lax.axis_index("gy"), 2)

    def cut(out, row):
        base = 0
        for block in (payload, *beside):
            planes = block.shape[0] // 2
            out[pl.ds(base, planes + 1)] = block[: planes + 1]
            for u in range(0, planes, 2):
                pairs = [block[planes + 1 + u + v].astype(jnp.int32) for v in range(2)]
                rows = [pair[r + row : r + row + 4] for pair in pairs for r in (0, 8)]
                out[base + planes + 1 + u // 2] = jnp.concatenate(rows).astype(jnp.int16)
            base += block_size(planes, 4)

    @pl.when(parity == 0)
    def _():
        cut(even, 4)
        cut(odd, 0)

    @pl.when(parity == 1)
    def _():
        cut(odd, 4)
        cut(even, 0)


def first_leap(place, start, count, window, old, old_start, coefs, inject, scratch, mats, store):
    leap(
        window, place.first_at + start, 8, coefs.shape[2], count, scratch, mats,
        lambda m, i, r, number: coefs[m, start + i, pl.ds(r, number), :],
        lambda f, i: old[f, old_start + start + i],
        lambda i: inject[0, start + i],
        store,
    )


def second_leap(
    place, start, count, source, source_start, tile, coefs, inject, scratch, mats, store
):
    rows = tile.shape[2]
    at = place.tile_at + start
    leap(
        source, source_start, 8, rows, count, scratch, mats,
        lambda m, i, r, number: coefs[m, at + i, pl.ds(4 + r, number), :],
        lambda f, i: tile[f, start + i],
        lambda i: inject[1, at + i, pl.ds(4, rows), :],
        store,
    )


def fill(place, tile, old, beside, even, odd, window, old_wide):
    size_x = tile.shape[1]
    opening = old_wide is not None
    for f in range(2):
        window[f, pl.ds(0, 4)] = jnp.zeros((4, 32, 128), F32)
        window[f, pl.ds(place.wide + 4, 4)] = jnp.zeros((4, 32, 128), F32)
        window[f, pl.ds(place.own_at + 4, size_x), pl.ds(12, 8), :] = tile[f]
        if opening:
            old_wide[f, pl.ds(place.own_at, size_x), pl.ds(4, 8), :] = old[f]

    def lay(block, base, planes, at, row):
        there = {-8: place.has_below, 0: 1.0, 8: place.has_above}[row]
        factor = factor_of(block[base + planes], 0) * there

        def group(g):
            def put(f, p, rows):
                window[f, at + g * GROUP + p + 4, pl.ds(row + 12, 8), :] = rows

            decode(block, base + g * TILES, factor, put)

        loop(planes // GROUP, group, 2)
        if not opening:
            return
        factor = factor_of(block[base + planes], 1) * there

        def old_group(g):
            def put(f, p, rows):
                first = 0 if row < 0 else row + 4
                old_wide[f, at + g * GROUP + p, pl.ds(first, rows.shape[0]), :] = rows

            start = base + planes + 1
            if row == 0:
                decode(block, start + g * TILES, factor, put)
            else:
                near = factor[4:] if row < 0 else factor[:4]
                decode_nearest(block, start + g * (TILES // 2), near, put)

        loop(planes // GROUP, old_group, 2)

    for k in range(place.sides):
        lay(beside[k], 0, GROUP, place.beside_at[k], 0)

    def lay_y(below, above):
        kept = 4 if opening else 0
        for block, row in ((below, -8), (above, 8)):
            lay(block, 0, size_x, place.own_at, row)
            for k in range(place.sides):
                base = block_size(size_x, kept) + k * block_size(GROUP, kept)
                lay(block, base, GROUP, place.beside_at[k], row)

    pl.when(place.parity == 0)(lambda: lay_y(odd, even))
    pl.when(place.parity == 1)(lambda: lay_y(even, odd))


def lead_kernel(opening, columns, tile, old, coefs, inject, mat_first, mat_second, *refs):
    place = Place(tile.shape[1], columns)
    refs = list(refs)

    def take(number):
        taken = refs[:number]
        del refs[:number]
        return taken

    sides = place.sides
    beside = take(sides)
    even, odd, window = take(3)
    old_wide = take(1)[0] if opening else None
    around_out, edges_out, codes_out = take(sides), take(sides), take(sides)
    middle = take(1)[0]
    scratch, mats = refs, (mat_first, mat_second)
    fill(place, tile, old, beside, even, odd, window, old_wide)
    for k in range(sides):
        def store_around(i, new_p, new_q):
            for f, new in enumerate((new_p, new_q)):
                around_out[k][f, i] = new
                middle[f, i, pl.ds(4, new.shape[0]), :] = new

        def store_edge(i, new_p, new_q):
            edges_out[k][0, i] = new_p
            edges_out[k][1, i] = new_q

        first_leap(
            place, place.around_at[k], AROUND, window, old_wide if opening else old,
            place.first_at if opening else 0, coefs, inject, scratch, mats, store_around,
        )
        second_leap(
            place, place.edge_at[k], GROUP, middle, 0, tile, coefs, inject, scratch, mats,
            store_edge,
        )
        encode(lambda f, p: edges_out[k][f, p], GROUP, codes_out[k])


def rest_kernel(opening, columns, tile, old, window, coefs, inject, mat_first, mat_second, *refs):
    size_x, size_y = tile.shape[1], tile.shape[2]
    place = Place(size_x, columns)
    sides, count = place.sides, place.count
    around, edges = refs[:sides], refs[sides : 2 * sides]
    tile_out, payload, old_out, middle, *scratch = refs[2 * sides :]
    mats = (mat_first, mat_second)
    for f in range(2):
        middle[f, pl.ds(0, 4)] = jnp.zeros((4, 24, 128), F32)
        middle[f, pl.ds(count + 4, 4)] = jnp.zeros((4, 24, 128), F32)
        for k in range(sides):
            at = place.around_at[k]
            middle[f, pl.ds(at + 4, AROUND), pl.ds(4, size_y + 8), :] = around[k][f]
            old_out[f, pl.ds(at, AROUND)] = around[k][f]
            tile_out[f, pl.ds(place.edge_at[k], GROUP)] = edges[k][f]

    def store_first(i, new_p, new_q):
        for f, new in enumerate((new_p, new_q)):
            old_out[f, place.first_rest_at + i] = new
            middle[f, place.first_rest_at + i + 4, pl.ds(4, size_y + 8), :] = new

    def store_second(i, new_p, new_q):
        tile_out[0, place.rest_at + i] = new_p
        tile_out[1, place.rest_at + i] = new_q

    first_leap(
        place, place.first_rest_at, count - AROUND * sides, window, old,
        place.first_at if opening else 0, coefs, inject, scratch, mats, store_first,
    )
    second_leap(
        place, place.rest_at, place.rest, middle, place.tile_at + place.rest_at, tile, coefs,
        inject, scratch, mats, store_second,
    )
    encode(lambda f, p: tile_out[f, p], size_x, payload)


def last_kernel(columns, tile, old, coefs, inject, mat_first, mat_second, *refs):
    size_x, size_y = tile.shape[1], tile.shape[2]
    place = Place(size_x, columns)
    sides, count = place.sides, place.count
    even, odd, kept, sent, middle, tile_out, window, *scratch = refs[sides:]
    mats = (mat_first, mat_second)
    fill(place, tile, old, refs[:sides], even, odd, window, None)
    for f in range(2):
        middle[f, pl.ds(0, 4)] = jnp.zeros((4, 24, 128), F32)
        middle[f, pl.ds(count + 4, 4)] = jnp.zeros((4, 24, 128), F32)

    def store_first(i, new_p, new_q):
        for f, new in enumerate((new_p, new_q)):
            middle[f, i + 4, pl.ds(4, size_y + 8), :] = new

    def store_second(i, new_p, new_q):
        tile_out[0, i] = new_p
        tile_out[1, i] = new_q

    first_leap(place, 0, count, window, old, 0, coefs, inject, scratch, mats, store_first)
    second_leap(
        place, 0, size_x, middle, place.tile_at, tile, coefs, inject, scratch, mats, store_second
    )
    half = size_x // 2
    for mine in range(2):
        @pl.when(place.core == mine)
        def _():
            for out, start in ((kept, mine * half), (sent, (1 - mine) * half)):
                planes = pl.ds(start, half)
                inner = pl.ds(place.tile_at + 4 + start, half)
                out[0] = middle[0, inner, pl.ds(8, size_y), :]
                out[1] = tile_out[0, planes]
                out[2] = tile_out[1, planes]


def sine_cosine(angle):
    square = angle * angle
    sine = 1.0 / 6227020800.0
    for factor in (-1.0 / 39916800.0, 1.0 / 362880.0, -1.0 / 5040.0, 1.0 / 120.0, -1.0 / 6.0):
        sine = sine * square + factor
    sine = angle + angle * square * sine
    cosine = 1.0 / 479001600.0
    for factor in (-1.0 / 3628800.0, 1.0 / 40320.0, -1.0 / 720.0, 1.0 / 24.0, -0.5):
        cosine = cosine * square + factor
    return sine, 1.0 + square * cosine


def open_kernel(
    velocity, epsilon, delta, tilt, azimuth, source, receiver, *refs
):
    models = (velocity, epsilon, delta, tilt, azimuth)
    parity = lax.rem(lax.axis_index("gy"), 2)
    core = lax.rem(lax.axis_index("gx"), 2)
    small, (even, odd, own, kept, given), brought, arrived = (
        refs[:3], refs[3:8], refs[8:11], refs[11]
    )
    copies = [pltpu.make_async_copy(models[m], own.at[m], arrived.at[m]) for m in range(5)]
    others = [
        pltpu.make_async_copy(small[m], brought[m], arrived.at[7 + m]) for m in range(3)
    ]

    def states(mine):
        stay, leave = (source, receiver) if mine == 0 else (receiver, source)
        return (
            pltpu.make_async_copy(stay, kept, arrived.at[5]),
            pltpu.make_async_copy(leave, given, arrived.at[6]),
        )

    for copy in copies + others:
        copy.start()
    for mine in range(2):
        @pl.when(core == mine)
        def _():
            for copy in states(mine):
                copy.start()

    for copy in copies:
        copy.wait()

    def pack(out, row):
        for m in range(5):
            for u in range(0, own.shape[1], 2):
                pairs = [own[m, u + k].astype(F32) for k in range(2)]
                values = [pair[v + row : v + row + 4] for pair in pairs for v in (0, 8)]
                out[m, u // 2] = jnp.concatenate(values).astype(BF16)

    @pl.when(parity == 0)
    def _():
        pack(even, 4)
        pack(odd, 0)

    @pl.when(parity == 1)
    def _():
        pack(odd, 4)
        pack(even, 0)

    for mine in range(2):
        @pl.when(core == mine)
        def _():
            for copy in states(mine):
                copy.wait()
    for copy in others:
        copy.wait()


def join_kernel(own, even, odd, out):
    at_y = lax.axis_index("gy")
    parity = lax.rem(at_y, 2)
    has_below = jnp.where(at_y > 0, 1.0, 0.0)
    has_above = jnp.where(at_y < lax.axis_size("gy") - 1, 1.0, 0.0)

    def fill(below, above):
        for m in range(5):
            for u in range(own.shape[1]):
                low = below[m, u // 2].astype(F32) * has_below
                high = above[m, u // 2].astype(F32) * has_above
                pair = own[m, u].astype(F32)
                for v in range(2):
                    k = 2 * (u % 2) + v
                    rows = [low[4 * k : 4 * k + 4], pair[8 * v : 8 * v + 8], high[4 * k : 4 * k + 4]]
                    out[m, 2 * u + v] = jnp.concatenate(rows).astype(BF16)

    pl.when(parity == 0)(lambda: fill(odd, even))
    pl.when(parity == 1)(lambda: fill(even, odd))


def setup_kernel(columns, size_x, total_x, aperture, *refs):
    models, coefs, blocks = refs[:-2], refs[-2], refs[-1]
    place = Place(2 * size_x, columns)
    if len(models) > 1:
        for k, column in enumerate((place.column, 1 - place.column)):
            for j, core in enumerate((place.core, 1 - place.core)):
                blocks[:, pl.ds((2 * column + core) * size_x, size_x)] = models[2 * k + j][...]
        source = blocks
    else:
        source = models[0]

    def medium(i):
        x = place.start_x + i
        block = jnp.clip(x // size_x, 0, total_x // size_x - 1)
        inside = jnp.logical_and(x >= 0, x < total_x)
        at = aperture[block] * size_x + lax.rem(x + size_x, size_x)
        speed, stretch, bending, tilt, azimuth = [source[m, at].astype(F32) for m in range(5)]
        speed = jnp.where(inside, speed, 0.0)
        sin_t, cos_t = sine_cosine(tilt)
        sin_half, cos_half = sine_cosine(0.5 * azimuth)
        normal_x = sin_t * (1.0 - 2.0 * sin_half * sin_half)
        normal_y = sin_t * (2.0 * sin_half * cos_half)
        coefs[0, i] = speed
        coefs[1, i] = speed * (1.0 + 2.0 * stretch)
        coefs[2, i] = speed * jnp.sqrt(1.0 + 2.0 * bending)
        coefs[3, i] = S1 * (normal_x * normal_x)
        coefs[4, i] = S1 * (normal_y * normal_y)
        coefs[5, i] = SECOND_UNIT * (cos_t * cos_t)
        coefs[6, i] = (2.0 * G1 * G1) * (normal_x * normal_y)
        coefs[7, i] = (2.0 * G1 * FIRST_UNIT) * (normal_y * cos_t)
        coefs[8, i] = (2.0 * G1 * FIRST_UNIT) * (normal_x * cos_t)

    loop(place.count, medium, 6)


def injection_kernel(
    columns, size_x, size_y, total_y, source_cell, wavelet, cells, traces, out, hits
):
    place = Place(size_x, columns)
    count, rows = hits.shape[:2]
    number = cells.shape[1]
    row = lax.broadcasted_iota(jnp.int32, (rows, number), 0)
    lane = lax.broadcasted_iota(jnp.int32, (1, number), 1)
    is_source = place.core == 0
    lonely = jnp.where(lane == 0, source_cell[0], -1)
    aims = jnp.where(is_source, lonely, cells[...])
    y = place.at_y * size_y - 4 + row
    valid = jnp.logical_and(y >= 0, y < total_y)

    def mark(i):
        code = jnp.where(valid, (place.start_x + i) * total_y + y, -2)
        hits[i] = jnp.where(code == aims, 1.0, 0.0).astype(BF16)

    loop(count, mark, 2)
    step = lax.broadcasted_iota(jnp.int32, (NT, number), 0)
    amounts = jnp.zeros((NT, number), F32)
    for k in range(NT):
        amounts = jnp.where(step == k, wavelet[:, k : k + 1], amounts)
    backward = jnp.concatenate([traces[k : k + 1] for k in reversed(range(NT))])
    rest = jnp.where(is_source, amounts, backward)
    total = None
    for _ in range(3):
        piece = rest.astype(BF16)
        rest = rest - piece.astype(F32)
        term = lax.dot_general(
            hits[...].reshape(count * rows, number), piece, (((1,), (1,)), ((), ())),
            preferred_element_type=F32,
        )
        total = term if total is None else total + term
    out[...] = total.reshape(count, rows, NT)


def spread_kernel(moment, lanes, out):
    core = lax.rem(lax.axis_index("gx"), 2)
    level = jnp.where(core == 0, SRC_DEPTH, REC_DEPTH)
    mask = (lax.broadcasted_iota(jnp.int32, (lanes.shape[1], 128), 1) == level).astype(F32)

    def expand(i):
        values = lanes[i]
        for k in range(2):
            out[k, i] = values[:, moment + k : moment + k + 1] * mask

    loop(lanes.shape[0], expand, 6)


def sort_kernel(columns, *refs):
    levels, (kept, sent) = refs[: NT - 1], refs[NT - 1 :]
    half, size_y = kept.shape[1:3]
    place = Place(2 * half, columns)

    def level_at(step, start):
        where = levels[step]
        if step % 2 == 0:
            return where[0, pl.ds(start, half)]
        return where[0, pl.ds(place.tile_at + start, half), pl.ds(4, size_y), :]

    for mine in range(2):
        @pl.when(place.core == mine)
        def _():
            for step in range(NT - 1):
                t = step if mine == 0 else NT - step
                if t > 0:
                    kept[t - 1] = level_at(step, mine * half)
                    sent[t - 1] = level_at(step, (1 - mine) * half)


def close_kernel(kept, got, last_kept, last_got, image, field):
    core = lax.rem(lax.axis_index("gx"), 2)
    total = kept[1] * got[1]
    for t in range(2, NT - 2):
        total = total + kept[t] * got[t]

    @pl.when(core == 0)
    def _():
        image[...] = (
            total + kept[0] * last_got[0] + last_kept[0] * got[NT - 2] + last_kept[1] * got[NT - 1]
        ) * (1.0 / NT)
        field[...] = last_got[pl.ds(1, 2)]

    @pl.when(core == 1)
    def _():
        image[...] = (
            total + last_kept[0] * got[0] + kept[NT - 2] * last_got[0] + kept[NT - 1] * last_got[1]
        ) * (1.0 / NT)
        field[...] = last_kept[pl.ds(1, 2)]


def per_device(
    velocity,
    epsilon,
    delta,
    tilt,
    azimuth,
    aperture,
    source_cell,
    wavelet,
    receiver_cell,
    traces,
    source_state,
    receiver_state,
):
    block_x, size_y, _ = velocity.shape
    devices_x, devices_y = lax.axis_size("gx"), lax.axis_size("gy")
    columns = devices_x // 2
    total_x, total_y = block_x * devices_x, size_y * devices_y
    size_x, rows = 2 * block_x, size_y + 8
    is_source = lax.axis_index("gx") % 2 == 0
    place = Place(size_x, columns)
    sides, count = place.sides, place.count
    mats = depth_matrices(128)
    chip_pairs = [even_pairs(columns), odd_pairs(columns)][:sides]
    row_pairs = [even_pairs(devices_y), odd_pairs(devices_y)]
    trade = both_ways([(2 * c, 2 * c + 1) for c in range(columns)])

    def over_gy(values, pairs):
        paired = {i for pair in pairs for i in pair}
        alone = [y for y in range(devices_y) if y not in paired]
        swaps = [(x * devices_y + a, x * devices_y + b) for x in range(devices_x) for a, b in pairs]
        swaps += [
            (a * devices_y + y, b * devices_y + y)
            for a, b in chip_swap(even_pairs(columns)) for y in alone
        ]
        return lax.ppermute(values, ("gx", "gy"), both_ways(swaps))

    def over_gx(values, pairs):
        return lax.ppermute(values, "gx", both_ways(chip_swap(pairs)))

    def beside_of(edges):
        return [over_gx(edge, pairs) for edge, pairs in zip(edges, chip_pairs)]

    def near_of(even, odd):
        odd = over_gy(odd, row_pairs[1])
        return over_gy(even, row_pairs[0]), odd

    def codes(planes, old_rows=0):
        return ((block_size(planes, old_rows), 16, 128), jnp.int16)

    models = [
        values.reshape(block_x // 2, 16, 128) for values in (velocity, epsilon, delta, tilt, azimuth)
    ]
    small = (wavelet[None, :], receiver_cell[None, :], traces)
    rim = ((5, block_x // 4, 16, 128), BF16)
    states = (source_state, receiver_state)
    state = (source_state.shape, F32)
    *rims, own, kept, given, series, cells, data = pl.pallas_call(
        open_kernel,
        out_shape=tuple(
            jax.ShapeDtypeStruct(*out)
            for out in (rim, rim, ((5, block_x // 2, 16, 128), BF16), state, state)
            + tuple((x.shape, x.dtype) for x in small)
        ),
        in_specs=[HBM] * 10,
        out_specs=(VMEM,) * 8,
        scratch_shapes=[pltpu.SemaphoreType.DMA((10,))],
        compiler_params=pltpu.CompilerParams(vmem_limit_bytes=8 * 2**20),
        name="open",
    )(*[pltpu.with_memory_space_constraint(x, pltpu.HBM) for x in (*models, *states, *small)])
    rims = [over_gy(values, pairs) for values, pairs in zip(rims, row_pairs)]

    got = lax.ppermute(given, "gx", trade)
    field = ((2, size_x, size_y, 128), F32)
    tile, old, payload, *edges = call(
        functools.partial(first_kernel, columns),
        (field, field, codes(size_x, 8)) + (codes(GROUP, 8),) * sides,
        (), 16, "first", (kept, got),
    )
    number = receiver_cell.shape[0]
    cells, _ = lax.optimization_barrier((cells, edges[0]))
    (amounts,) = call(
        functools.partial(injection_kernel, columns, size_x, size_y, total_y),
        (((count, rows, NT), F32),), (((count, rows, number), BF16),),
        16, "injection", (source_cell, series, cells, data), scalars=1,
    )
    beside = beside_of(edges)
    payload, _ = lax.optimization_barrier((payload, amounts))
    total = block_size(size_x, 4) + sides * block_size(GROUP, 4)
    wide = call(
        cut_kernel, (((total, 16, 128), jnp.int16),) * 2, (), 8, "cut", (payload, *beside)
    )
    near = near_of(*wide[::-1])

    def spread(moment, after):
        lanes, _ = lax.optimization_barrier((amounts, after[0]))
        (out,) = call(
            functools.partial(spread_kernel, moment), (((2, count, rows, 128), F32),), (), 8,
            "spread", (lanes,),
        )
        return out

    inject = spread(0, wide)

    rims = lax.optimization_barrier((*rims, edges[0]))[:2]
    (model,) = call(
        join_kernel, (((5, block_x, rows, 128), BF16),), (), 8, "join", (own, *rims), work=1000
    )
    if columns == 2:
        later, _ = lax.optimization_barrier((model, wide[0]))
        across = over_gx(later, chip_pairs[0])
        early, _ = lax.optimization_barrier((model, inject))
        other = lax.ppermute(early, "gx", trade)
        gathered = [model, other, across, lax.ppermute(across, "gx", trade)]
        held = (5, total_x, rows, 128)
    else:
        gathered, held = [lax.all_gather(model, "gx", axis=1, tiled=True)], (16, 128)
    (coefs,) = call(
        functools.partial(setup_kernel, columns, block_x, total_x),
        (((9, count, rows, 128), F32),), ((held, BF16),), 24, "setup", (aperture, *gathered),
        scalars=1, work=0,
    )

    window = ((2, place.wide + 8, 32, 128), F32)
    middle = ((2, count + 8, 24, 128), F32)
    lines = ((2, count, rows, 128), F32)
    levels = [tile]
    for moment in range(0, NT - 2, 2):
        opening = moment == 0
        inject = inject if opening else spread(moment, wide)
        old_wide = (((2, place.wide, rows, 128), F32),) * opening
        around = (((2, AROUND, rows, 128), F32),) * sides
        edge = (((2, GROUP, size_y, 128), F32),) * sides
        fields, *outs = call(
            functools.partial(lead_kernel, opening, columns),
            (window,) + old_wide + around + edge + (codes(GROUP),) * sides,
            [((2, AROUND, 24, 128), F32)] + leap_scratch(AROUND), 24, "lead",
            (tile, old, coefs, inject, *mats, *beside, *near), work=2 * 10**6,
        )
        if opening:
            old, *outs = outs
        beside = beside_of(outs[2 * sides :])
        tile, payload, old = call(
            functools.partial(rest_kernel, opening, columns),
            (field, codes(size_x), lines), [middle] + leap_scratch(place.rest), 24, "rest",
            (tile, old, fields, coefs, inject, *mats, *outs[: 2 * sides]), work=4 * 10**6,
        )
        wide = (jnp.concatenate([payload, *beside]),) * 2
        near = near_of(*wide)
        levels += [old, tile]
    shape = (block_x, size_y, 128)
    inject = spread(NT - 2, wide)
    share = ((NT,) + shape, F32)
    kept, sent = call(
        functools.partial(sort_kernel, columns), (share, share), (), 8, "sort",
        lax.optimization_barrier((*levels, *near, inject))[: NT - 1],
    )
    got = lax.ppermute(sent, "gx", trade)
    share = ((3,) + shape, F32)
    last_kept, last_sent = call(
        functools.partial(last_kernel, columns),
        (share, share), [middle, field, window] + leap_scratch(count), 24, "last",
        (tile, old, coefs, inject, *mats, *beside, *near),
    )
    last_got = lax.ppermute(last_sent, "gx", trade)
    return call(
        close_kernel, ((shape, F32), ((2,) + shape, F32)), (), 8, "close",
        (kept, got, last_kept, last_got),
    )


def solution(mesh):
    in_specs = (
        P("gx", "gy", None),
        P("gx", "gy", None),
        P("gx", "gy", None),
        P("gx", "gy", None),
        P("gx", "gy", None),
        P("shot"),
        P("shot"),
        P("shot"),
        P("shot"),
        P(None, "shot"),
        P(None, ("shot", "gx"), "gy", None),
        P(None, ("shot", "gx"), "gy", None),
    )
    out_specs = (P(("shot", "gx"), "gy", None), P(None, ("shot", "gx"), "gy", None))
    return jax.shard_map(
        per_device, mesh=mesh, in_specs=in_specs, out_specs=out_specs, check_vma=False
    )
```

```python
import functools

import jax
import jax.numpy as jnp
from jax import lax
from jax.experimental import pallas as pl
from jax.experimental.pallas import tpu as pltpu
from jax.sharding import PartitionSpec as P

NT = 8
SRC_DEPTH = 10
REC_DEPTH = 6
F32 = jnp.float32
BF16 = jnp.bfloat16

second_taps = (-205.0 / 72.0, 8.0 / 5.0, -1.0 / 5.0, 8.0 / 315.0, -1.0 / 560.0)
first_taps = (4.0 / 5.0, -1.0 / 5.0, 4.0 / 105.0, -1.0 / 280.0)
CENTRE = second_taps[0]
S1 = second_taps[1]
G1 = first_taps[0]
second_ratio = tuple(tap / S1 for tap in second_taps[2:])
first_ratio = tuple(tap / G1 for tap in first_taps[1:])
second_whole = (8064.0, -1008.0, 128.0, -9.0)
first_whole = (672.0, -168.0, 32.0, -3.0)
SECOND_UNIT = 1.0 / 5040.0
FIRST_UNIT = 1.0 / 840.0
VMEM = pl.BlockSpec(memory_space=pltpu.VMEM)
SMEM = pl.BlockSpec(memory_space=pltpu.SMEM)
HBM = pl.BlockSpec(memory_space=pltpu.HBM)


def even_pairs(count):
    return [(i, i + 1) for i in range(0, count - 1, 2)]


def odd_pairs(count):
    return [(i, i + 1) for i in range(1, count - 1, 2)]


def both_ways(pairs):
    return [pair for a, b in pairs for pair in ((a, b), (b, a))]


def chip_swap(pairs):
    return [(2 * a + c, 2 * b + c) for a, b in pairs for c in range(2)]


class Place:
    def __init__(self, size_x, columns):
        at_x = lax.axis_index("gx")
        self.core, self.column = lax.rem(at_x, 2), lax.div(at_x, 2)
        self.at_y = lax.axis_index("gy")
        self.parity = lax.rem(self.at_y, 2)
        self.has_below = jnp.where(self.at_y > 0, 1.0, 0.0)
        self.has_above = jnp.where(self.at_y < lax.axis_size("gy") - 1, 1.0, 0.0)
        if columns == 2:
            side = self.column
            self.count = size_x + 4
            self.first_at = self.tile_at = 4 * side
            self.start_x = side * (size_x - 4)
            self.beside_at = [size_x * (1 - side)]
            self.edge_at = [(size_x - GROUP) * (1 - side)]
            self.rest_at, self.rest = GROUP * side, size_x - GROUP
            self.first_rest_at = AROUND * side
        else:
            side = lax.rem(self.column, 2)
            self.count = size_x + 8
            self.first_at = self.tile_at = 4
            self.start_x = self.column * size_x - 4
            self.beside_at = [(size_x + GROUP) * (1 - side), (size_x + GROUP) * side]
            self.edge_at = [(size_x - GROUP) * (1 - side), (size_x - GROUP) * side]
            self.rest_at, self.rest = GROUP, size_x - 2 * GROUP
            self.first_rest_at = AROUND
        self.sides = len(self.beside_at)
        self.around_at = [self.tile_at + at - 4 for at in self.edge_at]
        self.own_at = self.first_at + self.tile_at
        self.wide = size_x + GROUP * self.sides


def call(kernel, outs, scratch, mebibytes, name, args, scalars=0, work=10**6):
    outs = tuple(jax.ShapeDtypeStruct(shape, dtype) for shape, dtype in outs)
    return pl.pallas_call(
        kernel,
        out_shape=outs,
        in_specs=[SMEM] * scalars + [VMEM] * (len(args) - scalars),
        out_specs=(VMEM,) * len(outs),
        scratch_shapes=[pltpu.VMEM(shape, dtype) for shape, dtype in scratch],
        compiler_params=pltpu.CompilerParams(vmem_limit_bytes=mebibytes * 2**20),
        cost_estimate=pl.CostEstimate(flops=work, bytes_accessed=work, transcendentals=0),
        name=name,
    )(*args)


def loop(trips, body, wanted):
    unroll = max(u for u in range(1, wanted + 1) if trips % u == 0)

    def step(i, carry):
        body(i)
        return carry

    lax.fori_loop(0, trips, step, 0, unroll=unroll)


def depth_matrices(size):
    rows = jnp.arange(size)[:, None]
    cols = jnp.arange(size)[None, :]
    first = jnp.zeros((size, size), F32)
    second = jnp.zeros((size, size), F32)
    for k in range(1, 5):
        up = (rows == cols + k).astype(F32)
        down = (rows == cols - k).astype(F32)
        first = first + first_whole[k - 1] * (up - down)
        second = second + second_whole[k - 1] * (up + down)
    return (
        jnp.concatenate([first, first]).astype(BF16),
        jnp.concatenate([second, second]).astype(BF16),
    )


def sums_and_slopes(shifted):
    up, down = shifted(1), shifted(-1)
    curve, slope = up + down, up - down
    for k in range(2, 5):
        up, down = shifted(k), shifted(-k)
        curve = curve + second_ratio[k - 2] * (up + down)
        slope = slope + first_ratio[k - 2] * (up - down)
    return curve, slope


def slope_only(shifted):
    slope = shifted(1) - shifted(-1)
    for k in range(2, 5):
        slope = slope + first_ratio[k - 2] * (shifted(k) - shifted(-k))
    return slope


def split(values):
    high = values.astype(BF16)
    low = (values - high.astype(F32)).astype(BF16)
    return high, low


TOP = 32000.0
GROUP = 8
AROUND = GROUP + 8
TILES = GROUP


def block_size(planes, old_rows=0):
    return planes + 1 + planes * old_rows // 8


def scale_of(value_at, planes):
    def grow(i, size):
        for f in range(2):
            size = jnp.maximum(size, jnp.abs(value_at(f, i)))
        return size

    size = lax.fori_loop(0, planes, grow, jnp.full((8, 128), 1e-30, F32), unroll=8)
    code = jnp.ceil(jnp.log2(size) * 256.0)
    return code, TOP * jnp.exp2(code * (-1.0 / 256.0))


def as_code(pieces):
    return jnp.concatenate(pieces).astype(jnp.int32).astype(jnp.int16)


def encode(value_at, planes, out, old_at=None):
    code, factor = scale_of(value_at, planes)
    old_code, old_factor = scale_of(old_at, planes) if old_at else (code, None)

    def put(source, base, by):
        def group(g):
            for f in range(2):
                for q in range(4):
                    pair = [source(f, g * GROUP + 2 * q + v) for v in range(2)]
                    whole = [jnp.floor(value * by + 0.5) for value in pair]
                    out[base + g * TILES + 4 * f + q] = as_code(whole)

        loop(planes // GROUP, group, 1)

    put(value_at, 0, factor)
    out[planes] = as_code([code, old_code])
    if old_at:
        put(old_at, planes + 1, old_factor)


def factor_of(scales, half):
    code = scales.astype(jnp.int32).astype(F32)[8 * half : 8 * half + 8]
    return jnp.exp2(code * (1.0 / 256.0)) * (1.0 / TOP)


def decode(block, base, factor, put):
    for f in range(2):
        for q in range(4):
            both = block[base + 4 * f + q].astype(jnp.int32).astype(F32)
            put(f, 2 * q, both[:8] * factor)
            put(f, 2 * q + 1, both[8:] * factor)


def decode_nearest(block, base, factor, put):
    by = jnp.concatenate([factor] * 4)
    for f in range(2):
        for q in range(2):
            rows = block[base + 2 * f + q].astype(jnp.int32).astype(F32) * by
            for v in range(4):
                put(f, 4 * q + v, rows[4 * v : 4 * v + 4])


def leap(src, x0, row0, rows, count, scratch, mats, coef, old_at, inject_at, store):
    slope_y, curve_y, part, halves, product = scratch
    mat_first, mat_second = mats
    planes = 16 // rows
    group = 4

    def field(f, p, r=0, number=rows):
        return src[f, x0 + p, pl.ds(row0 + r, number), :]

    def joined(values):
        return jnp.concatenate(values) if len(values) > 1 else values[0]

    def put_halves(kind, f, unit, values):
        high, low = split(values)
        halves[kind, f, unit, :, :128] = high
        halves[kind, f, unit, :, 128:] = low

    def along_y(u):
        for f in range(2):
            here, slopes = [], []
            for v in range(planes):
                p = u * planes + v
                curve, slope = sums_and_slopes(lambda k: field(f, p, k))
                slope_y[f, p, :rows] = slope
                curve_y[f, p, :rows] = curve
                slopes.append(slope)
                here.append(field(f, p))
            put_halves(0, f, u, joined(here))
            put_halves(1, f, u, joined(slopes))

    loop((count + 8) // planes, along_y, 24)

    def along_x(q):
        base = q * group
        for f in range(2):
            slopes = [[] for g in range(group)]
            for r in range(0, rows, 8):
                line = [field(f, base + k, r, 8) for k in range(group + 8)]
                slant = [slope_y[f, base + k, pl.ds(r, 8), :] for k in range(group + 8)]
                for g in range(group):
                    i = base + g
                    xx, slope = sums_and_slopes(lambda k: line[g + 4 + k])
                    xy = slope_only(lambda k: slant[g + 4 + k])
                    yy = curve_y[f, i + 4, pl.ds(r, 8), :]
                    wx, wy, wxy = [coef(m, i, r, 8) for m in (3, 4, 6)]
                    if f == 0:
                        total = (2.0 * CENTRE) * line[g + 4] + (S1 - wx) * xx
                        total = total + (S1 - wy) * yy - wxy * xy
                    else:
                        total = CENTRE * line[g + 4] + wx * xx
                        total = total + wy * yy + wxy * xy
                    part[f, i, pl.ds(r, 8), :] = total
                    slopes[g].append(slope)
            pieces = [piece for rest in slopes for piece in rest]
            for k in range(0, len(pieces), 2):
                put_halves(2, f, q * (len(pieces) // 2) + k // 2, joined(pieces[k : k + 2]))

    loop(count // group, along_x, 10)

    units = count // planes
    for kind, mat, at in ((0, mat_second, 4 // planes), (1, mat_first, 4 // planes), (2, mat_first, 0)):
        for f in range(2):
            both = halves[kind, f, pl.ds(at, units)].reshape(units * 16, 256)
            out = jnp.dot(both, mat[...], preferred_element_type=F32)
            product[kind, f, pl.ds(0, units)] = out.reshape(units, 16, 128)

    def combine(u):
        where = [u * planes + v for v in range(planes)]
        speed, speed_h, speed_v, wz, wyz, wxz = [
            joined([coef(m, i, 0, rows) for i in where]) for m in (0, 1, 2, 5, 7, 8)
        ]
        zz, yz, xz = [[product[kind, f, u] for f in range(2)] for kind in range(3)]
        parts = [joined([part[f, i, :rows] for i in where]) for f in range(2)]
        here = [joined([field(f, i + 4) for i in where]) for f in range(2)]
        old = [joined([old_at(f, i) for i in where]) for f in range(2)]
        add = joined([inject_at(i) for i in where])
        flat = parts[0] + (SECOND_UNIT - wz) * zz[0] - (wyz * yz[0] + wxz * xz[0])
        tilted = parts[1] + wz * zz[1] + (wyz * yz[1] + wxz * xz[1])
        new_p = (2.0 * here[0] - old[0] + add) + (speed_h * flat + speed_v * tilted)
        new_q = (2.0 * here[1] - old[1] + add) + (speed_v * flat + speed * tilted)
        for v, i in enumerate(where):
            cut = slice(v * rows, v * rows + rows)
            store(i, new_p[cut], new_q[cut])

    loop(units, combine, 36)


def leap_scratch(count):
    lines = (2, count + 8, 16, 128)
    return [
        (lines, F32),
        (lines, F32),
        ((2, count, 16, 128), F32),
        ((3, 2, count + 8, 16, 256), BF16),
        ((3, 2, count, 16, 128), F32),
    ]


def first_kernel(columns, kept, got, tile, old, payload, *edges):
    size = kept.shape[1]
    place = Place(2 * size, columns)
    for source, at in ((kept, place.core * size), (got, (1 - place.core) * size)):
        for f in range(2):
            tile[f, pl.ds(at, size)] = source[2 * f]
            old[f, pl.ds(at, size)] = source[2 * f + 1]

    encode(lambda f, p: tile[f, p], 2 * size, payload, lambda f, p: old[f, p])
    for k, edge in enumerate(edges):
        group = lax.div(place.edge_at[k], GROUP) * TILES
        for base in (0, 2 * size + 1):
            edge[pl.ds(base and GROUP + 1, TILES)] = payload[pl.ds(base + group, TILES)]
        edge[GROUP] = payload[2 * size]


def cut_kernel(payload, *refs):
    beside, (odd, even) = refs[:-2], refs[-2:]
    parity = lax.rem(lax.axis_index("gy"), 2)

    def cut(out, row):
        base = 0
        for block in (payload, *beside):
            planes = block.shape[0] // 2
            out[pl.ds(base, planes + 1)] = block[: planes + 1]
            for u in range(0, planes, 2):
                pairs = [block[planes + 1 + u + v].astype(jnp.int32) for v in range(2)]
                rows = [pair[r + row : r + row + 4] for pair in pairs for r in (0, 8)]
                out[base + planes + 1 + u // 2] = jnp.concatenate(rows).astype(jnp.int16)
            base += block_size(planes, 4)

    @pl.when(parity == 0)
    def _():
        cut(even, 4)
        cut(odd, 0)

    @pl.when(parity == 1)
    def _():
        cut(odd, 4)
        cut(even, 0)


def first_leap(place, start, count, window, old, old_start, coefs, inject, scratch, mats, store):
    leap(
        window, place.first_at + start, 8, coefs.shape[2], count, scratch, mats,
        lambda m, i, r, number: coefs[m, start + i, pl.ds(r, number), :],
        lambda f, i: old[f, old_start + start + i],
        lambda i: inject[0, start + i],
        store,
    )


def second_leap(
    place, start, count, source, source_start, tile, coefs, inject, scratch, mats, store
):
    rows = tile.shape[2]
    at = place.tile_at + start
    leap(
        source, source_start, 8, rows, count, scratch, mats,
        lambda m, i, r, number: coefs[m, at + i, pl.ds(4 + r, number), :],
        lambda f, i: tile[f, start + i],
        lambda i: inject[1, at + i, pl.ds(4, rows), :],
        store,
    )


def fill(place, tile, old, beside, even, odd, window, old_wide):
    size_x = tile.shape[1]
    opening = old_wide is not None
    for f in range(2):
        window[f, pl.ds(0, 4)] = jnp.zeros((4, 32, 128), F32)
        window[f, pl.ds(place.wide + 4, 4)] = jnp.zeros((4, 32, 128), F32)
        window[f, pl.ds(place.own_at + 4, size_x), pl.ds(12, 8), :] = tile[f]
        if opening:
            old_wide[f, pl.ds(place.own_at, size_x), pl.ds(4, 8), :] = old[f]

    def lay(block, base, planes, at, row):
        there = {-8: place.has_below, 0: 1.0, 8: place.has_above}[row]
        factor = factor_of(block[base + planes], 0) * there

        def group(g):
            def put(f, p, rows):
                window[f, at + g * GROUP + p + 4, pl.ds(row + 12, 8), :] = rows

            decode(block, base + g * TILES, factor, put)

        loop(planes // GROUP, group, 2)
        if not opening:
            return
        factor = factor_of(block[base + planes], 1) * there

        def old_group(g):
            def put(f, p, rows):
                first = 0 if row < 0 else row + 4
                old_wide[f, at + g * GROUP + p, pl.ds(first, rows.shape[0]), :] = rows

            start = base + planes + 1
            if row == 0:
                decode(block, start + g * TILES, factor, put)
            else:
                near = factor[4:] if row < 0 else factor[:4]
                decode_nearest(block, start + g * (TILES // 2), near, put)

        loop(planes // GROUP, old_group, 2)

    for k in range(place.sides):
        lay(beside[k], 0, GROUP, place.beside_at[k], 0)

    def lay_y(below, above):
        kept = 4 if opening else 0
        for block, row in ((below, -8), (above, 8)):
            lay(block, 0, size_x, place.own_at, row)
            for k in range(place.sides):
                base = block_size(size_x, kept) + k * block_size(GROUP, kept)
                lay(block, base, GROUP, place.beside_at[k], row)

    pl.when(place.parity == 0)(lambda: lay_y(odd, even))
    pl.when(place.parity == 1)(lambda: lay_y(even, odd))


def lead_kernel(opening, columns, tile, old, coefs, inject, mat_first, mat_second, *refs):
    place = Place(tile.shape[1], columns)
    refs = list(refs)

    def take(number):
        taken = refs[:number]
        del refs[:number]
        return taken

    sides = place.sides
    beside = take(sides)
    even, odd, window = take(3)
    old_wide = take(1)[0] if opening else None
    around_out, edges_out, codes_out = take(sides), take(sides), take(sides)
    middle = take(1)[0]
    scratch, mats = refs, (mat_first, mat_second)
    fill(place, tile, old, beside, even, odd, window, old_wide)
    for k in range(sides):
        def store_around(i, new_p, new_q):
            for f, new in enumerate((new_p, new_q)):
                around_out[k][f, i] = new
                middle[f, i, pl.ds(4, new.shape[0]), :] = new

        def store_edge(i, new_p, new_q):
            edges_out[k][0, i] = new_p
            edges_out[k][1, i] = new_q

        first_leap(
            place, place.around_at[k], AROUND, window, old_wide if opening else old,
            place.first_at if opening else 0, coefs, inject, scratch, mats, store_around,
        )
        second_leap(
            place, place.edge_at[k], GROUP, middle, 0, tile, coefs, inject, scratch, mats,
            store_edge,
        )
        encode(lambda f, p: edges_out[k][f, p], GROUP, codes_out[k])


def rest_kernel(opening, columns, tile, old, window, coefs, inject, mat_first, mat_second, *refs):
    size_x, size_y = tile.shape[1], tile.shape[2]
    place = Place(size_x, columns)
    sides, count = place.sides, place.count
    around, edges = refs[:sides], refs[sides : 2 * sides]
    tile_out, payload, old_out, middle, *scratch = refs[2 * sides :]
    mats = (mat_first, mat_second)
    for f in range(2):
        middle[f, pl.ds(0, 4)] = jnp.zeros((4, 24, 128), F32)
        middle[f, pl.ds(count + 4, 4)] = jnp.zeros((4, 24, 128), F32)
        for k in range(sides):
            at = place.around_at[k]
            middle[f, pl.ds(at + 4, AROUND), pl.ds(4, size_y + 8), :] = around[k][f]
            old_out[f, pl.ds(at, AROUND)] = around[k][f]
            tile_out[f, pl.ds(place.edge_at[k], GROUP)] = edges[k][f]

    def store_first(i, new_p, new_q):
        for f, new in enumerate((new_p, new_q)):
            old_out[f, place.first_rest_at + i] = new
            middle[f, place.first_rest_at + i + 4, pl.ds(4, size_y + 8), :] = new

    def store_second(i, new_p, new_q):
        tile_out[0, place.rest_at + i] = new_p
        tile_out[1, place.rest_at + i] = new_q

    first_leap(
        place, place.first_rest_at, count - AROUND * sides, window, old,
        place.first_at if opening else 0, coefs, inject, scratch, mats, store_first,
    )
    second_leap(
        place, place.rest_at, place.rest, middle, place.tile_at + place.rest_at, tile, coefs,
        inject, scratch, mats, store_second,
    )
    encode(lambda f, p: tile_out[f, p], size_x, payload)


def last_kernel(columns, tile, old, coefs, inject, mat_first, mat_second, *refs):
    size_x, size_y = tile.shape[1], tile.shape[2]
    place = Place(size_x, columns)
    sides, count = place.sides, place.count
    even, odd, kept, sent, middle, tile_out, window, *scratch = refs[sides:]
    mats = (mat_first, mat_second)
    fill(place, tile, old, refs[:sides], even, odd, window, None)
    for f in range(2):
        middle[f, pl.ds(0, 4)] = jnp.zeros((4, 24, 128), F32)
        middle[f, pl.ds(count + 4, 4)] = jnp.zeros((4, 24, 128), F32)

    def store_first(i, new_p, new_q):
        for f, new in enumerate((new_p, new_q)):
            middle[f, i + 4, pl.ds(4, size_y + 8), :] = new

    def store_second(i, new_p, new_q):
        tile_out[0, i] = new_p
        tile_out[1, i] = new_q

    first_leap(place, 0, count, window, old, 0, coefs, inject, scratch, mats, store_first)
    second_leap(
        place, 0, size_x, middle, place.tile_at, tile, coefs, inject, scratch, mats, store_second
    )
    half = size_x // 2
    for mine in range(2):
        @pl.when(place.core == mine)
        def _():
            for out, start in ((kept, mine * half), (sent, (1 - mine) * half)):
                planes = pl.ds(start, half)
                inner = pl.ds(place.tile_at + 4 + start, half)
                out[0] = middle[0, inner, pl.ds(8, size_y), :]
                out[1] = tile_out[0, planes]
                out[2] = tile_out[1, planes]


def sine_cosine(angle):
    square = angle * angle
    sine = 1.0 / 6227020800.0
    for factor in (-1.0 / 39916800.0, 1.0 / 362880.0, -1.0 / 5040.0, 1.0 / 120.0, -1.0 / 6.0):
        sine = sine * square + factor
    sine = angle + angle * square * sine
    cosine = 1.0 / 479001600.0
    for factor in (-1.0 / 3628800.0, 1.0 / 40320.0, -1.0 / 720.0, 1.0 / 24.0, -0.5):
        cosine = cosine * square + factor
    return sine, 1.0 + square * cosine


def open_kernel(
    velocity, epsilon, delta, tilt, azimuth, source, receiver, *refs
):
    models = (velocity, epsilon, delta, tilt, azimuth)
    parity = lax.rem(lax.axis_index("gy"), 2)
    core = lax.rem(lax.axis_index("gx"), 2)
    small, (even, odd, own, kept, given), brought, arrived = (
        refs[:3], refs[3:8], refs[8:11], refs[11]
    )
    copies = [pltpu.make_async_copy(models[m], own.at[m], arrived.at[m]) for m in range(5)]
    others = [
        pltpu.make_async_copy(small[m], brought[m], arrived.at[7 + m]) for m in range(3)
    ]

    def states(mine):
        stay, leave = (source, receiver) if mine == 0 else (receiver, source)
        return (
            pltpu.make_async_copy(stay, kept, arrived.at[5]),
            pltpu.make_async_copy(leave, given, arrived.at[6]),
        )

    for copy in copies + others:
        copy.start()
    for mine in range(2):
        @pl.when(core == mine)
        def _():
            for copy in states(mine):
                copy.start()

    for copy in copies:
        copy.wait()

    def pack(out, row):
        for m in range(5):
            for u in range(0, own.shape[1], 2):
                pairs = [own[m, u + k].astype(F32) for k in range(2)]
                values = [pair[v + row : v + row + 4] for pair in pairs for v in (0, 8)]
                out[m, u // 2] = jnp.concatenate(values).astype(BF16)

    @pl.when(parity == 0)
    def _():
        pack(even, 4)
        pack(odd, 0)

    @pl.when(parity == 1)
    def _():
        pack(odd, 4)
        pack(even, 0)

    for mine in range(2):
        @pl.when(core == mine)
        def _():
            for copy in states(mine):
                copy.wait()
    for copy in others:
        copy.wait()


def join_kernel(own, even, odd, out):
    at_y = lax.axis_index("gy")
    parity = lax.rem(at_y, 2)
    has_below = jnp.where(at_y > 0, 1.0, 0.0)
    has_above = jnp.where(at_y < lax.axis_size("gy") - 1, 1.0, 0.0)

    def fill(below, above):
        for m in range(5):
            for u in range(own.shape[1]):
                low = below[m, u // 2].astype(F32) * has_below
                high = above[m, u // 2].astype(F32) * has_above
                pair = own[m, u].astype(F32)
                for v in range(2):
                    k = 2 * (u % 2) + v
                    rows = [low[4 * k : 4 * k + 4], pair[8 * v : 8 * v + 8], high[4 * k : 4 * k + 4]]
                    out[m, 2 * u + v] = jnp.concatenate(rows).astype(BF16)

    pl.when(parity == 0)(lambda: fill(odd, even))
    pl.when(parity == 1)(lambda: fill(even, odd))


def setup_kernel(columns, size_x, total_x, aperture, *refs):
    models, coefs, blocks = refs[:-2], refs[-2], refs[-1]
    place = Place(2 * size_x, columns)
    if len(models) > 1:
        for k, column in enumerate((place.column, 1 - place.column)):
            for j, core in enumerate((place.core, 1 - place.core)):
                blocks[:, pl.ds((2 * column + core) * size_x, size_x)] = models[2 * k + j][...]
        source = blocks
    else:
        source = models[0]

    def medium(i):
        x = place.start_x + i
        block = jnp.clip(x // size_x, 0, total_x // size_x - 1)
        inside = jnp.logical_and(x >= 0, x < total_x)
        at = aperture[block] * size_x + lax.rem(x + size_x, size_x)
        speed, stretch, bending, tilt, azimuth = [source[m, at].astype(F32) for m in range(5)]
        speed = jnp.where(inside, speed, 0.0)
        sin_t, cos_t = sine_cosine(tilt)
        sin_half, cos_half = sine_cosine(0.5 * azimuth)
        normal_x = sin_t * (1.0 - 2.0 * sin_half * sin_half)
        normal_y = sin_t * (2.0 * sin_half * cos_half)
        coefs[0, i] = speed
        coefs[1, i] = speed * (1.0 + 2.0 * stretch)
        coefs[2, i] = speed * jnp.sqrt(1.0 + 2.0 * bending)
        coefs[3, i] = S1 * (normal_x * normal_x)
        coefs[4, i] = S1 * (normal_y * normal_y)
        coefs[5, i] = SECOND_UNIT * (cos_t * cos_t)
        coefs[6, i] = (2.0 * G1 * G1) * (normal_x * normal_y)
        coefs[7, i] = (2.0 * G1 * FIRST_UNIT) * (normal_y * cos_t)
        coefs[8, i] = (2.0 * G1 * FIRST_UNIT) * (normal_x * cos_t)

    loop(place.count, medium, 6)


def injection_kernel(
    columns, size_x, size_y, total_y, source_cell, wavelet, cells, traces, out, hits
):
    place = Place(size_x, columns)
    count, rows = hits.shape[:2]
    number = cells.shape[1]
    row = lax.broadcasted_iota(jnp.int32, (rows, number), 0)
    lane = lax.broadcasted_iota(jnp.int32, (1, number), 1)
    is_source = place.core == 0
    lonely = jnp.where(lane == 0, source_cell[0], -1)
    aims = jnp.where(is_source, lonely, cells[...])
    y = place.at_y * size_y - 4 + row
    valid = jnp.logical_and(y >= 0, y < total_y)

    def mark(i):
        code = jnp.where(valid, (place.start_x + i) * total_y + y, -2)
        hits[i] = jnp.where(code == aims, 1.0, 0.0).astype(BF16)

    loop(count, mark, 2)
    step = lax.broadcasted_iota(jnp.int32, (NT, number), 0)
    amounts = jnp.zeros((NT, number), F32)
    for k in range(NT):
        amounts = jnp.where(step == k, wavelet[:, k : k + 1], amounts)
    backward = jnp.concatenate([traces[k : k + 1] for k in reversed(range(NT))])
    rest = jnp.where(is_source, amounts, backward)
    total = None
    for _ in range(3):
        piece = rest.astype(BF16)
        rest = rest - piece.astype(F32)
        term = lax.dot_general(
            hits[...].reshape(count * rows, number), piece, (((1,), (1,)), ((), ())),
            preferred_element_type=F32,
        )
        total = term if total is None else total + term
    out[...] = total.reshape(count, rows, NT)


def spread_kernel(moment, lanes, out):
    core = lax.rem(lax.axis_index("gx"), 2)
    level = jnp.where(core == 0, SRC_DEPTH, REC_DEPTH)
    mask = (lax.broadcasted_iota(jnp.int32, (lanes.shape[1], 128), 1) == level).astype(F32)

    def expand(i):
        values = lanes[i]
        for k in range(2):
            out[k, i] = values[:, moment + k : moment + k + 1] * mask

    loop(lanes.shape[0], expand, 6)


def sort_kernel(columns, *refs):
    levels, (kept, sent) = refs[: NT - 1], refs[NT - 1 :]
    half, size_y = kept.shape[1:3]
    place = Place(2 * half, columns)

    def level_at(step, start):
        where = levels[step]
        if step % 2 == 0:
            return where[0, pl.ds(start, half)]
        return where[0, pl.ds(place.tile_at + start, half), pl.ds(4, size_y), :]

    for mine in range(2):
        @pl.when(place.core == mine)
        def _():
            for step in range(NT - 1):
                t = step if mine == 0 else NT - step
                if t > 0:
                    kept[t - 1] = level_at(step, mine * half)
                    sent[t - 1] = level_at(step, (1 - mine) * half)


def close_kernel(kept, got, last_kept, last_got, image, field):
    core = lax.rem(lax.axis_index("gx"), 2)
    total = kept[1] * got[1]
    for t in range(2, NT - 2):
        total = total + kept[t] * got[t]

    @pl.when(core == 0)
    def _():
        image[...] = (
            total + kept[0] * last_got[0] + last_kept[0] * got[NT - 2] + last_kept[1] * got[NT - 1]
        ) * (1.0 / NT)
        field[...] = last_got[pl.ds(1, 2)]

    @pl.when(core == 1)
    def _():
        image[...] = (
            total + last_kept[0] * got[0] + kept[NT - 2] * last_got[0] + kept[NT - 1] * last_got[1]
        ) * (1.0 / NT)
        field[...] = last_kept[pl.ds(1, 2)]


def per_device(
    velocity,
    epsilon,
    delta,
    tilt,
    azimuth,
    aperture,
    source_cell,
    wavelet,
    receiver_cell,
    traces,
    source_state,
    receiver_state,
):
    block_x, size_y, _ = velocity.shape
    devices_x, devices_y = lax.axis_size("gx"), lax.axis_size("gy")
    columns = devices_x // 2
    total_x, total_y = block_x * devices_x, size_y * devices_y
    size_x, rows = 2 * block_x, size_y + 8
    is_source = lax.axis_index("gx") % 2 == 0
    place = Place(size_x, columns)
    sides, count = place.sides, place.count
    mats = depth_matrices(128)
    chip_pairs = [even_pairs(columns), odd_pairs(columns)][:sides]
    row_pairs = [even_pairs(devices_y), odd_pairs(devices_y)]
    trade = both_ways([(2 * c, 2 * c + 1) for c in range(columns)])

    def over_gy(values, pairs, opening=False):
        paired = {i for pair in pairs for i in pair}
        alone = [y for y in range(devices_y) if y not in paired]
        swaps = [(x * devices_y + a, x * devices_y + b) for x in range(devices_x) for a, b in pairs]
        swaps += [
            (a * devices_y + y, b * devices_y + y)
            for a, b in (even_pairs(devices_x) if opening else chip_swap(even_pairs(columns)))
            for y in alone
        ]
        return lax.ppermute(values, ("gx", "gy"), both_ways(swaps))

    def over_gx(values, pairs):
        return lax.ppermute(values, "gx", both_ways(chip_swap(pairs)))

    def beside_of(edges):
        return [over_gx(edge, pairs) for edge, pairs in zip(edges, chip_pairs)]

    def near_of(even, odd, opening=False):
        odd = over_gy(odd, row_pairs[1], opening)
        return over_gy(even, row_pairs[0], opening), odd

    def codes(planes, old_rows=0):
        return ((block_size(planes, old_rows), 16, 128), jnp.int16)

    models = [
        values.reshape(block_x // 2, 16, 128) for values in (velocity, epsilon, delta, tilt, azimuth)
    ]
    small = (wavelet[None, :], receiver_cell[None, :], traces)
    rim = ((5, block_x // 4, 16, 128), BF16)
    states = (source_state, receiver_state)
    state = (source_state.shape, F32)
    *rims, own, kept, given, series, cells, data = pl.pallas_call(
        open_kernel,
        out_shape=tuple(
            jax.ShapeDtypeStruct(*out)
            for out in (rim, rim, ((5, block_x // 2, 16, 128), BF16), state, state)
            + tuple((x.shape, x.dtype) for x in small)
        ),
        in_specs=[HBM] * 10,
        out_specs=(VMEM,) * 8,
        scratch_shapes=[pltpu.SemaphoreType.DMA((10,))],
        compiler_params=pltpu.CompilerParams(vmem_limit_bytes=8 * 2**20),
        name="open",
    )(*[pltpu.with_memory_space_constraint(x, pltpu.HBM) for x in (*models, *states, *small)])
    rims = [over_gy(values, pairs, True) for values, pairs in zip(rims, row_pairs)]

    got = lax.ppermute(given, "gx", trade)
    field = ((2, size_x, size_y, 128), F32)
    tile, old, payload, *edges = call(
        functools.partial(first_kernel, columns),
        (field, field, codes(size_x, 8)) + (codes(GROUP, 8),) * sides,
        (), 16, "first", (kept, got),
    )
    number = receiver_cell.shape[0]
    cells, _ = lax.optimization_barrier((cells, edges[0]))
    (amounts,) = call(
        functools.partial(injection_kernel, columns, size_x, size_y, total_y),
        (((count, rows, NT), F32),), (((count, rows, number), BF16),),
        16, "injection", (source_cell, series, cells, data), scalars=1,
    )
    beside = beside_of(edges)
    payload, _ = lax.optimization_barrier((payload, amounts))
    total = block_size(size_x, 4) + sides * block_size(GROUP, 4)
    wide = call(
        cut_kernel, (((total, 16, 128), jnp.int16),) * 2, (), 8, "cut", (payload, *beside)
    )
    near = near_of(*wide[::-1], opening=True)

    def spread(moment, after):
        lanes, _ = lax.optimization_barrier((amounts, after[0]))
        (out,) = call(
            functools.partial(spread_kernel, moment), (((2, count, rows, 128), F32),), (), 8,
            "spread", (lanes,),
        )
        return out

    inject = spread(0, wide)

    rims = lax.optimization_barrier((*rims, edges[0]))[:2]
    (model,) = call(
        join_kernel, (((5, block_x, rows, 128), BF16),), (), 8, "join", (own, *rims), work=1000
    )
    if columns == 2:
        later, _ = lax.optimization_barrier((model, wide[0]))
        across = over_gx(later, chip_pairs[0])
        early, _ = lax.optimization_barrier((model, inject))
        other = lax.ppermute(early, "gx", trade)
        gathered = [model, other, across, lax.ppermute(across, "gx", trade)]
        held = (5, total_x, rows, 128)
    else:
        gathered, held = [lax.all_gather(model, "gx", axis=1, tiled=True)], (16, 128)
    (coefs,) = call(
        functools.partial(setup_kernel, columns, block_x, total_x),
        (((9, count, rows, 128), F32),), ((held, BF16),), 24, "setup", (aperture, *gathered),
        scalars=1, work=0,
    )

    window = ((2, place.wide + 8, 32, 128), F32)
    middle = ((2, count + 8, 24, 128), F32)
    lines = ((2, count, rows, 128), F32)
    levels = [tile]
    for moment in range(0, NT - 2, 2):
        opening = moment == 0
        inject = inject if opening else spread(moment, wide)
        old_wide = (((2, place.wide, rows, 128), F32),) * opening
        around = (((2, AROUND, rows, 128), F32),) * sides
        edge = (((2, GROUP, size_y, 128), F32),) * sides
        fields, *outs = call(
            functools.partial(lead_kernel, opening, columns),
            (window,) + old_wide + around + edge + (codes(GROUP),) * sides,
            [((2, AROUND, 24, 128), F32)] + leap_scratch(AROUND), 24, "lead",
            (tile, old, coefs, inject, *mats, *beside, *near), work=2 * 10**6,
        )
        if opening:
            old, *outs = outs
        beside = beside_of(outs[2 * sides :])
        tile, payload, old = call(
            functools.partial(rest_kernel, opening, columns),
            (field, codes(size_x), lines), [middle] + leap_scratch(place.rest), 24, "rest",
            (tile, old, fields, coefs, inject, *mats, *outs[: 2 * sides]), work=4 * 10**6,
        )
        wide = (jnp.concatenate([payload, *beside]),) * 2
        near = near_of(*wide)
        levels += [old, tile]
    shape = (block_x, size_y, 128)
    inject = spread(NT - 2, wide)
    share = ((NT,) + shape, F32)
    kept, sent = call(
        functools.partial(sort_kernel, columns), (share, share), (), 8, "sort",
        lax.optimization_barrier((*levels, *near, inject))[: NT - 1],
    )
    got = lax.ppermute(sent, "gx", trade)
    share = ((3,) + shape, F32)
    last_kept, last_sent = call(
        functools.partial(last_kernel, columns),
        (share, share), [middle, field, window] + leap_scratch(count), 24, "last",
        (tile, old, coefs, inject, *mats, *beside, *near),
    )
    last_got = lax.ppermute(last_sent, "gx", trade)
    return call(
        close_kernel, ((shape, F32), ((2,) + shape, F32)), (), 8, "close",
        (kept, got, last_kept, last_got),
    )


def solution(mesh):
    in_specs = (
        P("gx", "gy", None),
        P("gx", "gy", None),
        P("gx", "gy", None),
        P("gx", "gy", None),
        P("gx", "gy", None),
        P("shot"),
        P("shot"),
        P("shot"),
        P("shot"),
        P(None, "shot"),
        P(None, ("shot", "gx"), "gy", None),
        P(None, ("shot", "gx"), "gy", None),
    )
    out_specs = (P(("shot", "gx"), "gy", None), P(None, ("shot", "gx"), "gy", None))
    return jax.shard_map(
        per_device, mesh=mesh, in_specs=in_specs, out_specs=out_specs, check_vma=False
    )
```

```python
import functools

import jax
import jax.numpy as jnp
from jax import lax
from jax.experimental import pallas as pl
from jax.experimental.pallas import tpu as pltpu
from jax.sharding import PartitionSpec as P

NT = 8
SRC_DEPTH = 10
REC_DEPTH = 6
F32 = jnp.float32
BF16 = jnp.bfloat16

second_taps = (-205.0 / 72.0, 8.0 / 5.0, -1.0 / 5.0, 8.0 / 315.0, -1.0 / 560.0)
first_taps = (4.0 / 5.0, -1.0 / 5.0, 4.0 / 105.0, -1.0 / 280.0)
CENTRE = second_taps[0]
S1 = second_taps[1]
G1 = first_taps[0]
second_ratio = tuple(tap / S1 for tap in second_taps[2:])
first_ratio = tuple(tap / G1 for tap in first_taps[1:])
second_whole = (8064.0, -1008.0, 128.0, -9.0)
first_whole = (672.0, -168.0, 32.0, -3.0)
SECOND_UNIT = 1.0 / 5040.0
FIRST_UNIT = 1.0 / 840.0
VMEM = pl.BlockSpec(memory_space=pltpu.VMEM)
SMEM = pl.BlockSpec(memory_space=pltpu.SMEM)
HBM = pl.BlockSpec(memory_space=pltpu.HBM)


def even_pairs(count):
    return [(i, i + 1) for i in range(0, count - 1, 2)]


def odd_pairs(count):
    return [(i, i + 1) for i in range(1, count - 1, 2)]


def both_ways(pairs):
    return [pair for a, b in pairs for pair in ((a, b), (b, a))]


def chip_swap(pairs):
    return [(2 * a + c, 2 * b + c) for a, b in pairs for c in range(2)]


class Place:
    def __init__(self, size_x, columns):
        at_x = lax.axis_index("gx")
        self.core, self.column = lax.rem(at_x, 2), lax.div(at_x, 2)
        self.at_y = lax.axis_index("gy")
        self.parity = lax.rem(self.at_y, 2)
        self.has_below = jnp.where(self.at_y > 0, 1.0, 0.0)
        self.has_above = jnp.where(self.at_y < lax.axis_size("gy") - 1, 1.0, 0.0)
        if columns == 2:
            side = self.column
            self.count = size_x + 4
            self.first_at = self.tile_at = 4 * side
            self.start_x = side * (size_x - 4)
            self.beside_at = [size_x * (1 - side)]
            self.edge_at = [(size_x - GROUP) * (1 - side)]
            self.rest_at, self.rest = GROUP * side, size_x - GROUP
            self.first_rest_at = AROUND * side
        else:
            side = lax.rem(self.column, 2)
            self.count = size_x + 8
            self.first_at = self.tile_at = 4
            self.start_x = self.column * size_x - 4
            self.beside_at = [(size_x + GROUP) * (1 - side), (size_x + GROUP) * side]
            self.edge_at = [(size_x - GROUP) * (1 - side), (size_x - GROUP) * side]
            self.rest_at, self.rest = GROUP, size_x - 2 * GROUP
            self.first_rest_at = AROUND
        self.sides = len(self.beside_at)
        self.around_at = [self.tile_at + at - 4 for at in self.edge_at]
        self.own_at = self.first_at + self.tile_at
        self.wide = size_x + GROUP * self.sides


def call(kernel, outs, scratch, mebibytes, name, args, scalars=0, work=10**6):
    outs = tuple(jax.ShapeDtypeStruct(shape, dtype) for shape, dtype in outs)
    return pl.pallas_call(
        kernel,
        out_shape=outs,
        in_specs=[SMEM] * scalars + [VMEM] * (len(args) - scalars),
        out_specs=(VMEM,) * len(outs),
        scratch_shapes=[pltpu.VMEM(shape, dtype) for shape, dtype in scratch],
        compiler_params=pltpu.CompilerParams(vmem_limit_bytes=mebibytes * 2**20),
        cost_estimate=pl.CostEstimate(flops=work, bytes_accessed=work, transcendentals=0),
        name=name,
    )(*args)


def loop(trips, body, wanted):
    unroll = max(u for u in range(1, wanted + 1) if trips % u == 0)

    def step(i, carry):
        body(i)
        return carry

    lax.fori_loop(0, trips, step, 0, unroll=unroll)


def depth_matrices(size):
    rows = jnp.arange(size)[:, None]
    cols = jnp.arange(size)[None, :]
    first = jnp.zeros((size, size), F32)
    second = jnp.zeros((size, size), F32)
    for k in range(1, 5):
        up = (rows == cols + k).astype(F32)
        down = (rows == cols - k).astype(F32)
        first = first + first_whole[k - 1] * (up - down)
        second = second + second_whole[k - 1] * (up + down)
    return (
        jnp.concatenate([first, first]).astype(BF16),
        jnp.concatenate([second, second]).astype(BF16),
    )


def sums_and_slopes(shifted):
    up, down = shifted(1), shifted(-1)
    curve, slope = up + down, up - down
    for k in range(2, 5):
        up, down = shifted(k), shifted(-k)
        curve = curve + second_ratio[k - 2] * (up + down)
        slope = slope + first_ratio[k - 2] * (up - down)
    return curve, slope


def slope_only(shifted):
    slope = shifted(1) - shifted(-1)
    for k in range(2, 5):
        slope = slope + first_ratio[k - 2] * (shifted(k) - shifted(-k))
    return slope


def split(values):
    high = values.astype(BF16)
    low = (values - high.astype(F32)).astype(BF16)
    return high, low


TOP = 32000.0
GROUP = 8
AROUND = GROUP + 8
TILES = GROUP


def block_size(planes, old_rows=0):
    return planes + 1 + planes * old_rows // 8


def scale_of(value_at, planes):
    def grow(i, size):
        for f in range(2):
            size = jnp.maximum(size, jnp.abs(value_at(f, i)))
        return size

    size = lax.fori_loop(0, planes, grow, jnp.full((8, 128), 1e-30, F32), unroll=8)
    code = jnp.ceil(jnp.log2(size) * 256.0)
    return code, TOP * jnp.exp2(code * (-1.0 / 256.0))


def as_code(pieces):
    return jnp.concatenate(pieces).astype(jnp.int32).astype(jnp.int16)


def encode(value_at, planes, out, old_at=None):
    code, factor = scale_of(value_at, planes)
    old_code, old_factor = scale_of(old_at, planes) if old_at else (code, None)

    def put(source, base, by):
        def group(g):
            for f in range(2):
                for q in range(4):
                    pair = [source(f, g * GROUP + 2 * q + v) for v in range(2)]
                    whole = [jnp.floor(value * by + 0.5) for value in pair]
                    out[base + g * TILES + 4 * f + q] = as_code(whole)

        loop(planes // GROUP, group, 1)

    put(value_at, 0, factor)
    out[planes] = as_code([code, old_code])
    if old_at:
        put(old_at, planes + 1, old_factor)


def factor_of(scales, half):
    code = scales.astype(jnp.int32).astype(F32)[8 * half : 8 * half + 8]
    return jnp.exp2(code * (1.0 / 256.0)) * (1.0 / TOP)


def decode(block, base, factor, put):
    for f in range(2):
        for q in range(4):
            both = block[base + 4 * f + q].astype(jnp.int32).astype(F32)
            put(f, 2 * q, both[:8] * factor)
            put(f, 2 * q + 1, both[8:] * factor)


def decode_nearest(block, base, factor, put):
    by = jnp.concatenate([factor] * 4)
    for f in range(2):
        for q in range(2):
            rows = block[base + 2 * f + q].astype(jnp.int32).astype(F32) * by
            for v in range(4):
                put(f, 4 * q + v, rows[4 * v : 4 * v + 4])


def leap(src, x0, row0, rows, count, scratch, mats, coef, old_at, inject_at, store):
    slope_y, curve_y, part, halves, product = scratch
    mat_first, mat_second = mats
    planes = 16 // rows
    group = 4

    def field(f, p, r=0, number=rows):
        return src[f, x0 + p, pl.ds(row0 + r, number), :]

    def joined(values):
        return jnp.concatenate(values) if len(values) > 1 else values[0]

    def put_halves(kind, f, unit, values):
        high, low = split(values)
        halves[kind, f, unit, :, :128] = high
        halves[kind, f, unit, :, 128:] = low

    def along_y(u):
        for f in range(2):
            here, slopes = [], []
            for v in range(planes):
                p = u * planes + v
                curve, slope = sums_and_slopes(lambda k: field(f, p, k))
                slope_y[f, p, :rows] = slope
                curve_y[f, p, :rows] = curve
                slopes.append(slope)
                here.append(field(f, p))
            put_halves(0, f, u, joined(here))
            put_halves(1, f, u, joined(slopes))

    def beyond(p):
        for f in range(2):
            slope_y[f, p, :rows] = slope_only(lambda k: field(f, p, k))

    loop(4, beyond, 4)
    loop(4, lambda p: beyond(count + 4 + p), 4)
    first_unit = 4 // planes
    loop(count // planes, lambda u: along_y(first_unit + u), 24)

    def along_x(q):
        base = q * group
        for f in range(2):
            slopes = [[] for g in range(group)]
            for r in range(0, rows, 8):
                line = [field(f, base + k, r, 8) for k in range(group + 8)]
                slant = [slope_y[f, base + k, pl.ds(r, 8), :] for k in range(group + 8)]
                for g in range(group):
                    i = base + g
                    xx, slope = sums_and_slopes(lambda k: line[g + 4 + k])
                    xy = slope_only(lambda k: slant[g + 4 + k])
                    yy = curve_y[f, i + 4, pl.ds(r, 8), :]
                    wx, wy, wxy = [coef(m, i, r, 8) for m in ((9, 10, 6), (3, 4, 6))[f]]
                    if f == 0:
                        total = (2.0 * CENTRE) * line[g + 4] + wx * xx
                        total = total + wy * yy - wxy * xy
                    else:
                        total = CENTRE * line[g + 4] + wx * xx
                        total = total + wy * yy + wxy * xy
                    part[f, i, pl.ds(r, 8), :] = total
                    slopes[g].append(slope)
            pieces = [piece for rest in slopes for piece in rest]
            for k in range(0, len(pieces), 2):
                put_halves(2, f, q * (len(pieces) // 2) + k // 2, joined(pieces[k : k + 2]))

    loop(count // group, along_x, 10)

    units = count // planes
    for kind, mat, at in ((0, mat_second, 4 // planes), (1, mat_first, 4 // planes), (2, mat_first, 0)):
        for f in range(2):
            both = halves[kind, f, pl.ds(at, units)].reshape(units * 16, 256)
            out = jnp.dot(both, mat[...], preferred_element_type=F32)
            product[kind, f, pl.ds(0, units)] = out.reshape(units, 16, 128)

    def combine(u):
        where = [u * planes + v for v in range(planes)]
        speed, speed_h, speed_v, wz, wyz, wxz, rest_z = [
            joined([coef(m, i, 0, rows) for i in where]) for m in (0, 1, 2, 5, 7, 8, 11)
        ]
        zz, yz, xz = [[product[kind, f, u] for f in range(2)] for kind in range(3)]
        parts = [joined([part[f, i, :rows] for i in where]) for f in range(2)]
        here = [joined([field(f, i + 4) for i in where]) for f in range(2)]
        old = [joined([old_at(f, i) for i in where]) for f in range(2)]
        add = joined([inject_at(i) for i in where])
        flat = parts[0] + rest_z * zz[0] - (wyz * yz[0] + wxz * xz[0])
        tilted = parts[1] + wz * zz[1] + (wyz * yz[1] + wxz * xz[1])
        new_p = (2.0 * here[0] - old[0] + add) + (speed_h * flat + speed_v * tilted)
        new_q = (2.0 * here[1] - old[1] + add) + (speed_v * flat + speed * tilted)
        for v, i in enumerate(where):
            cut = slice(v * rows, v * rows + rows)
            store(i, new_p[cut], new_q[cut])

    loop(units, combine, 36)


def leap_scratch(count):
    lines = (2, count + 8, 16, 128)
    return [
        (lines, F32),
        (lines, F32),
        ((2, count, 16, 128), F32),
        ((3, 2, count + 8, 16, 256), BF16),
        ((3, 2, count, 16, 128), F32),
    ]


def first_kernel(columns, kept, got, tile, old, payload, *edges):
    size = kept.shape[1]
    place = Place(2 * size, columns)
    for source, at in ((kept, place.core * size), (got, (1 - place.core) * size)):
        for f in range(2):
            tile[f, pl.ds(at, size)] = source[2 * f]
            old[f, pl.ds(at, size)] = source[2 * f + 1]

    encode(lambda f, p: tile[f, p], 2 * size, payload, lambda f, p: old[f, p])
    for k, edge in enumerate(edges):
        group = lax.div(place.edge_at[k], GROUP) * TILES
        for base in (0, 2 * size + 1):
            edge[pl.ds(base and GROUP + 1, TILES)] = payload[pl.ds(base + group, TILES)]
        edge[GROUP] = payload[2 * size]


def cut_kernel(payload, *refs):
    beside, (odd, even) = refs[:-2], refs[-2:]
    parity = lax.rem(lax.axis_index("gy"), 2)

    def cut(out, row):
        base = 0
        for block in (payload, *beside):
            planes = block.shape[0] // 2
            out[pl.ds(base, planes + 1)] = block[: planes + 1]
            for u in range(0, planes, 2):
                pairs = [block[planes + 1 + u + v].astype(jnp.int32) for v in range(2)]
                rows = [pair[r + row : r + row + 4] for pair in pairs for r in (0, 8)]
                out[base + planes + 1 + u // 2] = jnp.concatenate(rows).astype(jnp.int16)
            base += block_size(planes, 4)

    @pl.when(parity == 0)
    def _():
        cut(even, 4)
        cut(odd, 0)

    @pl.when(parity == 1)
    def _():
        cut(odd, 4)
        cut(even, 0)


def first_leap(place, start, count, window, old, old_start, coefs, inject, scratch, mats, store):
    leap(
        window, place.first_at + start, 8, coefs.shape[2], count, scratch, mats,
        lambda m, i, r, number: coefs[m, start + i, pl.ds(r, number), :],
        lambda f, i: old[f, old_start + start + i],
        lambda i: inject[0, start + i],
        store,
    )


def second_leap(
    place, start, count, source, source_start, tile, coefs, inject, scratch, mats, store
):
    rows = tile.shape[2]
    at = place.tile_at + start
    leap(
        source, source_start, 8, rows, count, scratch, mats,
        lambda m, i, r, number: coefs[m, at + i, pl.ds(4 + r, number), :],
        lambda f, i: tile[f, start + i],
        lambda i: inject[1, at + i, pl.ds(4, rows), :],
        store,
    )


def fill(place, tile, old, beside, even, odd, window, old_wide):
    size_x = tile.shape[1]
    opening = old_wide is not None
    for f in range(2):
        window[f, pl.ds(0, 4)] = jnp.zeros((4, 32, 128), F32)
        window[f, pl.ds(place.wide + 4, 4)] = jnp.zeros((4, 32, 128), F32)
        window[f, pl.ds(place.own_at + 4, size_x), pl.ds(12, 8), :] = tile[f]
        if opening:
            old_wide[f, pl.ds(place.own_at, size_x), pl.ds(4, 8), :] = old[f]

    def lay(block, base, planes, at, row):
        there = {-8: place.has_below, 0: 1.0, 8: place.has_above}[row]
        factor = factor_of(block[base + planes], 0) * there

        def group(g):
            def put(f, p, rows):
                window[f, at + g * GROUP + p + 4, pl.ds(row + 12, 8), :] = rows

            decode(block, base + g * TILES, factor, put)

        loop(planes // GROUP, group, 2)
        if not opening:
            return
        factor = factor_of(block[base + planes], 1) * there

        def old_group(g):
            def put(f, p, rows):
                first = 0 if row < 0 else row + 4
                old_wide[f, at + g * GROUP + p, pl.ds(first, rows.shape[0]), :] = rows

            start = base + planes + 1
            if row == 0:
                decode(block, start + g * TILES, factor, put)
            else:
                near = factor[4:] if row < 0 else factor[:4]
                decode_nearest(block, start + g * (TILES // 2), near, put)

        loop(planes // GROUP, old_group, 2)

    for k in range(place.sides):
        lay(beside[k], 0, GROUP, place.beside_at[k], 0)

    def lay_y(below, above):
        kept = 4 if opening else 0
        for block, row in ((below, -8), (above, 8)):
            lay(block, 0, size_x, place.own_at, row)
            for k in range(place.sides):
                base = block_size(size_x, kept) + k * block_size(GROUP, kept)
                lay(block, base, GROUP, place.beside_at[k], row)

    pl.when(place.parity == 0)(lambda: lay_y(odd, even))
    pl.when(place.parity == 1)(lambda: lay_y(even, odd))


def lead_kernel(opening, columns, tile, old, coefs, inject, mat_first, mat_second, *refs):
    place = Place(tile.shape[1], columns)
    refs = list(refs)

    def take(number):
        taken = refs[:number]
        del refs[:number]
        return taken

    sides = place.sides
    beside = take(sides)
    even, odd, window = take(3)
    old_wide = take(1)[0] if opening else None
    around_out, edges_out, codes_out = take(sides), take(sides), take(sides)
    middle = take(1)[0]
    scratch, mats = refs, (mat_first, mat_second)
    fill(place, tile, old, beside, even, odd, window, old_wide)
    for k in range(sides):
        def store_around(i, new_p, new_q):
            for f, new in enumerate((new_p, new_q)):
                around_out[k][f, i] = new
                middle[f, i, pl.ds(4, new.shape[0]), :] = new

        def store_edge(i, new_p, new_q):
            edges_out[k][0, i] = new_p
            edges_out[k][1, i] = new_q

        first_leap(
            place, place.around_at[k], AROUND, window, old_wide if opening else old,
            place.first_at if opening else 0, coefs, inject, scratch, mats, store_around,
        )
        second_leap(
            place, place.edge_at[k], GROUP, middle, 0, tile, coefs, inject, scratch, mats,
            store_edge,
        )
        encode(lambda f, p: edges_out[k][f, p], GROUP, codes_out[k])


def rest_kernel(opening, columns, tile, old, window, coefs, inject, mat_first, mat_second, *refs):
    size_x, size_y = tile.shape[1], tile.shape[2]
    place = Place(size_x, columns)
    sides, count = place.sides, place.count
    around, edges = refs[:sides], refs[sides : 2 * sides]
    tile_out, payload, old_out, middle, *scratch = refs[2 * sides :]
    mats = (mat_first, mat_second)
    for f in range(2):
        middle[f, pl.ds(0, 4)] = jnp.zeros((4, 24, 128), F32)
        middle[f, pl.ds(count + 4, 4)] = jnp.zeros((4, 24, 128), F32)
        for k in range(sides):
            at = place.around_at[k]
            middle[f, pl.ds(at + 4, AROUND), pl.ds(4, size_y + 8), :] = around[k][f]
            old_out[f, pl.ds(at, AROUND)] = around[k][f]
            tile_out[f, pl.ds(place.edge_at[k], GROUP)] = edges[k][f]

    def store_first(i, new_p, new_q):
        for f, new in enumerate((new_p, new_q)):
            old_out[f, place.first_rest_at + i] = new
            middle[f, place.first_rest_at + i + 4, pl.ds(4, size_y + 8), :] = new

    def store_second(i, new_p, new_q):
        tile_out[0, place.rest_at + i] = new_p
        tile_out[1, place.rest_at + i] = new_q

    first_leap(
        place, place.first_rest_at, count - AROUND * sides, window, old,
        place.first_at if opening else 0, coefs, inject, scratch, mats, store_first,
    )
    second_leap(
        place, place.rest_at, place.rest, middle, place.tile_at + place.rest_at, tile, coefs,
        inject, scratch, mats, store_second,
    )
    encode(lambda f, p: tile_out[f, p], size_x, payload)


def last_kernel(columns, tile, old, coefs, inject, mat_first, mat_second, *refs):
    size_x, size_y = tile.shape[1], tile.shape[2]
    place = Place(size_x, columns)
    sides, count = place.sides, place.count
    even, odd, kept, sent, middle, tile_out, window, *scratch = refs[sides:]
    mats = (mat_first, mat_second)
    fill(place, tile, old, refs[:sides], even, odd, window, None)
    for f in range(2):
        middle[f, pl.ds(0, 4)] = jnp.zeros((4, 24, 128), F32)
        middle[f, pl.ds(count + 4, 4)] = jnp.zeros((4, 24, 128), F32)

    def store_first(i, new_p, new_q):
        for f, new in enumerate((new_p, new_q)):
            middle[f, i + 4, pl.ds(4, size_y + 8), :] = new

    def store_second(i, new_p, new_q):
        tile_out[0, i] = new_p
        tile_out[1, i] = new_q

    first_leap(place, 0, count, window, old, 0, coefs, inject, scratch, mats, store_first)
    second_leap(
        place, 0, size_x, middle, place.tile_at, tile, coefs, inject, scratch, mats, store_second
    )
    half = size_x // 2
    for mine in range(2):
        @pl.when(place.core == mine)
        def _():
            for out, start in ((kept, mine * half), (sent, (1 - mine) * half)):
                planes = pl.ds(start, half)
                inner = pl.ds(place.tile_at + 4 + start, half)
                out[0] = middle[0, inner, pl.ds(8, size_y), :]
                out[1] = tile_out[0, planes]
                out[2] = tile_out[1, planes]


def sine_cosine(angle):
    square = angle * angle
    sine = 1.0 / 6227020800.0
    for factor in (-1.0 / 39916800.0, 1.0 / 362880.0, -1.0 / 5040.0, 1.0 / 120.0, -1.0 / 6.0):
        sine = sine * square + factor
    sine = angle + angle * square * sine
    cosine = 1.0 / 479001600.0
    for factor in (-1.0 / 3628800.0, 1.0 / 40320.0, -1.0 / 720.0, 1.0 / 24.0, -0.5):
        cosine = cosine * square + factor
    return sine, 1.0 + square * cosine


def open_kernel(
    velocity, epsilon, delta, tilt, azimuth, source, receiver, *refs
):
    models = (velocity, epsilon, delta, tilt, azimuth)
    parity = lax.rem(lax.axis_index("gy"), 2)
    core = lax.rem(lax.axis_index("gx"), 2)
    small, (even, odd, own, kept, given), brought, arrived = (
        refs[:3], refs[3:8], refs[8:11], refs[11]
    )
    copies = [pltpu.make_async_copy(models[m], own.at[m], arrived.at[m]) for m in range(5)]
    others = [
        pltpu.make_async_copy(small[m], brought[m], arrived.at[7 + m]) for m in range(3)
    ]

    def states(mine):
        stay, leave = (source, receiver) if mine == 0 else (receiver, source)
        return (
            pltpu.make_async_copy(stay, kept, arrived.at[5]),
            pltpu.make_async_copy(leave, given, arrived.at[6]),
        )

    for copy in copies + others:
        copy.start()
    for mine in range(2):
        @pl.when(core == mine)
        def _():
            for copy in states(mine):
                copy.start()

    for copy in copies:
        copy.wait()

    def pack(out, row):
        for m in range(5):
            for u in range(0, own.shape[1], 2):
                pairs = [own[m, u + k].astype(F32) for k in range(2)]
                values = [pair[v + row : v + row + 4] for pair in pairs for v in (0, 8)]
                out[m, u // 2] = jnp.concatenate(values).astype(BF16)

    @pl.when(parity == 0)
    def _():
        pack(even, 4)
        pack(odd, 0)

    @pl.when(parity == 1)
    def _():
        pack(odd, 4)
        pack(even, 0)

    for mine in range(2):
        @pl.when(core == mine)
        def _():
            for copy in states(mine):
                copy.wait()
    for copy in others:
        copy.wait()


def join_kernel(own, even, odd, out):
    at_y = lax.axis_index("gy")
    parity = lax.rem(at_y, 2)
    has_below = jnp.where(at_y > 0, 1.0, 0.0)
    has_above = jnp.where(at_y < lax.axis_size("gy") - 1, 1.0, 0.0)

    def fill(below, above):
        for m in range(5):
            for u in range(own.shape[1]):
                low = below[m, u // 2].astype(F32) * has_below
                high = above[m, u // 2].astype(F32) * has_above
                pair = own[m, u].astype(F32)
                for v in range(2):
                    k = 2 * (u % 2) + v
                    rows = [low[4 * k : 4 * k + 4], pair[8 * v : 8 * v + 8], high[4 * k : 4 * k + 4]]
                    out[m, 2 * u + v] = jnp.concatenate(rows).astype(BF16)

    pl.when(parity == 0)(lambda: fill(odd, even))
    pl.when(parity == 1)(lambda: fill(even, odd))


def setup_kernel(columns, size_x, total_x, aperture, *refs):
    models, coefs, blocks = refs[:-2], refs[-2], refs[-1]
    place = Place(2 * size_x, columns)
    if len(models) > 1:
        for k, column in enumerate((place.column, 1 - place.column)):
            for j, core in enumerate((place.core, 1 - place.core)):
                blocks[:, pl.ds((2 * column + core) * size_x, size_x)] = models[2 * k + j][...]
        source = blocks
    else:
        source = models[0]

    def medium(i):
        x = place.start_x + i
        block = jnp.clip(x // size_x, 0, total_x // size_x - 1)
        inside = jnp.logical_and(x >= 0, x < total_x)
        at = aperture[block] * size_x + lax.rem(x + size_x, size_x)
        speed, stretch, bending, tilt, azimuth = [source[m, at].astype(F32) for m in range(5)]
        speed = jnp.where(inside, speed, 0.0)
        sin_t, cos_t = sine_cosine(tilt)
        sin_half, cos_half = sine_cosine(0.5 * azimuth)
        normal_x = sin_t * (1.0 - 2.0 * sin_half * sin_half)
        normal_y = sin_t * (2.0 * sin_half * cos_half)
        coefs[0, i] = speed
        coefs[1, i] = speed * (1.0 + 2.0 * stretch)
        coefs[2, i] = speed * jnp.sqrt(1.0 + 2.0 * bending)
        weights = (S1 * (normal_x * normal_x), S1 * (normal_y * normal_y), SECOND_UNIT * (cos_t * cos_t))
        for m, unit in enumerate((S1, S1, SECOND_UNIT)):
            coefs[3 + m, i] = weights[m]
            coefs[9 + m, i] = unit - weights[m]
        coefs[6, i] = (2.0 * G1 * G1) * (normal_x * normal_y)
        coefs[7, i] = (2.0 * G1 * FIRST_UNIT) * (normal_y * cos_t)
        coefs[8, i] = (2.0 * G1 * FIRST_UNIT) * (normal_x * cos_t)

    loop(place.count, medium, 12)


def injection_kernel(
    columns, size_x, size_y, total_y, source_cell, wavelet, cells, traces, out, hits
):
    place = Place(size_x, columns)
    count, rows = hits.shape[:2]
    number = cells.shape[1]
    row = lax.broadcasted_iota(jnp.int32, (rows, number), 0)
    lane = lax.broadcasted_iota(jnp.int32, (1, number), 1)
    is_source = place.core == 0
    lonely = jnp.where(lane == 0, source_cell[0], -1)
    aims = jnp.where(is_source, lonely, cells[...])
    y = place.at_y * size_y - 4 + row
    valid = jnp.logical_and(y >= 0, y < total_y)

    def mark(i):
        code = jnp.where(valid, (place.start_x + i) * total_y + y, -2)
        hits[i] = jnp.where(code == aims, 1.0, 0.0).astype(BF16)

    loop(count, mark, 2)
    step = lax.broadcasted_iota(jnp.int32, (NT, number), 0)
    amounts = jnp.zeros((NT, number), F32)
    for k in range(NT):
        amounts = jnp.where(step == k, wavelet[:, k : k + 1], amounts)
    backward = jnp.concatenate([traces[k : k + 1] for k in reversed(range(NT))])
    rest = jnp.where(is_source, amounts, backward)
    total = None
    for _ in range(3):
        piece = rest.astype(BF16)
        rest = rest - piece.astype(F32)
        term = lax.dot_general(
            hits[...].reshape(count * rows, number), piece, (((1,), (1,)), ((), ())),
            preferred_element_type=F32,
        )
        total = term if total is None else total + term
    out[...] = total.reshape(count, rows, NT)


def spread_kernel(moment, lanes, out):
    core = lax.rem(lax.axis_index("gx"), 2)
    level = jnp.where(core == 0, SRC_DEPTH, REC_DEPTH)
    mask = (lax.broadcasted_iota(jnp.int32, (lanes.shape[1], 128), 1) == level).astype(F32)

    def expand(i):
        values = lanes[i]
        for k in range(2):
            out[k, i] = values[:, moment + k : moment + k + 1] * mask

    loop(lanes.shape[0], expand, 6)


def sort_kernel(columns, *refs):
    levels, (kept, sent) = refs[: NT - 1], refs[NT - 1 :]
    half, size_y = kept.shape[1:3]
    place = Place(2 * half, columns)

    def level_at(step, start):
        where = levels[step]
        if step % 2 == 0:
            return where[0, pl.ds(start, half)]
        return where[0, pl.ds(place.tile_at + start, half), pl.ds(4, size_y), :]

    for mine in range(2):
        @pl.when(place.core == mine)
        def _():
            for step in range(NT - 1):
                t = step if mine == 0 else NT - step
                if t > 0:
                    kept[t - 1] = level_at(step, mine * half)
                    sent[t - 1] = level_at(step, (1 - mine) * half)


def close_kernel(kept, got, last_kept, last_got, image, field):
    core = lax.rem(lax.axis_index("gx"), 2)
    total = kept[1] * got[1]
    for t in range(2, NT - 2):
        total = total + kept[t] * got[t]

    @pl.when(core == 0)
    def _():
        image[...] = (
            total + kept[0] * last_got[0] + last_kept[0] * got[NT - 2] + last_kept[1] * got[NT - 1]
        ) * (1.0 / NT)
        field[...] = last_got[pl.ds(1, 2)]

    @pl.when(core == 1)
    def _():
        image[...] = (
            total + last_kept[0] * got[0] + kept[NT - 2] * last_got[0] + kept[NT - 1] * last_got[1]
        ) * (1.0 / NT)
        field[...] = last_kept[pl.ds(1, 2)]


def per_device(
    velocity,
    epsilon,
    delta,
    tilt,
    azimuth,
    aperture,
    source_cell,
    wavelet,
    receiver_cell,
    traces,
    source_state,
    receiver_state,
):
    block_x, size_y, _ = velocity.shape
    devices_x, devices_y = lax.axis_size("gx"), lax.axis_size("gy")
    columns = devices_x // 2
    total_x, total_y = block_x * devices_x, size_y * devices_y
    size_x, rows = 2 * block_x, size_y + 8
    is_source = lax.axis_index("gx") % 2 == 0
    place = Place(size_x, columns)
    sides, count = place.sides, place.count
    mats = depth_matrices(128)
    chip_pairs = [even_pairs(columns), odd_pairs(columns)][:sides]
    row_pairs = [even_pairs(devices_y), odd_pairs(devices_y)]
    trade = both_ways([(2 * c, 2 * c + 1) for c in range(columns)])

    def over_gy(values, pairs, opening=False):
        paired = {i for pair in pairs for i in pair}
        alone = [y for y in range(devices_y) if y not in paired]
        swaps = [(x * devices_y + a, x * devices_y + b) for x in range(devices_x) for a, b in pairs]
        swaps += [
            (a * devices_y + y, b * devices_y + y)
            for a, b in (even_pairs(devices_x) if opening else chip_swap(even_pairs(columns)))
            for y in alone
        ]
        return lax.ppermute(values, ("gx", "gy"), both_ways(swaps))

    def over_gx(values, pairs):
        return lax.ppermute(values, "gx", both_ways(chip_swap(pairs)))

    def beside_of(edges):
        return [over_gx(edge, pairs) for edge, pairs in zip(edges, chip_pairs)]

    def near_of(even, odd, opening=False):
        odd = over_gy(odd, row_pairs[1], opening)
        return over_gy(even, row_pairs[0], opening), odd

    def codes(planes, old_rows=0):
        return ((block_size(planes, old_rows), 16, 128), jnp.int16)

    models = [
        values.reshape(block_x // 2, 16, 128) for values in (velocity, epsilon, delta, tilt, azimuth)
    ]
    small = (wavelet[None, :], receiver_cell[None, :], traces)
    rim = ((5, block_x // 4, 16, 128), BF16)
    states = (source_state, receiver_state)
    state = (source_state.shape, F32)
    *rims, own, kept, given, series, cells, data = pl.pallas_call(
        open_kernel,
        out_shape=tuple(
            jax.ShapeDtypeStruct(*out)
            for out in (rim, rim, ((5, block_x // 2, 16, 128), BF16), state, state)
            + tuple((x.shape, x.dtype) for x in small)
        ),
        in_specs=[HBM] * 10,
        out_specs=(VMEM,) * 8,
        scratch_shapes=[pltpu.SemaphoreType.DMA((10,))],
        compiler_params=pltpu.CompilerParams(vmem_limit_bytes=8 * 2**20),
        name="open",
    )(*[pltpu.with_memory_space_constraint(x, pltpu.HBM) for x in (*models, *states, *small)])
    rims = [over_gy(values, pairs, True) for values, pairs in zip(rims, row_pairs)]

    got = lax.ppermute(given, "gx", trade)
    field = ((2, size_x, size_y, 128), F32)
    tile, old, payload, *edges = call(
        functools.partial(first_kernel, columns),
        (field, field, codes(size_x, 8)) + (codes(GROUP, 8),) * sides,
        (), 16, "first", (kept, got),
    )
    number = receiver_cell.shape[0]
    cells, _ = lax.optimization_barrier((cells, edges[0]))
    (amounts,) = call(
        functools.partial(injection_kernel, columns, size_x, size_y, total_y),
        (((count, rows, NT), F32),), (((count, rows, number), BF16),),
        16, "injection", (source_cell, series, cells, data), scalars=1,
    )
    beside = beside_of(edges)
    payload, _ = lax.optimization_barrier((payload, amounts))
    total = block_size(size_x, 4) + sides * block_size(GROUP, 4)
    wide = call(
        cut_kernel, (((total, 16, 128), jnp.int16),) * 2, (), 8, "cut", (payload, *beside)
    )
    near = near_of(*wide[::-1], opening=True)

    def spread(moment, after):
        lanes, _ = lax.optimization_barrier((amounts, after[0]))
        (out,) = call(
            functools.partial(spread_kernel, moment), (((2, count, rows, 128), F32),), (), 8,
            "spread", (lanes,),
        )
        return out

    inject = spread(0, wide)

    rims = lax.optimization_barrier((*rims, edges[0]))[:2]
    (model,) = call(
        join_kernel, (((5, block_x, rows, 128), BF16),), (), 8, "join", (own, *rims), work=1000
    )
    if columns == 2:
        later, _ = lax.optimization_barrier((model, wide[0]))
        across = over_gx(later, chip_pairs[0])
        early, _ = lax.optimization_barrier((model, inject))
        other = lax.ppermute(early, "gx", trade)
        gathered = [model, other, across, lax.ppermute(across, "gx", trade)]
        held = (5, total_x, rows, 128)
    else:
        gathered, held = [lax.all_gather(model, "gx", axis=1, tiled=True)], (16, 128)
    (coefs,) = call(
        functools.partial(setup_kernel, columns, block_x, total_x),
        (((12, count, rows, 128), F32),), ((held, BF16),), 24, "setup", (aperture, *gathered),
        scalars=1, work=0,
    )

    window = ((2, place.wide + 8, 32, 128), F32)
    middle = ((2, count + 8, 24, 128), F32)
    lines = ((2, count, rows, 128), F32)
    levels = [tile]
    for moment in range(0, NT - 2, 2):
        opening = moment == 0
        inject = inject if opening else spread(moment, wide)
        old_wide = (((2, place.wide, rows, 128), F32),) * opening
        around = (((2, AROUND, rows, 128), F32),) * sides
        edge = (((2, GROUP, size_y, 128), F32),) * sides
        fields, *outs = call(
            functools.partial(lead_kernel, opening, columns),
            (window,) + old_wide + around + edge + (codes(GROUP),) * sides,
            [((2, AROUND, 24, 128), F32)] + leap_scratch(AROUND), 24, "lead",
            (tile, old, coefs, inject, *mats, *beside, *near), work=2 * 10**6,
        )
        if opening:
            old, *outs = outs
        beside = beside_of(outs[2 * sides :])
        tile, payload, old = call(
            functools.partial(rest_kernel, opening, columns),
            (field, codes(size_x), lines), [middle] + leap_scratch(place.rest), 24, "rest",
            (tile, old, fields, coefs, inject, *mats, *outs[: 2 * sides]), work=4 * 10**6,
        )
        wide = (jnp.concatenate([payload, *beside]),) * 2
        near = near_of(*wide)
        levels += [old, tile]
    shape = (block_x, size_y, 128)
    inject = spread(NT - 2, wide)
    share = ((NT,) + shape, F32)
    kept, sent = call(
        functools.partial(sort_kernel, columns), (share, share), (), 8, "sort",
        lax.optimization_barrier((*levels, *near, inject))[: NT - 1],
    )
    got = lax.ppermute(sent, "gx", trade)
    share = ((3,) + shape, F32)
    last_kept, last_sent = call(
        functools.partial(last_kernel, columns),
        (share, share), [middle, field, window] + leap_scratch(count), 24, "last",
        (tile, old, coefs, inject, *mats, *beside, *near),
    )
    last_got = lax.ppermute(last_sent, "gx", trade)
    return call(
        close_kernel, ((shape, F32), ((2,) + shape, F32)), (), 8, "close",
        (kept, got, last_kept, last_got),
    )


def solution(mesh):
    in_specs = (
        P("gx", "gy", None),
        P("gx", "gy", None),
        P("gx", "gy", None),
        P("gx", "gy", None),
        P("gx", "gy", None),
        P("shot"),
        P("shot"),
        P("shot"),
        P("shot"),
        P(None, "shot"),
        P(None, ("shot", "gx"), "gy", None),
        P(None, ("shot", "gx"), "gy", None),
    )
    out_specs = (P(("shot", "gx"), "gy", None), P(None, ("shot", "gx"), "gy", None))
    return jax.shard_map(
        per_device, mesh=mesh, in_specs=in_specs, out_specs=out_specs, check_vma=False
    )
```

```python
import functools

import jax
import jax.numpy as jnp
from jax import lax
from jax.experimental import pallas as pl
from jax.experimental.pallas import tpu as pltpu
from jax.sharding import PartitionSpec as P

NT = 8
SRC_DEPTH = 10
REC_DEPTH = 6
F32 = jnp.float32
BF16 = jnp.bfloat16

second_taps = (-205.0 / 72.0, 8.0 / 5.0, -1.0 / 5.0, 8.0 / 315.0, -1.0 / 560.0)
first_taps = (4.0 / 5.0, -1.0 / 5.0, 4.0 / 105.0, -1.0 / 280.0)
CENTRE = second_taps[0]
S1 = second_taps[1]
G1 = first_taps[0]
second_ratio = tuple(tap / S1 for tap in second_taps[2:])
first_ratio = tuple(tap / G1 for tap in first_taps[1:])
second_whole = (8064.0, -1008.0, 128.0, -9.0)
first_whole = (672.0, -168.0, 32.0, -3.0)
SECOND_UNIT = 1.0 / 5040.0
FIRST_UNIT = 1.0 / 840.0
VMEM = pl.BlockSpec(memory_space=pltpu.VMEM)
SMEM = pl.BlockSpec(memory_space=pltpu.SMEM)
HBM = pl.BlockSpec(memory_space=pltpu.HBM)


def even_pairs(count):
    return [(i, i + 1) for i in range(0, count - 1, 2)]


def odd_pairs(count):
    return [(i, i + 1) for i in range(1, count - 1, 2)]


def both_ways(pairs):
    return [pair for a, b in pairs for pair in ((a, b), (b, a))]


def chip_swap(pairs):
    return [(2 * a + c, 2 * b + c) for a, b in pairs for c in range(2)]


class Place:
    def __init__(self, size_x, columns):
        at_x = lax.axis_index("gx")
        self.core, self.column = lax.rem(at_x, 2), lax.div(at_x, 2)
        self.at_y = lax.axis_index("gy")
        self.parity = lax.rem(self.at_y, 2)
        self.has_below = jnp.where(self.at_y > 0, 1.0, 0.0)
        self.has_above = jnp.where(self.at_y < lax.axis_size("gy") - 1, 1.0, 0.0)
        if columns == 2:
            side = self.column
            self.count = size_x + 4
            self.first_at = self.tile_at = 4 * side
            self.start_x = side * (size_x - 4)
            self.beside_at = [size_x * (1 - side)]
            self.edge_at = [(size_x - GROUP) * (1 - side)]
            self.rest_at, self.rest = GROUP * side, size_x - GROUP
            self.first_rest_at = AROUND * side
            groups = size_x // GROUP
            self.lead_groups = ((groups - 2) * (1 - side), 2)
            self.rest_groups = (side, groups - 1)
        else:
            side = lax.rem(self.column, 2)
            self.count = size_x + 8
            self.first_at = self.tile_at = 4
            self.start_x = self.column * size_x - 4
            self.beside_at = [(size_x + GROUP) * (1 - side), (size_x + GROUP) * side]
            self.edge_at = [(size_x - GROUP) * (1 - side), (size_x - GROUP) * side]
            self.rest_at, self.rest = GROUP, size_x - 2 * GROUP
            self.first_rest_at = AROUND
            self.lead_groups = self.rest_groups = (0, size_x // GROUP)
        self.sides = len(self.beside_at)
        self.around_at = [self.tile_at + at - 4 for at in self.edge_at]
        self.own_at = self.first_at + self.tile_at
        self.wide = size_x + GROUP * self.sides


def call(kernel, outs, scratch, mebibytes, name, args, scalars=0, work=10**6):
    outs = tuple(jax.ShapeDtypeStruct(shape, dtype) for shape, dtype in outs)
    return pl.pallas_call(
        kernel,
        out_shape=outs,
        in_specs=[SMEM] * scalars + [VMEM] * (len(args) - scalars),
        out_specs=(VMEM,) * len(outs),
        scratch_shapes=[pltpu.VMEM(shape, dtype) for shape, dtype in scratch],
        compiler_params=pltpu.CompilerParams(vmem_limit_bytes=mebibytes * 2**20),
        cost_estimate=pl.CostEstimate(flops=work, bytes_accessed=work, transcendentals=0),
        name=name,
    )(*args)


def loop(trips, body, wanted):
    unroll = max(u for u in range(1, wanted + 1) if trips % u == 0)

    def step(i, carry):
        body(i)
        return carry

    lax.fori_loop(0, trips, step, 0, unroll=unroll)


def depth_matrices(size):
    rows = jnp.arange(size)[:, None]
    cols = jnp.arange(size)[None, :]
    first = jnp.zeros((size, size), F32)
    second = jnp.zeros((size, size), F32)
    for k in range(1, 5):
        up = (rows == cols + k).astype(F32)
        down = (rows == cols - k).astype(F32)
        first = first + first_whole[k - 1] * (up - down)
        second = second + second_whole[k - 1] * (up + down)
    return (
        jnp.concatenate([first, first]).astype(BF16),
        jnp.concatenate([second, second]).astype(BF16),
    )


def sums_and_slopes(shifted):
    up, down = shifted(1), shifted(-1)
    curve, slope = up + down, up - down
    for k in range(2, 5):
        up, down = shifted(k), shifted(-k)
        curve = curve + second_ratio[k - 2] * (up + down)
        slope = slope + first_ratio[k - 2] * (up - down)
    return curve, slope


def slope_only(shifted):
    slope = shifted(1) - shifted(-1)
    for k in range(2, 5):
        slope = slope + first_ratio[k - 2] * (shifted(k) - shifted(-k))
    return slope


def split(values):
    high = values.astype(BF16)
    low = (values - high.astype(F32)).astype(BF16)
    return high, low


TOP = 32000.0
GROUP = 8
AROUND = GROUP + 8
TILES = GROUP


def block_size(planes, old_rows=0):
    return planes + 1 + planes * old_rows // 8


def scale_of(value_at, planes):
    def grow(i, size):
        for f in range(2):
            size = jnp.maximum(size, jnp.abs(value_at(f, i)))
        return size

    size = lax.fori_loop(0, planes, grow, jnp.full((8, 128), 1e-30, F32), unroll=8)
    code = jnp.ceil(jnp.log2(size) * 256.0)
    return code, TOP * jnp.exp2(code * (-1.0 / 256.0))


def as_code(pieces):
    return jnp.concatenate(pieces).astype(jnp.int32).astype(jnp.int16)


def encode(value_at, planes, out, old_at=None):
    code, factor = scale_of(value_at, planes)
    old_code, old_factor = scale_of(old_at, planes) if old_at else (code, None)

    def put(source, base, by):
        def group(g):
            for f in range(2):
                for q in range(4):
                    pair = [source(f, g * GROUP + 2 * q + v) for v in range(2)]
                    whole = [jnp.floor(value * by + 0.5) for value in pair]
                    out[base + g * TILES + 4 * f + q] = as_code(whole)

        loop(planes // GROUP, group, 1)

    put(value_at, 0, factor)
    out[planes] = as_code([code, old_code])
    if old_at:
        put(old_at, planes + 1, old_factor)


def factor_of(scales, half):
    code = scales.astype(jnp.int32).astype(F32)[8 * half : 8 * half + 8]
    return jnp.exp2(code * (1.0 / 256.0)) * (1.0 / TOP)


def decode(block, base, factor, put):
    for f in range(2):
        for q in range(4):
            both = block[base + 4 * f + q].astype(jnp.int32).astype(F32)
            put(f, 2 * q, both[:8] * factor)
            put(f, 2 * q + 1, both[8:] * factor)


def decode_nearest(block, base, factor, put):
    by = jnp.concatenate([factor] * 4)
    for f in range(2):
        for q in range(2):
            rows = block[base + 2 * f + q].astype(jnp.int32).astype(F32) * by
            for v in range(4):
                put(f, 4 * q + v, rows[4 * v : 4 * v + 4])


def leap(src, x0, row0, rows, count, scratch, mats, coef, old_at, inject_at, store):
    slope_y, curve_y, part, halves, product = scratch
    mat_first, mat_second = mats
    planes = 16 // rows
    group = 4

    def field(f, p, r=0, number=rows):
        return src[f, x0 + p, pl.ds(row0 + r, number), :]

    def joined(values):
        return jnp.concatenate(values) if len(values) > 1 else values[0]

    def put_halves(kind, f, unit, values):
        high, low = split(values)
        halves[kind, f, unit, :, :128] = high
        halves[kind, f, unit, :, 128:] = low

    def along_y(u):
        for f in range(2):
            here, slopes = [], []
            for v in range(planes):
                p = u * planes + v
                curve, slope = sums_and_slopes(lambda k: field(f, p, k))
                slope_y[f, p, :rows] = slope
                curve_y[f, p, :rows] = curve
                slopes.append(slope)
                here.append(field(f, p))
            put_halves(0, f, u, joined(here))
            put_halves(1, f, u, joined(slopes))

    loop((count + 8) // planes, along_y, 24)

    def along_x(q):
        base = q * group
        for f in range(2):
            slopes = [[] for g in range(group)]
            for r in range(0, rows, 8):
                line = [field(f, base + k, r, 8) for k in range(group + 8)]
                slant = [slope_y[f, base + k, pl.ds(r, 8), :] for k in range(group + 8)]
                for g in range(group):
                    i = base + g
                    xx, slope = sums_and_slopes(lambda k: line[g + 4 + k])
                    xy = slope_only(lambda k: slant[g + 4 + k])
                    yy = curve_y[f, i + 4, pl.ds(r, 8), :]
                    wx, wy, wxy = [coef(m, i, r, 8) for m in (3, 4, 6)]
                    if f == 0:
                        total = (2.0 * CENTRE) * line[g + 4] + (S1 - wx) * xx
                        total = total + (S1 - wy) * yy - wxy * xy
                    else:
                        total = CENTRE * line[g + 4] + wx * xx
                        total = total + wy * yy + wxy * xy
                    part[f, i, pl.ds(r, 8), :] = total
                    slopes[g].append(slope)
            pieces = [piece for rest in slopes for piece in rest]
            for k in range(0, len(pieces), 2):
                put_halves(2, f, q * (len(pieces) // 2) + k // 2, joined(pieces[k : k + 2]))

    loop(count // group, along_x, 10)

    units = count // planes
    for kind, mat, at in ((0, mat_second, 4 // planes), (1, mat_first, 4 // planes), (2, mat_first, 0)):
        for f in range(2):
            both = halves[kind, f, pl.ds(at, units)].reshape(units * 16, 256)
            out = jnp.dot(both, mat[...], preferred_element_type=F32)
            product[kind, f, pl.ds(0, units)] = out.reshape(units, 16, 128)

    def combine(u):
        where = [u * planes + v for v in range(planes)]
        speed, speed_h, speed_v, wz, wyz, wxz = [
            joined([coef(m, i, 0, rows) for i in where]) for m in (0, 1, 2, 5, 7, 8)
        ]
        zz, yz, xz = [[product[kind, f, u] for f in range(2)] for kind in range(3)]
        parts = [joined([part[f, i, :rows] for i in where]) for f in range(2)]
        here = [joined([field(f, i + 4) for i in where]) for f in range(2)]
        old = [joined([old_at(f, i) for i in where]) for f in range(2)]
        add = joined([inject_at(i) for i in where])
        flat = parts[0] + (SECOND_UNIT - wz) * zz[0] - (wyz * yz[0] + wxz * xz[0])
        tilted = parts[1] + wz * zz[1] + (wyz * yz[1] + wxz * xz[1])
        new_p = (2.0 * here[0] - old[0] + add) + (speed_h * flat + speed_v * tilted)
        new_q = (2.0 * here[1] - old[1] + add) + (speed_v * flat + speed * tilted)
        for v, i in enumerate(where):
            cut = slice(v * rows, v * rows + rows)
            store(i, new_p[cut], new_q[cut])

    loop(units, combine, 36)


def leap_scratch(count):
    lines = (2, count + 8, 16, 128)
    return [
        (lines, F32),
        (lines, F32),
        ((2, count, 16, 128), F32),
        ((3, 2, count + 8, 16, 256), BF16),
        ((3, 2, count, 16, 128), F32),
    ]


def first_kernel(columns, kept, got, tile, old, payload, *edges):
    size = kept.shape[1]
    place = Place(2 * size, columns)
    for source, at in ((kept, place.core * size), (got, (1 - place.core) * size)):
        for f in range(2):
            tile[f, pl.ds(at, size)] = source[2 * f]
            old[f, pl.ds(at, size)] = source[2 * f + 1]

    encode(lambda f, p: tile[f, p], 2 * size, payload, lambda f, p: old[f, p])
    for k, edge in enumerate(edges):
        group = lax.div(place.edge_at[k], GROUP) * TILES
        for base in (0, 2 * size + 1):
            edge[pl.ds(base and GROUP + 1, TILES)] = payload[pl.ds(base + group, TILES)]
        edge[GROUP] = payload[2 * size]


def cut_kernel(payload, *refs):
    beside, (odd, even) = refs[:-2], refs[-2:]
    parity = lax.rem(lax.axis_index("gy"), 2)

    def cut(out, row):
        base = 0
        for block in (payload, *beside):
            planes = block.shape[0] // 2
            out[pl.ds(base, planes + 1)] = block[: planes + 1]
            for u in range(0, planes, 2):
                pairs = [block[planes + 1 + u + v].astype(jnp.int32) for v in range(2)]
                rows = [pair[r + row : r + row + 4] for pair in pairs for r in (0, 8)]
                out[base + planes + 1 + u // 2] = jnp.concatenate(rows).astype(jnp.int16)
            base += block_size(planes, 4)

    @pl.when(parity == 0)
    def _():
        cut(even, 4)
        cut(odd, 0)

    @pl.when(parity == 1)
    def _():
        cut(odd, 4)
        cut(even, 0)


def first_leap(place, start, count, window, old, old_start, coefs, inject, scratch, mats, store):
    leap(
        window, place.first_at + start, 8, coefs.shape[2], count, scratch, mats,
        lambda m, i, r, number: coefs[m, start + i, pl.ds(r, number), :],
        lambda f, i: old[f, old_start + start + i],
        lambda i: inject[0, start + i],
        store,
    )


def second_leap(
    place, start, count, source, source_start, tile, coefs, inject, scratch, mats, store
):
    rows = tile.shape[2]
    at = place.tile_at + start
    leap(
        source, source_start, 8, rows, count, scratch, mats,
        lambda m, i, r, number: coefs[m, at + i, pl.ds(4 + r, number), :],
        lambda f, i: tile[f, start + i],
        lambda i: inject[1, at + i, pl.ds(4, rows), :],
        store,
    )


def fill(place, tile, old, beside, even, odd, window, old_wide, groups, with_beside=True):
    size_x = tile.shape[1]
    opening = old_wide is not None
    for f in range(2):
        window[f, pl.ds(0, 4)] = jnp.zeros((4, 32, 128), F32)
        window[f, pl.ds(place.wide + 4, 4)] = jnp.zeros((4, 32, 128), F32)
        needed = pl.ds(groups[0] * GROUP, groups[1] * GROUP)
        at = place.own_at + groups[0] * GROUP
        window[f, pl.ds(at + 4, groups[1] * GROUP), pl.ds(12, 8), :] = tile[f, needed]
        if opening:
            old_wide[f, pl.ds(at, groups[1] * GROUP), pl.ds(4, 8), :] = old[f, needed]

    def lay(block, base, planes, at, row):
        start, number = groups if planes == size_x else (0, 1)
        there = {-8: place.has_below, 0: 1.0, 8: place.has_above}[row]
        factor = factor_of(block[base + planes], 0) * there

        def group(g):
            def put(f, p, rows):
                window[f, at + g * GROUP + p + 4, pl.ds(row + 12, 8), :] = rows

            decode(block, base + g * TILES, factor, put)

        loop(number, lambda g: group(start + g), 2)
        if not opening:
            return
        factor = factor_of(block[base + planes], 1) * there

        def old_group(g):
            def put(f, p, rows):
                first = 0 if row < 0 else row + 4
                old_wide[f, at + g * GROUP + p, pl.ds(first, rows.shape[0]), :] = rows

            start = base + planes + 1
            if row == 0:
                decode(block, start + g * TILES, factor, put)
            else:
                near = factor[4:] if row < 0 else factor[:4]
                decode_nearest(block, start + g * (TILES // 2), near, put)

        loop(number, lambda g: old_group(start + g), 2)

    sides = place.sides if with_beside else 0
    for k in range(sides):
        lay(beside[k], 0, GROUP, place.beside_at[k], 0)

    def lay_y(below, above):
        kept = 4 if opening else 0
        for block, row in ((below, -8), (above, 8)):
            lay(block, 0, size_x, place.own_at, row)
            for k in range(sides):
                base = block_size(size_x, kept) + k * block_size(GROUP, kept)
                lay(block, base, GROUP, place.beside_at[k], row)

    pl.when(place.parity == 0)(lambda: lay_y(odd, even))
    pl.when(place.parity == 1)(lambda: lay_y(even, odd))


def lead_kernel(opening, columns, tile, old, coefs, inject, mat_first, mat_second, *refs):
    place = Place(tile.shape[1], columns)
    refs = list(refs)

    def take(number):
        taken = refs[:number]
        del refs[:number]
        return taken

    sides = place.sides
    beside = take(sides)
    even, odd = take(2)
    around_out, edges_out, codes_out = take(sides), take(sides), take(sides)
    middle, window = take(2)
    old_wide = take(1)[0] if opening else None
    scratch, mats = refs, (mat_first, mat_second)
    fill(place, tile, old, beside, even, odd, window, old_wide, place.lead_groups)
    for k in range(sides):
        def store_around(i, new_p, new_q):
            for f, new in enumerate((new_p, new_q)):
                around_out[k][f, i] = new
                middle[f, i, pl.ds(4, new.shape[0]), :] = new

        def store_edge(i, new_p, new_q):
            edges_out[k][0, i] = new_p
            edges_out[k][1, i] = new_q

        first_leap(
            place, place.around_at[k], AROUND, window, old_wide if opening else old,
            place.first_at if opening else 0, coefs, inject, scratch, mats, store_around,
        )
        second_leap(
            place, place.edge_at[k], GROUP, middle, 0, tile, coefs, inject, scratch, mats,
            store_edge,
        )
        encode(lambda f, p: edges_out[k][f, p], GROUP, codes_out[k])


def rest_kernel(opening, columns, tile, old, coefs, inject, mat_first, mat_second, *refs):
    size_x, size_y = tile.shape[1], tile.shape[2]
    place = Place(size_x, columns)
    sides, count = place.sides, place.count
    around, edges, beside = refs[:sides], refs[sides : 2 * sides], refs[2 * sides : 3 * sides]
    even, odd, tile_out, payload, old_out, middle, window, *scratch = refs[3 * sides :]
    old_wide = scratch.pop(0) if opening else None
    mats = (mat_first, mat_second)
    fill(place, tile, old, beside, even, odd, window, old_wide, place.rest_groups, sides > 1)
    old_now = old_wide if opening else old
    for f in range(2):
        middle[f, pl.ds(0, 4)] = jnp.zeros((4, 24, 128), F32)
        middle[f, pl.ds(count + 4, 4)] = jnp.zeros((4, 24, 128), F32)
        for k in range(sides):
            at = place.around_at[k]
            middle[f, pl.ds(at + 4, AROUND), pl.ds(4, size_y + 8), :] = around[k][f]
            old_out[f, pl.ds(at, AROUND)] = around[k][f]
            tile_out[f, pl.ds(place.edge_at[k], GROUP)] = edges[k][f]

    def store_first(i, new_p, new_q):
        for f, new in enumerate((new_p, new_q)):
            old_out[f, place.first_rest_at + i] = new
            middle[f, place.first_rest_at + i + 4, pl.ds(4, size_y + 8), :] = new

    def store_second(i, new_p, new_q):
        tile_out[0, place.rest_at + i] = new_p
        tile_out[1, place.rest_at + i] = new_q

    first_leap(
        place, place.first_rest_at, count - AROUND * sides, window, old_now,
        place.first_at if opening else 0, coefs, inject, scratch, mats, store_first,
    )
    second_leap(
        place, place.rest_at, place.rest, middle, place.tile_at + place.rest_at, tile, coefs,
        inject, scratch, mats, store_second,
    )
    encode(lambda f, p: tile_out[f, p], size_x, payload)


def last_kernel(columns, tile, old, coefs, inject, mat_first, mat_second, *refs):
    size_x, size_y = tile.shape[1], tile.shape[2]
    place = Place(size_x, columns)
    sides, count = place.sides, place.count
    even, odd, kept, sent, middle, tile_out, window, *scratch = refs[sides:]
    mats = (mat_first, mat_second)
    fill(place, tile, old, refs[:sides], even, odd, window, None, (0, size_x // GROUP))
    for f in range(2):
        middle[f, pl.ds(0, 4)] = jnp.zeros((4, 24, 128), F32)
        middle[f, pl.ds(count + 4, 4)] = jnp.zeros((4, 24, 128), F32)

    def store_first(i, new_p, new_q):
        for f, new in enumerate((new_p, new_q)):
            middle[f, i + 4, pl.ds(4, size_y + 8), :] = new

    def store_second(i, new_p, new_q):
        tile_out[0, i] = new_p
        tile_out[1, i] = new_q

    first_leap(place, 0, count, window, old, 0, coefs, inject, scratch, mats, store_first)
    second_leap(
        place, 0, size_x, middle, place.tile_at, tile, coefs, inject, scratch, mats, store_second
    )
    half = size_x // 2
    for mine in range(2):
        @pl.when(place.core == mine)
        def _():
            for out, start in ((kept, mine * half), (sent, (1 - mine) * half)):
                planes = pl.ds(start, half)
                inner = pl.ds(place.tile_at + 4 + start, half)
                out[0] = middle[0, inner, pl.ds(8, size_y), :]
                out[1] = tile_out[0, planes]
                out[2] = tile_out[1, planes]


def sine_cosine(angle):
    square = angle * angle
    sine = 1.0 / 6227020800.0
    for factor in (-1.0 / 39916800.0, 1.0 / 362880.0, -1.0 / 5040.0, 1.0 / 120.0, -1.0 / 6.0):
        sine = sine * square + factor
    sine = angle + angle * square * sine
    cosine = 1.0 / 479001600.0
    for factor in (-1.0 / 3628800.0, 1.0 / 40320.0, -1.0 / 720.0, 1.0 / 24.0, -0.5):
        cosine = cosine * square + factor
    return sine, 1.0 + square * cosine


def open_kernel(
    velocity, epsilon, delta, tilt, azimuth, source, receiver, *refs
):
    models = (velocity, epsilon, delta, tilt, azimuth)
    parity = lax.rem(lax.axis_index("gy"), 2)
    core = lax.rem(lax.axis_index("gx"), 2)
    small, (even, odd, own, kept, given), brought, arrived = (
        refs[:3], refs[3:8], refs[8:11], refs[11]
    )
    copies = [pltpu.make_async_copy(models[m], own.at[m], arrived.at[m]) for m in range(5)]
    others = [
        pltpu.make_async_copy(small[m], brought[m], arrived.at[7 + m]) for m in range(3)
    ]

    def states(mine):
        stay, leave = (source, receiver) if mine == 0 else (receiver, source)
        return (
            pltpu.make_async_copy(stay, kept, arrived.at[5]),
            pltpu.make_async_copy(leave, given, arrived.at[6]),
        )

    for copy in copies + others:
        copy.start()
    for mine in range(2):
        @pl.when(core == mine)
        def _():
            for copy in states(mine):
                copy.start()

    for copy in copies:
        copy.wait()

    def pack(out, row):
        for m in range(5):
            for u in range(0, own.shape[1], 2):
                pairs = [own[m, u + k].astype(F32) for k in range(2)]
                values = [pair[v + row : v + row + 4] for pair in pairs for v in (0, 8)]
                out[m, u // 2] = jnp.concatenate(values).astype(BF16)

    @pl.when(parity == 0)
    def _():
        pack(even, 4)
        pack(odd, 0)

    @pl.when(parity == 1)
    def _():
        pack(odd, 4)
        pack(even, 0)

    for mine in range(2):
        @pl.when(core == mine)
        def _():
            for copy in states(mine):
                copy.wait()
    for copy in others:
        copy.wait()


def join_kernel(own, even, odd, out):
    at_y = lax.axis_index("gy")
    parity = lax.rem(at_y, 2)
    has_below = jnp.where(at_y > 0, 1.0, 0.0)
    has_above = jnp.where(at_y < lax.axis_size("gy") - 1, 1.0, 0.0)

    def fill(below, above):
        for m in range(5):
            for u in range(own.shape[1]):
                low = below[m, u // 2].astype(F32) * has_below
                high = above[m, u // 2].astype(F32) * has_above
                pair = own[m, u].astype(F32)
                for v in range(2):
                    k = 2 * (u % 2) + v
                    rows = [low[4 * k : 4 * k + 4], pair[8 * v : 8 * v + 8], high[4 * k : 4 * k + 4]]
                    out[m, 2 * u + v] = jnp.concatenate(rows).astype(BF16)

    pl.when(parity == 0)(lambda: fill(odd, even))
    pl.when(parity == 1)(lambda: fill(even, odd))


def setup_kernel(columns, size_x, total_x, aperture, *refs):
    models, coefs, blocks = refs[:-2], refs[-2], refs[-1]
    place = Place(2 * size_x, columns)
    if len(models) > 1:
        for k, column in enumerate((place.column, 1 - place.column)):
            for j, core in enumerate((place.core, 1 - place.core)):
                blocks[:, pl.ds((2 * column + core) * size_x, size_x)] = models[2 * k + j][...]
        source = blocks
    else:
        source = models[0]

    def medium(i):
        x = place.start_x + i
        block = jnp.clip(x // size_x, 0, total_x // size_x - 1)
        inside = jnp.logical_and(x >= 0, x < total_x)
        at = aperture[block] * size_x + lax.rem(x + size_x, size_x)
        speed, stretch, bending, tilt, azimuth = [source[m, at].astype(F32) for m in range(5)]
        speed = jnp.where(inside, speed, 0.0)
        sin_t, cos_t = sine_cosine(tilt)
        sin_half, cos_half = sine_cosine(0.5 * azimuth)
        normal_x = sin_t * (1.0 - 2.0 * sin_half * sin_half)
        normal_y = sin_t * (2.0 * sin_half * cos_half)
        coefs[0, i] = speed
        coefs[1, i] = speed * (1.0 + 2.0 * stretch)
        coefs[2, i] = speed * jnp.sqrt(1.0 + 2.0 * bending)
        coefs[3, i] = S1 * (normal_x * normal_x)
        coefs[4, i] = S1 * (normal_y * normal_y)
        coefs[5, i] = SECOND_UNIT * (cos_t * cos_t)
        coefs[6, i] = (2.0 * G1 * G1) * (normal_x * normal_y)
        coefs[7, i] = (2.0 * G1 * FIRST_UNIT) * (normal_y * cos_t)
        coefs[8, i] = (2.0 * G1 * FIRST_UNIT) * (normal_x * cos_t)

    loop(place.count, medium, 6)


def injection_kernel(
    columns, size_x, size_y, total_y, source_cell, wavelet, cells, traces, out, hits
):
    place = Place(size_x, columns)
    count, rows = hits.shape[:2]
    number = cells.shape[1]
    row = lax.broadcasted_iota(jnp.int32, (rows, number), 0)
    lane = lax.broadcasted_iota(jnp.int32, (1, number), 1)
    is_source = place.core == 0
    lonely = jnp.where(lane == 0, source_cell[0], -1)
    aims = jnp.where(is_source, lonely, cells[...])
    y = place.at_y * size_y - 4 + row
    valid = jnp.logical_and(y >= 0, y < total_y)

    def mark(i):
        code = jnp.where(valid, (place.start_x + i) * total_y + y, -2)
        hits[i] = jnp.where(code == aims, 1.0, 0.0).astype(BF16)

    loop(count, mark, 2)
    step = lax.broadcasted_iota(jnp.int32, (NT, number), 0)
    amounts = jnp.zeros((NT, number), F32)
    for k in range(NT):
        amounts = jnp.where(step == k, wavelet[:, k : k + 1], amounts)
    backward = jnp.concatenate([traces[k : k + 1] for k in reversed(range(NT))])
    rest = jnp.where(is_source, amounts, backward)
    total = None
    for _ in range(3):
        piece = rest.astype(BF16)
        rest = rest - piece.astype(F32)
        term = lax.dot_general(
            hits[...].reshape(count * rows, number), piece, (((1,), (1,)), ((), ())),
            preferred_element_type=F32,
        )
        total = term if total is None else total + term
    out[...] = total.reshape(count, rows, NT)


def spread_kernel(moment, lanes, out):
    core = lax.rem(lax.axis_index("gx"), 2)
    level = jnp.where(core == 0, SRC_DEPTH, REC_DEPTH)
    mask = (lax.broadcasted_iota(jnp.int32, (lanes.shape[1], 128), 1) == level).astype(F32)

    def expand(i):
        values = lanes[i]
        for k in range(2):
            out[k, i] = values[:, moment + k : moment + k + 1] * mask

    loop(lanes.shape[0], expand, 6)


def sort_kernel(columns, *refs):
    levels, (kept, sent) = refs[: NT - 1], refs[NT - 1 :]
    half, size_y = kept.shape[1:3]
    place = Place(2 * half, columns)

    def level_at(step, start):
        where = levels[step]
        if step % 2 == 0:
            return where[0, pl.ds(start, half)]
        return where[0, pl.ds(place.tile_at + start, half), pl.ds(4, size_y), :]

    for mine in range(2):
        @pl.when(place.core == mine)
        def _():
            for step in range(NT - 1):
                t = step if mine == 0 else NT - step
                if t > 0:
                    kept[t - 1] = level_at(step, mine * half)
                    sent[t - 1] = level_at(step, (1 - mine) * half)


def close_kernel(kept, got, last_kept, last_got, image, field):
    core = lax.rem(lax.axis_index("gx"), 2)
    total = kept[1] * got[1]
    for t in range(2, NT - 2):
        total = total + kept[t] * got[t]

    @pl.when(core == 0)
    def _():
        image[...] = (
            total + kept[0] * last_got[0] + last_kept[0] * got[NT - 2] + last_kept[1] * got[NT - 1]
        ) * (1.0 / NT)
        field[...] = last_got[pl.ds(1, 2)]

    @pl.when(core == 1)
    def _():
        image[...] = (
            total + last_kept[0] * got[0] + kept[NT - 2] * last_got[0] + kept[NT - 1] * last_got[1]
        ) * (1.0 / NT)
        field[...] = last_kept[pl.ds(1, 2)]


def per_device(
    velocity,
    epsilon,
    delta,
    tilt,
    azimuth,
    aperture,
    source_cell,
    wavelet,
    receiver_cell,
    traces,
    source_state,
    receiver_state,
):
    block_x, size_y, _ = velocity.shape
    devices_x, devices_y = lax.axis_size("gx"), lax.axis_size("gy")
    columns = devices_x // 2
    total_x, total_y = block_x * devices_x, size_y * devices_y
    size_x, rows = 2 * block_x, size_y + 8
    is_source = lax.axis_index("gx") % 2 == 0
    place = Place(size_x, columns)
    sides, count = place.sides, place.count
    mats = depth_matrices(128)
    chip_pairs = [even_pairs(columns), odd_pairs(columns)][:sides]
    row_pairs = [even_pairs(devices_y), odd_pairs(devices_y)]
    trade = both_ways([(2 * c, 2 * c + 1) for c in range(columns)])

    def over_gy(values, pairs, opening=False):
        paired = {i for pair in pairs for i in pair}
        alone = [y for y in range(devices_y) if y not in paired]
        swaps = [(x * devices_y + a, x * devices_y + b) for x in range(devices_x) for a, b in pairs]
        swaps += [
            (a * devices_y + y, b * devices_y + y)
            for a, b in (even_pairs(devices_x) if opening else chip_swap(even_pairs(columns)))
            for y in alone
        ]
        return lax.ppermute(values, ("gx", "gy"), both_ways(swaps))

    def over_gx(values, pairs):
        return lax.ppermute(values, "gx", both_ways(chip_swap(pairs)))

    def beside_of(edges):
        return [over_gx(edge, pairs) for edge, pairs in zip(edges, chip_pairs)]

    def near_of(even, odd, opening=False):
        odd = over_gy(odd, row_pairs[1], opening)
        return over_gy(even, row_pairs[0], opening), odd

    def codes(planes, old_rows=0):
        return ((block_size(planes, old_rows), 16, 128), jnp.int16)

    models = [
        values.reshape(block_x // 2, 16, 128) for values in (velocity, epsilon, delta, tilt, azimuth)
    ]
    small = (wavelet[None, :], receiver_cell[None, :], traces)
    rim = ((5, block_x // 4, 16, 128), BF16)
    states = (source_state, receiver_state)
    state = (source_state.shape, F32)
    *rims, own, kept, given, series, cells, data = pl.pallas_call(
        open_kernel,
        out_shape=tuple(
            jax.ShapeDtypeStruct(*out)
            for out in (rim, rim, ((5, block_x // 2, 16, 128), BF16), state, state)
            + tuple((x.shape, x.dtype) for x in small)
        ),
        in_specs=[HBM] * 10,
        out_specs=(VMEM,) * 8,
        scratch_shapes=[pltpu.SemaphoreType.DMA((10,))],
        compiler_params=pltpu.CompilerParams(vmem_limit_bytes=8 * 2**20),
        name="open",
    )(*[pltpu.with_memory_space_constraint(x, pltpu.HBM) for x in (*models, *states, *small)])
    rims = [over_gy(values, pairs, True) for values, pairs in zip(rims, row_pairs)]

    got = lax.ppermute(given, "gx", trade)
    field = ((2, size_x, size_y, 128), F32)
    tile, old, payload, *edges = call(
        functools.partial(first_kernel, columns),
        (field, field, codes(size_x, 8)) + (codes(GROUP, 8),) * sides,
        (), 16, "first", (kept, got),
    )
    number = receiver_cell.shape[0]
    cells, _ = lax.optimization_barrier((cells, edges[0]))
    (amounts,) = call(
        functools.partial(injection_kernel, columns, size_x, size_y, total_y),
        (((count, rows, NT), F32),), (((count, rows, number), BF16),),
        16, "injection", (source_cell, series, cells, data), scalars=1,
    )
    beside = beside_of(edges)
    payload, _ = lax.optimization_barrier((payload, amounts))
    total = block_size(size_x, 4) + sides * block_size(GROUP, 4)
    wide = call(
        cut_kernel, (((total, 16, 128), jnp.int16),) * 2, (), 8, "cut", (payload, *beside)
    )
    near = near_of(*wide[::-1], opening=True)

    def spread(moment, after):
        lanes, _ = lax.optimization_barrier((amounts, after[0]))
        (out,) = call(
            functools.partial(spread_kernel, moment), (((2, count, rows, 128), F32),), (), 8,
            "spread", (lanes,),
        )
        return out

    inject = spread(0, wide)

    rims = lax.optimization_barrier((*rims, edges[0]))[:2]
    (model,) = call(
        join_kernel, (((5, block_x, rows, 128), BF16),), (), 8, "join", (own, *rims), work=1000
    )
    if columns == 2:
        later, _ = lax.optimization_barrier((model, wide[0]))
        across = over_gx(later, chip_pairs[0])
        early, _ = lax.optimization_barrier((model, inject))
        other = lax.ppermute(early, "gx", trade)
        gathered = [model, other, across, lax.ppermute(across, "gx", trade)]
        held = (5, total_x, rows, 128)
    else:
        gathered, held = [lax.all_gather(model, "gx", axis=1, tiled=True)], (16, 128)
    (coefs,) = call(
        functools.partial(setup_kernel, columns, block_x, total_x),
        (((9, count, rows, 128), F32),), ((held, BF16),), 24, "setup", (aperture, *gathered),
        scalars=1, work=0,
    )

    window = ((2, place.wide + 8, 32, 128), F32)
    middle = ((2, count + 8, 24, 128), F32)
    lines = ((2, count, rows, 128), F32)
    levels = [tile]
    for moment in range(0, NT - 2, 2):
        opening = moment == 0
        inject = inject if opening else spread(moment, wide)
        old_wide = (((2, place.wide, rows, 128), F32),) * opening
        around = (((2, AROUND, rows, 128), F32),) * sides
        edge = (((2, GROUP, size_y, 128), F32),) * sides
        filled = (window,) + old_wide
        outs = call(
            functools.partial(lead_kernel, opening, columns),
            around + edge + (codes(GROUP),) * sides,
            (((2, AROUND, 24, 128), F32),) + filled + tuple(leap_scratch(AROUND)), 24, "lead",
            (tile, old, coefs, inject, *mats, *beside, *near), work=2 * 10**6,
        )
        came = (*beside, *near)
        beside = beside_of(outs[2 * sides :])
        tile, payload, old = call(
            functools.partial(rest_kernel, opening, columns),
            (field, codes(size_x), lines),
            (middle,) + filled + tuple(leap_scratch(place.rest)), 24, "rest",
            (tile, old, coefs, inject, *mats, *outs[: 2 * sides], *came), work=4 * 10**6,
        )
        wide = (jnp.concatenate([payload, *beside]),) * 2
        near = near_of(*wide)
        levels += [old, tile]
    shape = (block_x, size_y, 128)
    inject = spread(NT - 2, wide)
    share = ((NT,) + shape, F32)
    kept, sent = call(
        functools.partial(sort_kernel, columns), (share, share), (), 8, "sort",
        lax.optimization_barrier((*levels, *near, inject))[: NT - 1],
    )
    got = lax.ppermute(sent, "gx", trade)
    share = ((3,) + shape, F32)
    last_kept, last_sent = call(
        functools.partial(last_kernel, columns),
        (share, share), [middle, field, window] + leap_scratch(count), 24, "last",
        (tile, old, coefs, inject, *mats, *beside, *near),
    )
    last_got = lax.ppermute(last_sent, "gx", trade)
    return call(
        close_kernel, ((shape, F32), ((2,) + shape, F32)), (), 8, "close",
        (kept, got, last_kept, last_got),
    )


def solution(mesh):
    in_specs = (
        P("gx", "gy", None),
        P("gx", "gy", None),
        P("gx", "gy", None),
        P("gx", "gy", None),
        P("gx", "gy", None),
        P("shot"),
        P("shot"),
        P("shot"),
        P("shot"),
        P(None, "shot"),
        P(None, ("shot", "gx"), "gy", None),
        P(None, ("shot", "gx"), "gy", None),
    )
    out_specs = (P(("shot", "gx"), "gy", None), P(None, ("shot", "gx"), "gy", None))
    return jax.shard_map(
        per_device, mesh=mesh, in_specs=in_specs, out_specs=out_specs, check_vma=False
    )
```

```python
import functools

import jax
import jax.numpy as jnp
from jax import lax
from jax.experimental import pallas as pl
from jax.experimental.pallas import tpu as pltpu
from jax.sharding import PartitionSpec as P

NT = 8
SRC_DEPTH = 10
REC_DEPTH = 6
F32 = jnp.float32
BF16 = jnp.bfloat16

second_taps = (-205.0 / 72.0, 8.0 / 5.0, -1.0 / 5.0, 8.0 / 315.0, -1.0 / 560.0)
first_taps = (4.0 / 5.0, -1.0 / 5.0, 4.0 / 105.0, -1.0 / 280.0)
CENTRE = second_taps[0]
S1 = second_taps[1]
G1 = first_taps[0]
second_ratio = tuple(tap / S1 for tap in second_taps[2:])
first_ratio = tuple(tap / G1 for tap in first_taps[1:])
second_whole = (8064.0, -1008.0, 128.0, -9.0)
first_whole = (672.0, -168.0, 32.0, -3.0)
SECOND_UNIT = 1.0 / 5040.0
FIRST_UNIT = 1.0 / 840.0
VMEM = pl.BlockSpec(memory_space=pltpu.VMEM)
SMEM = pl.BlockSpec(memory_space=pltpu.SMEM)
HBM = pl.BlockSpec(memory_space=pltpu.HBM)


def even_pairs(count):
    return [(i, i + 1) for i in range(0, count - 1, 2)]


def odd_pairs(count):
    return [(i, i + 1) for i in range(1, count - 1, 2)]


def both_ways(pairs):
    return [pair for a, b in pairs for pair in ((a, b), (b, a))]


def chip_swap(pairs):
    return [(2 * a + c, 2 * b + c) for a, b in pairs for c in range(2)]


class Place:
    def __init__(self, size_x, columns):
        at_x = lax.axis_index("gx")
        self.core, self.column = lax.rem(at_x, 2), lax.div(at_x, 2)
        self.at_y = lax.axis_index("gy")
        self.parity = lax.rem(self.at_y, 2)
        self.has_below = jnp.where(self.at_y > 0, 1.0, 0.0)
        self.has_above = jnp.where(self.at_y < lax.axis_size("gy") - 1, 1.0, 0.0)
        if columns == 2:
            side = self.column
            self.count = size_x + 4
            self.first_at = self.tile_at = 4 * side
            self.start_x = side * (size_x - 4)
            self.beside_at = [size_x * (1 - side)]
            self.edge_at = [(size_x - GROUP) * (1 - side)]
            self.rest_at, self.rest = GROUP * side, size_x - GROUP
            self.first_rest_at = AROUND * side
            groups = size_x // GROUP
            self.lead_groups = ((groups - 2) * (1 - side), 2)
            self.rest_groups = (side, groups - 1)
        else:
            side = lax.rem(self.column, 2)
            self.count = size_x + 8
            self.first_at = self.tile_at = 4
            self.start_x = self.column * size_x - 4
            self.beside_at = [(size_x + GROUP) * (1 - side), (size_x + GROUP) * side]
            self.edge_at = [(size_x - GROUP) * (1 - side), (size_x - GROUP) * side]
            self.rest_at, self.rest = GROUP, size_x - 2 * GROUP
            self.first_rest_at = AROUND
            self.lead_groups = self.rest_groups = (0, size_x // GROUP)
        self.sides = len(self.beside_at)
        self.around_at = [self.tile_at + at - 4 for at in self.edge_at]
        self.own_at = self.first_at + self.tile_at
        self.wide = size_x + GROUP * self.sides


def call(kernel, outs, scratch, mebibytes, name, args, scalars=0, work=10**6):
    outs = tuple(jax.ShapeDtypeStruct(shape, dtype) for shape, dtype in outs)
    return pl.pallas_call(
        kernel,
        out_shape=outs,
        in_specs=[SMEM] * scalars + [VMEM] * (len(args) - scalars),
        out_specs=(VMEM,) * len(outs),
        scratch_shapes=[pltpu.VMEM(shape, dtype) for shape, dtype in scratch],
        compiler_params=pltpu.CompilerParams(vmem_limit_bytes=mebibytes * 2**20),
        cost_estimate=pl.CostEstimate(flops=work, bytes_accessed=work, transcendentals=0),
        name=name,
    )(*args)


def loop(trips, body, wanted):
    unroll = max(u for u in range(1, wanted + 1) if trips % u == 0)

    def step(i, carry):
        body(i)
        return carry

    lax.fori_loop(0, trips, step, 0, unroll=unroll)


def depth_matrices(size):
    rows = jnp.arange(size)[:, None]
    cols = jnp.arange(size)[None, :]
    first = jnp.zeros((size, size), F32)
    second = jnp.zeros((size, size), F32)
    for k in range(1, 5):
        up = (rows == cols + k).astype(F32)
        down = (rows == cols - k).astype(F32)
        first = first + first_whole[k - 1] * (up - down)
        second = second + second_whole[k - 1] * (up + down)
    return (
        jnp.concatenate([first, first]).astype(BF16),
        jnp.concatenate([second, second]).astype(BF16),
    )


def sums_and_slopes(shifted):
    up, down = shifted(1), shifted(-1)
    curve, slope = up + down, up - down
    for k in range(2, 5):
        up, down = shifted(k), shifted(-k)
        curve = curve + second_ratio[k - 2] * (up + down)
        slope = slope + first_ratio[k - 2] * (up - down)
    return curve, slope


def slope_only(shifted):
    slope = shifted(1) - shifted(-1)
    for k in range(2, 5):
        slope = slope + first_ratio[k - 2] * (shifted(k) - shifted(-k))
    return slope


def split(values):
    high = values.astype(BF16)
    low = (values - high.astype(F32)).astype(BF16)
    return high, low


TOP = 32000.0
GROUP = 8
AROUND = GROUP + 8
TILES = GROUP


def block_size(planes, old_rows=0):
    return planes + 1 + planes * old_rows // 8


def scale_of(value_at, planes):
    def grow(i, size):
        for f in range(2):
            size = jnp.maximum(size, jnp.abs(value_at(f, i)))
        return size

    size = lax.fori_loop(0, planes, grow, jnp.full((8, 128), 1e-30, F32), unroll=8)
    code = jnp.ceil(jnp.log2(size) * 256.0)
    return code, TOP * jnp.exp2(code * (-1.0 / 256.0))


def as_code(pieces):
    return jnp.concatenate(pieces).astype(jnp.int32).astype(jnp.int16)


def encode(value_at, planes, out, old_at=None):
    code, factor = scale_of(value_at, planes)
    old_code, old_factor = scale_of(old_at, planes) if old_at else (code, None)

    def put(source, base, by):
        def group(g):
            for f in range(2):
                for q in range(4):
                    pair = [source(f, g * GROUP + 2 * q + v) for v in range(2)]
                    whole = [jnp.floor(value * by + 0.5) for value in pair]
                    out[base + g * TILES + 4 * f + q] = as_code(whole)

        loop(planes // GROUP, group, 1)

    put(value_at, 0, factor)
    out[planes] = as_code([code, old_code])
    if old_at:
        put(old_at, planes + 1, old_factor)


def factor_of(scales, half):
    code = scales.astype(jnp.int32).astype(F32)[8 * half : 8 * half + 8]
    return jnp.exp2(code * (1.0 / 256.0)) * (1.0 / TOP)


def decode(block, base, factor, put):
    for f in range(2):
        for q in range(4):
            both = block[base + 4 * f + q].astype(jnp.int32).astype(F32)
            put(f, 2 * q, both[:8] * factor)
            put(f, 2 * q + 1, both[8:] * factor)


def decode_nearest(block, base, factor, put):
    by = jnp.concatenate([factor] * 4)
    for f in range(2):
        for q in range(2):
            rows = block[base + 2 * f + q].astype(jnp.int32).astype(F32) * by
            for v in range(4):
                put(f, 4 * q + v, rows[4 * v : 4 * v + 4])


def leap(src, x0, row0, rows, count, scratch, mats, coef, old_at, inject_at, store):
    slope_y, curve_y, part, halves, product = scratch
    mat_first, mat_second = mats
    planes = 16 // rows
    group = 4

    def field(f, p, r=0, number=rows):
        return src[f, x0 + p, pl.ds(row0 + r, number), :]

    def joined(values):
        return jnp.concatenate(values) if len(values) > 1 else values[0]

    def put_halves(kind, f, unit, values):
        high, low = split(values)
        halves[kind, f, unit, :, :128] = high
        halves[kind, f, unit, :, 128:] = low

    def along_y(u):
        for f in range(2):
            here, slopes = [], []
            for v in range(planes):
                p = u * planes + v
                curve, slope = sums_and_slopes(lambda k: field(f, p, k))
                slope_y[f, p, :rows] = slope
                curve_y[f, p, :rows] = curve
                slopes.append(slope)
                here.append(field(f, p))
            put_halves(0, f, u, joined(here))
            put_halves(1, f, u, joined(slopes))

    loop((count + 8) // planes, along_y, 24)

    def along_x(q):
        base = q * group
        for f in range(2):
            slopes = [[] for g in range(group)]
            for r in range(0, rows, 8):
                line = [field(f, base + k, r, 8) for k in range(group + 8)]
                slant = [slope_y[f, base + k, pl.ds(r, 8), :] for k in range(group + 8)]
                for g in range(group):
                    i = base + g
                    xx, slope = sums_and_slopes(lambda k: line[g + 4 + k])
                    xy = slope_only(lambda k: slant[g + 4 + k])
                    yy = curve_y[f, i + 4, pl.ds(r, 8), :]
                    wx, wy, wxy = [coef(m, i, r, 8) for m in ((9, 10, 6), (3, 4, 6))[f]]
                    if f == 0:
                        total = (2.0 * CENTRE) * line[g + 4] + wx * xx
                        total = total + wy * yy - wxy * xy
                    else:
                        total = CENTRE * line[g + 4] + wx * xx
                        total = total + wy * yy + wxy * xy
                    part[f, i, pl.ds(r, 8), :] = total
                    slopes[g].append(slope)
            pieces = [piece for rest in slopes for piece in rest]
            for k in range(0, len(pieces), 2):
                put_halves(2, f, q * (len(pieces) // 2) + k // 2, joined(pieces[k : k + 2]))

    loop(count // group, along_x, 10)

    units = count // planes
    for kind, mat, at in ((0, mat_second, 4 // planes), (1, mat_first, 4 // planes), (2, mat_first, 0)):
        for f in range(2):
            both = halves[kind, f, pl.ds(at, units)].reshape(units * 16, 256)
            out = jnp.dot(both, mat[...], preferred_element_type=F32)
            product[kind, f, pl.ds(0, units)] = out.reshape(units, 16, 128)

    def combine(u):
        where = [u * planes + v for v in range(planes)]
        speed, speed_h, speed_v, wz, wyz, wxz, rest_z = [
            joined([coef(m, i, 0, rows) for i in where]) for m in (0, 1, 2, 5, 7, 8, 11)
        ]
        zz, yz, xz = [[product[kind, f, u] for f in range(2)] for kind in range(3)]
        parts = [joined([part[f, i, :rows] for i in where]) for f in range(2)]
        here = [joined([field(f, i + 4) for i in where]) for f in range(2)]
        old = [joined([old_at(f, i) for i in where]) for f in range(2)]
        add = joined([inject_at(i) for i in where])
        flat = parts[0] + rest_z * zz[0] - (wyz * yz[0] + wxz * xz[0])
        tilted = parts[1] + wz * zz[1] + (wyz * yz[1] + wxz * xz[1])
        new_p = (2.0 * here[0] - old[0] + add) + (speed_h * flat + speed_v * tilted)
        new_q = (2.0 * here[1] - old[1] + add) + (speed_v * flat + speed * tilted)
        for v, i in enumerate(where):
            cut = slice(v * rows, v * rows + rows)
            store(i, new_p[cut], new_q[cut])

    loop(units, combine, 36)


def leap_scratch(count):
    lines = (2, count + 8, 16, 128)
    return [
        (lines, F32),
        (lines, F32),
        ((2, count, 16, 128), F32),
        ((3, 2, count + 8, 16, 256), BF16),
        ((3, 2, count, 16, 128), F32),
    ]


def first_kernel(columns, kept, got, tile, old, payload, *edges):
    size = kept.shape[1]
    place = Place(2 * size, columns)
    for source, at in ((kept, place.core * size), (got, (1 - place.core) * size)):
        for f in range(2):
            tile[f, pl.ds(at, size)] = source[2 * f]
            old[f, pl.ds(at, size)] = source[2 * f + 1]

    encode(lambda f, p: tile[f, p], 2 * size, payload, lambda f, p: old[f, p])
    for k, edge in enumerate(edges):
        group = lax.div(place.edge_at[k], GROUP) * TILES
        edge[pl.ds(0, TILES)] = payload[pl.ds(group, TILES)]
        edge[GROUP] = payload[2 * size]
        nearest = 2 * lax.div(place.edge_at[k], 2 * size - GROUP)
        for f in range(2):
            start = 2 * size + 1 + group + 4 * f + nearest
            edge[pl.ds(GROUP + 1 + 2 * f, 2)] = payload[pl.ds(start, 2)]


def cut_kernel(payload, *refs):
    beside, (odd, even) = refs[:-2], refs[-2:]
    parity = lax.rem(lax.axis_index("gy"), 2)

    def cut(out, row):
        base = 0
        for block in (payload, *beside):
            planes = block.shape[0] // 2 if block is payload else GROUP
            out[pl.ds(base, planes + 1)] = block[: planes + 1]
            old_tiles = block.shape[0] - planes - 1
            for u in range(0, old_tiles, 2):
                pairs = [block[planes + 1 + u + v].astype(jnp.int32) for v in range(2)]
                rows = [pair[r + row : r + row + 4] for pair in pairs for r in (0, 8)]
                out[base + planes + 1 + u // 2] = jnp.concatenate(rows).astype(jnp.int16)
            base += planes + 1 + old_tiles // 2

    @pl.when(parity == 0)
    def _():
        cut(even, 4)
        cut(odd, 0)

    @pl.when(parity == 1)
    def _():
        cut(odd, 4)
        cut(even, 0)


def first_leap(place, start, count, window, old, old_start, coefs, inject, scratch, mats, store):
    leap(
        window, place.first_at + start, 8, coefs.shape[2], count, scratch, mats,
        lambda m, i, r, number: coefs[m, start + i, pl.ds(r, number), :],
        lambda f, i: old[f, old_start + start + i],
        lambda i: inject[0, start + i],
        store,
    )


def second_leap(
    place, start, count, source, source_start, tile, coefs, inject, scratch, mats, store
):
    rows = tile.shape[2]
    at = place.tile_at + start
    leap(
        source, source_start, 8, rows, count, scratch, mats,
        lambda m, i, r, number: coefs[m, at + i, pl.ds(4 + r, number), :],
        lambda f, i: tile[f, start + i],
        lambda i: inject[1, at + i, pl.ds(4, rows), :],
        store,
    )


def fill(place, tile, old, beside, even, odd, window, old_wide, groups, with_beside=True):
    size_x = tile.shape[1]
    opening = old_wide is not None
    for f in range(2):
        window[f, pl.ds(0, 4)] = jnp.zeros((4, 32, 128), F32)
        window[f, pl.ds(place.wide + 4, 4)] = jnp.zeros((4, 32, 128), F32)
        needed = pl.ds(groups[0] * GROUP, groups[1] * GROUP)
        at = place.own_at + groups[0] * GROUP
        window[f, pl.ds(at + 4, groups[1] * GROUP), pl.ds(12, 8), :] = tile[f, needed]
        if opening:
            old_wide[f, pl.ds(at, groups[1] * GROUP), pl.ds(4, 8), :] = old[f, needed]

    def lay(block, base, planes, at, row):
        start, number = groups if planes == size_x else (0, 1)
        there = {-8: place.has_below, 0: 1.0, 8: place.has_above}[row]
        factor = factor_of(block[base + planes], 0) * there

        def group(g):
            def put(f, p, rows):
                window[f, at + g * GROUP + p + 4, pl.ds(row + 12, 8), :] = rows

            decode(block, base + g * TILES, factor, put)

        loop(number, lambda g: group(start + g), 2)
        if not opening:
            return
        factor = factor_of(block[base + planes], 1) * there
        if planes == GROUP:
            plane = at + jnp.where(at > 0, 0, 4)
            for f in range(2):
                for q in range(2 if row == 0 else 1):
                    tile_at = base + planes + 1 + (2 * f + q if row == 0 else f)
                    rows = block[tile_at].astype(jnp.int32).astype(F32)
                    if row == 0:
                        for v in range(2):
                            old_wide[f, plane + 2 * q + v, pl.ds(4, 8), :] = (
                                rows[8 * v : 8 * v + 8] * factor
                            )
                    else:
                        near = factor[4:] if row < 0 else factor[:4]
                        for v in range(4):
                            old_wide[f, plane + v, pl.ds(0 if row < 0 else 12, 4), :] = (
                                rows[4 * v : 4 * v + 4] * near
                            )
            return

        def old_group(g):
            def put(f, p, rows):
                first = 0 if row < 0 else row + 4
                old_wide[f, at + g * GROUP + p, pl.ds(first, rows.shape[0]), :] = rows

            start = base + planes + 1
            if row == 0:
                decode(block, start + g * TILES, factor, put)
            else:
                near = factor[4:] if row < 0 else factor[:4]
                decode_nearest(block, start + g * (TILES // 2), near, put)

        loop(number, lambda g: old_group(start + g), 2)

    sides = place.sides if with_beside else 0
    for k in range(sides):
        lay(beside[k], 0, GROUP, place.beside_at[k], 0)

    def lay_y(below, above):
        kept = 4 if opening else 0
        for block, row in ((below, -8), (above, 8)):
            lay(block, 0, size_x, place.own_at, row)
            for k in range(sides):
                base = block_size(size_x, kept) + k * block_size(GROUP, kept // 2)
                lay(block, base, GROUP, place.beside_at[k], row)

    pl.when(place.parity == 0)(lambda: lay_y(odd, even))
    pl.when(place.parity == 1)(lambda: lay_y(even, odd))


def lead_kernel(opening, columns, tile, old, coefs, inject, mat_first, mat_second, *refs):
    place = Place(tile.shape[1], columns)
    refs = list(refs)

    def take(number):
        taken = refs[:number]
        del refs[:number]
        return taken

    sides = place.sides
    beside = take(sides)
    even, odd = take(2)
    around_out, edges_out, codes_out = take(sides), take(sides), take(sides)
    middle, window = take(2)
    old_wide = take(1)[0] if opening else None
    scratch, mats = refs, (mat_first, mat_second)
    fill(place, tile, old, beside, even, odd, window, old_wide, place.lead_groups)
    for k in range(sides):
        def store_around(i, new_p, new_q):
            for f, new in enumerate((new_p, new_q)):
                around_out[k][f, i] = new
                middle[f, i, pl.ds(4, new.shape[0]), :] = new

        def store_edge(i, new_p, new_q):
            edges_out[k][0, i] = new_p
            edges_out[k][1, i] = new_q

        first_leap(
            place, place.around_at[k], AROUND, window, old_wide if opening else old,
            place.first_at if opening else 0, coefs, inject, scratch, mats, store_around,
        )
        second_leap(
            place, place.edge_at[k], GROUP, middle, 0, tile, coefs, inject, scratch, mats,
            store_edge,
        )
        encode(lambda f, p: edges_out[k][f, p], GROUP, codes_out[k])


def rest_kernel(opening, columns, tile, old, coefs, inject, mat_first, mat_second, *refs):
    size_x, size_y = tile.shape[1], tile.shape[2]
    place = Place(size_x, columns)
    sides, count = place.sides, place.count
    around, edges, beside = refs[:sides], refs[sides : 2 * sides], refs[2 * sides : 3 * sides]
    even, odd, tile_out, payload, old_out, middle, window, *scratch = refs[3 * sides :]
    old_wide = scratch.pop(0) if opening else None
    mats = (mat_first, mat_second)
    fill(place, tile, old, beside, even, odd, window, old_wide, place.rest_groups, sides > 1)
    old_now = old_wide if opening else old
    for f in range(2):
        middle[f, pl.ds(0, 4)] = jnp.zeros((4, 24, 128), F32)
        middle[f, pl.ds(count + 4, 4)] = jnp.zeros((4, 24, 128), F32)
        for k in range(sides):
            at = place.around_at[k]
            middle[f, pl.ds(at + 4, AROUND), pl.ds(4, size_y + 8), :] = around[k][f]
            old_out[f, pl.ds(at, AROUND)] = around[k][f]
            tile_out[f, pl.ds(place.edge_at[k], GROUP)] = edges[k][f]

    def store_first(i, new_p, new_q):
        for f, new in enumerate((new_p, new_q)):
            old_out[f, place.first_rest_at + i] = new
            middle[f, place.first_rest_at + i + 4, pl.ds(4, size_y + 8), :] = new

    def store_second(i, new_p, new_q):
        tile_out[0, place.rest_at + i] = new_p
        tile_out[1, place.rest_at + i] = new_q

    first_leap(
        place, place.first_rest_at, count - AROUND * sides, window, old_now,
        place.first_at if opening else 0, coefs, inject, scratch, mats, store_first,
    )
    second_leap(
        place, place.rest_at, place.rest, middle, place.tile_at + place.rest_at, tile, coefs,
        inject, scratch, mats, store_second,
    )
    encode(lambda f, p: tile_out[f, p], size_x, payload)


def last_kernel(columns, tile, old, coefs, inject, mat_first, mat_second, *refs):
    size_x, size_y = tile.shape[1], tile.shape[2]
    place = Place(size_x, columns)
    sides, count = place.sides, place.count
    even, odd, kept, sent, middle, tile_out, window, *scratch = refs[sides:]
    mats = (mat_first, mat_second)
    fill(place, tile, old, refs[:sides], even, odd, window, None, (0, size_x // GROUP))
    for f in range(2):
        middle[f, pl.ds(0, 4)] = jnp.zeros((4, 24, 128), F32)
        middle[f, pl.ds(count + 4, 4)] = jnp.zeros((4, 24, 128), F32)

    def store_first(i, new_p, new_q):
        for f, new in enumerate((new_p, new_q)):
            middle[f, i + 4, pl.ds(4, size_y + 8), :] = new

    def store_second(i, new_p, new_q):
        tile_out[0, i] = new_p
        tile_out[1, i] = new_q

    first_leap(place, 0, count, window, old, 0, coefs, inject, scratch, mats, store_first)
    second_leap(
        place, 0, size_x, middle, place.tile_at, tile, coefs, inject, scratch, mats, store_second
    )
    half = size_x // 2
    for mine in range(2):
        @pl.when(place.core == mine)
        def _():
            for out, start in ((kept, mine * half), (sent, (1 - mine) * half)):
                planes = pl.ds(start, half)
                inner = pl.ds(place.tile_at + 4 + start, half)
                out[0] = middle[0, inner, pl.ds(8, size_y), :]
                out[1] = tile_out[0, planes]
                out[2] = tile_out[1, planes]


def sine_cosine(angle):
    square = angle * angle
    sine = 1.0 / 6227020800.0
    for factor in (-1.0 / 39916800.0, 1.0 / 362880.0, -1.0 / 5040.0, 1.0 / 120.0, -1.0 / 6.0):
        sine = sine * square + factor
    sine = angle + angle * square * sine
    cosine = 1.0 / 479001600.0
    for factor in (-1.0 / 3628800.0, 1.0 / 40320.0, -1.0 / 720.0, 1.0 / 24.0, -0.5):
        cosine = cosine * square + factor
    return sine, 1.0 + square * cosine


def open_kernel(
    velocity, epsilon, delta, tilt, azimuth, source, receiver, *refs
):
    models = (velocity, epsilon, delta, tilt, azimuth)
    parity = lax.rem(lax.axis_index("gy"), 2)
    core = lax.rem(lax.axis_index("gx"), 2)
    small, (even, odd, own, kept, given), brought, arrived = (
        refs[:3], refs[3:8], refs[8:11], refs[11]
    )
    copies = [pltpu.make_async_copy(models[m], own.at[m], arrived.at[m]) for m in range(5)]
    others = [
        pltpu.make_async_copy(small[m], brought[m], arrived.at[7 + m]) for m in range(3)
    ]

    def states(mine):
        stay, leave = (source, receiver) if mine == 0 else (receiver, source)
        return (
            pltpu.make_async_copy(stay, kept, arrived.at[5]),
            pltpu.make_async_copy(leave, given, arrived.at[6]),
        )

    for copy in copies + others:
        copy.start()
    for mine in range(2):
        @pl.when(core == mine)
        def _():
            for copy in states(mine):
                copy.start()

    for copy in copies:
        copy.wait()

    def pack(out, row):
        for m in range(5):
            for u in range(0, own.shape[1], 2):
                pairs = [own[m, u + k].astype(F32) for k in range(2)]
                values = [pair[v + row : v + row + 4] for pair in pairs for v in (0, 8)]
                out[m, u // 2] = jnp.concatenate(values).astype(BF16)

    @pl.when(parity == 0)
    def _():
        pack(even, 4)
        pack(odd, 0)

    @pl.when(parity == 1)
    def _():
        pack(odd, 4)
        pack(even, 0)

    for mine in range(2):
        @pl.when(core == mine)
        def _():
            for copy in states(mine):
                copy.wait()
    for copy in others:
        copy.wait()


def join_kernel(own, even, odd, out):
    at_y = lax.axis_index("gy")
    parity = lax.rem(at_y, 2)
    has_below = jnp.where(at_y > 0, 1.0, 0.0)
    has_above = jnp.where(at_y < lax.axis_size("gy") - 1, 1.0, 0.0)

    def fill(below, above):
        for m in range(5):
            for u in range(own.shape[1]):
                low = below[m, u // 2].astype(F32) * has_below
                high = above[m, u // 2].astype(F32) * has_above
                pair = own[m, u].astype(F32)
                for v in range(2):
                    k = 2 * (u % 2) + v
                    rows = [low[4 * k : 4 * k + 4], pair[8 * v : 8 * v + 8], high[4 * k : 4 * k + 4]]
                    out[m, 2 * u + v] = jnp.concatenate(rows).astype(BF16)

    pl.when(parity == 0)(lambda: fill(odd, even))
    pl.when(parity == 1)(lambda: fill(even, odd))


def setup_kernel(columns, size_x, total_x, aperture, *refs):
    models, coefs, blocks = refs[:-2], refs[-2], refs[-1]
    place = Place(2 * size_x, columns)
    if len(models) > 1:
        for k, column in enumerate((place.column, 1 - place.column)):
            for j, core in enumerate((place.core, 1 - place.core)):
                blocks[:, pl.ds((2 * column + core) * size_x, size_x)] = models[2 * k + j][...]
        source = blocks
    else:
        source = models[0]

    def medium(i):
        x = place.start_x + i
        block = jnp.clip(x // size_x, 0, total_x // size_x - 1)
        inside = jnp.logical_and(x >= 0, x < total_x)
        at = aperture[block] * size_x + lax.rem(x + size_x, size_x)
        speed, stretch, bending, tilt, azimuth = [source[m, at].astype(F32) for m in range(5)]
        speed = jnp.where(inside, speed, 0.0)
        sin_t, cos_t = sine_cosine(tilt)
        sin_half, cos_half = sine_cosine(0.5 * azimuth)
        normal_x = sin_t * (1.0 - 2.0 * sin_half * sin_half)
        normal_y = sin_t * (2.0 * sin_half * cos_half)
        coefs[0, i] = speed
        coefs[1, i] = speed * (1.0 + 2.0 * stretch)
        coefs[2, i] = speed * jnp.sqrt(1.0 + 2.0 * bending)
        weights = (S1 * (normal_x * normal_x), S1 * (normal_y * normal_y), SECOND_UNIT * (cos_t * cos_t))
        for m, unit in enumerate((S1, S1, SECOND_UNIT)):
            coefs[3 + m, i] = weights[m]
            coefs[9 + m, i] = unit - weights[m]
        coefs[6, i] = (2.0 * G1 * G1) * (normal_x * normal_y)
        coefs[7, i] = (2.0 * G1 * FIRST_UNIT) * (normal_y * cos_t)
        coefs[8, i] = (2.0 * G1 * FIRST_UNIT) * (normal_x * cos_t)

    loop(place.count, medium, 6)


def injection_kernel(
    columns, size_x, size_y, total_y, source_cell, wavelet, cells, traces, out, hits
):
    place = Place(size_x, columns)
    count, rows = hits.shape[:2]
    number = cells.shape[1]
    row = lax.broadcasted_iota(jnp.int32, (rows, number), 0)
    lane = lax.broadcasted_iota(jnp.int32, (1, number), 1)
    is_source = place.core == 0
    lonely = jnp.where(lane == 0, source_cell[0], -1)
    aims = jnp.where(is_source, lonely, cells[...])
    y = place.at_y * size_y - 4 + row
    valid = jnp.logical_and(y >= 0, y < total_y)

    def mark(i):
        code = jnp.where(valid, (place.start_x + i) * total_y + y, -2)
        hits[i] = jnp.where(code == aims, 1.0, 0.0).astype(BF16)

    loop(count, mark, 2)
    step = lax.broadcasted_iota(jnp.int32, (NT, number), 0)
    amounts = jnp.zeros((NT, number), F32)
    for k in range(NT):
        amounts = jnp.where(step == k, wavelet[:, k : k + 1], amounts)
    backward = jnp.concatenate([traces[k : k + 1] for k in reversed(range(NT))])
    rest = jnp.where(is_source, amounts, backward)
    total = None
    for _ in range(3):
        piece = rest.astype(BF16)
        rest = rest - piece.astype(F32)
        term = lax.dot_general(
            hits[...].reshape(count * rows, number), piece, (((1,), (1,)), ((), ())),
            preferred_element_type=F32,
        )
        total = term if total is None else total + term
    out[...] = total.reshape(count, rows, NT)


def spread_kernel(moment, lanes, out):
    core = lax.rem(lax.axis_index("gx"), 2)
    level = jnp.where(core == 0, SRC_DEPTH, REC_DEPTH)
    mask = (lax.broadcasted_iota(jnp.int32, (lanes.shape[1], 128), 1) == level).astype(F32)

    def expand(i):
        values = lanes[i]
        for k in range(2):
            out[k, i] = values[:, moment + k : moment + k + 1] * mask

    loop(lanes.shape[0], expand, 6)


def sort_kernel(columns, *refs):
    levels, (kept, sent) = refs[: NT - 1], refs[NT - 1 :]
    half, size_y = kept.shape[1:3]
    place = Place(2 * half, columns)

    def level_at(step, start):
        where = levels[step]
        if step % 2 == 0:
            return where[0, pl.ds(start, half)]
        return where[0, pl.ds(place.tile_at + start, half), pl.ds(4, size_y), :]

    for mine in range(2):
        @pl.when(place.core == mine)
        def _():
            for step in range(NT - 1):
                t = step if mine == 0 else NT - step
                if t > 0:
                    kept[t - 1] = level_at(step, mine * half)
                    sent[t - 1] = level_at(step, (1 - mine) * half)


def close_kernel(kept, got, last_kept, last_got, image, field):
    core = lax.rem(lax.axis_index("gx"), 2)
    total = kept[1] * got[1]
    for t in range(2, NT - 2):
        total = total + kept[t] * got[t]

    @pl.when(core == 0)
    def _():
        image[...] = (
            total + kept[0] * last_got[0] + last_kept[0] * got[NT - 2] + last_kept[1] * got[NT - 1]
        ) * (1.0 / NT)
        field[...] = last_got[pl.ds(1, 2)]

    @pl.when(core == 1)
    def _():
        image[...] = (
            total + last_kept[0] * got[0] + kept[NT - 2] * last_got[0] + kept[NT - 1] * last_got[1]
        ) * (1.0 / NT)
        field[...] = last_kept[pl.ds(1, 2)]


def per_device(
    velocity,
    epsilon,
    delta,
    tilt,
    azimuth,
    aperture,
    source_cell,
    wavelet,
    receiver_cell,
    traces,
    source_state,
    receiver_state,
):
    block_x, size_y, _ = velocity.shape
    devices_x, devices_y = lax.axis_size("gx"), lax.axis_size("gy")
    columns = devices_x // 2
    total_x, total_y = block_x * devices_x, size_y * devices_y
    size_x, rows = 2 * block_x, size_y + 8
    is_source = lax.axis_index("gx") % 2 == 0
    place = Place(size_x, columns)
    sides, count = place.sides, place.count
    mats = depth_matrices(128)
    chip_pairs = [even_pairs(columns), odd_pairs(columns)][:sides]
    row_pairs = [even_pairs(devices_y), odd_pairs(devices_y)]
    trade = both_ways([(2 * c, 2 * c + 1) for c in range(columns)])

    def over_gy(values, pairs, opening=False):
        paired = {i for pair in pairs for i in pair}
        alone = [y for y in range(devices_y) if y not in paired]
        swaps = [(x * devices_y + a, x * devices_y + b) for x in range(devices_x) for a, b in pairs]
        swaps += [
            (a * devices_y + y, b * devices_y + y)
            for a, b in (even_pairs(devices_x) if opening else chip_swap(even_pairs(columns)))
            for y in alone
        ]
        return lax.ppermute(values, ("gx", "gy"), both_ways(swaps))

    def over_gx(values, pairs):
        return lax.ppermute(values, "gx", both_ways(chip_swap(pairs)))

    def beside_of(edges):
        return [over_gx(edge, pairs) for edge, pairs in zip(edges, chip_pairs)]

    def near_of(even, odd, opening=False):
        odd = over_gy(odd, row_pairs[1], opening)
        return over_gy(even, row_pairs[0], opening), odd

    def codes(planes, old_rows=0):
        return ((block_size(planes, old_rows), 16, 128), jnp.int16)

    models = [
        values.reshape(block_x // 2, 16, 128) for values in (velocity, epsilon, delta, tilt, azimuth)
    ]
    small = (wavelet[None, :], receiver_cell[None, :], traces)
    rim = ((5, block_x // 4, 16, 128), BF16)
    states = (source_state, receiver_state)
    state = (source_state.shape, F32)
    *rims, own, kept, given, series, cells, data = pl.pallas_call(
        open_kernel,
        out_shape=tuple(
            jax.ShapeDtypeStruct(*out)
            for out in (rim, rim, ((5, block_x // 2, 16, 128), BF16), state, state)
            + tuple((x.shape, x.dtype) for x in small)
        ),
        in_specs=[HBM] * 10,
        out_specs=(VMEM,) * 8,
        scratch_shapes=[pltpu.SemaphoreType.DMA((10,))],
        compiler_params=pltpu.CompilerParams(vmem_limit_bytes=8 * 2**20),
        name="open",
    )(*[pltpu.with_memory_space_constraint(x, pltpu.HBM) for x in (*models, *states, *small)])
    rims = [over_gy(values, pairs, True) for values, pairs in zip(rims, row_pairs)]

    got = lax.ppermute(given, "gx", trade)
    field = ((2, size_x, size_y, 128), F32)
    tile, old, payload, *edges = call(
        functools.partial(first_kernel, columns),
        (field, field, codes(size_x, 8)) + (codes(GROUP, 4),) * sides,
        (), 16, "first", (kept, got),
    )
    number = receiver_cell.shape[0]
    cells, _ = lax.optimization_barrier((cells, edges[0]))
    (amounts,) = call(
        functools.partial(injection_kernel, columns, size_x, size_y, total_y),
        (((count, rows, NT), F32),), (((count, rows, number), BF16),),
        16, "injection", (source_cell, series, cells, data), scalars=1,
    )
    beside = beside_of(edges)
    payload, _ = lax.optimization_barrier((payload, amounts))
    total = block_size(size_x, 4) + sides * block_size(GROUP, 2)
    wide = call(
        cut_kernel, (((total, 16, 128), jnp.int16),) * 2, (), 8, "cut", (payload, *beside)
    )
    near = near_of(*wide[::-1], opening=True)

    def spread(moment, after):
        lanes, _ = lax.optimization_barrier((amounts, after[0]))
        (out,) = call(
            functools.partial(spread_kernel, moment), (((2, count, rows, 128), F32),), (), 8,
            "spread", (lanes,),
        )
        return out

    inject = spread(0, wide)

    rims = lax.optimization_barrier((*rims, edges[0]))[:2]
    (model,) = call(
        join_kernel, (((5, block_x, rows, 128), BF16),), (), 8, "join", (own, *rims), work=1000
    )
    if columns == 2:
        later, _ = lax.optimization_barrier((model, wide[0]))
        across = over_gx(later, chip_pairs[0])
        early, _ = lax.optimization_barrier((model, inject))
        other = lax.ppermute(early, "gx", trade)
        gathered = [model, other, across, lax.ppermute(across, "gx", trade)]
        held = (5, total_x, rows, 128)
    else:
        gathered, held = [lax.all_gather(model, "gx", axis=1, tiled=True)], (16, 128)
    (coefs,) = call(
        functools.partial(setup_kernel, columns, block_x, total_x),
        (((12, count, rows, 128), F32),), ((held, BF16),), 24, "setup", (aperture, *gathered),
        scalars=1, work=0,
    )

    window = ((2, place.wide + 8, 32, 128), F32)
    middle = ((2, count + 8, 24, 128), F32)
    lines = ((2, count, rows, 128), F32)
    levels = [tile]
    for moment in range(0, NT - 2, 2):
        opening = moment == 0
        inject = inject if opening else spread(moment, wide)
        old_wide = (((2, place.wide, rows, 128), F32),) * opening
        around = (((2, AROUND, rows, 128), F32),) * sides
        edge = (((2, GROUP, size_y, 128), F32),) * sides
        filled = (window,) + old_wide
        outs = call(
            functools.partial(lead_kernel, opening, columns),
            around + edge + (codes(GROUP),) * sides,
            (((2, AROUND, 24, 128), F32),) + filled + tuple(leap_scratch(AROUND)), 24, "lead",
            (tile, old, coefs, inject, *mats, *beside, *near), work=2 * 10**6,
        )
        came = (*beside, *near)
        beside = beside_of(outs[2 * sides :])
        tile, payload, old = call(
            functools.partial(rest_kernel, opening, columns),
            (field, codes(size_x), lines),
            (middle,) + filled + tuple(leap_scratch(place.rest)), 24, "rest",
            (tile, old, coefs, inject, *mats, *outs[: 2 * sides], *came), work=4 * 10**6,
        )
        wide = (jnp.concatenate([payload, *beside]),) * 2
        near = near_of(*wide)
        levels += [old, tile]
    shape = (block_x, size_y, 128)
    inject = spread(NT - 2, wide)
    share = ((NT,) + shape, F32)
    kept, sent = call(
        functools.partial(sort_kernel, columns), (share, share), (), 8, "sort",
        lax.optimization_barrier((*levels, *near, inject))[: NT - 1],
    )
    got = lax.ppermute(sent, "gx", trade)
    share = ((3,) + shape, F32)
    last_kept, last_sent = call(
        functools.partial(last_kernel, columns),
        (share, share), [middle, field, window] + leap_scratch(count), 24, "last",
        (tile, old, coefs, inject, *mats, *beside, *near),
    )
    last_got = lax.ppermute(last_sent, "gx", trade)
    return call(
        close_kernel, ((shape, F32), ((2,) + shape, F32)), (), 8, "close",
        (kept, got, last_kept, last_got),
    )


def solution(mesh):
    in_specs = (
        P("gx", "gy", None),
        P("gx", "gy", None),
        P("gx", "gy", None),
        P("gx", "gy", None),
        P("gx", "gy", None),
        P("shot"),
        P("shot"),
        P("shot"),
        P("shot"),
        P(None, "shot"),
        P(None, ("shot", "gx"), "gy", None),
        P(None, ("shot", "gx"), "gy", None),
    )
    out_specs = (P(("shot", "gx"), "gy", None), P(None, ("shot", "gx"), "gy", None))
    return jax.shard_map(
        per_device, mesh=mesh, in_specs=in_specs, out_specs=out_specs, check_vma=False
    )
```

```python
import functools

import jax
import jax.numpy as jnp
from jax import lax
from jax.experimental import pallas as pl
from jax.experimental.pallas import tpu as pltpu
from jax.sharding import PartitionSpec as P

NT = 8
SRC_DEPTH = 10
REC_DEPTH = 6
F32 = jnp.float32
BF16 = jnp.bfloat16

second_taps = (-205.0 / 72.0, 8.0 / 5.0, -1.0 / 5.0, 8.0 / 315.0, -1.0 / 560.0)
first_taps = (4.0 / 5.0, -1.0 / 5.0, 4.0 / 105.0, -1.0 / 280.0)
CENTRE = second_taps[0]
S1 = second_taps[1]
G1 = first_taps[0]
second_ratio = tuple(tap / S1 for tap in second_taps[2:])
first_ratio = tuple(tap / G1 for tap in first_taps[1:])
second_whole = (8064.0, -1008.0, 128.0, -9.0)
first_whole = (672.0, -168.0, 32.0, -3.0)
SECOND_UNIT = 1.0 / 5040.0
FIRST_UNIT = 1.0 / 840.0
VMEM = pl.BlockSpec(memory_space=pltpu.VMEM)
SMEM = pl.BlockSpec(memory_space=pltpu.SMEM)
HBM = pl.BlockSpec(memory_space=pltpu.HBM)


def even_pairs(count):
    return [(i, i + 1) for i in range(0, count - 1, 2)]


def odd_pairs(count):
    return [(i, i + 1) for i in range(1, count - 1, 2)]


def both_ways(pairs):
    return [pair for a, b in pairs for pair in ((a, b), (b, a))]


def chip_swap(pairs):
    return [(2 * a + c, 2 * b + c) for a, b in pairs for c in range(2)]


class Place:
    def __init__(self, size_x, columns):
        at_x = lax.axis_index("gx")
        self.core, self.column = lax.rem(at_x, 2), lax.div(at_x, 2)
        self.at_y = lax.axis_index("gy")
        self.parity = lax.rem(self.at_y, 2)
        self.has_below = jnp.where(self.at_y > 0, 1.0, 0.0)
        self.has_above = jnp.where(self.at_y < lax.axis_size("gy") - 1, 1.0, 0.0)
        if columns == 2:
            side = self.column
            self.count = size_x + 4
            self.first_at = self.tile_at = 4 * side
            self.start_x = side * (size_x - 4)
            self.beside_at = [size_x * (1 - side)]
            self.edge_at = [(size_x - GROUP) * (1 - side)]
            self.rest_at, self.rest = GROUP * side, size_x - GROUP
            self.first_rest_at = AROUND * side
            groups = size_x // GROUP
            self.lead_groups = ((groups - 2) * (1 - side), 2)
            self.rest_groups = (side, groups - 1)
        else:
            side = lax.rem(self.column, 2)
            self.count = size_x + 8
            self.first_at = self.tile_at = 4
            self.start_x = self.column * size_x - 4
            self.beside_at = [(size_x + GROUP) * (1 - side), (size_x + GROUP) * side]
            self.edge_at = [(size_x - GROUP) * (1 - side), (size_x - GROUP) * side]
            self.rest_at, self.rest = GROUP, size_x - 2 * GROUP
            self.first_rest_at = AROUND
            self.lead_groups = self.rest_groups = (0, size_x // GROUP)
        self.sides = len(self.beside_at)
        self.around_at = [self.tile_at + at - 4 for at in self.edge_at]
        self.own_at = self.first_at + self.tile_at
        self.wide = size_x + GROUP * self.sides


def call(kernel, outs, scratch, mebibytes, name, args, scalars=0, work=10**6):
    outs = tuple(jax.ShapeDtypeStruct(shape, dtype) for shape, dtype in outs)
    return pl.pallas_call(
        kernel,
        out_shape=outs,
        in_specs=[SMEM] * scalars + [VMEM] * (len(args) - scalars),
        out_specs=(VMEM,) * len(outs),
        scratch_shapes=[pltpu.VMEM(shape, dtype) for shape, dtype in scratch],
        compiler_params=pltpu.CompilerParams(vmem_limit_bytes=mebibytes * 2**20),
        cost_estimate=pl.CostEstimate(flops=work, bytes_accessed=work, transcendentals=0),
        name=name,
    )(*args)


def loop(trips, body, wanted):
    unroll = max(u for u in range(1, wanted + 1) if trips % u == 0)

    def step(i, carry):
        body(i)
        return carry

    lax.fori_loop(0, trips, step, 0, unroll=unroll)


def depth_matrices(size):
    rows = jnp.arange(size)[:, None]
    cols = jnp.arange(size)[None, :]
    first = jnp.zeros((size, size), F32)
    second = jnp.zeros((size, size), F32)
    for k in range(1, 5):
        up = (rows == cols + k).astype(F32)
        down = (rows == cols - k).astype(F32)
        first = first + first_whole[k - 1] * (up - down)
        second = second + second_whole[k - 1] * (up + down)
    return (
        jnp.concatenate([first, first]).astype(BF16),
        jnp.concatenate([second, second]).astype(BF16),
    )


def sums_and_slopes(shifted):
    up, down = shifted(1), shifted(-1)
    curve, slope = up + down, up - down
    for k in range(2, 5):
        up, down = shifted(k), shifted(-k)
        curve = curve + second_ratio[k - 2] * (up + down)
        slope = slope + first_ratio[k - 2] * (up - down)
    return curve, slope


def slope_only(shifted):
    slope = shifted(1) - shifted(-1)
    for k in range(2, 5):
        slope = slope + first_ratio[k - 2] * (shifted(k) - shifted(-k))
    return slope


def split(values):
    high = values.astype(BF16)
    low = (values - high.astype(F32)).astype(BF16)
    return high, low


TOP = 32000.0
GROUP = 8
AROUND = GROUP + 8
TILES = GROUP


def block_size(planes, old_rows=0):
    return planes + 1 + planes * old_rows // 8


def scale_of(value_at, planes):
    def grow(i, size):
        for f in range(2):
            size = jnp.maximum(size, jnp.abs(value_at(f, i)))
        return size

    size = lax.fori_loop(0, planes, grow, jnp.full((8, 128), 1e-30, F32), unroll=8)
    code = jnp.ceil(jnp.log2(size) * 256.0)
    return code, TOP * jnp.exp2(code * (-1.0 / 256.0))


def as_code(pieces):
    return jnp.concatenate(pieces).astype(jnp.int32).astype(jnp.int16)


def encode(value_at, planes, out, old_at=None):
    code, factor = scale_of(value_at, planes)
    old_code, old_factor = scale_of(old_at, planes) if old_at else (code, None)

    def put(source, base, by):
        def group(g):
            for f in range(2):
                for q in range(4):
                    pair = [source(f, g * GROUP + 2 * q + v) for v in range(2)]
                    whole = [jnp.floor(value * by + 0.5) for value in pair]
                    out[base + g * TILES + 4 * f + q] = as_code(whole)

        loop(planes // GROUP, group, 1)

    put(value_at, 0, factor)
    out[planes] = as_code([code, old_code])
    if old_at:
        put(old_at, planes + 1, old_factor)


def factor_of(scales, half):
    code = scales.astype(jnp.int32).astype(F32)[8 * half : 8 * half + 8]
    return jnp.exp2(code * (1.0 / 256.0)) * (1.0 / TOP)


def decode(block, base, factor, put):
    for f in range(2):
        for q in range(4):
            both = block[base + 4 * f + q].astype(jnp.int32).astype(F32)
            put(f, 2 * q, both[:8] * factor)
            put(f, 2 * q + 1, both[8:] * factor)


def decode_nearest(block, base, factor, put):
    by = jnp.concatenate([factor] * 4)
    for f in range(2):
        for q in range(2):
            rows = block[base + 2 * f + q].astype(jnp.int32).astype(F32) * by
            for v in range(4):
                put(f, 4 * q + v, rows[4 * v : 4 * v + 4])


def leap(src, x0, row0, rows, count, scratch, mats, coef, old_at, inject_at, store):
    slope_y, curve_y, part, halves, product = scratch
    mat_first, mat_second = mats
    planes = 16 // rows
    group = 4

    def field(f, p, r=0, number=rows):
        return src[f, x0 + p, pl.ds(row0 + r, number), :]

    def joined(values):
        return jnp.concatenate(values) if len(values) > 1 else values[0]

    def put_halves(kind, f, unit, values):
        high, low = split(values)
        halves[kind, f, unit, :, :128] = high
        halves[kind, f, unit, :, 128:] = low

    def along_y(u):
        for f in range(2):
            here, slopes = [], []
            for v in range(planes):
                p = u * planes + v
                curve, slope = sums_and_slopes(lambda k: field(f, p, k))
                slope_y[f, p, :rows] = slope
                curve_y[f, p, :rows] = curve
                slopes.append(slope)
                here.append(field(f, p))
            put_halves(0, f, u, joined(here))
            put_halves(1, f, u, joined(slopes))

    loop((count + 8) // planes, along_y, 24)

    def along_x(q):
        base = q * group
        for f in range(2):
            slopes = [[] for g in range(group)]
            for r in range(0, rows, 8):
                line = [field(f, base + k, r, 8) for k in range(group + 8)]
                slant = [slope_y[f, base + k, pl.ds(r, 8), :] for k in range(group + 8)]
                for g in range(group):
                    i = base + g
                    xx, slope = sums_and_slopes(lambda k: line[g + 4 + k])
                    xy = slope_only(lambda k: slant[g + 4 + k])
                    yy = curve_y[f, i + 4, pl.ds(r, 8), :]
                    wx, wy, wxy = [coef(m, i, r, 8) for m in (3, 4, 6)]
                    if f == 0:
                        total = (2.0 * CENTRE) * line[g + 4] + (S1 - wx) * xx
                        total = total + (S1 - wy) * yy - wxy * xy
                    else:
                        total = CENTRE * line[g + 4] + wx * xx
                        total = total + wy * yy + wxy * xy
                    part[f, i, pl.ds(r, 8), :] = total
                    slopes[g].append(slope)
            pieces = [piece for rest in slopes for piece in rest]
            for k in range(0, len(pieces), 2):
                put_halves(2, f, q * (len(pieces) // 2) + k // 2, joined(pieces[k : k + 2]))

    loop(count // group, along_x, 10)

    units = count // planes
    for kind, mat, at in ((0, mat_second, 4 // planes), (1, mat_first, 4 // planes), (2, mat_first, 0)):
        for f in range(2):
            both = halves[kind, f, pl.ds(at, units)].reshape(units * 16, 256)
            out = jnp.dot(both, mat[...], preferred_element_type=F32)
            product[kind, f, pl.ds(0, units)] = out.reshape(units, 16, 128)

    def combine(u):
        where = [u * planes + v for v in range(planes)]
        speed, speed_h, speed_v, wz, wyz, wxz = [
            joined([coef(m, i, 0, rows) for i in where]) for m in (0, 1, 2, 5, 7, 8)
        ]
        zz, yz, xz = [[product[kind, f, u] for f in range(2)] for kind in range(3)]
        parts = [joined([part[f, i, :rows] for i in where]) for f in range(2)]
        here = [joined([field(f, i + 4) for i in where]) for f in range(2)]
        old = [joined([old_at(f, i) for i in where]) for f in range(2)]
        add = joined([inject_at(i) for i in where])
        flat = parts[0] + (SECOND_UNIT - wz) * zz[0] - (wyz * yz[0] + wxz * xz[0])
        tilted = parts[1] + wz * zz[1] + (wyz * yz[1] + wxz * xz[1])
        new_p = (2.0 * here[0] - old[0] + add) + (speed_h * flat + speed_v * tilted)
        new_q = (2.0 * here[1] - old[1] + add) + (speed_v * flat + speed * tilted)
        for v, i in enumerate(where):
            cut = slice(v * rows, v * rows + rows)
            store(i, new_p[cut], new_q[cut])

    loop(units, combine, 36)


def leap_scratch(count):
    lines = (2, count + 8, 16, 128)
    return [
        (lines, F32),
        (lines, F32),
        ((2, count, 16, 128), F32),
        ((3, 2, count + 8, 16, 256), BF16),
        ((3, 2, count, 16, 128), F32),
    ]


def first_kernel(columns, kept, got, tile, old, payload, *edges):
    size = kept.shape[1]
    place = Place(2 * size, columns)
    for source, at in ((kept, place.core * size), (got, (1 - place.core) * size)):
        for f in range(2):
            tile[f, pl.ds(at, size)] = source[2 * f]
            old[f, pl.ds(at, size)] = source[2 * f + 1]

    encode(lambda f, p: tile[f, p], 2 * size, payload, lambda f, p: old[f, p])
    for k, edge in enumerate(edges):
        group = lax.div(place.edge_at[k], GROUP) * TILES
        edge[pl.ds(0, TILES)] = payload[pl.ds(group, TILES)]
        edge[GROUP] = payload[2 * size]
        nearest = 2 * lax.div(place.edge_at[k], 2 * size - GROUP)
        for f in range(2):
            start = 2 * size + 1 + group + 4 * f + nearest
            edge[pl.ds(GROUP + 1 + 2 * f, 2)] = payload[pl.ds(start, 2)]


def cut_kernel(payload, *refs):
    beside, (odd, even) = refs[:-2], refs[-2:]
    parity = lax.rem(lax.axis_index("gy"), 2)

    def cut(out, row):
        base = 0
        for block in (payload, *beside):
            planes = block.shape[0] // 2 if block is payload else GROUP
            out[pl.ds(base, planes + 1)] = block[: planes + 1]
            old_tiles = block.shape[0] - planes - 1
            for u in range(0, old_tiles, 2):
                pairs = [block[planes + 1 + u + v].astype(jnp.int32) for v in range(2)]
                rows = [pair[r + row : r + row + 4] for pair in pairs for r in (0, 8)]
                out[base + planes + 1 + u // 2] = jnp.concatenate(rows).astype(jnp.int16)
            base += planes + 1 + old_tiles // 2

    @pl.when(parity == 0)
    def _():
        cut(even, 4)
        cut(odd, 0)

    @pl.when(parity == 1)
    def _():
        cut(odd, 4)
        cut(even, 0)


def first_leap(place, start, count, window, old, old_start, coefs, inject, scratch, mats, store):
    leap(
        window, place.first_at + start, 8, coefs.shape[2], count, scratch, mats,
        lambda m, i, r, number: coefs[m, start + i, pl.ds(r, number), :],
        lambda f, i: old[f, old_start + start + i],
        lambda i: inject[0, start + i],
        store,
    )


def second_leap(
    place, start, count, source, source_start, tile, coefs, inject, scratch, mats, store
):
    rows = tile.shape[2]
    at = place.tile_at + start
    leap(
        source, source_start, 8, rows, count, scratch, mats,
        lambda m, i, r, number: coefs[m, at + i, pl.ds(4 + r, number), :],
        lambda f, i: tile[f, start + i],
        lambda i: inject[1, at + i, pl.ds(4, rows), :],
        store,
    )


def fill(place, tile, old, beside, even, odd, window, old_wide, groups, with_beside=True):
    size_x = tile.shape[1]
    opening = old_wide is not None
    for f in range(2):
        window[f, pl.ds(0, 4)] = jnp.zeros((4, 32, 128), F32)
        window[f, pl.ds(place.wide + 4, 4)] = jnp.zeros((4, 32, 128), F32)
        needed = pl.ds(groups[0] * GROUP, groups[1] * GROUP)
        at = place.own_at + groups[0] * GROUP
        window[f, pl.ds(at + 4, groups[1] * GROUP), pl.ds(12, 8), :] = tile[f, needed]
        if opening:
            old_wide[f, pl.ds(at, groups[1] * GROUP), pl.ds(4, 8), :] = old[f, needed]

    def lay(block, base, planes, at, row):
        start, number = groups if planes == size_x else (0, 1)
        there = {-8: place.has_below, 0: 1.0, 8: place.has_above}[row]
        factor = factor_of(block[base + planes], 0) * there

        def group(g):
            def put(f, p, rows):
                window[f, at + g * GROUP + p + 4, pl.ds(row + 12, 8), :] = rows

            decode(block, base + g * TILES, factor, put)

        loop(number, lambda g: group(start + g), 2)
        if not opening:
            return
        factor = factor_of(block[base + planes], 1) * there
        if planes == GROUP:
            plane = at + jnp.where(at > 0, 0, 4)
            for f in range(2):
                for q in range(2 if row == 0 else 1):
                    tile_at = base + planes + 1 + (2 * f + q if row == 0 else f)
                    rows = block[tile_at].astype(jnp.int32).astype(F32)
                    if row == 0:
                        for v in range(2):
                            old_wide[f, plane + 2 * q + v, pl.ds(4, 8), :] = (
                                rows[8 * v : 8 * v + 8] * factor
                            )
                    else:
                        near = factor[4:] if row < 0 else factor[:4]
                        for v in range(4):
                            old_wide[f, plane + v, pl.ds(0 if row < 0 else 12, 4), :] = (
                                rows[4 * v : 4 * v + 4] * near
                            )
            return

        def old_group(g):
            def put(f, p, rows):
                first = 0 if row < 0 else row + 4
                old_wide[f, at + g * GROUP + p, pl.ds(first, rows.shape[0]), :] = rows

            start = base + planes + 1
            if row == 0:
                decode(block, start + g * TILES, factor, put)
            else:
                near = factor[4:] if row < 0 else factor[:4]
                decode_nearest(block, start + g * (TILES // 2), near, put)

        loop(number, lambda g: old_group(start + g), 2)

    sides = place.sides if with_beside else 0
    for k in range(sides):
        lay(beside[k], 0, GROUP, place.beside_at[k], 0)

    def lay_y(below, above):
        kept = 4 if opening else 0
        for block, row in ((below, -8), (above, 8)):
            lay(block, 0, size_x, place.own_at, row)
            for k in range(sides):
                base = block_size(size_x, kept) + k * block_size(GROUP, kept // 2)
                lay(block, base, GROUP, place.beside_at[k], row)

    pl.when(place.parity == 0)(lambda: lay_y(odd, even))
    pl.when(place.parity == 1)(lambda: lay_y(even, odd))


def lead_kernel(opening, columns, tile, old, coefs, inject, mat_first, mat_second, *refs):
    place = Place(tile.shape[1], columns)
    refs = list(refs)

    def take(number):
        taken = refs[:number]
        del refs[:number]
        return taken

    sides = place.sides
    beside = take(sides)
    even, odd = take(2)
    around_out, edges_out, codes_out = take(sides), take(sides), take(sides)
    middle, window = take(2)
    old_wide = take(1)[0] if opening else None
    scratch, mats = refs, (mat_first, mat_second)
    fill(place, tile, old, beside, even, odd, window, old_wide, place.lead_groups)
    for k in range(sides):
        def store_around(i, new_p, new_q):
            for f, new in enumerate((new_p, new_q)):
                around_out[k][f, i] = new
                middle[f, i, pl.ds(4, new.shape[0]), :] = new

        def store_edge(i, new_p, new_q):
            edges_out[k][0, i] = new_p
            edges_out[k][1, i] = new_q

        first_leap(
            place, place.around_at[k], AROUND, window, old_wide if opening else old,
            place.first_at if opening else 0, coefs, inject, scratch, mats, store_around,
        )
        second_leap(
            place, place.edge_at[k], GROUP, middle, 0, tile, coefs, inject, scratch, mats,
            store_edge,
        )
        encode(lambda f, p: edges_out[k][f, p], GROUP, codes_out[k])


def rest_kernel(opening, columns, tile, old, coefs, inject, mat_first, mat_second, *refs):
    size_x, size_y = tile.shape[1], tile.shape[2]
    place = Place(size_x, columns)
    sides, count = place.sides, place.count
    around, edges, beside = refs[:sides], refs[sides : 2 * sides], refs[2 * sides : 3 * sides]
    even, odd, tile_out, payload, old_out, middle, window, *scratch = refs[3 * sides :]
    old_wide = scratch.pop(0) if opening else None
    mats = (mat_first, mat_second)
    fill(place, tile, old, beside, even, odd, window, old_wide, place.rest_groups, sides > 1)
    old_now = old_wide if opening else old
    for f in range(2):
        middle[f, pl.ds(0, 4)] = jnp.zeros((4, 24, 128), F32)
        middle[f, pl.ds(count + 4, 4)] = jnp.zeros((4, 24, 128), F32)
        for k in range(sides):
            at = place.around_at[k]
            middle[f, pl.ds(at + 4, AROUND), pl.ds(4, size_y + 8), :] = around[k][f]
            old_out[f, pl.ds(at, AROUND)] = around[k][f]
            tile_out[f, pl.ds(place.edge_at[k], GROUP)] = edges[k][f]

    def store_first(i, new_p, new_q):
        for f, new in enumerate((new_p, new_q)):
            old_out[f, place.first_rest_at + i] = new
            middle[f, place.first_rest_at + i + 4, pl.ds(4, size_y + 8), :] = new

    def store_second(i, new_p, new_q):
        tile_out[0, place.rest_at + i] = new_p
        tile_out[1, place.rest_at + i] = new_q

    first_leap(
        place, place.first_rest_at, count - AROUND * sides, window, old_now,
        place.first_at if opening else 0, coefs, inject, scratch, mats, store_first,
    )
    second_leap(
        place, place.rest_at, place.rest, middle, place.tile_at + place.rest_at, tile, coefs,
        inject, scratch, mats, store_second,
    )
    encode(lambda f, p: tile_out[f, p], size_x, payload)


def last_kernel(columns, tile, old, coefs, inject, mat_first, mat_second, *refs):
    size_x, size_y = tile.shape[1], tile.shape[2]
    place = Place(size_x, columns)
    sides, count = place.sides, place.count
    even, odd, kept, sent, middle, tile_out, window, *scratch = refs[sides:]
    mats = (mat_first, mat_second)
    fill(place, tile, old, refs[:sides], even, odd, window, None, (0, size_x // GROUP))
    for f in range(2):
        middle[f, pl.ds(0, 4)] = jnp.zeros((4, 24, 128), F32)
        middle[f, pl.ds(count + 4, 4)] = jnp.zeros((4, 24, 128), F32)

    def store_first(i, new_p, new_q):
        for f, new in enumerate((new_p, new_q)):
            middle[f, i + 4, pl.ds(4, size_y + 8), :] = new

    def store_second(i, new_p, new_q):
        tile_out[0, i] = new_p
        tile_out[1, i] = new_q

    first_leap(place, 0, count, window, old, 0, coefs, inject, scratch, mats, store_first)
    second_leap(
        place, 0, size_x, middle, place.tile_at, tile, coefs, inject, scratch, mats, store_second
    )
    half = size_x // 2
    for mine in range(2):
        @pl.when(place.core == mine)
        def _():
            for out, start in ((kept, mine * half), (sent, (1 - mine) * half)):
                planes = pl.ds(start, half)
                inner = pl.ds(place.tile_at + 4 + start, half)
                out[0] = middle[0, inner, pl.ds(8, size_y), :]
                out[1] = tile_out[0, planes]
                out[2] = tile_out[1, planes]


def sine_cosine(angle):
    square = angle * angle
    sine = 1.0 / 6227020800.0
    for factor in (-1.0 / 39916800.0, 1.0 / 362880.0, -1.0 / 5040.0, 1.0 / 120.0, -1.0 / 6.0):
        sine = sine * square + factor
    sine = angle + angle * square * sine
    cosine = 1.0 / 479001600.0
    for factor in (-1.0 / 3628800.0, 1.0 / 40320.0, -1.0 / 720.0, 1.0 / 24.0, -0.5):
        cosine = cosine * square + factor
    return sine, 1.0 + square * cosine


def open_kernel(
    velocity, epsilon, delta, tilt, azimuth, source, receiver, *refs
):
    models = (velocity, epsilon, delta, tilt, azimuth)
    parity = lax.rem(lax.axis_index("gy"), 2)
    core = lax.rem(lax.axis_index("gx"), 2)
    small, (even, odd, own, kept, given), brought, arrived = (
        refs[:3], refs[3:8], refs[8:11], refs[11]
    )
    copies = [pltpu.make_async_copy(models[m], own.at[m], arrived.at[m]) for m in range(5)]
    others = [
        pltpu.make_async_copy(small[m], brought[m], arrived.at[7 + m]) for m in range(3)
    ]

    def states(mine):
        stay, leave = (source, receiver) if mine == 0 else (receiver, source)
        return (
            pltpu.make_async_copy(stay, kept, arrived.at[5]),
            pltpu.make_async_copy(leave, given, arrived.at[6]),
        )

    for copy in copies + others:
        copy.start()
    for mine in range(2):
        @pl.when(core == mine)
        def _():
            for copy in states(mine):
                copy.start()

    for copy in copies:
        copy.wait()

    def pack(out, row):
        for m in range(5):
            for u in range(0, own.shape[1], 2):
                pairs = [own[m, u + k].astype(F32) for k in range(2)]
                values = [pair[v + row : v + row + 4] for pair in pairs for v in (0, 8)]
                out[m, u // 2] = jnp.concatenate(values).astype(BF16)

    @pl.when(parity == 0)
    def _():
        pack(even, 4)
        pack(odd, 0)

    @pl.when(parity == 1)
    def _():
        pack(odd, 4)
        pack(even, 0)

    for mine in range(2):
        @pl.when(core == mine)
        def _():
            for copy in states(mine):
                copy.wait()
    for copy in others:
        copy.wait()


def join_kernel(own, even, odd, out):
    at_y = lax.axis_index("gy")
    parity = lax.rem(at_y, 2)
    has_below = jnp.where(at_y > 0, 1.0, 0.0)
    has_above = jnp.where(at_y < lax.axis_size("gy") - 1, 1.0, 0.0)

    def fill(below, above):
        for m in range(5):
            for u in range(own.shape[1]):
                low = below[m, u // 2].astype(F32) * has_below
                high = above[m, u // 2].astype(F32) * has_above
                pair = own[m, u].astype(F32)
                for v in range(2):
                    k = 2 * (u % 2) + v
                    rows = [low[4 * k : 4 * k + 4], pair[8 * v : 8 * v + 8], high[4 * k : 4 * k + 4]]
                    out[m, 2 * u + v] = jnp.concatenate(rows).astype(BF16)

    pl.when(parity == 0)(lambda: fill(odd, even))
    pl.when(parity == 1)(lambda: fill(even, odd))


def setup_kernel(columns, size_x, total_x, aperture, *refs):
    models, coefs, blocks = refs[:-2], refs[-2], refs[-1]
    place = Place(2 * size_x, columns)
    if len(models) > 1:
        for k, column in enumerate((place.column, 1 - place.column)):
            for j, core in enumerate((place.core, 1 - place.core)):
                blocks[:, pl.ds((2 * column + core) * size_x, size_x)] = models[2 * k + j][...]
        source = blocks
    else:
        source = models[0]

    def medium(i):
        x = place.start_x + i
        block = jnp.clip(x // size_x, 0, total_x // size_x - 1)
        inside = jnp.logical_and(x >= 0, x < total_x)
        at = aperture[block] * size_x + lax.rem(x + size_x, size_x)
        speed, stretch, bending, tilt, azimuth = [source[m, at].astype(F32) for m in range(5)]
        speed = jnp.where(inside, speed, 0.0)
        sin_t, cos_t = sine_cosine(tilt)
        sin_half, cos_half = sine_cosine(0.5 * azimuth)
        normal_x = sin_t * (1.0 - 2.0 * sin_half * sin_half)
        normal_y = sin_t * (2.0 * sin_half * cos_half)
        coefs[0, i] = speed
        coefs[1, i] = speed * (1.0 + 2.0 * stretch)
        coefs[2, i] = speed * jnp.sqrt(1.0 + 2.0 * bending)
        coefs[3, i] = S1 * (normal_x * normal_x)
        coefs[4, i] = S1 * (normal_y * normal_y)
        coefs[5, i] = SECOND_UNIT * (cos_t * cos_t)
        coefs[6, i] = (2.0 * G1 * G1) * (normal_x * normal_y)
        coefs[7, i] = (2.0 * G1 * FIRST_UNIT) * (normal_y * cos_t)
        coefs[8, i] = (2.0 * G1 * FIRST_UNIT) * (normal_x * cos_t)

    loop(place.count, medium, 6)


def injection_kernel(
    columns, size_x, size_y, total_y, source_cell, wavelet, cells, traces, out, hits
):
    place = Place(size_x, columns)
    count, rows = hits.shape[:2]
    number = cells.shape[1]
    row = lax.broadcasted_iota(jnp.int32, (rows, number), 0)
    lane = lax.broadcasted_iota(jnp.int32, (1, number), 1)
    is_source = place.core == 0
    lonely = jnp.where(lane == 0, source_cell[0], -1)
    aims = jnp.where(is_source, lonely, cells[...])
    y = place.at_y * size_y - 4 + row
    valid = jnp.logical_and(y >= 0, y < total_y)

    def mark(i):
        code = jnp.where(valid, (place.start_x + i) * total_y + y, -2)
        hits[i] = jnp.where(code == aims, 1.0, 0.0).astype(BF16)

    loop(count, mark, 2)
    step = lax.broadcasted_iota(jnp.int32, (NT, number), 0)
    amounts = jnp.zeros((NT, number), F32)
    for k in range(NT):
        amounts = jnp.where(step == k, wavelet[:, k : k + 1], amounts)
    backward = jnp.concatenate([traces[k : k + 1] for k in reversed(range(NT))])
    rest = jnp.where(is_source, amounts, backward)
    total = None
    for _ in range(3):
        piece = rest.astype(BF16)
        rest = rest - piece.astype(F32)
        term = lax.dot_general(
            hits[...].reshape(count * rows, number), piece, (((1,), (1,)), ((), ())),
            preferred_element_type=F32,
        )
        total = term if total is None else total + term
    out[...] = total.reshape(count, rows, NT)


def spread_kernel(moment, lanes, out):
    core = lax.rem(lax.axis_index("gx"), 2)
    level = jnp.where(core == 0, SRC_DEPTH, REC_DEPTH)
    mask = (lax.broadcasted_iota(jnp.int32, (lanes.shape[1], 128), 1) == level).astype(F32)

    def expand(i):
        values = lanes[i]
        for k in range(2):
            out[k, i] = values[:, moment + k : moment + k + 1] * mask

    loop(lanes.shape[0], expand, 6)


def sort_kernel(columns, *refs):
    levels, (kept, sent) = refs[: NT - 1], refs[NT - 1 :]
    half, size_y = kept.shape[1:3]
    place = Place(2 * half, columns)

    def level_at(step, start):
        where = levels[step]
        if step % 2 == 0:
            return where[0, pl.ds(start, half)]
        return where[0, pl.ds(place.tile_at + start, half), pl.ds(4, size_y), :]

    for mine in range(2):
        @pl.when(place.core == mine)
        def _():
            for step in range(NT - 1):
                t = step if mine == 0 else NT - step
                if t > 0:
                    kept[t - 1] = level_at(step, mine * half)
                    sent[t - 1] = level_at(step, (1 - mine) * half)


def close_kernel(kept, got, last_kept, last_got, image, field):
    core = lax.rem(lax.axis_index("gx"), 2)
    total = kept[1] * got[1]
    for t in range(2, NT - 2):
        total = total + kept[t] * got[t]

    @pl.when(core == 0)
    def _():
        image[...] = (
            total + kept[0] * last_got[0] + last_kept[0] * got[NT - 2] + last_kept[1] * got[NT - 1]
        ) * (1.0 / NT)
        field[...] = last_got[pl.ds(1, 2)]

    @pl.when(core == 1)
    def _():
        image[...] = (
            total + last_kept[0] * got[0] + kept[NT - 2] * last_got[0] + kept[NT - 1] * last_got[1]
        ) * (1.0 / NT)
        field[...] = last_kept[pl.ds(1, 2)]


def per_device(
    velocity,
    epsilon,
    delta,
    tilt,
    azimuth,
    aperture,
    source_cell,
    wavelet,
    receiver_cell,
    traces,
    source_state,
    receiver_state,
):
    block_x, size_y, _ = velocity.shape
    devices_x, devices_y = lax.axis_size("gx"), lax.axis_size("gy")
    columns = devices_x // 2
    total_x, total_y = block_x * devices_x, size_y * devices_y
    size_x, rows = 2 * block_x, size_y + 8
    is_source = lax.axis_index("gx") % 2 == 0
    place = Place(size_x, columns)
    sides, count = place.sides, place.count
    mats = depth_matrices(128)
    chip_pairs = [even_pairs(columns), odd_pairs(columns)][:sides]
    row_pairs = [even_pairs(devices_y), odd_pairs(devices_y)]
    trade = both_ways([(2 * c, 2 * c + 1) for c in range(columns)])

    def over_gy(values, pairs, opening=False):
        paired = {i for pair in pairs for i in pair}
        alone = [y for y in range(devices_y) if y not in paired]
        swaps = [(x * devices_y + a, x * devices_y + b) for x in range(devices_x) for a, b in pairs]
        swaps += [
            (a * devices_y + y, b * devices_y + y)
            for a, b in (even_pairs(devices_x) if opening else chip_swap(even_pairs(columns)))
            for y in alone
        ]
        return lax.ppermute(values, ("gx", "gy"), both_ways(swaps))

    def over_gx(values, pairs):
        return lax.ppermute(values, "gx", both_ways(chip_swap(pairs)))

    def beside_of(edges):
        return [over_gx(edge, pairs) for edge, pairs in zip(edges, chip_pairs)]

    def near_of(even, odd, opening=False):
        odd = over_gy(odd, row_pairs[1], opening)
        return over_gy(even, row_pairs[0], opening), odd

    def codes(planes, old_rows=0):
        return ((block_size(planes, old_rows), 16, 128), jnp.int16)

    models = [
        values.reshape(block_x // 2, 16, 128) for values in (velocity, epsilon, delta, tilt, azimuth)
    ]
    small = (wavelet[None, :], receiver_cell[None, :], traces)
    rim = ((5, block_x // 4, 16, 128), BF16)
    states = (source_state, receiver_state)
    state = (source_state.shape, F32)
    *rims, own, kept, given, series, cells, data = pl.pallas_call(
        open_kernel,
        out_shape=tuple(
            jax.ShapeDtypeStruct(*out)
            for out in (rim, rim, ((5, block_x // 2, 16, 128), BF16), state, state)
            + tuple((x.shape, x.dtype) for x in small)
        ),
        in_specs=[HBM] * 10,
        out_specs=(VMEM,) * 8,
        scratch_shapes=[pltpu.SemaphoreType.DMA((10,))],
        compiler_params=pltpu.CompilerParams(vmem_limit_bytes=8 * 2**20),
        name="open",
    )(*[pltpu.with_memory_space_constraint(x, pltpu.HBM) for x in (*models, *states, *small)])
    rims = [over_gy(values, pairs, True) for values, pairs in zip(rims, row_pairs)]

    got = lax.ppermute(given, "gx", trade)
    field = ((2, size_x, size_y, 128), F32)
    tile, old, payload, *edges = call(
        functools.partial(first_kernel, columns),
        (field, field, codes(size_x, 8)) + (codes(GROUP, 4),) * sides,
        (), 16, "first", (kept, got),
    )
    number = receiver_cell.shape[0]
    cells, _ = lax.optimization_barrier((cells, edges[0]))
    (amounts,) = call(
        functools.partial(injection_kernel, columns, size_x, size_y, total_y),
        (((count, rows, NT), F32),), (((count, rows, number), BF16),),
        16, "injection", (source_cell, series, cells, data), scalars=1,
    )
    beside = beside_of(edges)
    payload, _ = lax.optimization_barrier((payload, amounts))
    total = block_size(size_x, 4) + sides * block_size(GROUP, 2)
    wide = call(
        cut_kernel, (((total, 16, 128), jnp.int16),) * 2, (), 8, "cut", (payload, *beside)
    )
    near = near_of(*wide[::-1], opening=True)

    def spread(moment, after):
        lanes, _ = lax.optimization_barrier((amounts, after[0]))
        (out,) = call(
            functools.partial(spread_kernel, moment), (((2, count, rows, 128), F32),), (), 8,
            "spread", (lanes,),
        )
        return out

    inject = spread(0, wide)

    rims = lax.optimization_barrier((*rims, edges[0]))[:2]
    (model,) = call(
        join_kernel, (((5, block_x, rows, 128), BF16),), (), 8, "join", (own, *rims), work=1000
    )
    if columns == 2:
        later, _ = lax.optimization_barrier((model, wide[0]))
        across = over_gx(later, chip_pairs[0])
        early, _ = lax.optimization_barrier((model, inject))
        other = lax.ppermute(early, "gx", trade)
        gathered = [model, other, across, lax.ppermute(across, "gx", trade)]
        held = (5, total_x, rows, 128)
    else:
        gathered, held = [lax.all_gather(model, "gx", axis=1, tiled=True)], (16, 128)
    (coefs,) = call(
        functools.partial(setup_kernel, columns, block_x, total_x),
        (((9, count, rows, 128), F32),), ((held, BF16),), 24, "setup", (aperture, *gathered),
        scalars=1, work=0,
    )

    window = ((2, place.wide + 8, 32, 128), F32)
    middle = ((2, count + 8, 24, 128), F32)
    lines = ((2, count, rows, 128), F32)
    levels = [tile]
    for moment in range(0, NT - 2, 2):
        opening = moment == 0
        inject = inject if opening else spread(moment, wide)
        old_wide = (((2, place.wide, rows, 128), F32),) * opening
        around = (((2, AROUND, rows, 128), F32),) * sides
        edge = (((2, GROUP, size_y, 128), F32),) * sides
        filled = (window,) + old_wide
        outs = call(
            functools.partial(lead_kernel, opening, columns),
            around + edge + (codes(GROUP),) * sides,
            (((2, AROUND, 24, 128), F32),) + filled + tuple(leap_scratch(AROUND)), 24, "lead",
            (tile, old, coefs, inject, *mats, *beside, *near), work=2 * 10**6,
        )
        came = (*beside, *near)
        beside = beside_of(outs[2 * sides :])
        tile, payload, old = call(
            functools.partial(rest_kernel, opening, columns),
            (field, codes(size_x), lines),
            (middle,) + filled + tuple(leap_scratch(place.rest)), 24, "rest",
            (tile, old, coefs, inject, *mats, *outs[: 2 * sides], *came), work=4 * 10**6,
        )
        wide = (jnp.concatenate([payload, *beside]),) * 2
        near = near_of(*wide)
        levels += [old, tile]
    shape = (block_x, size_y, 128)
    inject = spread(NT - 2, wide)
    share = ((NT,) + shape, F32)
    kept, sent = call(
        functools.partial(sort_kernel, columns), (share, share), (), 8, "sort",
        lax.optimization_barrier((*levels, *near, inject))[: NT - 1],
    )
    got = lax.ppermute(sent, "gx", trade)
    share = ((3,) + shape, F32)
    last_kept, last_sent = call(
        functools.partial(last_kernel, columns),
        (share, share), [middle, field, window] + leap_scratch(count), 24, "last",
        (tile, old, coefs, inject, *mats, *beside, *near),
    )
    last_got = lax.ppermute(last_sent, "gx", trade)
    return call(
        close_kernel, ((shape, F32), ((2,) + shape, F32)), (), 8, "close",
        (kept, got, last_kept, last_got),
    )


def solution(mesh):
    in_specs = (
        P("gx", "gy", None),
        P("gx", "gy", None),
        P("gx", "gy", None),
        P("gx", "gy", None),
        P("gx", "gy", None),
        P("shot"),
        P("shot"),
        P("shot"),
        P("shot"),
        P(None, "shot"),
        P(None, ("shot", "gx"), "gy", None),
        P(None, ("shot", "gx"), "gy", None),
    )
    out_specs = (P(("shot", "gx"), "gy", None), P(None, ("shot", "gx"), "gy", None))
    return jax.shard_map(
        per_device, mesh=mesh, in_specs=in_specs, out_specs=out_specs, check_vma=False
    )
```
